32 devices in a mesh: group: 2 (over x), tile: 8 (over z, y), draw: 2 (over core).
Axes of the slice: x: 2, y: 2, z: 4, core: 2. Of those that a mesh axis runs over, the one named last changes fastest.
Arguments:
- inputs: bfloat16 [4, 32, 270, 256], P(('group', 'draw'), 'tile'), parts along dimension 0, may hold values from -6 to 6
- land_mask: int32 [32, 270], P('tile'), may hold values 0 or 1
- kernel: float32 [7, 7, 256], replicated, may hold values from -0.875 to 0.875
- conv_bias: float32 [256], replicated, may hold values from -3 to 3
- norm_gain: float32 [256], replicated, may hold values from 0.1 to 1.9
- norm_bias: float32 [256], replicated, may hold values from -3 to 3
- w_in: bfloat16 [256, 1024], replicated, may hold values from -0.375 to 0.375
- b_in: float32 [1024], replicated, may hold values from -3 to 3
- w_out: bfloat16 [1024, 256], replicated, may hold values from -0.1875 to 0.1875
- b_out: float32 [256], replicated, may hold values from -3 to 3
- layer_scale: float32 [256], replicated, may hold values from 0.1 to 1.9
- cotangent: bfloat16 [4, 32, 270, 256], P(('group', 'draw'), 'tile'), parts along dimension 0, may hold values from -6 to 6
Outputs:
- output: bfloat16 [4, 32, 270, 256], P(('group', 'draw'), 'tile'), parts along dimension 0
- input_grad: bfloat16 [4, 32, 270, 256], P(('group', 'draw'), 'tile'), parts along dimension 0
- kernel_grad: float32 [14, 7, 256], P('group'), parts along dimension 0
- w_in_grad: float32 [512, 1024], P('group'), parts along dimension 0
- w_out_grad: float32 [2048, 256], P('group'), parts along dimension 0
- b_in_grad: float32 [2048], P('group'), parts along dimension 0
- channel_grads: float32 [10, 256], P('group'), parts along dimension 0
The draws below stay inside these ranges and needn't reach their ends.
There are 2 independent parts, one for each index of `group`. The reference program is written for one: setup_inputs(seed, part) draws one part's arguments, and reference() takes and returns one part's arrays. A program takes and returns all parts, laid end to end along the dimension named above; an argument that names none is the same for every part. Nothing has to cross between parts.
All inputs are finite; a program needn't handle non-finite values. No bound on the sum of `land_mask` on one device may be relied on, other than what follows from the above.
Results may differ from the reference program's by a relative error of at most 0.007.
Values may be sent and summed in bfloat16 or wider, within the bound.
No kernel may reach another device: no remote copies, remote signals or barrier semaphores. Data moves between devices by JAX's collectives and lax.ppermute only.
A program may use at most 64 MiB of HBM per device.

```python
import jax
import jax.numpy as jnp
from jax import lax

C = 256
HID = 1024
NLON = 270
NLAT = 32
NDRAW = 2


def touch_ends(array, own_key, least, top_value):
    longest = array.shape.index(max(array.shape))
    spots = []
    for shift in (0, 1):
        where = [jax.random.randint(jax.random.fold_in(own_key, axis), (), 0, length) for axis, length in enumerate(array.shape)]
        where[longest] = (where[longest] + shift) % array.shape[longest]
        spots.append(tuple(where))
    return array.at[spots[0]].set(least).at[spots[1]].set(top_value)


def steps_of(key, dims, pieces, least, high):
    def one(axis_at, shards_of):
        heights = jax.random.uniform(jax.random.fold_in(jax.random.fold_in(key, 6), axis_at), (shards_of,), jnp.float32, least / len(pieces), high / len(pieces))
        return jnp.repeat(jnp.exp(heights), dims[axis_at] // shards_of).reshape((-1,) + (1,) * (len(dims) - axis_at - 1))

    gain = one(*pieces[0])
    for cut in pieces[1:]:
        gain = gain * one(*cut)
    return gain


def bell_draw(rng, extent, width, reach, shards=(), held_as=jnp.bfloat16):
    gain = steps_of(rng, extent, shards, -0.22, 0.18) if shards else 1.0
    values = jax.random.normal(rng, extent, jnp.float32) * width * gain
    return jnp.minimum(jnp.maximum(values, -reach), reach).astype(held_as)


def setup_inputs(seed: int = 0, part: int = 0) -> dict:
    splits = jax.random.split(jax.random.key(seed), 13)
    part_keys = jax.random.split(jax.random.fold_in(splits[12], part), 13)
    return {
        "inputs": bell_draw(part_keys[0], (NDRAW, NLAT, NLON, C), 1.0, 6.0, ((0, 2), (1, 8))),
        "land_mask": touch_ends((jax.random.randint(splits[1], (NLAT, NLON), 0, 4) < 3).astype(jnp.int32), jax.random.fold_in(splits[1], 1), 0, 1),
        "kernel": bell_draw(splits[2], (7, 7, C), 49 ** -0.5, 0.875, (), jnp.float32),
        "conv_bias": bell_draw(splits[3], (C,), 0.5, 3.0, (), jnp.float32),
        "norm_gain": jnp.clip(1.0 + 0.18 * jax.random.normal(splits[4], (C,), jnp.float32), 0.1, 1.9),
        "norm_bias": bell_draw(splits[5], (C,), 0.5, 3.0, (), jnp.float32),
        "w_in": bell_draw(splits[6], (C, HID), C ** -0.5, 0.375),
        "b_in": bell_draw(splits[7], (HID,), 0.5, 3.0, (), jnp.float32),
        "w_out": bell_draw(splits[8], (HID, C), HID ** -0.5, 0.1875),
        "b_out": bell_draw(splits[9], (C,), 0.5, 3.0, (), jnp.float32),
        "layer_scale": jnp.clip(1.0 + 0.18 * jax.random.normal(splits[10], (C,), jnp.float32), 0.1, 1.9),
        "cotangent": bell_draw(part_keys[11], (NDRAW, NLAT, NLON, C), 1.0, 6.0, ((0, 2), (1, 8))),
    }


ROOT_TERM = 0.7978845608028654
CUBIC = 0.044715
EPSILON = 1e-06

def lon_wrap(values):
    return jnp.concatenate([values[:, :, -3:], values, values[:, :, :3]], axis=2)

def apply_taps(padded, weights, height, breadth):
    total = jnp.zeros((padded.shape[0], height, breadth, padded.shape[3]), jnp.float32)
    for row_off in range(7):
        for col_off in range(7):
            total = total + padded[:, row_off:row_off + height, col_off:col_off + breadth, :] * weights[row_off, col_off]
    return total

def kernel_terms(padded, grad_map, height, breadth):
    rows_list = []
    for row_off in range(7):
        cells_list = []
        for col_off in range(7):
            window = padded[:, row_off:row_off + height, col_off:col_off + breadth, :]
            cells_list.append(lax.optimization_barrier(jnp.sum(window * grad_map, axis=(0, 1, 2))))
        rows_list.append(jnp.stack(cells_list))
    return jnp.stack(rows_list)

def gelu_slope(hidden):
    inner = ROOT_TERM * (hidden + CUBIC * hidden * hidden * hidden)
    tanh_value = jnp.tanh(inner)
    return 0.5 * (1.0 + tanh_value) + 0.5 * hidden * (1.0 - tanh_value * tanh_value) * ROOT_TERM * (1.0 + 3.0 * CUBIC * hidden * hidden)

def forward_backward(state, padded_state, land_mask, kernel, conv_bias, norm_gain, norm_bias, w_in, b_in, w_out, b_out, layer_scale, cotangent, extend):
    height = state.shape[1]
    breadth = state.shape[2]
    channels = state.shape[3]
    wrapped = lon_wrap(padded_state.astype(jnp.float32))
    conv_out = apply_taps(wrapped, kernel, height, breadth) + conv_bias
    center = lax.optimization_barrier(jnp.mean(conv_out, axis=-1, keepdims=True))
    deviation = conv_out - center
    inv_std = lax.rsqrt(lax.optimization_barrier(jnp.mean(deviation * deviation, axis=-1, keepdims=True)) + EPSILON)
    unit = deviation * inv_std
    normed = (unit * norm_gain + norm_bias).astype(jnp.bfloat16).reshape(-1, channels)
    hidden = jnp.dot(normed, w_in, preferred_element_type=jnp.float32) + b_in
    inner = ROOT_TERM * (hidden + CUBIC * hidden * hidden * hidden)
    activated = (0.5 * hidden * (1.0 + jnp.tanh(inner))).astype(jnp.bfloat16)
    mixed = (jnp.dot(activated, w_out, preferred_element_type=jnp.float32) + b_out).reshape(state.shape)
    ocean = land_mask.astype(jnp.float32)[None, :, :, None]
    output = (state.astype(jnp.float32) + ocean * layer_scale * mixed).astype(jnp.bfloat16)
    upstream = cotangent.astype(jnp.float32)
    scale_part = lax.optimization_barrier(jnp.sum(ocean * upstream * mixed, axis=(0, 1, 2)))
    grad_mixed = (ocean * layer_scale * upstream).astype(jnp.bfloat16).reshape(-1, channels)
    out_bias_part = lax.optimization_barrier(jnp.sum(grad_mixed.astype(jnp.float32), axis=0))
    w_out_part = lax.dot_general(activated, grad_mixed, (((0,), (0,)), ((), ())), preferred_element_type=jnp.float32)
    grad_act = lax.dot_general(grad_mixed, w_out, (((1,), (1,)), ((), ())), preferred_element_type=jnp.float32)
    grad_hidden = (grad_act * gelu_slope(hidden)).astype(jnp.bfloat16)
    w_in_part = lax.dot_general(normed, grad_hidden, (((0,), (0,)), ((), ())), preferred_element_type=jnp.float32)
    hidden_bias_part = lax.optimization_barrier(jnp.sum(grad_hidden.astype(jnp.float32), axis=0))
    grad_normed = lax.dot_general(grad_hidden, w_in, (((1,), (1,)), ((), ())), preferred_element_type=jnp.float32).reshape(state.shape)
    gain_part = lax.optimization_barrier(jnp.sum(grad_normed * unit, axis=(0, 1, 2)))
    nbias_part = lax.optimization_barrier(jnp.sum(grad_normed, axis=(0, 1, 2)))
    scaled = grad_normed * norm_gain
    grad_conv = (inv_std * (scaled - lax.optimization_barrier(jnp.mean(scaled, axis=-1, keepdims=True)) - unit * lax.optimization_barrier(jnp.mean(scaled * unit, axis=-1, keepdims=True)))).astype(jnp.bfloat16)
    grad_float = grad_conv.astype(jnp.float32)
    conv_bias_part = lax.optimization_barrier(jnp.sum(grad_float, axis=(0, 1, 2)))
    kernel_part = kernel_terms(wrapped, grad_float, height, breadth)
    grad_padded = lon_wrap(extend(grad_conv).astype(jnp.float32))
    input_grad = (upstream + apply_taps(grad_padded, kernel[::-1, ::-1], height, breadth)).astype(jnp.bfloat16)
    channel_part = jnp.stack([conv_bias_part, gain_part, nbias_part, out_bias_part, scale_part])
    return (output, input_grad, kernel_part, w_in_part, w_out_part, hidden_bias_part, channel_part)

def lat_zeros(values):
    return jnp.pad(values, ((0, 0), (3, 3), (0, 0), (0, 0)))

def reference(inputs, land_mask, kernel, conv_bias, norm_gain, norm_bias, w_in, b_in, w_out, b_out, layer_scale, cotangent):
    results = forward_backward(inputs, lat_zeros(inputs), land_mask, kernel, conv_bias, norm_gain, norm_bias, w_in, b_in, w_out, b_out, layer_scale, cotangent, lat_zeros)
    output, input_grad, kernel_part, w_in_part, w_out_part, hidden_bias_part, channel_part = results
    factor = 1.0 / jnp.sqrt(jnp.float32(NDRAW * NLAT * NLON))
    return (output, input_grad, kernel_part * factor, w_in_part * factor, w_out_part * factor, hidden_bias_part * factor, channel_part * factor)
```

```python
import functools

import jax
import jax.numpy as jnp
from jax import lax
from jax.experimental import pallas as pl
from jax.experimental.pallas import tpu as pltpu
from jax.sharding import PartitionSpec as P

ROOT_TERM = 0.7978845608028654
CUBIC = 0.044715
EPSILON = 1e-06
F32 = jnp.float32
BF16 = jnp.bfloat16
LANES = 128
SUBS = 8
EDGE = 3
VMEM_LIMIT = 56 * 1024 * 1024


def dims_of(breadth):
    steps = -(-breadth // SUBS)
    return steps, steps * SUBS


def spread_row(row, nat, spread, slot, halves, breadth):
    steps, cells = dims_of(breadth)
    row = row.astype(F32)
    over = cells - breadth + EDGE
    for h in range(halves):
        part = row[:, h * LANES : (h + 1) * LANES]
        nat[h, SUBS : SUBS + breadth, :] = part
        nat[h, SUBS - EDGE : SUBS, :] = part[breadth - EDGE :]
        nat[h, SUBS + breadth : SUBS + breadth + over, :] = part[:over]
    for h in range(halves):
        for t in range(steps + 2 * EDGE):
            spread[h, slot, t] = nat[h, pl.ds(SUBS - EDGE + t, SUBS, stride=steps), :]


def gather_row(nat, h, breadth):
    return nat[h, SUBS : SUBS + breadth, :]


def fill_taps(kern_ref, taps, halves, flip):
    for i in range(7):
        for j in range(7):
            src = kern_ref[6 - i, 6 - j : 7 - j, :] if flip else kern_ref[i, j : j + 1, :]
            for h in range(halves):
                taps[h, i * 7 + j] = jnp.broadcast_to(src[:, h * LANES : (h + 1) * LANES], (SUBS, LANES))


def conv_run(spread, taps, h, p, start, length):
    total = [None] * length
    for i in range(7):
        weights = [taps[h, i * 7 + j] for j in range(7)]
        for u in range(length + 6):
            cell = spread[h, p + i, start + u]
            for j in range(7):
                t = u - j
                if 0 <= t < length:
                    term = cell * weights[j]
                    total[t] = term if total[t] is None else total[t] + term
    return total


def runs_of(steps):
    length = steps // 2 if steps % 2 == 0 else steps
    return steps // length, length


def main_kernel(
    own_ref, top_ref, bottom_ref, cot_ref, mask_ref, kern_ref, cbias_ref, gain_ref, nbias_ref, w_in_ref, b_in_ref,
    w_out_ref, b_out_ref, scale_ref,
    out_ref, gconv_ref, wgrad_ref, hsum_ref, chan_ref,
    nat, spread, taps, conv, units, cots, normed_s, act_s, gmix_s, ghid_s,
):
    height, breadth, channels = own_ref.shape
    hidden_units = w_in_ref.shape[1]
    halves = channels // LANES
    steps, cells = dims_of(breadth)

    fill_taps(kern_ref, taps, halves, False)
    for r in range(EDGE):
        spread_row(top_ref[r], nat, spread, r, halves, breadth)
        spread_row(bottom_ref[r], nat, spread, EDGE + height + r, halves, breadth)

    def spread_own(p, carry):
        spread_row(own_ref[p], nat, spread, EDGE + p, halves, breadth)
        return carry

    lax.fori_loop(0, height, spread_own, 0)

    n_runs, length = runs_of(steps)

    def conv_body(index, carry):
        run = index % n_runs
        p = (index // n_runs) % height
        h = index // (n_runs * height)
        start = run * length
        total = conv_run(spread, taps, h, p, start, length)
        base = pl.multiple_of((p * steps + start) * SUBS, SUBS)
        for t in range(length):
            conv[h, pl.ds(base + t * SUBS, SUBS), :] = total[t]
        return carry

    lax.fori_loop(0, halves * height * n_runs, conv_body, 0)

    hsum_ref[...] = jnp.zeros_like(hsum_ref)
    chan_ref[...] = jnp.zeros_like(chan_ref)
    width = 256
    inv_c = 1.0 / channels

    def joined(pieces):
        return jnp.concatenate(pieces, axis=1)

    def column_sum(values):
        return jnp.sum(values.reshape(values.shape[0] // SUBS, SUBS, values.shape[1]), axis=0)

    def row_body(p, carry):
        base = pl.multiple_of(p * cells, 16)
        rows = pl.ds(base, cells)
        cot = cot_ref[p].astype(F32)
        for h in range(halves):
            nat[h, SUBS : SUBS + breadth, :] = cot[:, h * LANES : (h + 1) * LANES]
        for h in range(halves):
            for t in range(steps):
                cots[t * SUBS : (t + 1) * SUBS, h * LANES : (h + 1) * LANES] = nat[
                    h, pl.ds(SUBS + t, SUBS, stride=steps), :
                ]
        values = joined([conv[h, rows, :] for h in range(halves)]) + cbias_ref[...]
        center = jnp.sum(values, axis=1, keepdims=True) * inv_c
        deviation = values - center
        inv_std = lax.rsqrt(jnp.sum(deviation * deviation, axis=1, keepdims=True) * inv_c + EPSILON)
        unit = deviation * inv_std
        units[...] = unit
        normed = (unit * gain_ref[...] + nbias_ref[...]).astype(BF16)
        normed_s[rows, :] = normed
        ocean = joined([mask_ref[rows, :]] * halves)
        upstream = jnp.where(ocean > 0, cots[...], 0.0)
        gmix = (scale_ref[...] * upstream).astype(BF16)
        gmix_s[rows, :] = gmix
        mixed = jnp.zeros((cells, channels), F32)
        grad_normed = jnp.zeros((cells, channels), F32)
        for c in range(0, hidden_units, width):
            cols = slice(c, c + width)
            hidden = jnp.dot(normed, w_in_ref[:, cols], preferred_element_type=F32) + b_in_ref[:, cols]
            grad_act = lax.dot_general(
                gmix, w_out_ref[cols, :], (((1,), (1,)), ((), ())), preferred_element_type=F32
            )
            square = hidden * hidden
            inner = hidden * (ROOT_TERM * CUBIC * square + ROOT_TERM)
            half_tanh = 0.5 * jnp.tanh(inner)
            gate = 0.5 + half_tanh
            active = hidden * gate
            slope = gate + active * (0.5 - half_tanh) * (6.0 * CUBIC * ROOT_TERM * square + 2.0 * ROOT_TERM)
            act = active.astype(BF16)
            act_s[rows, cols] = act
            mixed = mixed + jnp.dot(act, w_out_ref[cols, :], preferred_element_type=F32)
            ghid = (grad_act * slope).astype(BF16)
            ghid_s[rows, cols] = ghid
            hsum_ref[:, cols] += column_sum(ghid.astype(F32))
            grad_normed = grad_normed + lax.dot_general(
                ghid, w_in_ref[:, cols], (((1,), (1,)), ((), ())), preferred_element_type=F32
            )
        mixed = mixed + b_out_ref[...]
        unit = units[...]
        chan_ref[1] += column_sum(grad_normed * unit)
        chan_ref[2] += column_sum(grad_normed)
        chan_ref[3] += column_sum(gmix.astype(F32))
        upstream = jnp.where(ocean > 0, cots[...], 0.0)
        chan_ref[4] += column_sum(upstream * mixed)
        residual = jnp.where(ocean > 0, scale_ref[...] * mixed, 0.0)
        for h in range(halves):
            for t in range(steps):
                nat[h, pl.ds(SUBS + t, SUBS, stride=steps), :] = (
                    spread[h, EDGE + p, EDGE + t] + residual[t * SUBS : (t + 1) * SUBS, h * LANES : (h + 1) * LANES]
                )
        out_ref[p] = joined([gather_row(nat, h, breadth) for h in range(halves)]).astype(BF16)
        scaled = grad_normed * gain_ref[...]
        mean_scaled = jnp.sum(scaled, axis=1, keepdims=True) * inv_c
        mean_product = jnp.sum(scaled * unit, axis=1, keepdims=True) * inv_c
        grad_conv = (inv_std * (scaled - mean_scaled - unit * mean_product)).astype(BF16).astype(F32)
        chan_ref[0] += column_sum(grad_conv)
        for h in range(halves):
            for t in range(steps):
                nat[h, pl.ds(SUBS + t, SUBS, stride=steps), :] = grad_conv[
                    t * SUBS : (t + 1) * SUBS, h * LANES : (h + 1) * LANES
                ]
        gconv_ref[p] = joined([gather_row(nat, h, breadth) for h in range(halves)]).astype(BF16)
        return carry

    lax.fori_loop(0, height, row_body, 0)

    first = (((0,), (0,)), ((), ()))
    normed = normed_s[...]
    for c in range(0, hidden_units, width):
        cols = slice(c, c + width)
        wgrad_ref[cols, :] = lax.dot_general(normed, ghid_s[:, cols], first, preferred_element_type=F32)
    gmix = gmix_s[...]
    for c in range(0, hidden_units, width):
        cols = slice(c, c + width)
        wgrad_ref[hidden_units + c : hidden_units + c + width, :] = lax.dot_general(
            act_s[:, cols], gmix, first, preferred_element_type=F32
        )


def kernel_grad_kernel(own_ref, top_ref, bottom_ref, gconv_ref, hsum_ref, chan_ref, small_ref, nat, spread, grads, sums):
    height, breadth, channels = own_ref.shape
    halves = channels // LANES
    steps, cells = dims_of(breadth)
    for r in range(EDGE):
        spread_row(top_ref[r], nat, spread, r, halves, breadth)
        spread_row(bottom_ref[r], nat, spread, EDGE + height + r, halves, breadth)

    def spread_own(p, carry):
        spread_row(own_ref[p], nat, spread, EDGE + p, halves, breadth)
        return carry

    lax.fori_loop(0, height, spread_own, 0)

    nat[:, SUBS + breadth : SUBS + cells, :] = jnp.zeros((halves, cells - breadth, LANES), F32)

    def spread_grad(p, carry):
        row = gconv_ref[p].astype(F32)
        for h in range(halves):
            nat[h, SUBS : SUBS + breadth, :] = row[:, h * LANES : (h + 1) * LANES]
        for h in range(halves):
            for t in range(steps):
                grads[h, p, t] = nat[h, pl.ds(SUBS + t, SUBS, stride=steps), :]
        return carry

    lax.fori_loop(0, height, spread_grad, 0)

    def tap_body(index, carry):
        h = index // 7
        i = index % 7
        total = [None] * 7
        for p in range(height):
            window = [spread[h, p + i, t] for t in range(6)]
            for t in range(steps):
                window.append(spread[h, p + i, t + 6])
                grad = grads[h, p, t]
                for j in range(7):
                    term = window[t + j] * grad
                    total[j] = term if total[j] is None else total[j] + term
        for j in range(7):
            sums[h, i * 7 + j] = jnp.sum(total[j], axis=0, keepdims=True)
        return carry

    lax.fori_loop(0, halves * 7, tap_body, 0)
    rows = hsum_ref.shape[1] // channels
    small_ref[...] = jnp.zeros_like(small_ref)
    for h in range(halves):
        small_ref[0:49, h * LANES : (h + 1) * LANES] = sums[h].reshape(49, LANES)
    for c in range(rows):
        small_ref[49 + c : 50 + c, :] = jnp.sum(hsum_ref[:, c * channels : (c + 1) * channels], axis=0, keepdims=True)
    for c in range(5):
        small_ref[49 + rows + c : 50 + rows + c, :] = jnp.sum(chan_ref[c], axis=0, keepdims=True)


def input_grad_kernel(own_ref, top_ref, bottom_ref, kern_ref, cot_ref, grad_ref, nat, spread, taps):
    height, breadth, channels = own_ref.shape
    halves = channels // LANES
    steps, cells = dims_of(breadth)
    fill_taps(kern_ref, taps, halves, True)
    for r in range(EDGE):
        spread_row(top_ref[r], nat, spread, r, halves, breadth)
        spread_row(bottom_ref[r], nat, spread, EDGE + height + r, halves, breadth)

    def spread_own(p, carry):
        spread_row(own_ref[p], nat, spread, EDGE + p, halves, breadth)
        return carry

    lax.fori_loop(0, height, spread_own, 0)
    n_runs, length = runs_of(steps)

    def row_body(p, carry):
        def run_body(index, inner):
            h = index // n_runs
            start = (index % n_runs) * length
            total = conv_run(spread, taps, h, p, start, length)
            for t in range(length):
                nat[h, pl.ds(SUBS + start + t, SUBS, stride=steps), :] = total[t]
            return inner

        lax.fori_loop(0, halves * n_runs, run_body, 0)
        values = jnp.concatenate([gather_row(nat, h, breadth) for h in range(halves)], axis=1)
        grad_ref[p] = (cot_ref[p].astype(F32) + values).astype(BF16)
        return carry

    lax.fori_loop(0, height, row_body, 0)


def call(kernel, out_shape, scratch, flops, nbytes, name):
    def run(*operands):
        whole = pl.BlockSpec(memory_space=pltpu.VMEM)
        return pl.pallas_call(
            kernel,
            out_shape=out_shape,
            in_specs=[whole] * len(operands),
            out_specs=jax.tree.map(lambda _: whole, out_shape),
            scratch_shapes=scratch,
            compiler_params=pltpu.CompilerParams(vmem_limit_bytes=VMEM_LIMIT),
            cost_estimate=pl.CostEstimate(flops=flops, bytes_accessed=nbytes, transcendentals=0),
            name=name,
        )(*operands)

    return run


def digits_of(count):
    digits = []
    stride = 1
    while stride < count:
        size = 2 if (count // stride) % 4 or stride == 1 else 4
        digits.append((stride, size))
        stride *= size
    return digits


def exchange(values, axis, count, stride, size, k):
    return lax.ppermute(values, axis, [(i, i - (i // stride % size) * stride + ((i // stride % size) ^ k) * stride) for i in range(count)])


def scatter_sum(values, axis, count, stride, size):
    mine = lax.axis_index(axis) // stride % size
    share = values.shape[0] // size
    rounded = values.astype(BF16)
    received = [
        exchange(lax.dynamic_slice_in_dim(rounded, (mine ^ k) * share, share, 0), axis, count, stride, size, k)
        for k in range(1, size)
    ]
    total = lax.dynamic_slice_in_dim(values, mine * share, share, 0)
    for piece in received:
        total = total + piece.astype(F32)
    return total


def gather_shares(values, axis, count, stride, size):
    mine = lax.axis_index(axis) // stride % size
    share = values.shape[0]
    pieces = [values] + [exchange(values, axis, count, stride, size, k) for k in range(1, size)]
    if size == 2:
        low = jnp.where(mine == 0, pieces[0], pieces[1])
        high = jnp.where(mine == 0, pieces[1], pieces[0])
        return jnp.concatenate([low, high], axis=0)
    whole = jnp.zeros((share * size,) + values.shape[1:], values.dtype)
    for k in range(size):
        whole = lax.dynamic_update_slice_in_dim(whole, pieces[k], (mine ^ k) * share, 0)
    return whole


def sum_over(values, tiles, draws):
    plan = [("draw", draws, s, f) for s, f in digits_of(draws)] + [("tile", tiles, s, f) for s, f in digits_of(tiles)]
    for step in plan:
        values = scatter_sum(values, *step)
    values = values.astype(BF16)
    for step in plan[::-1]:
        values = gather_shares(values, *step)
    return values


def sum_small(values, tiles, draws):
    for axis, count in (("draw", draws), ("tile", tiles)):
        stride = 1
        while stride < count:
            values = values + exchange(values, axis, count, stride, 2, 1)
            stride *= 2
    return values


def halo(cells, tiles):
    after = [(i, i + 1) for i in range(tiles - 1)]
    before = [(i + 1, i) for i in range(tiles - 1)]
    top = lax.ppermute(cells[-EDGE:], "tile", after)
    bottom = lax.ppermute(cells[:EDGE], "tile", before)
    return top, bottom


def per_device(
    tiles,
    draws,
    inputs,
    land_mask,
    kernel,
    conv_bias,
    norm_gain,
    norm_bias,
    w_in,
    b_in,
    w_out,
    b_out,
    layer_scale,
    cotangent,
):
    _, height, breadth, channels = inputs.shape
    hidden_units = w_in.shape[1]
    halves = channels // LANES
    steps, cells = dims_of(breadth)
    own = inputs[0]
    cot = cotangent[0]
    top, bottom = halo(own, tiles)
    mask = jnp.pad(land_mask.astype(F32), ((0, 0), (0, cells - breadth)))
    mask = mask.reshape(height, SUBS, steps).transpose(0, 2, 1).reshape(height * cells, 1)
    mask = jnp.broadcast_to(mask, (height * cells, LANES))

    def row(vector):
        return vector.reshape(1, -1)

    nat = pltpu.VMEM((halves, cells + 2 * SUBS, LANES), F32)
    spread = pltpu.VMEM((halves, height + 2 * EDGE, steps + 2 * EDGE, SUBS, LANES), F32)
    taps = pltpu.VMEM((halves, 49, SUBS, LANES), F32)
    count = height * cells
    out, gconv, wgrad, hsum, chan = call(
        main_kernel,
        (
            jax.ShapeDtypeStruct((height, breadth, channels), BF16),
            jax.ShapeDtypeStruct((height, breadth, channels), BF16),
            jax.ShapeDtypeStruct((2 * hidden_units, channels), F32),
            jax.ShapeDtypeStruct((SUBS, hidden_units), F32),
            jax.ShapeDtypeStruct((5, SUBS, channels), F32),
        ),
        [
            nat,
            spread,
            taps,
            pltpu.VMEM((halves, count, LANES), F32),
            pltpu.VMEM((cells, channels), F32),
            pltpu.VMEM((cells, channels), F32),
            pltpu.VMEM((count, channels), BF16),
            pltpu.VMEM((count, hidden_units), BF16),
            pltpu.VMEM((count, channels), BF16),
            pltpu.VMEM((count, hidden_units), BF16),
        ],
        12 * count * channels * hidden_units,
        8 * 1024 * 1024,
        "block_main",
    )(
        own, top, bottom, cot, mask, kernel, row(conv_bias), row(norm_gain), row(norm_bias), w_in, row(b_in), w_out,
        row(b_out), row(layer_scale),
    )
    grad_top, grad_bottom = halo(gconv, tiles)
    small_rows = 64
    small = call(
        kernel_grad_kernel,
        jax.ShapeDtypeStruct((small_rows, channels), F32),
        [nat, spread, pltpu.VMEM((halves, height, steps, SUBS, LANES), F32), pltpu.VMEM((halves, 49, 1, LANES), F32)],
        4 * 1024 * 1024 * 1024,
        4 * 1024 * 1024,
        "kernel_grad",
    )(own, top, bottom, gconv, hsum, chan)
    input_grad = call(
        input_grad_kernel,
        jax.ShapeDtypeStruct((height, breadth, channels), BF16),
        [nat, spread, taps],
        4 * 1024 * 1024 * 1024,
        4 * 1024 * 1024,
        "input_grad",
    )(gconv, grad_top, grad_bottom, kernel, cot)

    total_cells = draws * height * tiles * breadth
    factor = 1.0 / jnp.sqrt(jnp.float32(total_cells))
    weights = sum_over(wgrad, tiles, draws).astype(F32) * factor
    small = sum_small(small, tiles, draws) * factor
    w_in_sum = weights[:hidden_units].reshape(hidden_units // channels, channels, channels)
    w_in_sum = jnp.concatenate([w_in_sum[c] for c in range(hidden_units // channels)], axis=1)
    rows = hidden_units // channels
    return (
        out[None],
        input_grad[None],
        small[:49].reshape(7, 7, channels),
        w_in_sum,
        weights[hidden_units:],
        small[49 : 49 + rows].reshape(-1),
        small[49 + rows : 54 + rows],
    )


def solution(mesh):
    placed = (
        P(("group", "draw"), "tile", None, None),
        P("tile", None),
        P(),
        P(),
        P(),
        P(),
        P(),
        P(),
        P(),
        P(),
        P(),
        P(("group", "draw"), "tile", None, None),
    )
    return jax.shard_map(
        functools.partial(per_device, mesh.shape["tile"], mesh.shape["draw"]),
        mesh=mesh,
        in_specs=placed,
        out_specs=(
            P(("group", "draw"), "tile", None, None),
            P(("group", "draw"), "tile", None, None),
            P("group", None, None),
            P("group", None),
            P("group", None),
            P("group"),
            P("group", None),
        ),
        check_vma=False,
    )
```

```python
import functools

import jax
import jax.numpy as jnp
import numpy as np
from jax import lax
from jax.experimental import pallas as pl
from jax.experimental.pallas import tpu as pltpu
from jax.sharding import PartitionSpec as P

ROOT_TERM = 0.7978845608028654
CUBIC = 0.044715
EPSILON = 1e-06
F32 = jnp.float32
BF16 = jnp.bfloat16
LANES = 128
SUBS = 8
EDGE = 3


def dims_of(breadth):
    steps = -(-breadth // SUBS)
    return steps, steps * SUBS


def spread_row(row, nat, spread, slot, halves, breadth):
    steps, cells = dims_of(breadth)
    row = row.astype(F32)
    over = cells - breadth + EDGE
    for h in range(halves):
        part = row[:, h * LANES : (h + 1) * LANES]
        nat[h, SUBS : SUBS + breadth, :] = part
        nat[h, SUBS - EDGE : SUBS, :] = part[breadth - EDGE :]
        nat[h, SUBS + breadth : SUBS + breadth + over, :] = part[:over]
    for h in range(halves):
        for t in range(steps + 2 * EDGE):
            spread[h, slot, t] = nat[h, pl.ds(SUBS - EDGE + t, SUBS, stride=steps), :]


def gather_row(nat, h, breadth):
    return nat[h, SUBS : SUBS + breadth, :]


def fill_taps(kern_ref, taps, halves, flip):
    for i in range(7):
        for j in range(7):
            src = kern_ref[6 - i, 6 - j : 7 - j, :] if flip else kern_ref[i, j : j + 1, :]
            for h in range(halves):
                taps[h, i * 7 + j] = jnp.broadcast_to(src[:, h * LANES : (h + 1) * LANES], (SUBS, LANES))


def conv_run(spread, taps, h, p, start, length):
    total = [None] * length
    for i in range(7):
        weights = [taps[h, i * 7 + j] for j in range(7)]
        for u in range(length + 6):
            cell = spread[h, p + i, start + u]
            for j in range(7):
                t = u - j
                if 0 <= t < length:
                    term = cell * weights[j]
                    total[t] = term if total[t] is None else total[t] + term
    return total


def runs_of(steps):
    length = steps // 2 if steps % 2 == 0 else steps
    return steps // length, length


def main_kernel(
    place_ref, own_ref, top_ref, bottom_ref, cot_ref, mask_ref, kern_ref, cbias_ref, gain_ref, nbias_ref, w_in_ref,
    b_in_ref, w_out_ref, b_out_ref, scale_ref,
    out_ref, gconv_ref, keep_ref, send_ref, hsum_ref, chan_ref,
    nat, spread, taps, conv, units, cots, normed_s, act_s, gmix_s, ghid_s,
):
    height, breadth, channels = own_ref.shape
    hidden_units = w_in_ref.shape[1]
    halves = channels // LANES
    steps, cells = dims_of(breadth)

    fill_taps(kern_ref, taps, halves, False)
    for r in range(EDGE):
        spread_row(top_ref[r], nat, spread, r, halves, breadth)
        spread_row(bottom_ref[r], nat, spread, EDGE + height + r, halves, breadth)

    def spread_own(p, carry):
        spread_row(own_ref[p], nat, spread, EDGE + p, halves, breadth)
        return carry

    lax.fori_loop(0, height, spread_own, 0)

    n_runs, length = runs_of(steps)

    def conv_body(index, carry):
        run = index % n_runs
        p = (index // n_runs) % height
        h = index // (n_runs * height)
        start = run * length
        total = conv_run(spread, taps, h, p, start, length)
        base = pl.multiple_of((p * steps + start) * SUBS, SUBS)
        for t in range(length):
            conv[h, pl.ds(base + t * SUBS, SUBS), :] = total[t]
        return carry

    lax.fori_loop(0, halves * height * n_runs, conv_body, 0)

    hsum_ref[...] = jnp.zeros_like(hsum_ref)
    chan_ref[...] = jnp.zeros_like(chan_ref)
    width = 256
    inv_c = 1.0 / channels

    def joined(pieces):
        return jnp.concatenate(pieces, axis=1)

    def column_sum(values):
        return jnp.sum(values.reshape(values.shape[0] // SUBS, SUBS, values.shape[1]), axis=0)

    def row_body(p, carry):
        base = pl.multiple_of(p * cells, 16)
        rows = pl.ds(base, cells)
        cot = cot_ref[p].astype(F32)
        for h in range(halves):
            nat[h, SUBS : SUBS + breadth, :] = cot[:, h * LANES : (h + 1) * LANES]
        for h in range(halves):
            for t in range(steps):
                cots[t * SUBS : (t + 1) * SUBS, h * LANES : (h + 1) * LANES] = nat[
                    h, pl.ds(SUBS + t, SUBS, stride=steps), :
                ]
        values = joined([conv[h, rows, :] for h in range(halves)]) + cbias_ref[...]
        center = jnp.sum(values, axis=1, keepdims=True) * inv_c
        deviation = values - center
        inv_std = lax.rsqrt(jnp.sum(deviation * deviation, axis=1, keepdims=True) * inv_c + EPSILON)
        unit = deviation * inv_std
        units[...] = unit
        normed = (unit * gain_ref[...] + nbias_ref[...]).astype(BF16)
        normed_s[rows, :] = normed
        ocean = joined([mask_ref[rows, :]] * halves)
        upstream = jnp.where(ocean > 0, cots[...], 0.0)
        gmix = (scale_ref[...] * upstream).astype(BF16)
        gmix_s[rows, :] = gmix
        mixed = jnp.zeros((cells, channels), F32)
        grad_normed = jnp.zeros((cells, channels), F32)
        for c in range(0, hidden_units, width):
            cols = slice(c, c + width)
            hidden = jnp.dot(normed, w_in_ref[:, cols], preferred_element_type=F32) + b_in_ref[:, cols]
            grad_act = lax.dot_general(
                gmix, w_out_ref[cols, :], (((1,), (1,)), ((), ())), preferred_element_type=F32
            )
            square = hidden * hidden
            inner = hidden * (ROOT_TERM * CUBIC * square + ROOT_TERM)
            half_tanh = 0.5 * jnp.tanh(inner)
            gate = 0.5 + half_tanh
            active = hidden * gate
            slope = gate + active * (0.5 - half_tanh) * (6.0 * CUBIC * ROOT_TERM * square + 2.0 * ROOT_TERM)
            act = active.astype(BF16)
            act_s[rows, cols] = act
            mixed = mixed + jnp.dot(act, w_out_ref[cols, :], preferred_element_type=F32)
            ghid = (grad_act * slope).astype(BF16)
            ghid_s[rows, cols] = ghid
            hsum_ref[:, cols] += column_sum(ghid.astype(F32))
            grad_normed = grad_normed + lax.dot_general(
                ghid, w_in_ref[:, cols], (((1,), (1,)), ((), ())), preferred_element_type=F32
            )
        mixed = mixed + b_out_ref[...]
        unit = units[...]
        chan_ref[1] += column_sum(grad_normed * unit)
        chan_ref[2] += column_sum(grad_normed)
        chan_ref[3] += column_sum(gmix.astype(F32))
        upstream = jnp.where(ocean > 0, cots[...], 0.0)
        chan_ref[4] += column_sum(upstream * mixed)
        residual = jnp.where(ocean > 0, scale_ref[...] * mixed, 0.0)
        for h in range(halves):
            for t in range(steps):
                nat[h, pl.ds(SUBS + t, SUBS, stride=steps), :] = (
                    spread[h, EDGE + p, EDGE + t] + residual[t * SUBS : (t + 1) * SUBS, h * LANES : (h + 1) * LANES]
                )
        out_ref[p] = joined([gather_row(nat, h, breadth) for h in range(halves)]).astype(BF16)
        scaled = grad_normed * gain_ref[...]
        mean_scaled = jnp.sum(scaled, axis=1, keepdims=True) * inv_c
        mean_product = jnp.sum(scaled * unit, axis=1, keepdims=True) * inv_c
        grad_conv = (inv_std * (scaled - mean_scaled - unit * mean_product)).astype(BF16).astype(F32)
        chan_ref[0] += column_sum(grad_conv)
        for h in range(halves):
            for t in range(steps):
                nat[h, pl.ds(SUBS + t, SUBS, stride=steps), :] = grad_conv[
                    t * SUBS : (t + 1) * SUBS, h * LANES : (h + 1) * LANES
                ]
        gconv_ref[p] = joined([gather_row(nat, h, breadth) for h in range(halves)]).astype(BF16)
        return carry

    lax.fori_loop(0, height, row_body, 0)

    first = (((0,), (0,)), ((), ()))

    def store_block(half, c, block):
        @pl.when(place_ref[0] == half)
        def _():
            keep_ref[c : c + width, :] = block

        @pl.when(place_ref[0] != half)
        def _():
            send_ref[c : c + width, :] = block.astype(BF16)

    normed = normed_s[...]
    for c in range(0, hidden_units, width):
        cols = slice(c, c + width)
        store_block(0, c, lax.dot_general(normed, ghid_s[:, cols], first, preferred_element_type=F32))
    gmix = gmix_s[...]
    for c in range(0, hidden_units, width):
        cols = slice(c, c + width)
        store_block(1, c, lax.dot_general(act_s[:, cols], gmix, first, preferred_element_type=F32))


def kernel_grad_kernel(
    size, place_ref, own_ref, top_ref, bottom_ref, gconv_ref, hsum_ref, chan_ref, keep_ref, got_ref, *rest
):
    shares, (nat, spread, grads, sums, total) = rest[:size], rest[size:]
    height, breadth, channels = own_ref.shape
    halves = channels // LANES
    steps, cells = dims_of(breadth)
    for r in range(EDGE):
        spread_row(top_ref[r], nat, spread, r, halves, breadth)
        spread_row(bottom_ref[r], nat, spread, EDGE + height + r, halves, breadth)

    def spread_own(p, carry):
        spread_row(own_ref[p], nat, spread, EDGE + p, halves, breadth)
        return carry

    lax.fori_loop(0, height, spread_own, 0)

    nat[:, SUBS + breadth : SUBS + cells, :] = jnp.zeros((halves, cells - breadth, LANES), F32)

    def spread_grad(p, carry):
        row = gconv_ref[p].astype(F32)
        for h in range(halves):
            nat[h, SUBS : SUBS + breadth, :] = row[:, h * LANES : (h + 1) * LANES]
        for h in range(halves):
            for t in range(steps):
                grads[h, p, t] = nat[h, pl.ds(SUBS + t, SUBS, stride=steps), :]
        return carry

    lax.fori_loop(0, height, spread_grad, 0)

    def tap_body(index, carry):
        h = index // 7
        i = index % 7
        total = [None] * 7
        for p in range(height):
            window = [spread[h, p + i, t] for t in range(6)]
            for t in range(steps):
                window.append(spread[h, p + i, t + 6])
                grad = grads[h, p, t]
                for j in range(7):
                    term = window[t + j] * grad
                    total[j] = term if total[j] is None else total[j] + term
        for j in range(7):
            sums[h, i * 7 + j] = jnp.sum(total[j], axis=0, keepdims=True)
        return carry

    lax.fori_loop(0, halves * 7, tap_body, 0)
    big = keep_ref.shape[0]
    total[0:big, :] = keep_ref[...] + got_ref[...].astype(F32)
    total[big:, :] = jnp.zeros((total.shape[0] - big, channels), F32)
    for h in range(halves):
        total[big : big + 49, h * LANES : (h + 1) * LANES] = sums[h].reshape(49, LANES)
    rows = hsum_ref.shape[1] // channels
    at = big + 49
    for c in range(rows):
        total[at + c : at + c + 1, :] = jnp.sum(hsum_ref[:, c * channels : (c + 1) * channels], axis=0, keepdims=True)
    at += rows
    for c in range(5):
        total[at + c : at + c + 1, :] = jnp.sum(chan_ref[c], axis=0, keepdims=True)
    share = shares[0].shape[0]
    for k in range(size):
        start = pl.multiple_of((place_ref[1] ^ k) * share, SUBS)
        shares[k][...] = total[pl.ds(start, share), :].astype(shares[k].dtype)


def input_grad_kernel(own_ref, top_ref, bottom_ref, kern_ref, cot_ref, grad_ref, nat, spread, taps):
    height, breadth, channels = own_ref.shape
    halves = channels // LANES
    steps, cells = dims_of(breadth)
    fill_taps(kern_ref, taps, halves, True)
    for r in range(EDGE):
        spread_row(top_ref[r], nat, spread, r, halves, breadth)
        spread_row(bottom_ref[r], nat, spread, EDGE + height + r, halves, breadth)

    def spread_own(p, carry):
        spread_row(own_ref[p], nat, spread, EDGE + p, halves, breadth)
        return carry

    lax.fori_loop(0, height, spread_own, 0)
    n_runs, length = runs_of(steps)

    def row_body(p, carry):
        def run_body(index, inner):
            h = index // n_runs
            start = (index % n_runs) * length
            total = conv_run(spread, taps, h, p, start, length)
            for t in range(length):
                nat[h, pl.ds(SUBS + start + t, SUBS, stride=steps), :] = total[t]
            return inner

        lax.fori_loop(0, halves * n_runs, run_body, 0)
        values = jnp.concatenate([gather_row(nat, h, breadth) for h in range(halves)], axis=1)
        grad_ref[p] = (cot_ref[p].astype(F32) + values).astype(BF16)
        return carry

    lax.fori_loop(0, height, row_body, 0)


def call(kernel, out_shape, scratch, flops, nbytes, name, mebibytes):
    def run(*operands):
        whole = pl.BlockSpec(memory_space=pltpu.VMEM)
        scalars = pl.BlockSpec(memory_space=pltpu.SMEM)
        return pl.pallas_call(
            kernel,
            out_shape=out_shape,
            in_specs=[scalars if x.dtype == jnp.int32 else whole for x in operands],
            out_specs=jax.tree.map(lambda _: whole, out_shape),
            scratch_shapes=scratch,
            compiler_params=pltpu.CompilerParams(vmem_limit_bytes=mebibytes * 1024 * 1024),
            cost_estimate=pl.CostEstimate(flops=flops, bytes_accessed=nbytes, transcendentals=0),
            name=name,
        )(*operands)

    return run


def place_kernel(digits, rows, factor, place_ref, here_ref, across_ref, other_ref, other_across_ref, *rest):
    w_in_ref, w_out_ref, kernel_ref, hidden_ref, chan_ref, total = rest
    channels = here_ref.shape[1]
    order = [[]]
    for stride, size in digits[:-1]:
        order = [[k] + tail for k in range(size) for tail in order]
    order = [ks[::-1] for ks in order]
    share = here_ref.shape[0] // len(order)
    draw = place_ref[0]
    for flip, refs in ((0, (here_ref, across_ref)), (1, (other_ref, other_across_ref))):
        for last, ref in enumerate(refs):
            values = ref[...].astype(F32)
            for n, ks in enumerate(order):
                extent = rows
                start = 0
                for d, (stride, size) in enumerate(digits):
                    extent = extent // size
                    k = ks[d] if d < len(ks) else last
                    start = start + (place_ref[1 + d] ^ k) * extent
                start = pl.multiple_of(start, SUBS)
                total[draw ^ flip, pl.ds(start, share), :] = values[n * share : (n + 1) * share]
    big = w_out_ref.shape[0]
    for c in range(big // channels):
        cols = slice(c * channels, (c + 1) * channels)
        w_in_ref[:, cols] = total[0, cols, :] * factor
    w_out_ref[...] = total[1, 0:big, :] * factor
    small = (total[0, big : big + 64, :] + total[1, big : big + 64, :]) * factor
    for i in range(7):
        kernel_ref[i] = small[i * 7 : i * 7 + 7]
    blocks = big // channels
    halves = channels // LANES
    for c in range(blocks):
        for h in range(halves):
            hidden_ref[c * halves + h : c * halves + h + 1, :] = small[49 + c : 50 + c, h * LANES : (h + 1) * LANES]
    chan_ref[...] = small[49 + blocks : 54 + blocks]


def digits_of(count):
    digits = [(1, 2)]
    stride = 2
    while stride < count:
        size = min(4, count // stride)
        digits.append((stride, size))
        stride *= size
    return digits[::-1]


def exchange(values, count, stride, size, k):
    pairs = []
    for i in range(count):
        digit = i // stride % size
        pairs.append((i, i + ((digit ^ k) - digit) * stride))
    return lax.ppermute(values, "tile", pairs)


def other_core(values, draws):
    return lax.ppermute(values, "draw", [(i, i ^ 1) for i in range(draws)])


def halo(cells, tiles):
    after = [(i, i + 1) for i in range(tiles - 1)]
    before = [(i + 1, i) for i in range(tiles - 1)]
    top = lax.ppermute(cells[-EDGE:], "tile", after)
    bottom = lax.ppermute(cells[:EDGE], "tile", before)
    return top, bottom


def per_device(
    tiles,
    draws,
    inputs,
    land_mask,
    kernel,
    conv_bias,
    norm_gain,
    norm_bias,
    w_in,
    b_in,
    w_out,
    b_out,
    layer_scale,
    cotangent,
):
    _, height, breadth, channels = inputs.shape
    hidden_units = w_in.shape[1]
    halves = channels // LANES
    steps, cells = dims_of(breadth)
    own = inputs[0]
    cot = cotangent[0]
    top, bottom = halo(own, tiles)
    mask = jnp.pad(land_mask.astype(F32), ((0, 0), (0, cells - breadth)))
    mask = mask.reshape(height, SUBS, steps).transpose(0, 2, 1).reshape(height * cells, 1)
    mask = jnp.broadcast_to(mask, (height * cells, LANES))

    def row(vector):
        return vector.reshape(1, -1)

    nat = pltpu.VMEM((halves, cells + 2 * SUBS, LANES), F32)
    spread = pltpu.VMEM((halves, height + 2 * EDGE, steps + 2 * EDGE, SUBS, LANES), F32)
    taps = pltpu.VMEM((halves, 49, SUBS, LANES), F32)
    count = height * cells
    big = hidden_units
    digits = digits_of(tiles)
    unit = tiles * SUBS
    rows = -(-(big + 64) // unit) * unit
    tile = lax.axis_index("tile")
    place = jnp.stack([lax.axis_index("draw")] + [tile // stride % size for stride, size in digits]).astype(jnp.int32)
    out, gconv, keep, send, hsum, chan = call(
        main_kernel,
        (
            jax.ShapeDtypeStruct((height, breadth, channels), BF16),
            jax.ShapeDtypeStruct((height, breadth, channels), BF16),
            jax.ShapeDtypeStruct((big, channels), F32),
            jax.ShapeDtypeStruct((big, channels), BF16),
            jax.ShapeDtypeStruct((SUBS, hidden_units), F32),
            jax.ShapeDtypeStruct((5, SUBS, channels), F32),
        ),
        [
            nat,
            spread,
            taps,
            pltpu.VMEM((halves, count, LANES), F32),
            pltpu.VMEM((cells, channels), F32),
            pltpu.VMEM((cells, channels), F32),
            pltpu.VMEM((count, channels), BF16),
            pltpu.VMEM((count, hidden_units), BF16),
            pltpu.VMEM((count, channels), BF16),
            pltpu.VMEM((count, hidden_units), BF16),
        ],
        12 * count * channels * hidden_units,
        8 * 1024 * 1024,
        "block_main",
        32,
    )(
        place, own, top, bottom, cot, mask, kernel, row(conv_bias), row(norm_gain), row(norm_bias), w_in, row(b_in), w_out,
        row(b_out), row(layer_scale),
    )
    got = other_core(send, draws)
    grad_top, grad_bottom = halo(gconv, tiles)

    stride, size = digits[0]
    share = rows // size
    keep, *sends = call(
        functools.partial(kernel_grad_kernel, size),
        (jax.ShapeDtypeStruct((share, channels), F32),)
        + (jax.ShapeDtypeStruct((share, channels), BF16),) * (size - 1),
        [
            nat,
            spread,
            pltpu.VMEM((halves, height, steps, SUBS, LANES), F32),
            pltpu.VMEM((halves, 49, 1, LANES), F32),
            pltpu.VMEM((rows, channels), F32),
        ],
        4 * 1024 * 1024 * 1024,
        4 * 1024 * 1024,
        "kernel_grad",
        24,
    )(place, own, top, bottom, gconv, hsum, chan, keep, got)
    for step, (stride, size) in enumerate(digits):
        if step:
            share = keep.shape[0] // size
            mine = place[1 + step]
            sends = [lax.dynamic_slice_in_dim(keep, (mine ^ k) * share, share, 0).astype(BF16) for k in range(1, size)]
            keep = lax.dynamic_slice_in_dim(keep, mine * share, share, 0)
        received = [exchange(sends[k - 1], tiles, stride, size, k) for k in range(1, size)]
        for piece in received:
            keep = keep + piece.astype(F32)
    gathered = keep.astype(BF16)
    for stride, size in digits[:-1]:
        gathered = jnp.concatenate([gathered] + [exchange(gathered, tiles, stride, size, k) for k in range(1, size)], axis=0)

    input_grad = call(
        input_grad_kernel,
        jax.ShapeDtypeStruct((height, breadth, channels), BF16),
        [nat, spread, taps],
        4 * 1024 * 1024 * 1024,
        4 * 1024 * 1024,
        "input_grad",
        24,
    )(gconv, grad_top, grad_bottom, kernel, cot)
    gathered, input_grad = lax.optimization_barrier((gathered, input_grad))

    stride, size = digits[-1]
    across = exchange(gathered, tiles, stride, size, 1)
    other = other_core(gathered, draws)
    other_across = other_core(across, draws)
    factor = float(1.0 / np.sqrt(np.float32(draws * height * tiles * breadth)))
    w_in_sum, w_out_sum, kernel_sum, hidden_sum, chan_sum = call(
        functools.partial(place_kernel, digits, rows, factor),
        (
            jax.ShapeDtypeStruct((channels, hidden_units), F32),
            jax.ShapeDtypeStruct((hidden_units, channels), F32),
            jax.ShapeDtypeStruct((7, 7, channels), F32),
            jax.ShapeDtypeStruct((hidden_units // LANES, LANES), F32),
            jax.ShapeDtypeStruct((5, channels), F32),
        ),
        [pltpu.VMEM((2, rows, channels), F32)],
        1024 * 1024,
        4 * 1024 * 1024,
        "place",
        24,
    )(place, gathered, across, other, other_across)
    return (
        out[None],
        input_grad[None],
        kernel_sum,
        w_in_sum,
        w_out_sum,
        hidden_sum.reshape(-1),
        chan_sum,
    )


def solution(mesh):
    placed = (
        P(("group", "draw"), "tile", None, None),
        P("tile", None),
        P(),
        P(),
        P(),
        P(),
        P(),
        P(),
        P(),
        P(),
        P(),
        P(("group", "draw"), "tile", None, None),
    )
    return jax.shard_map(
        functools.partial(per_device, mesh.shape["tile"], mesh.shape["draw"]),
        mesh=mesh,
        in_specs=placed,
        out_specs=(
            P(("group", "draw"), "tile", None, None),
            P(("group", "draw"), "tile", None, None),
            P("group", None, None),
            P("group", None),
            P("group", None),
            P("group"),
            P("group", None),
        ),
        check_vma=False,
    )
```

```python
import functools

import jax
import jax.numpy as jnp
import numpy as np
from jax import lax
from jax.experimental import pallas as pl
from jax.experimental.pallas import tpu as pltpu
from jax.sharding import PartitionSpec as P

ROOT_TERM = 0.7978845608028654
CUBIC = 0.044715
EPSILON = 1e-06
F32 = jnp.float32
BF16 = jnp.bfloat16
LANES = 128
SUBS = 8
EDGE = 3
VMEM_LIMIT = 56 * 1024 * 1024


def dims_of(breadth):
    steps = -(-breadth // SUBS)
    return steps, steps * SUBS


def spread_row(row, nat, spread, slot, halves, breadth):
    steps, cells = dims_of(breadth)
    row = row.astype(F32)
    over = cells - breadth + EDGE
    for h in range(halves):
        part = row[:, h * LANES : (h + 1) * LANES]
        nat[h, SUBS : SUBS + breadth, :] = part
        nat[h, SUBS - EDGE : SUBS, :] = part[breadth - EDGE :]
        nat[h, SUBS + breadth : SUBS + breadth + over, :] = part[:over]
    for h in range(halves):
        for t in range(steps + 2 * EDGE):
            spread[h, slot, t] = nat[h, pl.ds(SUBS - EDGE + t, SUBS, stride=steps), :]


def gather_row(nat, h, breadth):
    return nat[h, SUBS : SUBS + breadth, :]


def fill_taps(kern_ref, taps, halves, flip):
    for i in range(7):
        for j in range(7):
            src = kern_ref[6 - i, 6 - j : 7 - j, :] if flip else kern_ref[i, j : j + 1, :]
            for h in range(halves):
                taps[h, i * 7 + j] = jnp.broadcast_to(src[:, h * LANES : (h + 1) * LANES], (SUBS, LANES))


def conv_run(spread, taps, h, p, start, length):
    total = [None] * length
    for i in range(7):
        weights = [taps[h, i * 7 + j] for j in range(7)]
        for u in range(length + 6):
            cell = spread[h, p + i, start + u]
            for j in range(7):
                t = u - j
                if 0 <= t < length:
                    term = cell * weights[j]
                    total[t] = term if total[t] is None else total[t] + term
    return total


def runs_of(steps):
    length = steps // 2 if steps % 2 == 0 else steps
    return steps // length, length


def main_kernel(
    place_ref, own_ref, top_ref, bottom_ref, cot_ref, mask_ref, kern_ref, cbias_ref, gain_ref, nbias_ref, w_in_ref,
    b_in_ref, w_out_ref, b_out_ref, scale_ref,
    out_ref, gconv_ref, keep_ref, send_ref, hsum_ref, chan_ref,
    nat, spread, taps, conv, units, cots, ocean_s, normed_s, act_s, gmix_s, ghid_s,
):
    height, breadth, channels = own_ref.shape
    hidden_units = w_in_ref.shape[1]
    halves = channels // LANES
    steps, cells = dims_of(breadth)

    fill_taps(kern_ref, taps, halves, False)
    for r in range(EDGE):
        spread_row(top_ref[r], nat, spread, r, halves, breadth)
        spread_row(bottom_ref[r], nat, spread, EDGE + height + r, halves, breadth)

    def spread_own(p, carry):
        spread_row(own_ref[p], nat, spread, EDGE + p, halves, breadth)
        return carry

    lax.fori_loop(0, height, spread_own, 0)

    n_runs, length = runs_of(steps)

    def conv_body(index, carry):
        run = index % n_runs
        p = (index // n_runs) % height
        h = index // (n_runs * height)
        start = run * length
        total = conv_run(spread, taps, h, p, start, length)
        base = pl.multiple_of((p * steps + start) * SUBS, SUBS)
        for t in range(length):
            conv[h, pl.ds(base + t * SUBS, SUBS), :] = total[t]
        return carry

    lax.fori_loop(0, halves * height * n_runs, conv_body, 0)

    hsum_ref[...] = jnp.zeros_like(hsum_ref)
    chan_ref[...] = jnp.zeros_like(chan_ref)
    width = 256
    inv_c = 1.0 / channels

    def joined(pieces):
        return jnp.concatenate(pieces, axis=1)

    def column_sum(values):
        return jnp.sum(values.reshape(values.shape[0] // SUBS, SUBS, values.shape[1]), axis=0)

    def row_body(p, carry):
        base = pl.multiple_of(p * cells, 16)
        rows = pl.ds(base, cells)
        cot = cot_ref[p].astype(F32)
        for h in range(halves):
            nat[h, SUBS : SUBS + breadth, :] = cot[:, h * LANES : (h + 1) * LANES]
        for h in range(halves):
            for t in range(steps):
                cots[t * SUBS : (t + 1) * SUBS, h * LANES : (h + 1) * LANES] = nat[
                    h, pl.ds(SUBS + t, SUBS, stride=steps), :
                ]
        values = joined([conv[h, rows, :] for h in range(halves)]) + cbias_ref[...]
        center = jnp.sum(values, axis=1, keepdims=True) * inv_c
        deviation = values - center
        inv_std = lax.rsqrt(jnp.sum(deviation * deviation, axis=1, keepdims=True) * inv_c + EPSILON)
        unit = deviation * inv_std
        units[...] = unit
        normed = (unit * gain_ref[...] + nbias_ref[...]).astype(BF16)
        normed_s[rows, :] = normed
        land = mask_ref[p]
        for t in range(steps):
            ocean_s[t * SUBS : (t + 1) * SUBS, :] = jnp.broadcast_to(land[:, t : t + 1], (SUBS, LANES))
        ocean = joined([ocean_s[...]] * halves)
        upstream = jnp.where(ocean > 0, cots[...], 0.0)
        gmix = (scale_ref[...] * upstream).astype(BF16)
        gmix_s[rows, :] = gmix
        mixed = jnp.zeros((cells, channels), F32)
        grad_normed = jnp.zeros((cells, channels), F32)
        for c in range(0, hidden_units, width):
            cols = slice(c, c + width)
            hidden = jnp.dot(normed, w_in_ref[:, cols], preferred_element_type=F32) + b_in_ref[:, cols]
            grad_act = lax.dot_general(
                gmix, w_out_ref[cols, :], (((1,), (1,)), ((), ())), preferred_element_type=F32
            )
            square = hidden * hidden
            inner = hidden * (ROOT_TERM * CUBIC * square + ROOT_TERM)
            half_tanh = 0.5 * jnp.tanh(inner)
            gate = 0.5 + half_tanh
            active = hidden * gate
            slope = gate + active * (0.5 - half_tanh) * (6.0 * CUBIC * ROOT_TERM * square + 2.0 * ROOT_TERM)
            act = active.astype(BF16)
            act_s[rows, cols] = act
            mixed = mixed + jnp.dot(act, w_out_ref[cols, :], preferred_element_type=F32)
            ghid = (grad_act * slope).astype(BF16)
            ghid_s[rows, cols] = ghid
            hsum_ref[:, cols] += column_sum(ghid.astype(F32))
            grad_normed = grad_normed + lax.dot_general(
                ghid, w_in_ref[:, cols], (((1,), (1,)), ((), ())), preferred_element_type=F32
            )
        mixed = mixed + b_out_ref[...]
        unit = units[...]
        chan_ref[1] += column_sum(grad_normed * unit)
        chan_ref[2] += column_sum(grad_normed)
        chan_ref[3] += column_sum(gmix.astype(F32))
        upstream = jnp.where(ocean > 0, cots[...], 0.0)
        chan_ref[4] += column_sum(upstream * mixed)
        residual = jnp.where(ocean > 0, scale_ref[...] * mixed, 0.0)
        for h in range(halves):
            for t in range(steps):
                nat[h, pl.ds(SUBS + t, SUBS, stride=steps), :] = (
                    spread[h, EDGE + p, EDGE + t] + residual[t * SUBS : (t + 1) * SUBS, h * LANES : (h + 1) * LANES]
                )
        out_ref[p] = joined([gather_row(nat, h, breadth) for h in range(halves)]).astype(BF16)
        scaled = grad_normed * gain_ref[...]
        mean_scaled = jnp.sum(scaled, axis=1, keepdims=True) * inv_c
        mean_product = jnp.sum(scaled * unit, axis=1, keepdims=True) * inv_c
        grad_conv = (inv_std * (scaled - mean_scaled - unit * mean_product)).astype(BF16).astype(F32)
        chan_ref[0] += column_sum(grad_conv)
        for h in range(halves):
            for t in range(steps):
                nat[h, pl.ds(SUBS + t, SUBS, stride=steps), :] = grad_conv[
                    t * SUBS : (t + 1) * SUBS, h * LANES : (h + 1) * LANES
                ]
        gconv_ref[p] = joined([gather_row(nat, h, breadth) for h in range(halves)]).astype(BF16)
        return carry

    lax.fori_loop(0, height, row_body, 0)

    first = (((0,), (0,)), ((), ()))

    def store_block(half, c, block):
        @pl.when(place_ref[0] == half)
        def _():
            keep_ref[c : c + width, :] = block

        @pl.when(place_ref[0] != half)
        def _():
            send_ref[c : c + width, :] = block.astype(BF16)

    normed = normed_s[...]
    for c in range(0, hidden_units, width):
        cols = slice(c, c + width)
        store_block(0, c, lax.dot_general(normed, ghid_s[:, cols], first, preferred_element_type=F32))
    gmix = gmix_s[...]
    for c in range(0, hidden_units, width):
        cols = slice(c, c + width)
        store_block(1, c, lax.dot_general(act_s[:, cols], gmix, first, preferred_element_type=F32))


def kernel_grad_kernel(
    size, place_ref, own_ref, top_ref, bottom_ref, gconv_ref, hsum_ref, chan_ref, keep_ref, got_ref, *rest
):
    shares, (nat, spread, grads, sums, total) = rest[:size], rest[size:]
    height, breadth, channels = own_ref.shape
    halves = channels // LANES
    steps, cells = dims_of(breadth)
    for r in range(EDGE):
        spread_row(top_ref[r], nat, spread, r, halves, breadth)
        spread_row(bottom_ref[r], nat, spread, EDGE + height + r, halves, breadth)

    def spread_own(p, carry):
        spread_row(own_ref[p], nat, spread, EDGE + p, halves, breadth)
        return carry

    lax.fori_loop(0, height, spread_own, 0)

    nat[:, SUBS + breadth : SUBS + cells, :] = jnp.zeros((halves, cells - breadth, LANES), F32)

    def spread_grad(p, carry):
        row = gconv_ref[p].astype(F32)
        for h in range(halves):
            nat[h, SUBS : SUBS + breadth, :] = row[:, h * LANES : (h + 1) * LANES]
        for h in range(halves):
            for t in range(steps):
                grads[h, p, t] = nat[h, pl.ds(SUBS + t, SUBS, stride=steps), :]
        return carry

    lax.fori_loop(0, height, spread_grad, 0)

    def tap_body(index, carry):
        h = index // 7
        i = index % 7
        total = [None] * 7
        for p in range(height):
            window = [spread[h, p + i, t] for t in range(6)]
            for t in range(steps):
                window.append(spread[h, p + i, t + 6])
                grad = grads[h, p, t]
                for j in range(7):
                    term = window[t + j] * grad
                    total[j] = term if total[j] is None else total[j] + term
        for j in range(7):
            sums[h, i * 7 + j] = jnp.sum(total[j], axis=0, keepdims=True)
        return carry

    lax.fori_loop(0, halves * 7, tap_body, 0)
    big = keep_ref.shape[0]
    total[0:big, :] = keep_ref[...] + got_ref[...].astype(F32)
    total[big:, :] = jnp.zeros((total.shape[0] - big, channels), F32)
    for h in range(halves):
        total[big : big + 49, h * LANES : (h + 1) * LANES] = sums[h].reshape(49, LANES)
    rows = hsum_ref.shape[1] // channels
    at = big + 49
    for c in range(rows):
        total[at + c : at + c + 1, :] = jnp.sum(hsum_ref[:, c * channels : (c + 1) * channels], axis=0, keepdims=True)
    at += rows
    for c in range(5):
        total[at + c : at + c + 1, :] = jnp.sum(chan_ref[c], axis=0, keepdims=True)
    share = shares[0].shape[0]
    for k in range(size):
        start = pl.multiple_of((place_ref[1] ^ k) * share, SUBS)
        shares[k][...] = total[pl.ds(start, share), :].astype(shares[k].dtype)


def input_grad_kernel(own_ref, top_ref, bottom_ref, kern_ref, cot_ref, grad_ref, nat, spread, taps):
    height, breadth, channels = own_ref.shape
    halves = channels // LANES
    steps, cells = dims_of(breadth)
    fill_taps(kern_ref, taps, halves, True)
    for r in range(EDGE):
        spread_row(top_ref[r], nat, spread, r, halves, breadth)
        spread_row(bottom_ref[r], nat, spread, EDGE + height + r, halves, breadth)

    def spread_own(p, carry):
        spread_row(own_ref[p], nat, spread, EDGE + p, halves, breadth)
        return carry

    lax.fori_loop(0, height, spread_own, 0)
    n_runs, length = runs_of(steps)

    def row_body(p, carry):
        def run_body(index, inner):
            h = index // n_runs
            start = (index % n_runs) * length
            total = conv_run(spread, taps, h, p, start, length)
            for t in range(length):
                nat[h, pl.ds(SUBS + start + t, SUBS, stride=steps), :] = total[t]
            return inner

        lax.fori_loop(0, halves * n_runs, run_body, 0)
        values = jnp.concatenate([gather_row(nat, h, breadth) for h in range(halves)], axis=1)
        grad_ref[p] = (cot_ref[p].astype(F32) + values).astype(BF16)
        return carry

    lax.fori_loop(0, height, row_body, 0)


def call(kernel, out_shape, scratch, flops, nbytes, name):
    def run(*operands):
        whole = pl.BlockSpec(memory_space=pltpu.VMEM)
        scalars = pl.BlockSpec(memory_space=pltpu.SMEM)
        return pl.pallas_call(
            kernel,
            out_shape=out_shape,
            in_specs=[scalars if x.dtype == jnp.int32 else whole for x in operands],
            out_specs=jax.tree.map(lambda _: whole, out_shape),
            scratch_shapes=scratch,
            compiler_params=pltpu.CompilerParams(vmem_limit_bytes=VMEM_LIMIT),
            cost_estimate=pl.CostEstimate(flops=flops, bytes_accessed=nbytes, transcendentals=0),
            name=name,
        )(*operands)

    return run


def place_kernel(digits, rows, factor, place_ref, here_ref, across_ref, other_ref, other_across_ref, *rest):
    w_in_ref, w_out_ref, kernel_ref, hidden_ref, chan_ref, total = rest
    channels = here_ref.shape[1]
    order = [[]]
    for stride, size in digits[:-1]:
        order = [[k] + tail for k in range(size) for tail in order]
    order = [ks[::-1] for ks in order]
    share = here_ref.shape[0] // len(order)
    draw = place_ref[0]
    for flip, refs in ((0, (here_ref, across_ref)), (1, (other_ref, other_across_ref))):
        for last, ref in enumerate(refs):
            values = ref[...].astype(F32)
            for n, ks in enumerate(order):
                extent = rows
                start = 0
                for d, (stride, size) in enumerate(digits):
                    extent = extent // size
                    k = ks[d] if d < len(ks) else last
                    start = start + (place_ref[1 + d] ^ k) * extent
                start = pl.multiple_of(start, SUBS)
                total[draw ^ flip, pl.ds(start, share), :] = values[n * share : (n + 1) * share]
    big = w_out_ref.shape[0]
    for c in range(big // channels):
        cols = slice(c * channels, (c + 1) * channels)
        w_in_ref[:, cols] = total[0, cols, :] * factor
    w_out_ref[...] = total[1, 0:big, :] * factor
    small = (total[0, big : big + 64, :] + total[1, big : big + 64, :]) * factor
    for i in range(7):
        kernel_ref[i] = small[i * 7 : i * 7 + 7]
    blocks = big // channels
    halves = channels // LANES
    for c in range(blocks):
        for h in range(halves):
            hidden_ref[c * halves + h : c * halves + h + 1, :] = small[49 + c : 50 + c, h * LANES : (h + 1) * LANES]
    chan_ref[...] = small[49 + blocks : 54 + blocks]


def digits_of(count):
    digits = [(1, 2)]
    stride = 2
    while stride < count:
        size = min(4, count // stride)
        digits.append((stride, size))
        stride *= size
    return digits[::-1]


def exchange(values, count, stride, size, k):
    pairs = []
    for i in range(count):
        digit = i // stride % size
        pairs.append((i, i + ((digit ^ k) - digit) * stride))
    return lax.ppermute(values, "tile", pairs)


def other_core(values, draws):
    return lax.ppermute(values, "draw", [(i, i ^ 1) for i in range(draws)])


def halo(cells, tiles):
    after = [(i, i + 1) for i in range(tiles - 1)]
    before = [(i + 1, i) for i in range(tiles - 1)]
    top = lax.ppermute(cells[-EDGE:], "tile", after)
    bottom = lax.ppermute(cells[:EDGE], "tile", before)
    return top, bottom


def per_device(
    tiles,
    draws,
    inputs,
    land_mask,
    kernel,
    conv_bias,
    norm_gain,
    norm_bias,
    w_in,
    b_in,
    w_out,
    b_out,
    layer_scale,
    cotangent,
):
    _, height, breadth, channels = inputs.shape
    hidden_units = w_in.shape[1]
    halves = channels // LANES
    steps, cells = dims_of(breadth)
    own = inputs[0]
    cot = cotangent[0]
    top, bottom = halo(own, tiles)
    mask = jnp.pad(land_mask.astype(F32), ((0, 0), (0, cells - breadth)))
    mask = mask.reshape(height, SUBS, steps)

    def row(vector):
        return vector.reshape(1, -1)

    nat = pltpu.VMEM((halves, cells + 2 * SUBS, LANES), F32)
    spread = pltpu.VMEM((halves, height + 2 * EDGE, steps + 2 * EDGE, SUBS, LANES), F32)
    taps = pltpu.VMEM((halves, 49, SUBS, LANES), F32)
    count = height * cells
    big = hidden_units
    digits = digits_of(tiles)
    unit = tiles * SUBS
    rows = -(-(big + 64) // unit) * unit
    tile = lax.axis_index("tile")
    place = jnp.stack([lax.axis_index("draw")] + [tile // stride % size for stride, size in digits]).astype(jnp.int32)
    out, gconv, keep, send, hsum, chan = call(
        main_kernel,
        (
            jax.ShapeDtypeStruct((height, breadth, channels), BF16),
            jax.ShapeDtypeStruct((height, breadth, channels), BF16),
            jax.ShapeDtypeStruct((big, channels), F32),
            jax.ShapeDtypeStruct((big, channels), BF16),
            jax.ShapeDtypeStruct((SUBS, hidden_units), F32),
            jax.ShapeDtypeStruct((5, SUBS, channels), F32),
        ),
        [
            nat,
            spread,
            taps,
            pltpu.VMEM((halves, count, LANES), F32),
            pltpu.VMEM((cells, channels), F32),
            pltpu.VMEM((cells, channels), F32),
            pltpu.VMEM((cells, LANES), F32),
            pltpu.VMEM((count, channels), BF16),
            pltpu.VMEM((count, hidden_units), BF16),
            pltpu.VMEM((count, channels), BF16),
            pltpu.VMEM((count, hidden_units), BF16),
        ],
        12 * count * channels * hidden_units,
        8 * 1024 * 1024,
        "block_main",
    )(
        place, own, top, bottom, cot, mask, kernel, row(conv_bias), row(norm_gain), row(norm_bias), w_in, row(b_in), w_out,
        row(b_out), row(layer_scale),
    )
    got = other_core(send, draws)
    grad_top, grad_bottom = halo(gconv, tiles)

    stride, size = digits[0]
    share = rows // size
    keep, *sends = call(
        functools.partial(kernel_grad_kernel, size),
        (jax.ShapeDtypeStruct((share, channels), F32),)
        + (jax.ShapeDtypeStruct((share, channels), BF16),) * (size - 1),
        [
            nat,
            spread,
            pltpu.VMEM((halves, height, steps, SUBS, LANES), F32),
            pltpu.VMEM((halves, 49, 1, LANES), F32),
            pltpu.VMEM((rows, channels), F32),
        ],
        4 * 1024 * 1024 * 1024,
        4 * 1024 * 1024,
        "kernel_grad",
    )(place, own, top, bottom, gconv, hsum, chan, keep, got)
    input_grad = call(
        input_grad_kernel,
        jax.ShapeDtypeStruct((height, breadth, channels), BF16),
        [nat, spread, taps],
        4 * 1024 * 1024 * 1024,
        4 * 1024 * 1024,
        "input_grad",
    )(gconv, grad_top, grad_bottom, kernel, cot)
    for step, (stride, size) in enumerate(digits):
        if step:
            share = keep.shape[0] // size
            mine = place[1 + step]
            sends = [lax.dynamic_slice_in_dim(keep, (mine ^ k) * share, share, 0).astype(BF16) for k in range(1, size)]
            keep = lax.dynamic_slice_in_dim(keep, mine * share, share, 0)
        received = [exchange(sends[k - 1], tiles, stride, size, k) for k in range(1, size)]
        if not step:
            received, input_grad = lax.optimization_barrier((received, input_grad))
        for piece in received:
            keep = keep + piece.astype(F32)
    gathered = keep.astype(BF16)
    for stride, size in digits[:-1]:
        gathered = jnp.concatenate([gathered] + [exchange(gathered, tiles, stride, size, k) for k in range(1, size)], axis=0)

    stride, size = digits[-1]
    across = exchange(gathered, tiles, stride, size, 1)
    other = other_core(gathered, draws)
    other_across = other_core(across, draws)
    factor = float(1.0 / np.sqrt(np.float32(draws * height * tiles * breadth)))
    w_in_sum, w_out_sum, kernel_sum, hidden_sum, chan_sum = call(
        functools.partial(place_kernel, digits, rows, factor),
        (
            jax.ShapeDtypeStruct((channels, hidden_units), F32),
            jax.ShapeDtypeStruct((hidden_units, channels), F32),
            jax.ShapeDtypeStruct((7, 7, channels), F32),
            jax.ShapeDtypeStruct((hidden_units // LANES, LANES), F32),
            jax.ShapeDtypeStruct((5, channels), F32),
        ),
        [pltpu.VMEM((2, rows, channels), F32)],
        1024 * 1024,
        4 * 1024 * 1024,
        "place",
    )(place, gathered, across, other, other_across)
    return (
        out[None],
        input_grad[None],
        kernel_sum,
        w_in_sum,
        w_out_sum,
        hidden_sum.reshape(-1),
        chan_sum,
    )


def solution(mesh):
    placed = (
        P(("group", "draw"), "tile", None, None),
        P("tile", None),
        P(),
        P(),
        P(),
        P(),
        P(),
        P(),
        P(),
        P(),
        P(),
        P(("group", "draw"), "tile", None, None),
    )
    return jax.shard_map(
        functools.partial(per_device, mesh.shape["tile"], mesh.shape["draw"]),
        mesh=mesh,
        in_specs=placed,
        out_specs=(
            P(("group", "draw"), "tile", None, None),
            P(("group", "draw"), "tile", None, None),
            P("group", None, None),
            P("group", None),
            P("group", None),
            P("group"),
            P("group", None),
        ),
        check_vma=False,
    )
```

```python
import functools

import jax
import jax.numpy as jnp
import numpy as np
from jax import lax
from jax.experimental import pallas as pl
from jax.experimental.pallas import tpu as pltpu
from jax.sharding import PartitionSpec as P

ROOT_TERM = 0.7978845608028654
CUBIC = 0.044715
EPSILON = 1e-06
F32 = jnp.float32
BF16 = jnp.bfloat16
LANES = 128
SUBS = 8
EDGE = 3
SMALL = 64
VMEM_LIMIT = 56 * 1024 * 1024


def dims_of(breadth):
    steps = -(-breadth // SUBS)
    return steps, steps * SUBS


def spread_row(row, nat, spread, slot, halves, breadth):
    steps, cells = dims_of(breadth)
    row = row.astype(F32)
    over = cells - breadth + EDGE
    for h in range(halves):
        part = row[:, h * LANES : (h + 1) * LANES]
        nat[h, SUBS : SUBS + breadth, :] = part
        nat[h, SUBS - EDGE : SUBS, :] = part[breadth - EDGE :]
        nat[h, SUBS + breadth : SUBS + breadth + over, :] = part[:over]
    for h in range(halves):
        for t in range(steps + 2 * EDGE):
            spread[h, slot, t] = nat[h, pl.ds(SUBS - EDGE + t, SUBS, stride=steps), :]


def gather_row(nat, h, breadth):
    return nat[h, SUBS : SUBS + breadth, :]


def fill_taps(kern_ref, taps, halves, flip):
    for i in range(7):
        for j in range(7):
            src = kern_ref[6 - i, 6 - j : 7 - j, :] if flip else kern_ref[i, j : j + 1, :]
            for h in range(halves):
                taps[h, i * 7 + j] = jnp.broadcast_to(src[:, h * LANES : (h + 1) * LANES], (SUBS, LANES))


def conv_run(cells_at, taps, h, row_taps, length, total):
    total = list(total)
    for i, slot in row_taps:
        weights = [taps[h, i * 7 + j] for j in range(7)]
        for u in range(length + 6):
            cell = cells_at(slot, u)
            for j in range(7):
                t = u - j
                if 0 <= t < length:
                    term = cell * weights[j]
                    total[t] = term if total[t] is None else total[t] + term
    return total


def own_taps(p, height):
    return [(i, p + i - EDGE) for i in range(7) if 0 <= p + i - EDGE < height]


def halo_taps(p, height):
    found = []
    for i in range(7):
        row = p + i
        if row < EDGE:
            found.append((i, row))
        elif row >= EDGE + height:
            found.append((i, row - height))
    return found


def runs_of(steps):
    length = steps // 2 if steps % 2 == 0 else steps
    return steps // length, length


def own_conv_kernel(flip, own_ref, kern_ref, part_ref, nat, spread, taps):
    height, breadth, channels = own_ref.shape
    halves = channels // LANES
    steps, cells = dims_of(breadth)
    fill_taps(kern_ref, taps, halves, flip)

    def spread_own(p, carry):
        spread_row(own_ref[p], nat, spread, p, halves, breadth)
        return carry

    lax.fori_loop(0, height, spread_own, 0)
    n_runs, length = runs_of(steps)
    for p in range(height):

        def run_body(index, carry, p=p):
            h = index // n_runs
            start = (index % n_runs) * length
            total = conv_run(
                lambda slot, u: spread[h, slot, start + u], taps, h, own_taps(p, height), length, [None] * length
            )
            for t in range(length):
                part_ref[h, p * steps + start + t] = total[t]
            return carry

        lax.fori_loop(0, halves * n_runs, run_body, 0)


def main_kernel(
    place_ref, own_ref, top_ref, bottom_ref, part_ref, cot_ref, mask_ref, kern_ref, cbias_ref, gain_ref, nbias_ref, w_in_ref,
    b_in_ref, w_out_ref, b_out_ref, scale_ref,
    out_ref, gconv_ref, keep_ref, send_ref, hsum_ref, chan_ref,
    nat, out_s, spread, taps, conv, units, cots, state_s, mixed_s, gnorm_s, ocean_s, inv_s, normed_s, act_s, gmix_s, ghid_s,
):
    height, breadth, channels = own_ref.shape
    hidden_units = w_in_ref.shape[1]
    halves = channels // LANES
    steps, cells = dims_of(breadth)

    fill_taps(kern_ref, taps, halves, False)
    for r in range(EDGE):
        spread_row(top_ref[r], nat, spread, r, halves, breadth)
        spread_row(bottom_ref[r], nat, spread, EDGE + r, halves, breadth)
    n_runs, length = runs_of(steps)
    for p in range(height):

        def conv_body(index, carry, p=p):
            h = index // n_runs
            start = (index % n_runs) * length
            base = p * steps + start
            total = conv_run(
                lambda slot, u: spread[h, slot, start + u],
                taps,
                h,
                halo_taps(p, height),
                length,
                [part_ref[h, base + t] for t in range(length)],
            )
            for t in range(length):
                conv[h, pl.ds(pl.multiple_of((base + t) * SUBS, SUBS), SUBS), :] = total[t]
            return carry

        lax.fori_loop(0, halves * n_runs, conv_body, 0)

    hsum_ref[...] = jnp.zeros_like(hsum_ref)
    chan_ref[...] = jnp.zeros_like(chan_ref)
    width = 256
    inv_c = 1.0 / channels
    sides = range(halves)
    lanes = [slice(h * LANES, (h + 1) * LANES) for h in sides]

    def column_sum(values):
        return jnp.sum(values.reshape(values.shape[0] // SUBS, SUBS, values.shape[1]), axis=0)

    def mean_of(parts):
        return jnp.sum(functools.reduce(jnp.add, parts), axis=1, keepdims=True) * inv_c

    pack = 2 if height % 2 == 0 else 1

    def row_body(pp, carry):
        base2 = pl.multiple_of(pp * (pack * cells), 16)
        rows = pl.ds(base2, pack * cells)
        for q in range(pack):
            p = pp * pack + q
            base = pl.multiple_of(base2 + q * cells, 16)
            cot = cot_ref[p].astype(F32)
            for h in sides:
                nat[h, SUBS : SUBS + breadth, :] = cot[:, lanes[h]]
                out_s[h, SUBS : SUBS + breadth, :] = own_ref[p, :, lanes[h]].astype(F32)
            land = mask_ref[p]
            for t in range(0, steps, 2):
                here = pl.ds(base + t * SUBS, 2 * SUBS)
                local = slice(q * cells + t * SUBS, q * cells + (t + 2) * SUBS)
                values = [conv[h, here, :] + cbias_ref[:, lanes[h]] for h in sides]
                center = mean_of(values)
                deviation = [v - center for v in values]
                inv_std = lax.rsqrt(mean_of([d * d for d in deviation]) + EPSILON)
                inv_s[local, :] = jnp.broadcast_to(inv_std, (2 * SUBS, LANES))
                ocean = jnp.concatenate([jnp.broadcast_to(land[:, t + k : t + k + 1], (SUBS, LANES)) for k in range(2)], axis=0)
                ocean_s[local, :] = ocean
                for h in sides:
                    unit = deviation[h] * inv_std
                    units[local, lanes[h]] = unit
                    normed_s[here, lanes[h]] = (unit * gain_ref[:, lanes[h]] + nbias_ref[:, lanes[h]]).astype(BF16)
                    cell = jnp.concatenate(
                        [nat[h, pl.ds(SUBS + t + k, SUBS, stride=steps), :] for k in range(2)], axis=0
                    )
                    upstream = jnp.where(ocean > 0, cell, 0.0)
                    cots[local, lanes[h]] = upstream
                    state_s[local, lanes[h]] = jnp.concatenate(
                        [out_s[h, pl.ds(SUBS + t + k, SUBS, stride=steps), :] for k in range(2)], axis=0
                    )
                    gmix_s[here, lanes[h]] = (scale_ref[:, lanes[h]] * upstream).astype(BF16)
        normed = normed_s[rows, :]
        gmix = gmix_s[rows, :]
        for c in range(0, hidden_units, width):
            cols = slice(c, c + width)
            hidden = jnp.dot(normed, w_in_ref[:, cols], preferred_element_type=F32) + b_in_ref[:, cols]
            grad_act = lax.dot_general(
                gmix, w_out_ref[cols, :], (((1,), (1,)), ((), ())), preferred_element_type=F32
            )
            square = hidden * hidden
            inner = hidden * (ROOT_TERM * CUBIC * square + ROOT_TERM)
            half_tanh = 0.5 * jnp.tanh(inner)
            gate = 0.5 + half_tanh
            active = hidden * gate
            slope = gate + active * (0.5 - half_tanh) * (6.0 * CUBIC * ROOT_TERM * square + 2.0 * ROOT_TERM)
            act = active.astype(BF16)
            act_s[rows, cols] = act
            mixed = jnp.dot(act, w_out_ref[cols, :], preferred_element_type=F32)
            ghid = (grad_act * slope).astype(BF16)
            ghid_s[rows, cols] = ghid
            hsum_ref[:, cols] += column_sum(ghid.astype(F32))
            grad_normed = lax.dot_general(
                ghid, w_in_ref[:, cols], (((1,), (1,)), ((), ())), preferred_element_type=F32
            )
            if c:
                mixed_s[...] += mixed
                gnorm_s[...] += grad_normed
            else:
                mixed_s[...] = mixed
                gnorm_s[...] = grad_normed
        for q in range(pack):
            p = pp * pack + q
            base = pl.multiple_of(base2 + q * cells, 16)
            sums = [[None] * halves for _ in range(5)]

            def add_to(n, h, values):
                folded = values[:SUBS] + values[SUBS:]
                sums[n][h] = folded if sums[n][h] is None else sums[n][h] + folded

            for t in range(0, steps, 2):
                here = pl.ds(base + t * SUBS, 2 * SUBS)
                local = slice(q * cells + t * SUBS, q * cells + (t + 2) * SUBS)
                ocean = ocean_s[local, :]
                scaled, products, units_here = [], [], []
                for h in sides:
                    mixed = mixed_s[local, lanes[h]] + b_out_ref[:, lanes[h]]
                    add_to(4, h, cots[local, lanes[h]] * mixed)
                    residual = jnp.where(ocean > 0, scale_ref[:, lanes[h]] * mixed, 0.0)
                    result = state_s[local, lanes[h]] + residual
                    for k in range(2):
                        out_s[h, pl.ds(SUBS + t + k, SUBS, stride=steps), :] = result[k * SUBS : (k + 1) * SUBS]
                    grad_normed = gnorm_s[local, lanes[h]]
                    unit = units[local, lanes[h]]
                    add_to(1, h, grad_normed * unit)
                    add_to(2, h, grad_normed)
                    add_to(3, h, gmix_s[here, lanes[h]].astype(F32))
                    scaled.append(grad_normed * gain_ref[:, lanes[h]])
                    units_here.append(unit)
                    products.append(scaled[h] * unit)
                mean_scaled = mean_of(scaled)
                mean_product = mean_of(products)
                inv_std = inv_s[local, :]
                for h in sides:
                    grad_conv = (inv_std * (scaled[h] - mean_scaled - units_here[h] * mean_product)).astype(BF16).astype(F32)
                    add_to(0, h, grad_conv)
                    for k in range(2):
                        nat[h, pl.ds(SUBS + t + k, SUBS, stride=steps), :] = grad_conv[k * SUBS : (k + 1) * SUBS]
            for n in range(5):
                for h in sides:
                    chan_ref[n, :, lanes[h]] += sums[n][h]
            for h in sides:
                out_ref[p, :, lanes[h]] = gather_row(out_s, h, breadth).astype(BF16)
                gconv_ref[p, :, lanes[h]] = gather_row(nat, h, breadth).astype(BF16)
        return carry

    lax.fori_loop(0, height // pack, row_body, 0)

    first = (((0,), (0,)), ((), ()))

    def store_block(half, c, block):
        @pl.when(place_ref[0] == half)
        def _():
            keep_ref[c : c + width, :] = block

        @pl.when(place_ref[0] != half)
        def _():
            send_ref[c : c + width, :] = block.astype(BF16)

    normed = normed_s[...]
    for c in range(0, hidden_units, width):
        cols = slice(c, c + width)
        store_block(0, c, lax.dot_general(normed, ghid_s[:, cols], first, preferred_element_type=F32))
    gmix = gmix_s[...]
    for c in range(0, hidden_units, width):
        cols = slice(c, c + width)
        store_block(1, c, lax.dot_general(act_s[:, cols], gmix, first, preferred_element_type=F32))


def kernel_grad_kernel(
    own_ref, top_ref, bottom_ref, gconv_ref, hsum_ref, chan_ref, small_ref, nat, spread, grads, sums, total
):
    height, breadth, channels = own_ref.shape
    halves = channels // LANES
    steps, cells = dims_of(breadth)
    for r in range(EDGE):
        spread_row(top_ref[r], nat, spread, r, halves, breadth)
        spread_row(bottom_ref[r], nat, spread, EDGE + height + r, halves, breadth)

    def spread_own(p, carry):
        spread_row(own_ref[p], nat, spread, EDGE + p, halves, breadth)
        return carry

    lax.fori_loop(0, height, spread_own, 0)

    nat[:, SUBS + breadth : SUBS + cells, :] = jnp.zeros((halves, cells - breadth, LANES), F32)

    def spread_grad(p, carry):
        row = gconv_ref[p].astype(F32)
        for h in range(halves):
            nat[h, SUBS : SUBS + breadth, :] = row[:, h * LANES : (h + 1) * LANES]
        for h in range(halves):
            for t in range(steps):
                grads[h, p, t] = nat[h, pl.ds(SUBS + t, SUBS, stride=steps), :]
        return carry

    lax.fori_loop(0, height, spread_grad, 0)

    def tap_body(i, carry):
        total = [[None] * 7 for _ in range(halves)]
        for p in range(height):
            window = [[spread[h, p + i, t] for t in range(6)] for h in range(halves)]
            for t in range(steps):
                for h in range(halves):
                    window[h].append(spread[h, p + i, t + 6])
                    grad = grads[h, p, t]
                    for j in range(7):
                        term = window[h][t + j] * grad
                        total[h][j] = term if total[h][j] is None else total[h][j] + term
        for h in range(halves):
            for j in range(7):
                sums[h, i * 7 + j] = jnp.sum(total[h][j], axis=0, keepdims=True)
        return carry

    lax.fori_loop(0, 7, tap_body, 0)
    total[...] = jnp.zeros_like(total)
    for h in range(halves):
        total[0:49, h * LANES : (h + 1) * LANES] = sums[h].reshape(49, LANES)
    rows = hsum_ref.shape[1] // channels
    at = 49
    for c in range(rows):
        total[at + c : at + c + 1, :] = jnp.sum(hsum_ref[:, c * channels : (c + 1) * channels], axis=0, keepdims=True)
    at += rows
    for c in range(5):
        total[at + c : at + c + 1, :] = jnp.sum(chan_ref[c], axis=0, keepdims=True)
    small_ref[...] = total[...]


def input_grad_kernel(top_ref, bottom_ref, part_ref, kern_ref, cot_ref, grad_ref, nat, spread, taps):
    height, breadth, channels = cot_ref.shape
    halves = channels // LANES
    steps, cells = dims_of(breadth)
    fill_taps(kern_ref, taps, halves, True)
    for r in range(EDGE):
        spread_row(top_ref[r], nat, spread, r, halves, breadth)
        spread_row(bottom_ref[r], nat, spread, EDGE + r, halves, breadth)
    n_runs, length = runs_of(steps)
    for p in range(height):

        def run_body(index, carry, p=p):
            h = index // n_runs
            start = (index % n_runs) * length
            base = p * steps + start
            total = conv_run(
                lambda slot, u: spread[h, slot, start + u],
                taps,
                h,
                halo_taps(p, height),
                length,
                [part_ref[h, base + t] for t in range(length)],
            )
            for t in range(length):
                nat[h, pl.ds(SUBS + start + t, SUBS, stride=steps), :] = total[t]
            return carry

        lax.fori_loop(0, halves * n_runs, run_body, 0)
        for h in range(halves):
            lanes = slice(h * LANES, (h + 1) * LANES)
            grad_ref[p, :, lanes] = (cot_ref[p, :, lanes].astype(F32) + gather_row(nat, h, breadth)).astype(BF16)


def call(kernel, out_shape, scratch, flops, nbytes, name):
    def run(*operands):
        whole = pl.BlockSpec(memory_space=pltpu.VMEM)
        scalars = pl.BlockSpec(memory_space=pltpu.SMEM)
        return pl.pallas_call(
            kernel,
            out_shape=out_shape,
            in_specs=[scalars if x.dtype == jnp.int32 else whole for x in operands],
            out_specs=jax.tree.map(lambda _: whole, out_shape),
            scratch_shapes=scratch,
            compiler_params=pltpu.CompilerParams(vmem_limit_bytes=VMEM_LIMIT),
            cost_estimate=pl.CostEstimate(flops=flops, bytes_accessed=nbytes, transcendentals=0),
            name=name,
        )(*operands)

    return run


def place_kernel(digits, rows, factor, place_ref, here_ref, across_ref, other_ref, other_across_ref, *rest):
    w_in_ref, w_out_ref, kernel_ref, hidden_ref, chan_ref, total = rest
    channels = here_ref.shape[1]
    order = [[]]
    for stride, size in digits[:-1]:
        order = [[k] + tail for k in range(size) for tail in order]
    order = [ks[::-1] for ks in order]
    share = (here_ref.shape[0] - SMALL) // len(order)
    draw = place_ref[0]
    small = jnp.zeros((SMALL, channels), F32)
    for flip, refs in ((0, (here_ref, across_ref)), (1, (other_ref, other_across_ref))):
        for last, ref in enumerate(refs):
            values = ref[...].astype(F32)
            small = small + values[-SMALL:]
            for n, ks in enumerate(order):
                extent = rows
                start = 0
                for d, (stride, size) in enumerate(digits):
                    extent = extent // size
                    k = ks[d] if d < len(ks) else last
                    start = start + (place_ref[1 + d] ^ k) * extent
                start = pl.multiple_of(start, SUBS)
                total[draw ^ flip, pl.ds(start, share), :] = values[n * share : (n + 1) * share]
    big = w_out_ref.shape[0]
    for c in range(big // channels):
        cols = slice(c * channels, (c + 1) * channels)
        w_in_ref[:, cols] = total[0, cols, :] * factor
    w_out_ref[...] = total[1, 0:big, :] * factor
    small = small * factor
    for i in range(7):
        kernel_ref[i] = small[i * 7 : i * 7 + 7]
    blocks = big // channels
    halves = channels // LANES
    for c in range(blocks):
        for h in range(halves):
            hidden_ref[c * halves + h : c * halves + h + 1, :] = small[49 + c : 50 + c, h * LANES : (h + 1) * LANES]
    chan_ref[...] = small[49 + blocks : 54 + blocks]


def digits_of(count):
    digits = [(1, 2)]
    stride = 2
    while stride < count:
        size = min(4, count // stride)
        digits.append((stride, size))
        stride *= size
    return digits[::-1]


def exchange(values, count, stride, size, k):
    pairs = []
    for i in range(count):
        digit = i // stride % size
        pairs.append((i, i + ((digit ^ k) - digit) * stride))
    return lax.ppermute(values, "tile", pairs)


def other_core(values, draws):
    return lax.ppermute(values, "draw", [(i, i ^ 1) for i in range(draws)])


def halo(cells, tiles):
    after = [(i, i + 1) for i in range(tiles - 1)]
    before = [(i + 1, i) for i in range(tiles - 1)]
    top = lax.ppermute(cells[-EDGE:], "tile", after)
    bottom = lax.ppermute(cells[:EDGE], "tile", before)
    return top, bottom


def per_device(
    tiles,
    draws,
    inputs,
    land_mask,
    kernel,
    conv_bias,
    norm_gain,
    norm_bias,
    w_in,
    b_in,
    w_out,
    b_out,
    layer_scale,
    cotangent,
):
    _, height, breadth, channels = inputs.shape
    hidden_units = w_in.shape[1]
    halves = channels // LANES
    steps, cells = dims_of(breadth)
    own = inputs[0]
    cot = cotangent[0]
    top, bottom = halo(own, tiles)
    mask = jnp.pad(land_mask.astype(F32), ((0, 0), (0, cells - breadth)))
    mask = mask.reshape(height, SUBS, steps)

    def row(vector):
        return vector.reshape(1, -1)

    nat = pltpu.VMEM((halves, cells + 2 * SUBS, LANES), F32)

    def spread(slots):
        return pltpu.VMEM((halves, slots, steps + 2 * EDGE, SUBS, LANES), F32)

    taps = pltpu.VMEM((halves, 49, SUBS, LANES), F32)
    big_row = pltpu.VMEM((2 * cells, channels), F32)
    narrow = pltpu.VMEM((2 * cells, LANES), F32)
    count = height * cells
    big = hidden_units
    digits = digits_of(tiles)
    unit = tiles * SUBS
    rows = -(-big // unit) * unit
    tile = lax.axis_index("tile")
    place = jnp.stack([lax.axis_index("draw")] + [tile // stride % size for stride, size in digits]).astype(jnp.int32)
    part_shape = jax.ShapeDtypeStruct((halves, height * steps, SUBS, LANES), F32)
    mega = 1024 * 1024

    def own_conv(rows_here, flip, name):
        return call(
            functools.partial(own_conv_kernel, flip), part_shape, [nat, spread(height), taps], 4096 * mega, 2 * mega, name
        )(rows_here, kernel)

    part = own_conv(own, False, "own_conv")
    out, gconv, keep, send, hsum, chan = call(
        main_kernel,
        (
            jax.ShapeDtypeStruct((height, breadth, channels), BF16),
            jax.ShapeDtypeStruct((height, breadth, channels), BF16),
            jax.ShapeDtypeStruct((big, channels), F32),
            jax.ShapeDtypeStruct((big, channels), BF16),
            jax.ShapeDtypeStruct((SUBS, hidden_units), F32),
            jax.ShapeDtypeStruct((5, SUBS, channels), F32),
        ),
        [
            nat,
            nat,
            spread(2 * EDGE),
            taps,
            pltpu.VMEM((halves, count, LANES), F32),
            big_row,
            big_row,
            big_row,
            big_row,
            big_row,
            narrow,
            narrow,
            pltpu.VMEM((count, channels), BF16),
            pltpu.VMEM((count, hidden_units), BF16),
            pltpu.VMEM((count, channels), BF16),
            pltpu.VMEM((count, hidden_units), BF16),
        ],
        12 * count * channels * hidden_units,
        8 * mega,
        "block_main",
    )(
        place, own, top, bottom, part, cot, mask, kernel, row(conv_bias), row(norm_gain), row(norm_bias), w_in, row(b_in),
        w_out, row(b_out), row(layer_scale),
    )
    grad_top, grad_bottom = halo(gconv, tiles)
    got = other_core(send, draws)
    if rows > big:
        keep = jnp.pad(keep, ((0, rows - big), (0, 0)))
        got = jnp.pad(got, ((0, rows - big), (0, 0)))
    for step, (stride, size) in enumerate(digits):
        share = keep.shape[0] // size
        mine = place[1 + step]
        pieces = []
        for k in range(size):
            piece = lax.dynamic_slice_in_dim(keep, (mine ^ k) * share, share, 0)
            if not step:
                piece = piece + lax.dynamic_slice_in_dim(got, (mine ^ k) * share, share, 0).astype(F32)
            pieces.append(piece)
        sends = [piece.astype(BF16) for piece in pieces[1:]]
        if not step:
            sends, hsum = lax.optimization_barrier((sends, hsum))
        received = [exchange(sends[k - 1], tiles, stride, size, k) for k in range(1, size)]
        if not step:
            small = call(
                kernel_grad_kernel,
                jax.ShapeDtypeStruct((SMALL, channels), F32),
                [
                    nat,
                    spread(height + 2 * EDGE),
                    pltpu.VMEM((halves, height, steps, SUBS, LANES), F32),
                    pltpu.VMEM((halves, 49, 1, LANES), F32),
                    pltpu.VMEM((SMALL, channels), F32),
                ],
                16384 * mega,
                4 * mega,
                "kernel_grad",
            )(own, top, bottom, gconv, hsum, chan)
            grad_part = own_conv(gconv, True, "own_conv_grad")
            received, small, grad_part = lax.optimization_barrier((received, small, grad_part))
        keep = pieces[0]
        for piece in received:
            keep = keep + piece.astype(F32)
    input_grad = call(
        input_grad_kernel,
        jax.ShapeDtypeStruct((height, breadth, channels), BF16),
        [nat, spread(2 * EDGE), taps],
        2048 * mega,
        4 * mega,
        "input_grad",
    )(grad_top, grad_bottom, grad_part, kernel, cot)
    gathered = keep.astype(BF16)
    for step, (stride, size) in enumerate(digits[:-1]):
        payload = jnp.concatenate([gathered, small.astype(BF16)], axis=0)
        received = [payload] + [exchange(payload, tiles, stride, size, k) for k in range(1, size)]
        if step == len(digits) - 2:
            received, input_grad = lax.optimization_barrier((received, input_grad))
        gathered = jnp.concatenate([piece[:-SMALL] for piece in received], axis=0)
        small = functools.reduce(jnp.add, [piece[-SMALL:].astype(F32) for piece in received])
    gathered = jnp.concatenate([gathered, small.astype(BF16)], axis=0)

    stride, size = digits[-1]
    across = exchange(gathered, tiles, stride, size, 1)
    other = other_core(gathered, draws)
    other_across = other_core(across, draws)
    factor = float(1.0 / np.sqrt(np.float32(draws * height * tiles * breadth)))
    w_in_sum, w_out_sum, kernel_sum, hidden_sum, chan_sum = call(
        functools.partial(place_kernel, digits, rows, factor),
        (
            jax.ShapeDtypeStruct((channels, hidden_units), F32),
            jax.ShapeDtypeStruct((hidden_units, channels), F32),
            jax.ShapeDtypeStruct((7, 7, channels), F32),
            jax.ShapeDtypeStruct((hidden_units // LANES, LANES), F32),
            jax.ShapeDtypeStruct((5, channels), F32),
        ),
        [pltpu.VMEM((2, rows, channels), F32)],
        1024 * 1024,
        4 * 1024 * 1024,
        "place",
    )(place, gathered, across, other, other_across)
    return (
        out[None],
        input_grad[None],
        kernel_sum,
        w_in_sum,
        w_out_sum,
        hidden_sum.reshape(-1),
        chan_sum,
    )


def solution(mesh):
    placed = (
        P(("group", "draw"), "tile", None, None),
        P("tile", None),
        P(),
        P(),
        P(),
        P(),
        P(),
        P(),
        P(),
        P(),
        P(),
        P(("group", "draw"), "tile", None, None),
    )
    return jax.shard_map(
        functools.partial(per_device, mesh.shape["tile"], mesh.shape["draw"]),
        mesh=mesh,
        in_specs=placed,
        out_specs=(
            P(("group", "draw"), "tile", None, None),
            P(("group", "draw"), "tile", None, None),
            P("group", None, None),
            P("group", None),
            P("group", None),
            P("group"),
            P("group", None),
        ),
        check_vma=False,
    )
```

```python
import functools

import jax
import jax.numpy as jnp
import numpy as np
from jax import lax
from jax.experimental import pallas as pl
from jax.experimental.pallas import tpu as pltpu
from jax.sharding import PartitionSpec as P

ROOT_TERM = 0.7978845608028654
CUBIC = 0.044715
EPSILON = 1e-06
F32 = jnp.float32
BF16 = jnp.bfloat16
LANES = 128
SUBS = 8
EDGE = 3
SMALL = 64
VMEM_LIMIT = 56 * 1024 * 1024


def dims_of(breadth):
    steps = -(-breadth // SUBS)
    return steps, steps * SUBS


def spread_row(row, nat, spread, slot, halves, breadth):
    steps, cells = dims_of(breadth)
    row = row.astype(F32)
    over = cells - breadth + EDGE
    for h in range(halves):
        part = row[:, h * LANES : (h + 1) * LANES]
        nat[h, SUBS : SUBS + breadth, :] = part
        nat[h, SUBS - EDGE : SUBS, :] = part[breadth - EDGE :]
        nat[h, SUBS + breadth : SUBS + breadth + over, :] = part[:over]
    for h in range(halves):
        for t in range(steps + 2 * EDGE):
            spread[h, slot, t] = nat[h, pl.ds(SUBS - EDGE + t, SUBS, stride=steps), :]


def gather_row(nat, h, breadth):
    return nat[h, SUBS : SUBS + breadth, :]


def fill_taps(kern_ref, taps, halves, flip):
    for i in range(7):
        for j in range(7):
            src = kern_ref[6 - i, 6 - j : 7 - j, :] if flip else kern_ref[i, j : j + 1, :]
            for h in range(halves):
                taps[h, i * 7 + j] = jnp.broadcast_to(src[:, h * LANES : (h + 1) * LANES], (SUBS, LANES))


def conv_run(cells_at, taps, h, row_taps, length, total):
    total = list(total)
    for i, slot in row_taps:
        weights = [taps[h, i * 7 + j] for j in range(7)]
        for u in range(length + 6):
            cell = cells_at(slot, u)
            for j in range(7):
                t = u - j
                if 0 <= t < length:
                    term = cell * weights[j]
                    total[t] = term if total[t] is None else total[t] + term
    return total


def own_taps(p, height):
    return [(i, p + i - EDGE) for i in range(7) if 0 <= p + i - EDGE < height]


def halo_taps(p, height):
    found = []
    for i in range(7):
        row = p + i
        if row < EDGE:
            found.append((i, row))
        elif row >= EDGE + height:
            found.append((i, row - height))
    return found


def runs_of(steps):
    length = steps // 2 if steps % 2 == 0 else steps
    return steps // length, length


def own_conv_kernel(flip, own_ref, kern_ref, part_ref, nat, spread, taps):
    height, breadth, channels = own_ref.shape
    halves = channels // LANES
    steps, cells = dims_of(breadth)
    fill_taps(kern_ref, taps, halves, flip)

    def spread_own(p, carry):
        spread_row(own_ref[p], nat, spread, p, halves, breadth)
        return carry

    lax.fori_loop(0, height, spread_own, 0)
    n_runs, length = runs_of(steps)
    for p in range(height):

        def run_body(index, carry, p=p):
            h = index // n_runs
            start = (index % n_runs) * length
            total = conv_run(
                lambda slot, u: spread[h, slot, start + u], taps, h, own_taps(p, height), length, [None] * length
            )
            for t in range(length):
                part_ref[h, p * steps + start + t] = total[t]
            return carry

        lax.fori_loop(0, halves * n_runs, run_body, 0)


def main_kernel(
    place_ref, own_ref, top_ref, bottom_ref, part_ref, cot_ref, mask_ref, kern_ref, cbias_ref, gain_ref, nbias_ref, w_in_ref,
    b_in_ref, w_out_ref, b_out_ref, scale_ref,
    out_ref, gconv_ref, keep_ref, send_ref, hsum_ref, chan_ref,
    nat, out_s, spread, taps, conv, units, cots, state_s, mixed_s, gnorm_s, ocean_s, inv_s, normed_s, act_s, gmix_s, ghid_s,
):
    height, breadth, channels = own_ref.shape
    hidden_units = w_in_ref.shape[1]
    halves = channels // LANES
    steps, cells = dims_of(breadth)

    fill_taps(kern_ref, taps, halves, False)
    for r in range(EDGE):
        spread_row(top_ref[r], nat, spread, r, halves, breadth)
        spread_row(bottom_ref[r], nat, spread, EDGE + r, halves, breadth)
    n_runs, length = runs_of(steps)
    for p in range(height):

        def conv_body(index, carry, p=p):
            h = index // n_runs
            start = (index % n_runs) * length
            base = p * steps + start
            total = conv_run(
                lambda slot, u: spread[h, slot, start + u],
                taps,
                h,
                halo_taps(p, height),
                length,
                [part_ref[h, base + t] for t in range(length)],
            )
            for t in range(length):
                conv[h, pl.ds(pl.multiple_of((base + t) * SUBS, SUBS), SUBS), :] = total[t]
            return carry

        lax.fori_loop(0, halves * n_runs, conv_body, 0)

    hsum_ref[...] = jnp.zeros_like(hsum_ref)
    chan_ref[...] = jnp.zeros_like(chan_ref)
    width = 256
    inv_c = 1.0 / channels
    sides = range(halves)
    lanes = [slice(h * LANES, (h + 1) * LANES) for h in sides]

    def column_sum(values):
        return jnp.sum(values.reshape(values.shape[0] // SUBS, SUBS, values.shape[1]), axis=0)

    def mean_of(parts):
        return jnp.sum(functools.reduce(jnp.add, parts), axis=1, keepdims=True) * inv_c

    pack = 2 if height % 2 == 0 else 1

    def row_body(pp, carry):
        base2 = pl.multiple_of(pp * (pack * cells), 16)
        rows = pl.ds(base2, pack * cells)
        for q in range(pack):
            p = pp * pack + q
            base = pl.multiple_of(base2 + q * cells, 16)
            cot = cot_ref[p].astype(F32)
            for h in sides:
                nat[h, SUBS : SUBS + breadth, :] = cot[:, lanes[h]]
                out_s[h, SUBS : SUBS + breadth, :] = own_ref[p, :, lanes[h]].astype(F32)
            land = mask_ref[p]
            for t in range(0, steps, 2):
                here = pl.ds(base + t * SUBS, 2 * SUBS)
                local = slice(q * cells + t * SUBS, q * cells + (t + 2) * SUBS)
                values = [conv[h, here, :] + cbias_ref[:, lanes[h]] for h in sides]
                center = mean_of(values)
                deviation = [v - center for v in values]
                inv_std = lax.rsqrt(mean_of([d * d for d in deviation]) + EPSILON)
                inv_s[local, :] = jnp.broadcast_to(inv_std, (2 * SUBS, LANES))
                ocean = jnp.concatenate([jnp.broadcast_to(land[:, t + k : t + k + 1], (SUBS, LANES)) for k in range(2)], axis=0)
                ocean_s[local, :] = ocean
                for h in sides:
                    unit = deviation[h] * inv_std
                    units[local, lanes[h]] = unit
                    normed_s[here, lanes[h]] = (unit * gain_ref[:, lanes[h]] + nbias_ref[:, lanes[h]]).astype(BF16)
                    cell = jnp.concatenate(
                        [nat[h, pl.ds(SUBS + t + k, SUBS, stride=steps), :] for k in range(2)], axis=0
                    )
                    upstream = jnp.where(ocean > 0, cell, 0.0)
                    cots[local, lanes[h]] = upstream
                    state_s[local, lanes[h]] = jnp.concatenate(
                        [out_s[h, pl.ds(SUBS + t + k, SUBS, stride=steps), :] for k in range(2)], axis=0
                    )
                    gmix_s[here, lanes[h]] = (scale_ref[:, lanes[h]] * upstream).astype(BF16)
        normed = normed_s[rows, :]
        gmix = gmix_s[rows, :]
        for c in range(0, hidden_units, width):
            cols = slice(c, c + width)
            hidden = jnp.dot(normed, w_in_ref[:, cols], preferred_element_type=F32) + b_in_ref[:, cols]
            grad_act = lax.dot_general(
                gmix, w_out_ref[cols, :], (((1,), (1,)), ((), ())), preferred_element_type=F32
            )
            square = hidden * hidden
            inner = hidden * (ROOT_TERM * CUBIC * square + ROOT_TERM)
            half_tanh = 0.5 * jnp.tanh(inner)
            gate = 0.5 + half_tanh
            active = hidden * gate
            slope = gate + active * (0.5 - half_tanh) * (6.0 * CUBIC * ROOT_TERM * square + 2.0 * ROOT_TERM)
            act = active.astype(BF16)
            act_s[rows, cols] = act
            mixed = jnp.dot(act, w_out_ref[cols, :], preferred_element_type=F32)
            ghid = (grad_act * slope).astype(BF16)
            ghid_s[rows, cols] = ghid
            hsum_ref[:, cols] += column_sum(ghid.astype(F32))
            grad_normed = lax.dot_general(
                ghid, w_in_ref[:, cols], (((1,), (1,)), ((), ())), preferred_element_type=F32
            )
            if c:
                mixed_s[...] += mixed
                gnorm_s[...] += grad_normed
            else:
                mixed_s[...] = mixed
                gnorm_s[...] = grad_normed
        for q in range(pack):
            p = pp * pack + q
            base = pl.multiple_of(base2 + q * cells, 16)
            sums = [[None] * halves for _ in range(5)]

            def add_to(n, h, values):
                folded = values[:SUBS] + values[SUBS:]
                sums[n][h] = folded if sums[n][h] is None else sums[n][h] + folded

            for t in range(0, steps, 2):
                here = pl.ds(base + t * SUBS, 2 * SUBS)
                local = slice(q * cells + t * SUBS, q * cells + (t + 2) * SUBS)
                ocean = ocean_s[local, :]
                scaled, products, units_here = [], [], []
                for h in sides:
                    mixed = mixed_s[local, lanes[h]] + b_out_ref[:, lanes[h]]
                    add_to(4, h, cots[local, lanes[h]] * mixed)
                    residual = jnp.where(ocean > 0, scale_ref[:, lanes[h]] * mixed, 0.0)
                    result = state_s[local, lanes[h]] + residual
                    for k in range(2):
                        out_s[h, pl.ds(SUBS + t + k, SUBS, stride=steps), :] = result[k * SUBS : (k + 1) * SUBS]
                    grad_normed = gnorm_s[local, lanes[h]]
                    unit = units[local, lanes[h]]
                    add_to(1, h, grad_normed * unit)
                    add_to(2, h, grad_normed)
                    add_to(3, h, gmix_s[here, lanes[h]].astype(F32))
                    scaled.append(grad_normed * gain_ref[:, lanes[h]])
                    units_here.append(unit)
                    products.append(scaled[h] * unit)
                mean_scaled = mean_of(scaled)
                mean_product = mean_of(products)
                inv_std = inv_s[local, :]
                for h in sides:
                    grad_conv = (inv_std * (scaled[h] - mean_scaled - units_here[h] * mean_product)).astype(BF16).astype(F32)
                    add_to(0, h, grad_conv)
                    for k in range(2):
                        nat[h, pl.ds(SUBS + t + k, SUBS, stride=steps), :] = grad_conv[k * SUBS : (k + 1) * SUBS]
            for n in range(5):
                for h in sides:
                    chan_ref[n, :, lanes[h]] += sums[n][h]
            for h in sides:
                out_ref[p, :, lanes[h]] = gather_row(out_s, h, breadth).astype(BF16)
                gconv_ref[p, :, lanes[h]] = gather_row(nat, h, breadth).astype(BF16)
        return carry

    lax.fori_loop(0, height // pack, row_body, 0)

    first = (((0,), (0,)), ((), ()))

    def store_block(half, c, block):
        @pl.when(place_ref[0] == half)
        def _():
            keep_ref[c : c + width, :] = block

        @pl.when(place_ref[0] != half)
        def _():
            send_ref[c : c + width, :] = block.astype(BF16)

    normed = normed_s[...]
    for c in range(0, hidden_units, width):
        cols = slice(c, c + width)
        store_block(0, c, lax.dot_general(normed, ghid_s[:, cols], first, preferred_element_type=F32))
    gmix = gmix_s[...]
    for c in range(0, hidden_units, width):
        cols = slice(c, c + width)
        store_block(1, c, lax.dot_general(act_s[:, cols], gmix, first, preferred_element_type=F32))


def kernel_grad_kernel(
    own_ref, top_ref, bottom_ref, gconv_ref, hsum_ref, chan_ref, small_ref, nat, spread, grads, sums, total
):
    height, breadth, channels = own_ref.shape
    halves = channels // LANES
    steps, cells = dims_of(breadth)
    for r in range(EDGE):
        spread_row(top_ref[r], nat, spread, r, halves, breadth)
        spread_row(bottom_ref[r], nat, spread, EDGE + height + r, halves, breadth)

    def spread_own(p, carry):
        spread_row(own_ref[p], nat, spread, EDGE + p, halves, breadth)
        return carry

    lax.fori_loop(0, height, spread_own, 0)

    nat[:, SUBS + breadth : SUBS + cells, :] = jnp.zeros((halves, cells - breadth, LANES), F32)

    def spread_grad(p, carry):
        row = gconv_ref[p].astype(F32)
        for h in range(halves):
            nat[h, SUBS : SUBS + breadth, :] = row[:, h * LANES : (h + 1) * LANES]
        for h in range(halves):
            for t in range(steps):
                grads[h, p, t] = nat[h, pl.ds(SUBS + t, SUBS, stride=steps), :]
        return carry

    lax.fori_loop(0, height, spread_grad, 0)

    def tap_body(i, carry):
        total = [[None] * 7 for _ in range(halves)]
        for p in range(height):
            window = [[spread[h, p + i, t] for t in range(6)] for h in range(halves)]
            for t in range(steps):
                for h in range(halves):
                    window[h].append(spread[h, p + i, t + 6])
                    grad = grads[h, p, t]
                    for j in range(7):
                        term = window[h][t + j] * grad
                        total[h][j] = term if total[h][j] is None else total[h][j] + term
        for h in range(halves):
            for j in range(7):
                sums[h, i * 7 + j] = jnp.sum(total[h][j], axis=0, keepdims=True)
        return carry

    lax.fori_loop(0, 7, tap_body, 0)
    total[...] = jnp.zeros_like(total)
    for h in range(halves):
        total[0:49, h * LANES : (h + 1) * LANES] = sums[h].reshape(49, LANES)
    rows = hsum_ref.shape[1] // channels
    at = 49
    for c in range(rows):
        total[at + c : at + c + 1, :] = jnp.sum(hsum_ref[:, c * channels : (c + 1) * channels], axis=0, keepdims=True)
    at += rows
    for c in range(5):
        total[at + c : at + c + 1, :] = jnp.sum(chan_ref[c], axis=0, keepdims=True)
    small_ref[...] = total[...]


def input_grad_kernel(top_ref, bottom_ref, part_ref, kern_ref, cot_ref, grad_ref, nat, spread, taps):
    height, breadth, channels = cot_ref.shape
    halves = channels // LANES
    steps, cells = dims_of(breadth)
    fill_taps(kern_ref, taps, halves, True)
    for r in range(EDGE):
        spread_row(top_ref[r], nat, spread, r, halves, breadth)
        spread_row(bottom_ref[r], nat, spread, EDGE + r, halves, breadth)
    n_runs, length = runs_of(steps)
    for p in range(height):

        def run_body(index, carry, p=p):
            h = index // n_runs
            start = (index % n_runs) * length
            base = p * steps + start
            total = conv_run(
                lambda slot, u: spread[h, slot, start + u],
                taps,
                h,
                halo_taps(p, height),
                length,
                [part_ref[h, base + t] for t in range(length)],
            )
            for t in range(length):
                nat[h, pl.ds(SUBS + start + t, SUBS, stride=steps), :] = total[t]
            return carry

        lax.fori_loop(0, halves * n_runs, run_body, 0)
        for h in range(halves):
            lanes = slice(h * LANES, (h + 1) * LANES)
            grad_ref[p, :, lanes] = (cot_ref[p, :, lanes].astype(F32) + gather_row(nat, h, breadth)).astype(BF16)


def call(kernel, out_shape, scratch, flops, nbytes, name, limit=VMEM_LIMIT):
    def run(*operands):
        whole = pl.BlockSpec(memory_space=pltpu.VMEM)
        scalars = pl.BlockSpec(memory_space=pltpu.SMEM)
        return pl.pallas_call(
            kernel,
            out_shape=out_shape,
            in_specs=[scalars if x.dtype == jnp.int32 else whole for x in operands],
            out_specs=jax.tree.map(lambda _: whole, out_shape),
            scratch_shapes=scratch,
            compiler_params=pltpu.CompilerParams(vmem_limit_bytes=limit),
            cost_estimate=pl.CostEstimate(flops=flops, bytes_accessed=nbytes, transcendentals=0),
            name=name,
        )(*operands)

    return run


def place_kernel(digits, rows, factor, place_ref, here_ref, across_ref, other_ref, other_across_ref, *rest):
    w_in_ref, w_out_ref, kernel_ref, hidden_ref, chan_ref, total = rest
    channels = here_ref.shape[1]
    order = [[]]
    for stride, size in digits[1:]:
        order = [tail + [k] for k in range(size) for tail in order]
    share = (here_ref.shape[0] - SMALL) // len(order)
    draw = place_ref[0]
    small = jnp.zeros((SMALL, channels), F32)
    for flip, refs in ((0, (here_ref, across_ref)), (1, (other_ref, other_across_ref))):
        for last, ref in enumerate(refs):
            values = ref[...].astype(F32)
            small = small + values[-SMALL:]
            for n, ks in enumerate(order):
                extent = rows
                start = 0
                for d, (stride, size) in enumerate(digits):
                    extent = extent // size
                    k = ks[d - 1] if d else last
                    start = start + (place_ref[1 + d] ^ k) * extent
                start = pl.multiple_of(start, SUBS)
                total[draw ^ flip, pl.ds(start, share), :] = values[n * share : (n + 1) * share]
    big = w_out_ref.shape[0]
    for c in range(big // channels):
        cols = slice(c * channels, (c + 1) * channels)
        w_in_ref[:, cols] = total[0, cols, :] * factor
    w_out_ref[...] = total[1, 0:big, :] * factor
    small = small * factor
    for i in range(7):
        kernel_ref[i] = small[i * 7 : i * 7 + 7]
    blocks = big // channels
    halves = channels // LANES
    for c in range(blocks):
        for h in range(halves):
            hidden_ref[c * halves + h : c * halves + h + 1, :] = small[49 + c : 50 + c, h * LANES : (h + 1) * LANES]
    chan_ref[...] = small[49 + blocks : 54 + blocks]


def digits_of(count):
    digits = []
    stride = 2
    while stride < count:
        size = min(4, count // stride)
        digits.append((stride, size))
        stride *= size
    return [(1, 2)] + digits[::-1]


def exchange(values, count, stride, size, k):
    pairs = []
    for i in range(count):
        digit = i // stride % size
        pairs.append((i, i + ((digit ^ k) - digit) * stride))
    return lax.ppermute(values, "tile", pairs)


def other_core(values, draws):
    return lax.ppermute(values, "draw", [(i, i ^ 1) for i in range(draws)])


def halo(cells, tiles):
    after = [(i, i + 1) for i in range(tiles - 1)]
    before = [(i + 1, i) for i in range(tiles - 1)]
    top = lax.ppermute(cells[-EDGE:], "tile", after)
    bottom = lax.ppermute(cells[:EDGE], "tile", before)
    return top, bottom


def per_device(
    tiles,
    draws,
    inputs,
    land_mask,
    kernel,
    conv_bias,
    norm_gain,
    norm_bias,
    w_in,
    b_in,
    w_out,
    b_out,
    layer_scale,
    cotangent,
):
    _, height, breadth, channels = inputs.shape
    hidden_units = w_in.shape[1]
    halves = channels // LANES
    steps, cells = dims_of(breadth)
    own = inputs[0]
    cot = cotangent[0]
    top, bottom = halo(own, tiles)
    mask = jnp.pad(land_mask.astype(F32), ((0, 0), (0, cells - breadth)))
    mask = mask.reshape(height, SUBS, steps)

    def row(vector):
        return vector.reshape(1, -1)

    nat = pltpu.VMEM((halves, cells + 2 * SUBS, LANES), F32)

    def spread(slots):
        return pltpu.VMEM((halves, slots, steps + 2 * EDGE, SUBS, LANES), F32)

    taps = pltpu.VMEM((halves, 49, SUBS, LANES), F32)
    big_row = pltpu.VMEM((2 * cells, channels), F32)
    narrow = pltpu.VMEM((2 * cells, LANES), F32)
    count = height * cells
    big = hidden_units
    digits = digits_of(tiles)
    unit = tiles * SUBS
    rows = -(-big // unit) * unit
    tile = lax.axis_index("tile")
    place = jnp.stack([lax.axis_index("draw")] + [tile // stride % size for stride, size in digits]).astype(jnp.int32)
    part_shape = jax.ShapeDtypeStruct((halves, height * steps, SUBS, LANES), F32)
    mega = 1024 * 1024

    def own_conv(rows_here, flip, name):
        return call(
            functools.partial(own_conv_kernel, flip), part_shape, [nat, spread(height), taps], 4096 * mega, 2 * mega, name
        )(rows_here, kernel)

    part = own_conv(own, False, "own_conv")
    out, gconv, keep, send, hsum, chan = call(
        main_kernel,
        (
            jax.ShapeDtypeStruct((height, breadth, channels), BF16),
            jax.ShapeDtypeStruct((height, breadth, channels), BF16),
            jax.ShapeDtypeStruct((big, channels), F32),
            jax.ShapeDtypeStruct((big, channels), BF16),
            jax.ShapeDtypeStruct((SUBS, hidden_units), F32),
            jax.ShapeDtypeStruct((5, SUBS, channels), F32),
        ),
        [
            nat,
            nat,
            spread(2 * EDGE),
            taps,
            pltpu.VMEM((halves, count, LANES), F32),
            big_row,
            big_row,
            big_row,
            big_row,
            big_row,
            narrow,
            narrow,
            pltpu.VMEM((count, channels), BF16),
            pltpu.VMEM((count, hidden_units), BF16),
            pltpu.VMEM((count, channels), BF16),
            pltpu.VMEM((count, hidden_units), BF16),
        ],
        12 * count * channels * hidden_units,
        8 * mega,
        "block_main",
    )(
        place, own, top, bottom, part, cot, mask, kernel, row(conv_bias), row(norm_gain), row(norm_bias), w_in, row(b_in),
        w_out, row(b_out), row(layer_scale),
    )
    got = other_core(send, draws)

    if rows > big:
        keep = jnp.pad(keep, ((0, rows - big), (0, 0)))
        got = jnp.pad(got, ((0, rows - big), (0, 0)))
    for step, (stride, size) in enumerate(digits):
        share = keep.shape[0] // size
        mine = place[1 + step]
        pieces = []
        for k in range(size):
            piece = lax.dynamic_slice_in_dim(keep, (mine ^ k) * share, share, 0)
            if not step:
                piece = piece + lax.dynamic_slice_in_dim(got, (mine ^ k) * share, share, 0).astype(F32)
            pieces.append(piece)
        sends = [piece.astype(BF16) for piece in pieces[1:]]
        if not step:
            sends, hsum = lax.optimization_barrier((sends, hsum))
        elif step == 1:
            sends, gconv = lax.optimization_barrier((sends, gconv))
            grad_part = own_conv(gconv, True, "own_conv_grad")
        received = [exchange(sends[k - 1], tiles, stride, size, k) for k in range(1, size)]
        if not step:
            small = call(
                kernel_grad_kernel,
                jax.ShapeDtypeStruct((SMALL, channels), F32),
                [
                    nat,
                    spread(height + 2 * EDGE),
                    pltpu.VMEM((halves, height, steps, SUBS, LANES), F32),
                    pltpu.VMEM((halves, 49, 1, LANES), F32),
                    pltpu.VMEM((SMALL, channels), F32),
                ],
                16384 * mega,
                4 * mega,
                "kernel_grad",
            )(own, top, bottom, gconv, hsum, chan)
            received, small, gconv = lax.optimization_barrier((received, small, gconv))
            grad_top, grad_bottom = halo(gconv, tiles)
        elif step == 1:
            received, grad_part = lax.optimization_barrier((received, grad_part))
        keep = pieces[0]
        for piece in received:
            keep = keep + piece.astype(F32)
    gathered = keep.astype(BF16)
    for stride, size in digits[1:]:
        payload = jnp.concatenate([gathered, small.astype(BF16)], axis=0)
        received = [payload] + [exchange(payload, tiles, stride, size, k) for k in range(1, size)]
        received, grad_top, grad_bottom = lax.optimization_barrier((received, grad_top, grad_bottom))
        gathered = jnp.concatenate([piece[:-SMALL] for piece in received], axis=0)
        small = functools.reduce(jnp.add, [piece[-SMALL:].astype(F32) for piece in received])
    gathered = jnp.concatenate([gathered, small.astype(BF16)], axis=0)
    stride, size = digits[0]
    across = exchange(gathered, tiles, stride, size, 1)
    other = other_core(gathered, draws)
    input_grad = call(
        input_grad_kernel,
        jax.ShapeDtypeStruct((height, breadth, channels), BF16),
        [nat, spread(2 * EDGE), taps],
        2048 * mega,
        4 * mega,
        "input_grad",
    )(grad_top, grad_bottom, grad_part, kernel, cot)
    across, input_grad = lax.optimization_barrier((across, input_grad))
    other_across = other_core(across, draws)
    factor = float(1.0 / np.sqrt(np.float32(draws * height * tiles * breadth)))
    w_in_sum, w_out_sum, kernel_sum, hidden_sum, chan_sum = call(
        functools.partial(place_kernel, digits, rows, factor),
        (
            jax.ShapeDtypeStruct((channels, hidden_units), F32),
            jax.ShapeDtypeStruct((hidden_units, channels), F32),
            jax.ShapeDtypeStruct((7, 7, channels), F32),
            jax.ShapeDtypeStruct((hidden_units // LANES, LANES), F32),
            jax.ShapeDtypeStruct((5, channels), F32),
        ),
        [pltpu.VMEM((2, rows, channels), F32)],
        mega,
        4 * mega,
        "place",
        16 * mega,
    )(place, gathered, across, other, other_across)
    return (
        out[None],
        input_grad[None],
        kernel_sum,
        w_in_sum,
        w_out_sum,
        hidden_sum.reshape(-1),
        chan_sum,
    )


def solution(mesh):
    placed = (
        P(("group", "draw"), "tile", None, None),
        P("tile", None),
        P(),
        P(),
        P(),
        P(),
        P(),
        P(),
        P(),
        P(),
        P(),
        P(("group", "draw"), "tile", None, None),
    )
    return jax.shard_map(
        functools.partial(per_device, mesh.shape["tile"], mesh.shape["draw"]),
        mesh=mesh,
        in_specs=placed,
        out_specs=(
            P(("group", "draw"), "tile", None, None),
            P(("group", "draw"), "tile", None, None),
            P("group", None, None),
            P("group", None),
            P("group", None),
            P("group"),
            P("group", None),
        ),
        check_vma=False,
    )
```

```python
import functools

import jax
import jax.numpy as jnp
import numpy as np
from jax import lax
from jax.experimental import pallas as pl
from jax.experimental.pallas import tpu as pltpu
from jax.sharding import PartitionSpec as P

ROOT_TERM = 0.7978845608028654
CUBIC = 0.044715
EPSILON = 1e-06
F32 = jnp.float32
BF16 = jnp.bfloat16
LANES = 128
SUBS = 8
EDGE = 3
SMALL = 64
VMEM_LIMIT = 56 * 1024 * 1024


def dims_of(breadth):
    steps = -(-breadth // SUBS)
    return steps, steps * SUBS


def spread_row(row, nat, spread, slot, halves, breadth):
    steps, cells = dims_of(breadth)
    row = row.astype(F32)
    over = cells - breadth + EDGE
    for h in range(halves):
        part = row[:, h * LANES : (h + 1) * LANES]
        nat[h, SUBS : SUBS + breadth, :] = part
        nat[h, SUBS - EDGE : SUBS, :] = part[breadth - EDGE :]
        nat[h, SUBS + breadth : SUBS + breadth + over, :] = part[:over]
    for h in range(halves):
        for t in range(steps + 2 * EDGE):
            spread[h, slot, t] = nat[h, pl.ds(SUBS - EDGE + t, SUBS, stride=steps), :]


def gather_row(nat, h, breadth):
    return nat[h, SUBS : SUBS + breadth, :]


def fill_taps(kern_ref, taps, halves, flip):
    for i in range(7):
        for j in range(7):
            src = kern_ref[6 - i, 6 - j : 7 - j, :] if flip else kern_ref[i, j : j + 1, :]
            for h in range(halves):
                taps[h, i * 7 + j] = jnp.broadcast_to(src[:, h * LANES : (h + 1) * LANES], (SUBS, LANES))


def conv_run(cells_at, taps, h, row_taps, length, total):
    total = list(total)
    for i, slot in row_taps:
        weights = [taps[h, i * 7 + j] for j in range(7)]
        for u in range(length + 6):
            cell = cells_at(slot, u)
            for j in range(7):
                t = u - j
                if 0 <= t < length:
                    term = cell * weights[j]
                    total[t] = term if total[t] is None else total[t] + term
    return total


def own_taps(p, height):
    return [(i, p + i - EDGE) for i in range(7) if 0 <= p + i - EDGE < height]


def halo_taps(p, height):
    found = []
    for i in range(7):
        row = p + i
        if row < EDGE:
            found.append((i, row))
        elif row >= EDGE + height:
            found.append((i, row - height))
    return found


def runs_of(steps):
    length = steps // 2 if steps % 2 == 0 else steps
    return steps // length, length


def own_conv_kernel(flip, own_ref, kern_ref, part_ref, nat, spread, taps):
    height, breadth, channels = own_ref.shape
    halves = channels // LANES
    steps, cells = dims_of(breadth)
    fill_taps(kern_ref, taps, halves, flip)

    def spread_own(p, carry):
        spread_row(own_ref[p], nat, spread, p, halves, breadth)
        return carry

    lax.fori_loop(0, height, spread_own, 0)
    n_runs, length = runs_of(steps)
    for p in range(height):

        def run_body(index, carry, p=p):
            h = index // n_runs
            start = (index % n_runs) * length
            total = conv_run(
                lambda slot, u: spread[h, slot, start + u], taps, h, own_taps(p, height), length, [None] * length
            )
            for t in range(length):
                part_ref[h, p * steps + start + t] = total[t]
            return carry

        lax.fori_loop(0, halves * n_runs, run_body, 0)


def main_kernel(
    place_ref, own_ref, top_ref, bottom_ref, part_ref, cot_ref, mask_ref, kern_ref, cbias_ref, gain_ref, nbias_ref, w_in_ref,
    b_in_ref, w_out_ref, b_out_ref, scale_ref,
    out_ref, gconv_ref, keep_ref, send_ref, hsum_ref, chan_ref,
    nat, out_s, spread, taps, conv, units, cots, state_s, mixed_s, gnorm_s, ocean_s, inv_s, normed_s, act_s, gmix_s, ghid_s,
):
    height, breadth, channels = own_ref.shape
    hidden_units = w_in_ref.shape[1]
    halves = channels // LANES
    steps, cells = dims_of(breadth)

    fill_taps(kern_ref, taps, halves, False)
    for r in range(EDGE):
        spread_row(top_ref[r], nat, spread, r, halves, breadth)
        spread_row(bottom_ref[r], nat, spread, EDGE + r, halves, breadth)
    n_runs, length = runs_of(steps)
    for p in range(height):

        def conv_body(index, carry, p=p):
            h = index // n_runs
            start = (index % n_runs) * length
            base = p * steps + start
            total = conv_run(
                lambda slot, u: spread[h, slot, start + u],
                taps,
                h,
                halo_taps(p, height),
                length,
                [part_ref[h, base + t] for t in range(length)],
            )
            for t in range(length):
                conv[h, pl.ds(pl.multiple_of((base + t) * SUBS, SUBS), SUBS), :] = total[t]
            return carry

        lax.fori_loop(0, halves * n_runs, conv_body, 0)

    hsum_ref[...] = jnp.zeros_like(hsum_ref)
    chan_ref[...] = jnp.zeros_like(chan_ref)
    width = 256
    inv_c = 1.0 / channels
    sides = range(halves)
    lanes = [slice(h * LANES, (h + 1) * LANES) for h in sides]

    def column_sum(values):
        return jnp.sum(values.reshape(values.shape[0] // SUBS, SUBS, values.shape[1]), axis=0)

    def mean_of(parts):
        return jnp.sum(functools.reduce(jnp.add, parts), axis=1, keepdims=True) * inv_c

    pack = 2 if height % 2 == 0 else 1

    def row_body(pp, carry):
        base2 = pl.multiple_of(pp * (pack * cells), 16)
        rows = pl.ds(base2, pack * cells)
        for q in range(pack):
            p = pp * pack + q
            base = pl.multiple_of(base2 + q * cells, 16)
            cot = cot_ref[p].astype(F32)
            for h in sides:
                nat[h, SUBS : SUBS + breadth, :] = cot[:, lanes[h]]
                out_s[h, SUBS : SUBS + breadth, :] = own_ref[p, :, lanes[h]].astype(F32)
            land = mask_ref[p]
            for t in range(0, steps, 2):
                here = pl.ds(base + t * SUBS, 2 * SUBS)
                local = slice(q * cells + t * SUBS, q * cells + (t + 2) * SUBS)
                values = [conv[h, here, :] + cbias_ref[:, lanes[h]] for h in sides]
                center = mean_of(values)
                deviation = [v - center for v in values]
                inv_std = lax.rsqrt(mean_of([d * d for d in deviation]) + EPSILON)
                inv_s[local, :] = jnp.broadcast_to(inv_std, (2 * SUBS, LANES))
                ocean = jnp.concatenate([jnp.broadcast_to(land[:, t + k : t + k + 1], (SUBS, LANES)) for k in range(2)], axis=0)
                ocean_s[local, :] = ocean
                for h in sides:
                    unit = deviation[h] * inv_std
                    units[local, lanes[h]] = unit
                    normed_s[here, lanes[h]] = (unit * gain_ref[:, lanes[h]] + nbias_ref[:, lanes[h]]).astype(BF16)
                    cell = jnp.concatenate(
                        [nat[h, pl.ds(SUBS + t + k, SUBS, stride=steps), :] for k in range(2)], axis=0
                    )
                    upstream = jnp.where(ocean > 0, cell, 0.0)
                    cots[local, lanes[h]] = upstream
                    state_s[local, lanes[h]] = jnp.concatenate(
                        [out_s[h, pl.ds(SUBS + t + k, SUBS, stride=steps), :] for k in range(2)], axis=0
                    )
                    gmix_s[here, lanes[h]] = (scale_ref[:, lanes[h]] * upstream).astype(BF16)
        normed = normed_s[rows, :]
        gmix = gmix_s[rows, :]
        for c in range(0, hidden_units, width):
            cols = slice(c, c + width)
            hidden = jnp.dot(normed, w_in_ref[:, cols], preferred_element_type=F32) + b_in_ref[:, cols]
            grad_act = lax.dot_general(
                gmix, w_out_ref[cols, :], (((1,), (1,)), ((), ())), preferred_element_type=F32
            )
            square = hidden * hidden
            inner = hidden * (ROOT_TERM * CUBIC * square + ROOT_TERM)
            half_tanh = 0.5 * jnp.tanh(inner)
            gate = 0.5 + half_tanh
            active = hidden * gate
            slope = gate + active * (0.5 - half_tanh) * (6.0 * CUBIC * ROOT_TERM * square + 2.0 * ROOT_TERM)
            act = active.astype(BF16)
            act_s[rows, cols] = act
            mixed = jnp.dot(act, w_out_ref[cols, :], preferred_element_type=F32)
            ghid = (grad_act * slope).astype(BF16)
            ghid_s[rows, cols] = ghid
            hsum_ref[:, cols] += column_sum(ghid.astype(F32))
            grad_normed = lax.dot_general(
                ghid, w_in_ref[:, cols], (((1,), (1,)), ((), ())), preferred_element_type=F32
            )
            if c:
                mixed_s[...] += mixed
                gnorm_s[...] += grad_normed
            else:
                mixed_s[...] = mixed
                gnorm_s[...] = grad_normed
        for q in range(pack):
            p = pp * pack + q
            base = pl.multiple_of(base2 + q * cells, 16)
            sums = [[None] * halves for _ in range(5)]

            def add_to(n, h, values):
                folded = values[:SUBS] + values[SUBS:]
                sums[n][h] = folded if sums[n][h] is None else sums[n][h] + folded

            for t in range(0, steps, 2):
                here = pl.ds(base + t * SUBS, 2 * SUBS)
                local = slice(q * cells + t * SUBS, q * cells + (t + 2) * SUBS)
                ocean = ocean_s[local, :]
                scaled, products, units_here = [], [], []
                for h in sides:
                    mixed = mixed_s[local, lanes[h]] + b_out_ref[:, lanes[h]]
                    add_to(4, h, cots[local, lanes[h]] * mixed)
                    residual = jnp.where(ocean > 0, scale_ref[:, lanes[h]] * mixed, 0.0)
                    result = state_s[local, lanes[h]] + residual
                    for k in range(2):
                        out_s[h, pl.ds(SUBS + t + k, SUBS, stride=steps), :] = result[k * SUBS : (k + 1) * SUBS]
                    grad_normed = gnorm_s[local, lanes[h]]
                    unit = units[local, lanes[h]]
                    add_to(1, h, grad_normed * unit)
                    add_to(2, h, grad_normed)
                    add_to(3, h, gmix_s[here, lanes[h]].astype(F32))
                    scaled.append(grad_normed * gain_ref[:, lanes[h]])
                    units_here.append(unit)
                    products.append(scaled[h] * unit)
                mean_scaled = mean_of(scaled)
                mean_product = mean_of(products)
                inv_std = inv_s[local, :]
                for h in sides:
                    grad_conv = (inv_std * (scaled[h] - mean_scaled - units_here[h] * mean_product)).astype(BF16).astype(F32)
                    add_to(0, h, grad_conv)
                    for k in range(2):
                        nat[h, pl.ds(SUBS + t + k, SUBS, stride=steps), :] = grad_conv[k * SUBS : (k + 1) * SUBS]
            for n in range(5):
                for h in sides:
                    chan_ref[n, :, lanes[h]] += sums[n][h]
            for h in sides:
                out_ref[p, :, lanes[h]] = gather_row(out_s, h, breadth).astype(BF16)
                gconv_ref[p, :, lanes[h]] = gather_row(nat, h, breadth).astype(BF16)
        return carry

    lax.fori_loop(0, height // pack, row_body, 0)

    first = (((0,), (0,)), ((), ()))

    def store_block(half, c, block):
        @pl.when(place_ref[0] == half)
        def _():
            keep_ref[c : c + width, :] = block

        @pl.when(place_ref[0] != half)
        def _():
            send_ref[c : c + width, :] = block.astype(BF16)

    normed = normed_s[...]
    for c in range(0, hidden_units, width):
        cols = slice(c, c + width)
        store_block(0, c, lax.dot_general(normed, ghid_s[:, cols], first, preferred_element_type=F32))
    gmix = gmix_s[...]
    for c in range(0, hidden_units, width):
        cols = slice(c, c + width)
        store_block(1, c, lax.dot_general(act_s[:, cols], gmix, first, preferred_element_type=F32))


def kernel_grad_kernel(
    own_ref, top_ref, bottom_ref, gconv_ref, hsum_ref, chan_ref, small_ref, nat, spread, grads, sums, total
):
    height, breadth, channels = own_ref.shape
    halves = channels // LANES
    steps, cells = dims_of(breadth)
    for r in range(EDGE):
        spread_row(top_ref[r], nat, spread, r, halves, breadth)
        spread_row(bottom_ref[r], nat, spread, EDGE + height + r, halves, breadth)

    def spread_own(p, carry):
        spread_row(own_ref[p], nat, spread, EDGE + p, halves, breadth)
        return carry

    lax.fori_loop(0, height, spread_own, 0)

    nat[:, SUBS + breadth : SUBS + cells, :] = jnp.zeros((halves, cells - breadth, LANES), F32)

    def spread_grad(p, carry):
        row = gconv_ref[p].astype(F32)
        for h in range(halves):
            nat[h, SUBS : SUBS + breadth, :] = row[:, h * LANES : (h + 1) * LANES]
        for h in range(halves):
            for t in range(steps):
                grads[h, p, t] = nat[h, pl.ds(SUBS + t, SUBS, stride=steps), :]
        return carry

    lax.fori_loop(0, height, spread_grad, 0)

    def tap_body(i, carry):
        total = [[None] * 7 for _ in range(halves)]
        for p in range(height):
            window = [[spread[h, p + i, t] for t in range(6)] for h in range(halves)]
            for t in range(steps):
                for h in range(halves):
                    window[h].append(spread[h, p + i, t + 6])
                    grad = grads[h, p, t]
                    for j in range(7):
                        term = window[h][t + j] * grad
                        total[h][j] = term if total[h][j] is None else total[h][j] + term
        for h in range(halves):
            for j in range(7):
                sums[h, i * 7 + j] = jnp.sum(total[h][j], axis=0, keepdims=True)
        return carry

    lax.fori_loop(0, 7, tap_body, 0)
    total[...] = jnp.zeros_like(total)
    for h in range(halves):
        total[0:49, h * LANES : (h + 1) * LANES] = sums[h].reshape(49, LANES)
    rows = hsum_ref.shape[1] // channels
    at = 49
    for c in range(rows):
        total[at + c : at + c + 1, :] = jnp.sum(hsum_ref[:, c * channels : (c + 1) * channels], axis=0, keepdims=True)
    at += rows
    for c in range(5):
        total[at + c : at + c + 1, :] = jnp.sum(chan_ref[c], axis=0, keepdims=True)
    small_ref[...] = total[...]


def input_grad_kernel(top_ref, bottom_ref, part_ref, kern_ref, cot_ref, grad_ref, nat, spread, taps):
    height, breadth, channels = cot_ref.shape
    halves = channels // LANES
    steps, cells = dims_of(breadth)
    fill_taps(kern_ref, taps, halves, True)
    for r in range(EDGE):
        spread_row(top_ref[r], nat, spread, r, halves, breadth)
        spread_row(bottom_ref[r], nat, spread, EDGE + r, halves, breadth)
    n_runs, length = runs_of(steps)
    for p in range(height):

        def run_body(index, carry, p=p):
            h = index // n_runs
            start = (index % n_runs) * length
            base = p * steps + start
            total = conv_run(
                lambda slot, u: spread[h, slot, start + u],
                taps,
                h,
                halo_taps(p, height),
                length,
                [part_ref[h, base + t] for t in range(length)],
            )
            for t in range(length):
                nat[h, pl.ds(SUBS + start + t, SUBS, stride=steps), :] = total[t]
            return carry

        lax.fori_loop(0, halves * n_runs, run_body, 0)
        for h in range(halves):
            lanes = slice(h * LANES, (h + 1) * LANES)
            grad_ref[p, :, lanes] = (cot_ref[p, :, lanes].astype(F32) + gather_row(nat, h, breadth)).astype(BF16)


def call(kernel, out_shape, scratch, flops, nbytes, name, limit=VMEM_LIMIT):
    def run(*operands):
        whole = pl.BlockSpec(memory_space=pltpu.VMEM)
        scalars = pl.BlockSpec(memory_space=pltpu.SMEM)
        return pl.pallas_call(
            kernel,
            out_shape=out_shape,
            in_specs=[scalars if x.dtype == jnp.int32 else whole for x in operands],
            out_specs=jax.tree.map(lambda _: whole, out_shape),
            scratch_shapes=scratch,
            compiler_params=pltpu.CompilerParams(vmem_limit_bytes=limit),
            cost_estimate=pl.CostEstimate(flops=flops, bytes_accessed=nbytes, transcendentals=0),
            name=name,
        )(*operands)

    return run


def place_kernel(digits, rows, factor, place_ref, here_ref, across_ref, other_ref, other_across_ref, *rest):
    w_in_ref, w_out_ref, kernel_ref, hidden_ref, chan_ref, total = rest
    channels = here_ref.shape[1]
    order = [[]]
    for stride, size in digits[1:]:
        order = [tail + [k] for k in range(size) for tail in order]
    share = (here_ref.shape[0] - SMALL) // len(order)
    draw = place_ref[0]
    small = jnp.zeros((SMALL, channels), F32)
    for flip, refs in ((0, (here_ref, across_ref)), (1, (other_ref, other_across_ref))):
        for last, ref in enumerate(refs):
            values = ref[...].astype(F32)
            small = small + values[-SMALL:]
            for n, ks in enumerate(order):
                extent = rows
                start = 0
                for d, (stride, size) in enumerate(digits):
                    extent = extent // size
                    k = ks[d - 1] if d else last
                    start = start + (place_ref[1 + d] ^ k) * extent
                start = pl.multiple_of(start, SUBS)
                total[draw ^ flip, pl.ds(start, share), :] = values[n * share : (n + 1) * share]
    big = w_out_ref.shape[0]
    for c in range(big // channels):
        cols = slice(c * channels, (c + 1) * channels)
        w_in_ref[:, cols] = total[0, cols, :] * factor
    w_out_ref[...] = total[1, 0:big, :] * factor
    small = small * factor
    for i in range(7):
        kernel_ref[i] = small[i * 7 : i * 7 + 7]
    blocks = big // channels
    halves = channels // LANES
    for c in range(blocks):
        for h in range(halves):
            hidden_ref[c * halves + h : c * halves + h + 1, :] = small[49 + c : 50 + c, h * LANES : (h + 1) * LANES]
    chan_ref[...] = small[49 + blocks : 54 + blocks]


def digits_of(count):
    digits = []
    stride = 2
    while stride < count:
        size = min(4, count // stride)
        digits.append((stride, size))
        stride *= size
    return [(1, 2)] + digits[::-1]


def exchange(values, count, stride, size, k):
    pairs = []
    for i in range(count):
        digit = i // stride % size
        pairs.append((i, i + ((digit ^ k) - digit) * stride))
    return lax.ppermute(values, "tile", pairs)


def other_core(values, draws):
    return lax.ppermute(values, "draw", [(i, i ^ 1) for i in range(draws)])


def halo(cells, tiles):
    after = [(i, i + 1) for i in range(tiles - 1)]
    before = [(i + 1, i) for i in range(tiles - 1)]
    top = lax.ppermute(cells[-EDGE:], "tile", after)
    bottom = lax.ppermute(cells[:EDGE], "tile", before)
    return top, bottom


def per_device(
    tiles,
    draws,
    inputs,
    land_mask,
    kernel,
    conv_bias,
    norm_gain,
    norm_bias,
    w_in,
    b_in,
    w_out,
    b_out,
    layer_scale,
    cotangent,
):
    _, height, breadth, channels = inputs.shape
    hidden_units = w_in.shape[1]
    halves = channels // LANES
    steps, cells = dims_of(breadth)
    own = inputs[0]
    cot = cotangent[0]
    top, bottom = halo(own, tiles)
    mask = jnp.pad(land_mask.astype(F32), ((0, 0), (0, cells - breadth)))
    mask = mask.reshape(height, SUBS, steps)

    def row(vector):
        return vector.reshape(1, -1)

    nat = pltpu.VMEM((halves, cells + 2 * SUBS, LANES), F32)

    def spread(slots):
        return pltpu.VMEM((halves, slots, steps + 2 * EDGE, SUBS, LANES), F32)

    taps = pltpu.VMEM((halves, 49, SUBS, LANES), F32)
    big_row = pltpu.VMEM((2 * cells, channels), F32)
    narrow = pltpu.VMEM((2 * cells, LANES), F32)
    count = height * cells
    big = hidden_units
    digits = digits_of(tiles)
    unit = tiles * SUBS
    rows = -(-big // unit) * unit
    tile = lax.axis_index("tile")
    place = jnp.stack([lax.axis_index("draw")] + [tile // stride % size for stride, size in digits]).astype(jnp.int32)
    part_shape = jax.ShapeDtypeStruct((halves, height * steps, SUBS, LANES), F32)
    mega = 1024 * 1024

    def own_conv(rows_here, flip, name):
        return call(functools.partial(own_conv_kernel, flip), part_shape, [nat, spread(height), taps], 1, 1, name)(rows_here, kernel)

    part = own_conv(own, False, "own_conv")
    out, gconv, keep, send, hsum, chan = call(
        main_kernel,
        (
            jax.ShapeDtypeStruct((height, breadth, channels), BF16),
            jax.ShapeDtypeStruct((height, breadth, channels), BF16),
            jax.ShapeDtypeStruct((big, channels), F32),
            jax.ShapeDtypeStruct((big, channels), BF16),
            jax.ShapeDtypeStruct((SUBS, hidden_units), F32),
            jax.ShapeDtypeStruct((5, SUBS, channels), F32),
        ),
        [
            nat,
            nat,
            spread(2 * EDGE),
            taps,
            pltpu.VMEM((halves, count, LANES), F32),
            big_row,
            big_row,
            big_row,
            big_row,
            big_row,
            narrow,
            narrow,
            pltpu.VMEM((count, channels), BF16),
            pltpu.VMEM((count, hidden_units), BF16),
            pltpu.VMEM((count, channels), BF16),
            pltpu.VMEM((count, hidden_units), BF16),
        ],
        12 * count * channels * hidden_units,
        8 * mega,
        "block_main",
    )(
        place, own, top, bottom, part, cot, mask, kernel, row(conv_bias), row(norm_gain), row(norm_bias), w_in, row(b_in),
        w_out, row(b_out), row(layer_scale),
    )
    got = other_core(send, draws)

    if rows > big:
        keep = jnp.pad(keep, ((0, rows - big), (0, 0)))
        got = jnp.pad(got, ((0, rows - big), (0, 0)))
    for step, (stride, size) in enumerate(digits):
        share = keep.shape[0] // size
        mine = place[1 + step]
        pieces = []
        for k in range(size):
            piece = lax.dynamic_slice_in_dim(keep, (mine ^ k) * share, share, 0)
            if not step:
                piece = piece + lax.dynamic_slice_in_dim(got, (mine ^ k) * share, share, 0).astype(F32)
            pieces.append(piece)
        sends = [piece.astype(BF16) for piece in pieces[1:]]
        if not step:
            sends, gconv = lax.optimization_barrier((sends, gconv))
            grad_top, grad_bottom = halo(gconv, tiles)
        elif step == 1:
            sends, hsum = lax.optimization_barrier((sends, hsum))
            small = call(
                kernel_grad_kernel,
                jax.ShapeDtypeStruct((SMALL, channels), F32),
                [
                    nat,
                    spread(height + 2 * EDGE),
                    pltpu.VMEM((halves, height, steps, SUBS, LANES), F32),
                    pltpu.VMEM((halves, 49, 1, LANES), F32),
                    pltpu.VMEM((SMALL, channels), F32),
                ],
                1,
                1,
                "kernel_grad",
            )(own, top, bottom, gconv, hsum, chan)
        received = [exchange(sends[k - 1], tiles, stride, size, k) for k in range(1, size)]
        if step == 1:
            received, small, grad_top, grad_bottom = lax.optimization_barrier((received, small, grad_top, grad_bottom))
        keep = pieces[0]
        for piece in received:
            keep = keep + piece.astype(F32)
    gathered = keep.astype(BF16)
    for stride, size in digits[1:]:
        payload = jnp.concatenate([gathered, small.astype(BF16)], axis=0)
        if (stride, size) == digits[1]:
            payload, gconv = lax.optimization_barrier((payload, gconv))
            grad_part = own_conv(gconv, True, "own_conv_grad")
        received = [payload] + [exchange(payload, tiles, stride, size, k) for k in range(1, size)]
        if (stride, size) == digits[1]:
            received, grad_part = lax.optimization_barrier((received, grad_part))
        gathered = jnp.concatenate([piece[:-SMALL] for piece in received], axis=0)
        small = functools.reduce(jnp.add, [piece[-SMALL:].astype(F32) for piece in received])
    gathered = jnp.concatenate([gathered, small.astype(BF16)], axis=0)
    stride, size = digits[0]
    across = exchange(gathered, tiles, stride, size, 1)
    other = other_core(gathered, draws)
    input_grad = call(
        input_grad_kernel,
        jax.ShapeDtypeStruct((height, breadth, channels), BF16),
        [nat, spread(2 * EDGE), taps],
        2048 * mega,
        4 * mega,
        "input_grad",
    )(grad_top, grad_bottom, grad_part, kernel, cot)
    across, input_grad = lax.optimization_barrier((across, input_grad))
    other_across = other_core(across, draws)
    factor = float(1.0 / np.sqrt(np.float32(draws * height * tiles * breadth)))
    w_in_sum, w_out_sum, kernel_sum, hidden_sum, chan_sum = call(
        functools.partial(place_kernel, digits, rows, factor),
        (
            jax.ShapeDtypeStruct((channels, hidden_units), F32),
            jax.ShapeDtypeStruct((hidden_units, channels), F32),
            jax.ShapeDtypeStruct((7, 7, channels), F32),
            jax.ShapeDtypeStruct((hidden_units // LANES, LANES), F32),
            jax.ShapeDtypeStruct((5, channels), F32),
        ),
        [pltpu.VMEM((2, rows, channels), F32)],
        mega,
        4 * mega,
        "place",
        16 * mega,
    )(place, gathered, across, other, other_across)
    return (
        out[None],
        input_grad[None],
        kernel_sum,
        w_in_sum,
        w_out_sum,
        hidden_sum.reshape(-1),
        chan_sum,
    )


def solution(mesh):
    placed = (
        P(("group", "draw"), "tile", None, None),
        P("tile", None),
        P(),
        P(),
        P(),
        P(),
        P(),
        P(),
        P(),
        P(),
        P(),
        P(("group", "draw"), "tile", None, None),
    )
    return jax.shard_map(
        functools.partial(per_device, mesh.shape["tile"], mesh.shape["draw"]),
        mesh=mesh,
        in_specs=placed,
        out_specs=(
            P(("group", "draw"), "tile", None, None),
            P(("group", "draw"), "tile", None, None),
            P("group", None, None),
            P("group", None),
            P("group", None),
            P("group"),
            P("group", None),
        ),
        check_vma=False,
    )
```

```python
import functools

import jax
import jax.numpy as jnp
import numpy as np
from jax import lax
from jax.experimental import pallas as pl
from jax.experimental.layout import Layout, with_layout_constraint
from jax.experimental.pallas import tpu as pltpu
from jax.sharding import PartitionSpec as P

ROOT_TERM = 0.7978845608028654
CUBIC = 0.044715
EPSILON = 1e-06
F32 = jnp.float32
BF16 = jnp.bfloat16
LANES = 128
SUBS = 8
EDGE = 3
SMALL = 64
VMEM_LIMIT = 56 * 1024 * 1024


def dims_of(breadth):
    steps = -(-breadth // SUBS)
    return steps, steps * SUBS


def spread_row(row, nat, spread, slot, halves, breadth):
    steps, cells = dims_of(breadth)
    row = row.astype(F32)
    over = cells - breadth + EDGE
    for h in range(halves):
        part = row[:, h * LANES : (h + 1) * LANES]
        nat[h, SUBS : SUBS + breadth, :] = part
        nat[h, SUBS - EDGE : SUBS, :] = part[breadth - EDGE :]
        nat[h, SUBS + breadth : SUBS + breadth + over, :] = part[:over]
    for h in range(halves):
        for t in range(steps + 2 * EDGE):
            spread[h, slot, t] = nat[h, pl.ds(SUBS - EDGE + t, SUBS, stride=steps), :]


def gather_row(nat, h, breadth):
    return nat[h, SUBS : SUBS + breadth, :]


def fill_taps(kern_ref, taps, halves, flip):
    for i in range(7):
        for j in range(7):
            src = kern_ref[6 - i, 6 - j : 7 - j, :] if flip else kern_ref[i, j : j + 1, :]
            for h in range(halves):
                taps[h, i * 7 + j] = jnp.broadcast_to(src[:, h * LANES : (h + 1) * LANES], (SUBS, LANES))


def conv_run(cells_at, taps, h, row_taps, length, total):
    total = list(total)
    for i, slot in row_taps:
        weights = [taps[h, i * 7 + j] for j in range(7)]
        for u in range(length + 6):
            cell = cells_at(slot, u)
            for j in range(7):
                t = u - j
                if 0 <= t < length:
                    term = cell * weights[j]
                    total[t] = term if total[t] is None else total[t] + term
    return total


def own_taps(p, height):
    return [(i, p + i - EDGE) for i in range(7) if 0 <= p + i - EDGE < height]


def halo_taps(p, height):
    found = []
    for i in range(7):
        row = p + i
        if row < EDGE:
            found.append((i, row))
        elif row >= EDGE + height:
            found.append((i, row - height))
    return found


def runs_of(steps):
    length = steps // 2 if steps % 2 == 0 else steps
    return steps // length, length


def own_conv_kernel(flip, own_ref, kern_ref, part_ref, nat, spread, taps):
    height, breadth, channels = own_ref.shape
    halves = channels // LANES
    steps, cells = dims_of(breadth)
    fill_taps(kern_ref, taps, halves, flip)

    def spread_own(p, carry):
        spread_row(own_ref[p], nat, spread, p, halves, breadth)
        return carry

    lax.fori_loop(0, height, spread_own, 0)
    n_runs, length = runs_of(steps)
    for p in range(height):

        def run_body(index, carry, p=p):
            h = index // n_runs
            start = (index % n_runs) * length
            total = conv_run(
                lambda slot, u: spread[h, slot, start + u], taps, h, own_taps(p, height), length, [None] * length
            )
            for t in range(length):
                part_ref[h, p * steps + start + t] = total[t]
            return carry

        lax.fori_loop(0, halves * n_runs, run_body, 0)


def main_kernel(
    place_ref, own_ref, top_ref, bottom_ref, part_ref, cot_ref, mask_ref, kern_ref, cbias_ref, gain_ref, nbias_ref, w_in_ref,
    b_in_ref, w_out_ref, b_out_ref, scale_ref,
    out_ref, gconv_ref, keep_ref, send_ref, hsum_ref, chan_ref,
    nat, out_s, spread, taps, conv, units, cots, state_s, mixed_s, gnorm_s, ocean_s, inv_s, normed_s, act_s, gmix_s, ghid_s,
):
    height, breadth, channels = own_ref.shape
    hidden_units = w_in_ref.shape[1]
    halves = channels // LANES
    steps, cells = dims_of(breadth)

    fill_taps(kern_ref, taps, halves, False)
    for r in range(EDGE):
        spread_row(top_ref[r], nat, spread, r, halves, breadth)
        spread_row(bottom_ref[r], nat, spread, EDGE + r, halves, breadth)
    n_runs, length = runs_of(steps)
    for p in range(height):

        def conv_body(index, carry, p=p):
            h = index // n_runs
            start = (index % n_runs) * length
            base = p * steps + start
            total = conv_run(
                lambda slot, u: spread[h, slot, start + u],
                taps,
                h,
                halo_taps(p, height),
                length,
                [part_ref[h, base + t] for t in range(length)],
            )
            for t in range(length):
                conv[h, pl.ds(pl.multiple_of((base + t) * SUBS, SUBS), SUBS), :] = total[t]
            return carry

        lax.fori_loop(0, halves * n_runs, conv_body, 0)

    hsum_ref[...] = jnp.zeros_like(hsum_ref)
    chan_ref[...] = jnp.zeros_like(chan_ref)
    width = 256
    inv_c = 1.0 / channels
    sides = range(halves)
    lanes = [slice(h * LANES, (h + 1) * LANES) for h in sides]

    def column_sum(values):
        return jnp.sum(values.reshape(values.shape[0] // SUBS, SUBS, values.shape[1]), axis=0)

    def mean_of(parts):
        return jnp.sum(functools.reduce(jnp.add, parts), axis=1, keepdims=True) * inv_c

    pack = 2 if height % 2 == 0 else 1

    def row_body(pp, carry):
        base2 = pl.multiple_of(pp * (pack * cells), 16)
        rows = pl.ds(base2, pack * cells)
        for q in range(pack):
            p = pp * pack + q
            base = pl.multiple_of(base2 + q * cells, 16)
            cot = cot_ref[p].astype(F32)
            for h in sides:
                nat[h, SUBS : SUBS + breadth, :] = cot[:, lanes[h]]
                out_s[h, SUBS : SUBS + breadth, :] = own_ref[p, :, lanes[h]].astype(F32)
            land = mask_ref[p]
            for t in range(0, steps, 2):
                here = pl.ds(base + t * SUBS, 2 * SUBS)
                local = slice(q * cells + t * SUBS, q * cells + (t + 2) * SUBS)
                values = [conv[h, here, :] + cbias_ref[:, lanes[h]] for h in sides]
                center = mean_of(values)
                deviation = [v - center for v in values]
                inv_std = lax.rsqrt(mean_of([d * d for d in deviation]) + EPSILON)
                inv_s[local, :] = jnp.broadcast_to(inv_std, (2 * SUBS, LANES))
                ocean = jnp.concatenate([jnp.broadcast_to(land[:, t + k : t + k + 1], (SUBS, LANES)) for k in range(2)], axis=0)
                ocean_s[local, :] = ocean
                for h in sides:
                    unit = deviation[h] * inv_std
                    units[local, lanes[h]] = unit
                    normed_s[here, lanes[h]] = (unit * gain_ref[:, lanes[h]] + nbias_ref[:, lanes[h]]).astype(BF16)
                    cell = jnp.concatenate(
                        [nat[h, pl.ds(SUBS + t + k, SUBS, stride=steps), :] for k in range(2)], axis=0
                    )
                    upstream = jnp.where(ocean > 0, cell, 0.0)
                    cots[local, lanes[h]] = upstream
                    state_s[local, lanes[h]] = jnp.concatenate(
                        [out_s[h, pl.ds(SUBS + t + k, SUBS, stride=steps), :] for k in range(2)], axis=0
                    )
                    gmix_s[here, lanes[h]] = (scale_ref[:, lanes[h]] * upstream).astype(BF16)
        normed = normed_s[rows, :]
        gmix = gmix_s[rows, :]
        for c in range(0, hidden_units, width):
            cols = slice(c, c + width)
            hidden = jnp.dot(normed, w_in_ref[:, cols], preferred_element_type=F32) + b_in_ref[:, cols]
            grad_act = lax.dot_general(
                gmix, w_out_ref[cols, :], (((1,), (1,)), ((), ())), preferred_element_type=F32
            )
            square = hidden * hidden
            inner = hidden * (ROOT_TERM * CUBIC * square + ROOT_TERM)
            half_tanh = 0.5 * jnp.tanh(inner)
            gate = 0.5 + half_tanh
            active = hidden * gate
            slope = gate + active * (0.5 - half_tanh) * (6.0 * CUBIC * ROOT_TERM * square + 2.0 * ROOT_TERM)
            act = active.astype(BF16)
            act_s[rows, cols] = act
            mixed = jnp.dot(act, w_out_ref[cols, :], preferred_element_type=F32)
            ghid = (grad_act * slope).astype(BF16)
            ghid_s[rows, cols] = ghid
            hsum_ref[:, cols] += column_sum(ghid.astype(F32))
            grad_normed = lax.dot_general(
                ghid, w_in_ref[:, cols], (((1,), (1,)), ((), ())), preferred_element_type=F32
            )
            if c:
                mixed_s[...] += mixed
                gnorm_s[...] += grad_normed
            else:
                mixed_s[...] = mixed
                gnorm_s[...] = grad_normed
        for q in range(pack):
            p = pp * pack + q
            base = pl.multiple_of(base2 + q * cells, 16)
            sums = [[None] * halves for _ in range(5)]

            def add_to(n, h, values):
                folded = values[:SUBS] + values[SUBS:]
                sums[n][h] = folded if sums[n][h] is None else sums[n][h] + folded

            for t in range(0, steps, 2):
                here = pl.ds(base + t * SUBS, 2 * SUBS)
                local = slice(q * cells + t * SUBS, q * cells + (t + 2) * SUBS)
                ocean = ocean_s[local, :]
                scaled, products, units_here = [], [], []
                for h in sides:
                    mixed = mixed_s[local, lanes[h]] + b_out_ref[:, lanes[h]]
                    add_to(4, h, cots[local, lanes[h]] * mixed)
                    residual = jnp.where(ocean > 0, scale_ref[:, lanes[h]] * mixed, 0.0)
                    result = state_s[local, lanes[h]] + residual
                    for k in range(2):
                        out_s[h, pl.ds(SUBS + t + k, SUBS, stride=steps), :] = result[k * SUBS : (k + 1) * SUBS]
                    grad_normed = gnorm_s[local, lanes[h]]
                    unit = units[local, lanes[h]]
                    add_to(1, h, grad_normed * unit)
                    add_to(2, h, grad_normed)
                    add_to(3, h, gmix_s[here, lanes[h]].astype(F32))
                    scaled.append(grad_normed * gain_ref[:, lanes[h]])
                    units_here.append(unit)
                    products.append(scaled[h] * unit)
                mean_scaled = mean_of(scaled)
                mean_product = mean_of(products)
                inv_std = inv_s[local, :]
                for h in sides:
                    grad_conv = (inv_std * (scaled[h] - mean_scaled - units_here[h] * mean_product)).astype(BF16).astype(F32)
                    add_to(0, h, grad_conv)
                    for k in range(2):
                        nat[h, pl.ds(SUBS + t + k, SUBS, stride=steps), :] = grad_conv[k * SUBS : (k + 1) * SUBS]
            for n in range(5):
                for h in sides:
                    chan_ref[n, :, lanes[h]] += sums[n][h]
            for h in sides:
                out_ref[p, :, lanes[h]] = gather_row(out_s, h, breadth).astype(BF16)
                gconv_ref[p, :, lanes[h]] = gather_row(nat, h, breadth).astype(BF16)
        return carry

    lax.fori_loop(0, height // pack, row_body, 0)

    first = (((0,), (0,)), ((), ()))

    def store_block(half, c, block):
        @pl.when(place_ref[0] == half)
        def _():
            keep_ref[c : c + width, :] = block

        @pl.when(place_ref[0] != half)
        def _():
            send_ref[c : c + width, :] = block.astype(BF16)

    normed = normed_s[...]
    for c in range(0, hidden_units, width):
        cols = slice(c, c + width)
        store_block(0, c, lax.dot_general(normed, ghid_s[:, cols], first, preferred_element_type=F32))
    gmix = gmix_s[...]
    for c in range(0, hidden_units, width):
        cols = slice(c, c + width)
        store_block(1, c, lax.dot_general(act_s[:, cols], gmix, first, preferred_element_type=F32))


def kernel_grad_kernel(
    own_ref, top_ref, bottom_ref, gconv_ref, hsum_ref, chan_ref, small_ref, nat, spread, grads, sums, total
):
    height, breadth, channels = own_ref.shape
    halves = channels // LANES
    steps, cells = dims_of(breadth)
    for r in range(EDGE):
        spread_row(top_ref[r], nat, spread, r, halves, breadth)
        spread_row(bottom_ref[r], nat, spread, EDGE + height + r, halves, breadth)

    def spread_own(p, carry):
        spread_row(own_ref[p], nat, spread, EDGE + p, halves, breadth)
        return carry

    lax.fori_loop(0, height, spread_own, 0)

    nat[:, SUBS + breadth : SUBS + cells, :] = jnp.zeros((halves, cells - breadth, LANES), F32)

    def spread_grad(p, carry):
        row = gconv_ref[p].astype(F32)
        for h in range(halves):
            nat[h, SUBS : SUBS + breadth, :] = row[:, h * LANES : (h + 1) * LANES]
        for h in range(halves):
            for t in range(steps):
                grads[h, p, t] = nat[h, pl.ds(SUBS + t, SUBS, stride=steps), :]
        return carry

    lax.fori_loop(0, height, spread_grad, 0)

    def tap_body(i, carry):
        total = [[None] * 7 for _ in range(halves)]
        for p in range(height):
            window = [[spread[h, p + i, t] for t in range(6)] for h in range(halves)]
            for t in range(steps):
                for h in range(halves):
                    window[h].append(spread[h, p + i, t + 6])
                    grad = grads[h, p, t]
                    for j in range(7):
                        term = window[h][t + j] * grad
                        total[h][j] = term if total[h][j] is None else total[h][j] + term
        for h in range(halves):
            for j in range(7):
                sums[h, i * 7 + j] = jnp.sum(total[h][j], axis=0, keepdims=True)
        return carry

    lax.fori_loop(0, 7, tap_body, 0)
    total[...] = jnp.zeros_like(total)
    for h in range(halves):
        total[0:49, h * LANES : (h + 1) * LANES] = sums[h].reshape(49, LANES)
    rows = hsum_ref.shape[1] // channels
    at = 49
    for c in range(rows):
        total[at + c : at + c + 1, :] = jnp.sum(hsum_ref[:, c * channels : (c + 1) * channels], axis=0, keepdims=True)
    at += rows
    for c in range(5):
        total[at + c : at + c + 1, :] = jnp.sum(chan_ref[c], axis=0, keepdims=True)
    small_ref[...] = total[...]


def input_grad_kernel(top_ref, bottom_ref, part_ref, kern_ref, cot_ref, grad_ref, nat, spread, taps):
    height, breadth, channels = cot_ref.shape
    halves = channels // LANES
    steps, cells = dims_of(breadth)
    fill_taps(kern_ref, taps, halves, True)
    for r in range(EDGE):
        spread_row(top_ref[r], nat, spread, r, halves, breadth)
        spread_row(bottom_ref[r], nat, spread, EDGE + r, halves, breadth)
    n_runs, length = runs_of(steps)
    for p in range(height):

        def run_body(index, carry, p=p):
            h = index // n_runs
            start = (index % n_runs) * length
            base = p * steps + start
            total = conv_run(
                lambda slot, u: spread[h, slot, start + u],
                taps,
                h,
                halo_taps(p, height),
                length,
                [part_ref[h, base + t] for t in range(length)],
            )
            for t in range(length):
                nat[h, pl.ds(SUBS + start + t, SUBS, stride=steps), :] = total[t]
            return carry

        lax.fori_loop(0, halves * n_runs, run_body, 0)
        for h in range(halves):
            lanes = slice(h * LANES, (h + 1) * LANES)
            grad_ref[p, :, lanes] = (cot_ref[p, :, lanes].astype(F32) + gather_row(nat, h, breadth)).astype(BF16)


def call(kernel, out_shape, scratch, flops, nbytes, name, limit=VMEM_LIMIT):
    def run(*operands):
        whole = pl.BlockSpec(memory_space=pltpu.VMEM)
        scalars = pl.BlockSpec(memory_space=pltpu.SMEM)
        return pl.pallas_call(
            kernel,
            out_shape=out_shape,
            in_specs=[scalars if x.dtype == jnp.int32 else whole for x in operands],
            out_specs=jax.tree.map(lambda _: whole, out_shape),
            scratch_shapes=scratch,
            compiler_params=pltpu.CompilerParams(vmem_limit_bytes=limit),
            cost_estimate=pl.CostEstimate(flops=flops, bytes_accessed=nbytes, transcendentals=0),
            name=name,
        )(*operands)

    return run


def place_kernel(digits, rows, factor, place_ref, here_ref, across_ref, other_ref, other_across_ref, *rest):
    w_in_ref, w_out_ref, kernel_ref, hidden_ref, chan_ref, total = rest
    channels = here_ref.shape[1]
    order = [[]]
    for stride, size in digits[1:]:
        order = [tail + [k] for k in range(size) for tail in order]
    share = (here_ref.shape[0] - SMALL) // len(order)
    draw = place_ref[0]
    small = jnp.zeros((SMALL, channels), F32)
    for flip, refs in ((0, (here_ref, across_ref)), (1, (other_ref, other_across_ref))):
        for last, ref in enumerate(refs):
            values = ref[...].astype(F32)
            small = small + values[-SMALL:]
            for n, ks in enumerate(order):
                extent = rows
                start = 0
                for d, (stride, size) in enumerate(digits):
                    extent = extent // size
                    k = ks[d - 1] if d else last
                    start = start + (place_ref[1 + d] ^ k) * extent
                start = pl.multiple_of(start, SUBS)
                total[draw ^ flip, pl.ds(start, share), :] = values[n * share : (n + 1) * share]
    big = w_out_ref.shape[0]
    for c in range(big // channels):
        cols = slice(c * channels, (c + 1) * channels)
        w_in_ref[:, cols] = total[0, cols, :] * factor
    w_out_ref[...] = total[1, 0:big, :] * factor
    small = small * factor
    for i in range(7):
        kernel_ref[i] = small[i * 7 : i * 7 + 7]
    blocks = big // channels
    halves = channels // LANES
    for c in range(blocks):
        for h in range(halves):
            hidden_ref[c * halves + h : c * halves + h + 1, :] = small[49 + c : 50 + c, h * LANES : (h + 1) * LANES]
    chan_ref[...] = small[49 + blocks : 54 + blocks]


def digits_of(count):
    digits = []
    stride = 2
    while stride < count:
        size = min(4, count // stride)
        digits.append((stride, size))
        stride *= size
    return [(1, 2)] + digits[::-1]


def exchange(values, count, stride, size, k):
    pairs = []
    for i in range(count):
        digit = i // stride % size
        pairs.append((i, i + ((digit ^ k) - digit) * stride))
    return lax.ppermute(values, "tile", pairs)


def other_core(values, draws):
    return lax.ppermute(values, "draw", [(i, i ^ 1) for i in range(draws)])


def halo(cells, tiles):
    after = [(i, i + 1) for i in range(tiles - 1)]
    before = [(i + 1, i) for i in range(tiles - 1)]
    top = lax.ppermute(cells[-EDGE:], "tile", after)
    bottom = lax.ppermute(cells[:EDGE], "tile", before)
    return top, bottom


def per_device(
    tiles,
    draws,
    inputs,
    land_mask,
    kernel,
    conv_bias,
    norm_gain,
    norm_bias,
    w_in,
    b_in,
    w_out,
    b_out,
    layer_scale,
    cotangent,
):
    _, height, breadth, channels = inputs.shape
    hidden_units = w_in.shape[1]
    halves = channels // LANES
    steps, cells = dims_of(breadth)
    own = inputs[0]
    cot = cotangent[0]
    top, bottom = halo(own, tiles)
    mask = jnp.pad(land_mask.astype(F32), ((0, 0), (0, cells - breadth)))
    mask = mask.reshape(height, SUBS, steps)

    def row(vector):
        return vector.reshape(1, -1)

    nat = pltpu.VMEM((halves, cells + 2 * SUBS, LANES), F32)

    def spread(slots):
        return pltpu.VMEM((halves, slots, steps + 2 * EDGE, SUBS, LANES), F32)

    taps = pltpu.VMEM((halves, 49, SUBS, LANES), F32)
    big_row = pltpu.VMEM((2 * cells, channels), F32)
    narrow = pltpu.VMEM((2 * cells, LANES), F32)
    count = height * cells
    big = hidden_units
    digits = digits_of(tiles)
    unit = tiles * SUBS
    rows = -(-big // unit) * unit
    tile = lax.axis_index("tile")
    place = jnp.stack([lax.axis_index("draw")] + [tile // stride % size for stride, size in digits]).astype(jnp.int32)
    part_shape = jax.ShapeDtypeStruct((halves, height * steps, SUBS, LANES), F32)
    mega = 1024 * 1024

    def own_conv(rows_here, flip, name):
        return call(functools.partial(own_conv_kernel, flip), part_shape, [nat, spread(height), taps], 1, 1, name)(rows_here, kernel)

    part = own_conv(own, False, "own_conv")
    out, gconv, keep, send, hsum, chan = call(
        main_kernel,
        (
            jax.ShapeDtypeStruct((height, breadth, channels), BF16),
            jax.ShapeDtypeStruct((height, breadth, channels), BF16),
            jax.ShapeDtypeStruct((big, channels), F32),
            jax.ShapeDtypeStruct((big, channels), BF16),
            jax.ShapeDtypeStruct((SUBS, hidden_units), F32),
            jax.ShapeDtypeStruct((5, SUBS, channels), F32),
        ),
        [
            nat,
            nat,
            spread(2 * EDGE),
            taps,
            pltpu.VMEM((halves, count, LANES), F32),
            big_row,
            big_row,
            big_row,
            big_row,
            big_row,
            narrow,
            narrow,
            pltpu.VMEM((count, channels), BF16),
            pltpu.VMEM((count, hidden_units), BF16),
            pltpu.VMEM((count, channels), BF16),
            pltpu.VMEM((count, hidden_units), BF16),
        ],
        12 * count * channels * hidden_units,
        8 * mega,
        "block_main",
    )(
        place, own, top, bottom, part, cot, mask, kernel, row(conv_bias), row(norm_gain), row(norm_bias), w_in, row(b_in),
        w_out, row(b_out), row(layer_scale),
    )
    got = other_core(send, draws)

    if rows > big:
        keep = jnp.pad(keep, ((0, rows - big), (0, 0)))
        got = jnp.pad(got, ((0, rows - big), (0, 0)))
    for step, (stride, size) in enumerate(digits):
        share = keep.shape[0] // size
        mine = place[1 + step]
        pieces = []
        for k in range(size):
            piece = lax.dynamic_slice_in_dim(keep, (mine ^ k) * share, share, 0)
            if not step:
                piece = piece + lax.dynamic_slice_in_dim(got, (mine ^ k) * share, share, 0).astype(F32)
            pieces.append(piece)
        sends = [piece.astype(BF16) for piece in pieces[1:]]
        if not step:
            sends, gconv, hsum = lax.optimization_barrier((sends, gconv, hsum))
            grad_top, grad_bottom = halo(gconv, tiles)
            small = call(
                kernel_grad_kernel,
                jax.ShapeDtypeStruct((SMALL, channels), F32),
                [
                    nat,
                    spread(height + 2 * EDGE),
                    pltpu.VMEM((halves, height, steps, SUBS, LANES), F32),
                    pltpu.VMEM((halves, 49, 1, LANES), F32),
                    pltpu.VMEM((SMALL, channels), F32),
                ],
                1,
                1,
                "kernel_grad",
            )(own, top, bottom, gconv, hsum, chan)
        elif step == 1:
            sends, gconv = lax.optimization_barrier((sends, gconv))
            grad_part = own_conv(gconv, True, "own_conv_grad")
        received = [exchange(sends[k - 1], tiles, stride, size, k) for k in range(1, size)]
        if not step:
            received, small = lax.optimization_barrier((received, small))
        elif step == 1:
            received, grad_part, grad_top, grad_bottom = lax.optimization_barrier(
                (received, grad_part, grad_top, grad_bottom)
            )
        keep = pieces[0]
        for piece in received:
            keep = keep + piece.astype(F32)
    gathered = keep.astype(BF16)
    for stride, size in digits[1:]:
        payload = jnp.concatenate([gathered, small.astype(BF16)], axis=0)
        if (stride, size) == digits[1]:
            payload, grad_part = lax.optimization_barrier((payload, grad_part))
            input_grad = call(
                input_grad_kernel,
                jax.ShapeDtypeStruct((height, breadth, channels), BF16),
                [nat, spread(2 * EDGE), taps],
                1,
                1,
                "input_grad",
            )(grad_top, grad_bottom, grad_part, kernel, cot)
        received = [payload] + [exchange(payload, tiles, stride, size, k) for k in range(1, size)]
        if (stride, size) == digits[1]:
            received, input_grad = lax.optimization_barrier((received, input_grad))
        gathered = jnp.concatenate([piece[:-SMALL] for piece in received], axis=0)
        small = functools.reduce(jnp.add, [piece[-SMALL:].astype(F32) for piece in received])
    gathered = jnp.concatenate([gathered, small.astype(BF16)], axis=0)
    stride, size = digits[0]
    across = exchange(gathered, tiles, stride, size, 1)
    other = other_core(gathered, draws)
    lon_first = Layout((0, 2, 1, 3))
    out = with_layout_constraint(out[None], lon_first)
    input_grad = with_layout_constraint(input_grad[None], lon_first)
    across, out, input_grad = lax.optimization_barrier((across, out, input_grad))
    other_across = other_core(across, draws)
    factor = float(1.0 / np.sqrt(np.float32(draws * height * tiles * breadth)))
    w_in_sum, w_out_sum, kernel_sum, hidden_sum, chan_sum = call(
        functools.partial(place_kernel, digits, rows, factor),
        (
            jax.ShapeDtypeStruct((channels, hidden_units), F32),
            jax.ShapeDtypeStruct((hidden_units, channels), F32),
            jax.ShapeDtypeStruct((7, 7, channels), F32),
            jax.ShapeDtypeStruct((hidden_units // LANES, LANES), F32),
            jax.ShapeDtypeStruct((5, channels), F32),
        ),
        [pltpu.VMEM((2, rows, channels), F32)],
        mega,
        4 * mega,
        "place",
        16 * mega,
    )(place, gathered, across, other, other_across)
    return (
        out,
        input_grad,
        kernel_sum,
        w_in_sum,
        w_out_sum,
        hidden_sum.reshape(-1),
        chan_sum,
    )


def solution(mesh):
    placed = (
        P(("group", "draw"), "tile", None, None),
        P("tile", None),
        P(),
        P(),
        P(),
        P(),
        P(),
        P(),
        P(),
        P(),
        P(),
        P(("group", "draw"), "tile", None, None),
    )
    return jax.shard_map(
        functools.partial(per_device, mesh.shape["tile"], mesh.shape["draw"]),
        mesh=mesh,
        in_specs=placed,
        out_specs=(
            P(("group", "draw"), "tile", None, None),
            P(("group", "draw"), "tile", None, None),
            P("group", None, None),
            P("group", None),
            P("group", None),
            P("group"),
            P("group", None),
        ),
        check_vma=False,
    )
```

```python
import functools

import jax
import jax.numpy as jnp
import numpy as np
from jax import lax
from jax.experimental import pallas as pl
from jax.experimental.layout import Layout, with_layout_constraint
from jax.experimental.pallas import tpu as pltpu
from jax.sharding import PartitionSpec as P

ROOT_TERM = 0.7978845608028654
CUBIC = 0.044715
EPSILON = 1e-06
F32 = jnp.float32
BF16 = jnp.bfloat16
LANES = 128
SUBS = 8
EDGE = 3
SMALL = 64
VMEM_LIMIT = 56 * 1024 * 1024


def dims_of(breadth):
    steps = -(-breadth // SUBS)
    return steps, steps * SUBS


def spread_row(row, nat, spread, slot, halves, breadth):
    steps, cells = dims_of(breadth)
    row = row.astype(F32)
    over = cells - breadth + EDGE
    for h in range(halves):
        part = row[:, h * LANES : (h + 1) * LANES]
        nat[h, SUBS : SUBS + breadth, :] = part
        nat[h, SUBS - EDGE : SUBS, :] = part[breadth - EDGE :]
        nat[h, SUBS + breadth : SUBS + breadth + over, :] = part[:over]
    for h in range(halves):
        for t in range(steps + 2 * EDGE):
            spread[h, slot, t] = nat[h, pl.ds(SUBS - EDGE + t, SUBS, stride=steps), :]


def gather_row(nat, h, breadth):
    return nat[h, SUBS : SUBS + breadth, :]


def fill_taps(kern_ref, taps, halves, flip):
    for i in range(7):
        for j in range(7):
            src = kern_ref[6 - i, 6 - j : 7 - j, :] if flip else kern_ref[i, j : j + 1, :]
            for h in range(halves):
                taps[h, i * 7 + j] = jnp.broadcast_to(src[:, h * LANES : (h + 1) * LANES], (SUBS, LANES))


def conv_run(cells_at, taps, h, row_taps, length, total):
    total = list(total)
    for i, slot in row_taps:
        weights = [taps[h, i * 7 + j] for j in range(7)]
        for u in range(length + 6):
            cell = cells_at(slot, u)
            for j in range(7):
                t = u - j
                if 0 <= t < length:
                    term = cell * weights[j]
                    total[t] = term if total[t] is None else total[t] + term
    return total


def own_taps(p, height):
    return [(i, p + i - EDGE) for i in range(7) if 0 <= p + i - EDGE < height]


def halo_taps(p, height):
    found = []
    for i in range(7):
        row = p + i
        if row < EDGE:
            found.append((i, row))
        elif row >= EDGE + height:
            found.append((i, row - height))
    return found


def runs_of(steps):
    length = steps // 2 if steps % 2 == 0 else steps
    return steps // length, length


def own_conv_kernel(flip, own_ref, kern_ref, part_ref, nat, spread, taps):
    height, breadth, channels = own_ref.shape
    halves = channels // LANES
    steps, cells = dims_of(breadth)
    fill_taps(kern_ref, taps, halves, flip)

    def spread_own(p, carry):
        spread_row(own_ref[p], nat, spread, p, halves, breadth)
        return carry

    lax.fori_loop(0, height, spread_own, 0)
    n_runs, length = runs_of(steps)
    for p in range(height):

        def run_body(index, carry, p=p):
            h = index // n_runs
            start = (index % n_runs) * length
            total = conv_run(
                lambda slot, u: spread[h, slot, start + u], taps, h, own_taps(p, height), length, [None] * length
            )
            for t in range(length):
                part_ref[h, p * steps + start + t] = total[t]
            return carry

        lax.fori_loop(0, halves * n_runs, run_body, 0)


def main_kernel(
    place_ref, own_ref, top_ref, bottom_ref, part_ref, cot_ref, mask_ref, kern_ref, cbias_ref, gain_ref, nbias_ref, w_in_ref,
    b_in_ref, w_out_ref, b_out_ref, scale_ref,
    out_ref, gconv_ref, keep_ref, send_ref, hsum_ref, chan_ref,
    nat, out_s, spread, taps, conv, units, cots, state_s, mixed_s, gnorm_s, ocean_s, inv_s, normed_s, act_s, gmix_s, ghid_s,
):
    height, breadth, channels = own_ref.shape
    hidden_units = w_in_ref.shape[1]
    halves = channels // LANES
    steps, cells = dims_of(breadth)

    fill_taps(kern_ref, taps, halves, False)
    for r in range(EDGE):
        spread_row(top_ref[r], nat, spread, r, halves, breadth)
        spread_row(bottom_ref[r], nat, spread, EDGE + r, halves, breadth)
    n_runs, length = runs_of(steps)
    for p in range(height):

        def conv_body(index, carry, p=p):
            h = index // n_runs
            start = (index % n_runs) * length
            base = p * steps + start
            total = conv_run(
                lambda slot, u: spread[h, slot, start + u],
                taps,
                h,
                halo_taps(p, height),
                length,
                [part_ref[h, base + t] for t in range(length)],
            )
            for t in range(length):
                conv[h, pl.ds(pl.multiple_of((base + t) * SUBS, SUBS), SUBS), :] = total[t]
            return carry

        lax.fori_loop(0, halves * n_runs, conv_body, 0)

    hsum_ref[...] = jnp.zeros_like(hsum_ref)
    chan_ref[...] = jnp.zeros_like(chan_ref)
    width = 256
    inv_c = 1.0 / channels
    sides = range(halves)
    lanes = [slice(h * LANES, (h + 1) * LANES) for h in sides]

    def column_sum(values):
        return jnp.sum(values.reshape(values.shape[0] // SUBS, SUBS, values.shape[1]), axis=0)

    def mean_of(parts):
        return jnp.sum(functools.reduce(jnp.add, parts), axis=1, keepdims=True) * inv_c

    pack = 2 if height % 2 == 0 else 1

    def row_body(pp, carry):
        base2 = pl.multiple_of(pp * (pack * cells), 16)
        rows = pl.ds(base2, pack * cells)
        for q in range(pack):
            p = pp * pack + q
            base = pl.multiple_of(base2 + q * cells, 16)
            cot = cot_ref[p].astype(F32)
            for h in sides:
                nat[h, SUBS : SUBS + breadth, :] = cot[:, lanes[h]]
                out_s[h, SUBS : SUBS + breadth, :] = own_ref[p, :, lanes[h]].astype(F32)
            land = mask_ref[p]
            for t in range(0, steps, 2):
                here = pl.ds(base + t * SUBS, 2 * SUBS)
                local = slice(q * cells + t * SUBS, q * cells + (t + 2) * SUBS)
                values = [conv[h, here, :] + cbias_ref[:, lanes[h]] for h in sides]
                center = mean_of(values)
                deviation = [v - center for v in values]
                inv_std = lax.rsqrt(mean_of([d * d for d in deviation]) + EPSILON)
                inv_s[local, :] = jnp.broadcast_to(inv_std, (2 * SUBS, LANES))
                ocean = jnp.concatenate([jnp.broadcast_to(land[:, t + k : t + k + 1], (SUBS, LANES)) for k in range(2)], axis=0)
                ocean_s[local, :] = ocean
                for h in sides:
                    unit = deviation[h] * inv_std
                    units[local, lanes[h]] = unit
                    normed_s[here, lanes[h]] = (unit * gain_ref[:, lanes[h]] + nbias_ref[:, lanes[h]]).astype(BF16)
                    cell = jnp.concatenate(
                        [nat[h, pl.ds(SUBS + t + k, SUBS, stride=steps), :] for k in range(2)], axis=0
                    )
                    upstream = jnp.where(ocean > 0, cell, 0.0)
                    cots[local, lanes[h]] = upstream
                    state_s[local, lanes[h]] = jnp.concatenate(
                        [out_s[h, pl.ds(SUBS + t + k, SUBS, stride=steps), :] for k in range(2)], axis=0
                    )
                    gmix_s[here, lanes[h]] = (scale_ref[:, lanes[h]] * upstream).astype(BF16)
        normed = normed_s[rows, :]
        gmix = gmix_s[rows, :]
        for c in range(0, hidden_units, width):
            cols = slice(c, c + width)
            hidden = jnp.dot(normed, w_in_ref[:, cols], preferred_element_type=F32) + b_in_ref[:, cols]
            grad_act = lax.dot_general(
                gmix, w_out_ref[cols, :], (((1,), (1,)), ((), ())), preferred_element_type=F32
            )
            square = hidden * hidden
            inner = hidden * (ROOT_TERM * CUBIC * square + ROOT_TERM)
            half_tanh = 0.5 * jnp.tanh(inner)
            gate = 0.5 + half_tanh
            active = hidden * gate
            slope = gate + active * (0.5 - half_tanh) * (6.0 * CUBIC * ROOT_TERM * square + 2.0 * ROOT_TERM)
            act = active.astype(BF16)
            act_s[rows, cols] = act
            mixed = jnp.dot(act, w_out_ref[cols, :], preferred_element_type=F32)
            ghid = (grad_act * slope).astype(BF16)
            ghid_s[rows, cols] = ghid
            hsum_ref[:, cols] += column_sum(ghid.astype(F32))
            grad_normed = lax.dot_general(
                ghid, w_in_ref[:, cols], (((1,), (1,)), ((), ())), preferred_element_type=F32
            )
            if c:
                mixed_s[...] += mixed
                gnorm_s[...] += grad_normed
            else:
                mixed_s[...] = mixed
                gnorm_s[...] = grad_normed
        for q in range(pack):
            p = pp * pack + q
            base = pl.multiple_of(base2 + q * cells, 16)
            sums = [[None] * halves for _ in range(5)]

            def add_to(n, h, values):
                folded = values[:SUBS] + values[SUBS:]
                sums[n][h] = folded if sums[n][h] is None else sums[n][h] + folded

            for t in range(0, steps, 2):
                here = pl.ds(base + t * SUBS, 2 * SUBS)
                local = slice(q * cells + t * SUBS, q * cells + (t + 2) * SUBS)
                ocean = ocean_s[local, :]
                scaled, products, units_here = [], [], []
                for h in sides:
                    mixed = mixed_s[local, lanes[h]] + b_out_ref[:, lanes[h]]
                    add_to(4, h, cots[local, lanes[h]] * mixed)
                    residual = jnp.where(ocean > 0, scale_ref[:, lanes[h]] * mixed, 0.0)
                    result = state_s[local, lanes[h]] + residual
                    for k in range(2):
                        out_s[h, pl.ds(SUBS + t + k, SUBS, stride=steps), :] = result[k * SUBS : (k + 1) * SUBS]
                    grad_normed = gnorm_s[local, lanes[h]]
                    unit = units[local, lanes[h]]
                    add_to(1, h, grad_normed * unit)
                    add_to(2, h, grad_normed)
                    add_to(3, h, gmix_s[here, lanes[h]].astype(F32))
                    scaled.append(grad_normed * gain_ref[:, lanes[h]])
                    units_here.append(unit)
                    products.append(scaled[h] * unit)
                mean_scaled = mean_of(scaled)
                mean_product = mean_of(products)
                inv_std = inv_s[local, :]
                for h in sides:
                    grad_conv = (inv_std * (scaled[h] - mean_scaled - units_here[h] * mean_product)).astype(BF16).astype(F32)
                    add_to(0, h, grad_conv)
                    for k in range(2):
                        nat[h, pl.ds(SUBS + t + k, SUBS, stride=steps), :] = grad_conv[k * SUBS : (k + 1) * SUBS]
            for n in range(5):
                for h in sides:
                    chan_ref[n, :, lanes[h]] += sums[n][h]
            for h in sides:
                out_ref[p, :, lanes[h]] = gather_row(out_s, h, breadth).astype(BF16)
                gconv_ref[p, :, lanes[h]] = gather_row(nat, h, breadth).astype(BF16)
        return carry

    lax.fori_loop(0, height // pack, row_body, 0)

    first = (((0,), (0,)), ((), ()))

    def store_block(half, c, block):
        @pl.when(place_ref[0] == half)
        def _():
            keep_ref[c : c + width, :] = block

        @pl.when(place_ref[0] != half)
        def _():
            send_ref[c : c + width, :] = block.astype(BF16)

    normed = normed_s[...]
    for c in range(0, hidden_units, width):
        cols = slice(c, c + width)
        store_block(0, c, lax.dot_general(normed, ghid_s[:, cols], first, preferred_element_type=F32))
    gmix = gmix_s[...]
    for c in range(0, hidden_units, width):
        cols = slice(c, c + width)
        store_block(1, c, lax.dot_general(act_s[:, cols], gmix, first, preferred_element_type=F32))


def kernel_grad_kernel(
    own_ref, top_ref, bottom_ref, gconv_ref, hsum_ref, chan_ref, small_ref, nat, spread, grads, sums, total
):
    height, breadth, channels = own_ref.shape
    halves = channels // LANES
    steps, cells = dims_of(breadth)
    for r in range(EDGE):
        spread_row(top_ref[r], nat, spread, r, halves, breadth)
        spread_row(bottom_ref[r], nat, spread, EDGE + height + r, halves, breadth)

    def spread_own(p, carry):
        spread_row(own_ref[p], nat, spread, EDGE + p, halves, breadth)
        return carry

    lax.fori_loop(0, height, spread_own, 0)

    nat[:, SUBS + breadth : SUBS + cells, :] = jnp.zeros((halves, cells - breadth, LANES), F32)

    def spread_grad(p, carry):
        row = gconv_ref[p].astype(F32)
        for h in range(halves):
            nat[h, SUBS : SUBS + breadth, :] = row[:, h * LANES : (h + 1) * LANES]
        for h in range(halves):
            for t in range(steps):
                grads[h, p, t] = nat[h, pl.ds(SUBS + t, SUBS, stride=steps), :]
        return carry

    lax.fori_loop(0, height, spread_grad, 0)

    def tap_body(i, carry):
        total = [[None] * 7 for _ in range(halves)]
        for p in range(height):
            window = [[spread[h, p + i, t] for t in range(6)] for h in range(halves)]
            for t in range(steps):
                for h in range(halves):
                    window[h].append(spread[h, p + i, t + 6])
                    grad = grads[h, p, t]
                    for j in range(7):
                        term = window[h][t + j] * grad
                        total[h][j] = term if total[h][j] is None else total[h][j] + term
        for h in range(halves):
            for j in range(7):
                sums[h, i * 7 + j] = jnp.sum(total[h][j], axis=0, keepdims=True)
        return carry

    lax.fori_loop(0, 7, tap_body, 0)
    total[...] = jnp.zeros_like(total)
    for h in range(halves):
        total[0:49, h * LANES : (h + 1) * LANES] = sums[h].reshape(49, LANES)
    rows = hsum_ref.shape[1] // channels
    at = 49
    for c in range(rows):
        total[at + c : at + c + 1, :] = jnp.sum(hsum_ref[:, c * channels : (c + 1) * channels], axis=0, keepdims=True)
    at += rows
    for c in range(5):
        total[at + c : at + c + 1, :] = jnp.sum(chan_ref[c], axis=0, keepdims=True)
    small_ref[...] = total[...]


def input_grad_kernel(top_ref, bottom_ref, part_ref, kern_ref, cot_ref, grad_ref, nat, spread, taps):
    height, breadth, channels = cot_ref.shape
    halves = channels // LANES
    steps, cells = dims_of(breadth)
    fill_taps(kern_ref, taps, halves, True)
    for r in range(EDGE):
        spread_row(top_ref[r], nat, spread, r, halves, breadth)
        spread_row(bottom_ref[r], nat, spread, EDGE + r, halves, breadth)
    n_runs, length = runs_of(steps)
    for p in range(height):

        def run_body(index, carry, p=p):
            h = index // n_runs
            start = (index % n_runs) * length
            base = p * steps + start
            total = conv_run(
                lambda slot, u: spread[h, slot, start + u],
                taps,
                h,
                halo_taps(p, height),
                length,
                [part_ref[h, base + t] for t in range(length)],
            )
            for t in range(length):
                nat[h, pl.ds(SUBS + start + t, SUBS, stride=steps), :] = total[t]
            return carry

        lax.fori_loop(0, halves * n_runs, run_body, 0)
        for h in range(halves):
            lanes = slice(h * LANES, (h + 1) * LANES)
            grad_ref[p, :, lanes] = (cot_ref[p, :, lanes].astype(F32) + gather_row(nat, h, breadth)).astype(BF16)


def call(kernel, out_shape, scratch, flops, nbytes, name, limit=VMEM_LIMIT):
    def run(*operands):
        whole = pl.BlockSpec(memory_space=pltpu.VMEM)
        scalars = pl.BlockSpec(memory_space=pltpu.SMEM)
        return pl.pallas_call(
            kernel,
            out_shape=out_shape,
            in_specs=[scalars if x.dtype == jnp.int32 else whole for x in operands],
            out_specs=jax.tree.map(lambda _: whole, out_shape),
            scratch_shapes=scratch,
            compiler_params=pltpu.CompilerParams(vmem_limit_bytes=limit),
            cost_estimate=pl.CostEstimate(flops=flops, bytes_accessed=nbytes, transcendentals=0),
            name=name,
        )(*operands)

    return run


def place_kernel(digits, rows, factor, place_ref, here_ref, across_ref, other_ref, other_across_ref, *rest):
    w_in_ref, w_out_ref, kernel_ref, hidden_ref, chan_ref, total = rest
    channels = here_ref.shape[1]
    order = [[]]
    for stride, size in digits[1:]:
        order = [tail + [k] for k in range(size) for tail in order]
    share = (here_ref.shape[0] - SMALL) // len(order)
    draw = place_ref[0]
    small = jnp.zeros((SMALL, channels), F32)
    for flip, refs in ((0, (here_ref, across_ref)), (1, (other_ref, other_across_ref))):
        for last, ref in enumerate(refs):
            values = ref[...].astype(F32)
            small = small + values[-SMALL:]
            for n, ks in enumerate(order):
                extent = rows
                start = 0
                for d, (stride, size) in enumerate(digits):
                    extent = extent // size
                    k = ks[d - 1] if d else last
                    start = start + (place_ref[1 + d] ^ k) * extent
                start = pl.multiple_of(start, SUBS)
                total[draw ^ flip, pl.ds(start, share), :] = values[n * share : (n + 1) * share]
    big = w_out_ref.shape[0]
    for c in range(big // channels):
        cols = slice(c * channels, (c + 1) * channels)
        w_in_ref[:, cols] = total[0, cols, :] * factor
    w_out_ref[...] = total[1, 0:big, :] * factor
    small = small * factor
    for i in range(7):
        kernel_ref[i] = small[i * 7 : i * 7 + 7]
    blocks = big // channels
    halves = channels // LANES
    for c in range(blocks):
        for h in range(halves):
            hidden_ref[c * halves + h : c * halves + h + 1, :] = small[49 + c : 50 + c, h * LANES : (h + 1) * LANES]
    chan_ref[...] = small[49 + blocks : 54 + blocks]


def digits_of(count):
    digits = []
    stride = 2
    while stride < count:
        size = min(4, count // stride)
        digits.append((stride, size))
        stride *= size
    return [(1, 2)] + digits[::-1]


def exchange(values, count, stride, size, k):
    pairs = []
    for i in range(count):
        digit = i // stride % size
        pairs.append((i, i + ((digit ^ k) - digit) * stride))
    return lax.ppermute(values, "tile", pairs)


def other_core(values, draws):
    return lax.ppermute(values, "draw", [(i, i ^ 1) for i in range(draws)])


def halo(cells, tiles):
    after = [(i, i + 1) for i in range(tiles - 1)]
    before = [(i + 1, i) for i in range(tiles - 1)]
    top = lax.ppermute(cells[-EDGE:], "tile", after)
    bottom = lax.ppermute(cells[:EDGE], "tile", before)
    return top, bottom


def per_device(
    tiles,
    draws,
    inputs,
    land_mask,
    kernel,
    conv_bias,
    norm_gain,
    norm_bias,
    w_in,
    b_in,
    w_out,
    b_out,
    layer_scale,
    cotangent,
):
    _, height, breadth, channels = inputs.shape
    hidden_units = w_in.shape[1]
    halves = channels // LANES
    steps, cells = dims_of(breadth)
    own = inputs[0]
    cot = cotangent[0]
    top, bottom = halo(own, tiles)
    mask = jnp.pad(land_mask.astype(F32), ((0, 0), (0, cells - breadth)))
    mask = mask.reshape(height, SUBS, steps)

    def row(vector):
        return vector.reshape(1, -1)

    nat = pltpu.VMEM((halves, cells + 2 * SUBS, LANES), F32)

    def spread(slots):
        return pltpu.VMEM((halves, slots, steps + 2 * EDGE, SUBS, LANES), F32)

    taps = pltpu.VMEM((halves, 49, SUBS, LANES), F32)
    big_row = pltpu.VMEM((2 * cells, channels), F32)
    narrow = pltpu.VMEM((2 * cells, LANES), F32)
    count = height * cells
    big = hidden_units
    digits = digits_of(tiles)
    unit = tiles * SUBS
    rows = -(-big // unit) * unit
    tile = lax.axis_index("tile")
    place = jnp.stack([lax.axis_index("draw")] + [tile // stride % size for stride, size in digits]).astype(jnp.int32)
    part_shape = jax.ShapeDtypeStruct((halves, height * steps, SUBS, LANES), F32)
    mega = 1024 * 1024

    def own_conv(rows_here, flip, name):
        return call(functools.partial(own_conv_kernel, flip), part_shape, [nat, spread(height), taps], 1, 1, name)(rows_here, kernel)

    part = own_conv(own, False, "own_conv")
    out, gconv, keep, send, hsum, chan = call(
        main_kernel,
        (
            jax.ShapeDtypeStruct((height, breadth, channels), BF16),
            jax.ShapeDtypeStruct((height, breadth, channels), BF16),
            jax.ShapeDtypeStruct((big, channels), F32),
            jax.ShapeDtypeStruct((big, channels), BF16),
            jax.ShapeDtypeStruct((SUBS, hidden_units), F32),
            jax.ShapeDtypeStruct((5, SUBS, channels), F32),
        ),
        [
            nat,
            nat,
            spread(2 * EDGE),
            taps,
            pltpu.VMEM((halves, count, LANES), F32),
            big_row,
            big_row,
            big_row,
            big_row,
            big_row,
            narrow,
            narrow,
            pltpu.VMEM((count, channels), BF16),
            pltpu.VMEM((count, hidden_units), BF16),
            pltpu.VMEM((count, channels), BF16),
            pltpu.VMEM((count, hidden_units), BF16),
        ],
        12 * count * channels * hidden_units,
        8 * mega,
        "block_main",
    )(
        place, own, top, bottom, part, cot, mask, kernel, row(conv_bias), row(norm_gain), row(norm_bias), w_in, row(b_in),
        w_out, row(b_out), row(layer_scale),
    )
    got = other_core(send, draws)

    if rows > big:
        keep = jnp.pad(keep, ((0, rows - big), (0, 0)))
        got = jnp.pad(got, ((0, rows - big), (0, 0)))
    for step, (stride, size) in enumerate(digits):
        share = keep.shape[0] // size
        mine = place[1 + step]
        pieces = []
        for k in range(size):
            piece = lax.dynamic_slice_in_dim(keep, (mine ^ k) * share, share, 0)
            if not step:
                piece = piece + lax.dynamic_slice_in_dim(got, (mine ^ k) * share, share, 0).astype(F32)
            pieces.append(piece)
        sends = [piece.astype(BF16) for piece in pieces[1:]]
        if not step:
            sends, gconv = lax.optimization_barrier((sends, gconv))
            grad_part = own_conv(gconv, True, "own_conv_grad")
        elif step == 1:
            grad_top, grad_bottom = halo(gconv, tiles)
            sends, hsum = lax.optimization_barrier((sends, hsum))
            small = call(
                kernel_grad_kernel,
                jax.ShapeDtypeStruct((SMALL, channels), F32),
                [
                    nat,
                    spread(height + 2 * EDGE),
                    pltpu.VMEM((halves, height, steps, SUBS, LANES), F32),
                    pltpu.VMEM((halves, 49, 1, LANES), F32),
                    pltpu.VMEM((SMALL, channels), F32),
                ],
                1,
                1,
                "kernel_grad",
            )(own, top, bottom, gconv, hsum, chan)
        received = [exchange(sends[k - 1], tiles, stride, size, k) for k in range(1, size)]
        if not step:
            received, grad_part, gconv = lax.optimization_barrier((received, grad_part, gconv))
        elif step == 1:
            received, small = lax.optimization_barrier((received, small))
        keep = pieces[0]
        for piece in received:
            keep = keep + piece.astype(F32)
    gathered = keep.astype(BF16)
    for stride, size in digits[1:]:
        payload = jnp.concatenate([gathered, small.astype(BF16)], axis=0)
        received = [payload] + [exchange(payload, tiles, stride, size, k) for k in range(1, size)]
        if (stride, size) == digits[1]:
            received, grad_top, grad_bottom = lax.optimization_barrier((received, grad_top, grad_bottom))
        gathered = jnp.concatenate([piece[:-SMALL] for piece in received], axis=0)
        small = functools.reduce(jnp.add, [piece[-SMALL:].astype(F32) for piece in received])
    gathered = jnp.concatenate([gathered, small.astype(BF16)], axis=0)
    stride, size = digits[0]
    gathered, grad_part = lax.optimization_barrier((gathered, grad_part))
    input_grad = call(
        input_grad_kernel,
        jax.ShapeDtypeStruct((height, breadth, channels), BF16),
        [nat, spread(2 * EDGE), taps],
        1,
        1,
        "input_grad",
    )(grad_top, grad_bottom, grad_part, kernel, cot)
    across = exchange(gathered, tiles, stride, size, 1)
    other = other_core(gathered, draws)
    lon_first = Layout((0, 2, 1, 3))
    out = with_layout_constraint(out[None], lon_first)
    input_grad = with_layout_constraint(input_grad[None], lon_first)
    across, out, input_grad = lax.optimization_barrier((across, out, input_grad))
    other_across = other_core(across, draws)
    factor = float(1.0 / np.sqrt(np.float32(draws * height * tiles * breadth)))
    w_in_sum, w_out_sum, kernel_sum, hidden_sum, chan_sum = call(
        functools.partial(place_kernel, digits, rows, factor),
        (
            jax.ShapeDtypeStruct((channels, hidden_units), F32),
            jax.ShapeDtypeStruct((hidden_units, channels), F32),
            jax.ShapeDtypeStruct((7, 7, channels), F32),
            jax.ShapeDtypeStruct((hidden_units // LANES, LANES), F32),
            jax.ShapeDtypeStruct((5, channels), F32),
        ),
        [pltpu.VMEM((2, rows, channels), F32)],
        mega,
        4 * mega,
        "place",
        16 * mega,
    )(place, gathered, across, other, other_across)
    return (
        out,
        input_grad,
        kernel_sum,
        w_in_sum,
        w_out_sum,
        hidden_sum.reshape(-1),
        chan_sum,
    )


def solution(mesh):
    placed = (
        P(("group", "draw"), "tile", None, None),
        P("tile", None),
        P(),
        P(),
        P(),
        P(),
        P(),
        P(),
        P(),
        P(),
        P(),
        P(("group", "draw"), "tile", None, None),
    )
    return jax.shard_map(
        functools.partial(per_device, mesh.shape["tile"], mesh.shape["draw"]),
        mesh=mesh,
        in_specs=placed,
        out_specs=(
            P(("group", "draw"), "tile", None, None),
            P(("group", "draw"), "tile", None, None),
            P("group", None, None),
            P("group", None),
            P("group", None),
            P("group"),
            P("group", None),
        ),
        check_vma=False,
    )
```

```python
import functools

import jax
import jax.numpy as jnp
import numpy as np
from jax import lax
from jax.experimental import pallas as pl
from jax.experimental.layout import Layout, with_layout_constraint
from jax.experimental.pallas import tpu as pltpu
from jax.sharding import PartitionSpec as P

ROOT_TERM = 0.7978845608028654
CUBIC = 0.044715
EPSILON = 1e-06
F32 = jnp.float32
BF16 = jnp.bfloat16
LANES = 128
SUBS = 8
EDGE = 3
SMALL = 64
VMEM_LIMIT = 56 * 1024 * 1024


def dims_of(breadth):
    steps = -(-breadth // SUBS)
    return steps, steps * SUBS


def spread_row(row, nat, spread, slot, halves, breadth):
    steps, cells = dims_of(breadth)
    row = row.astype(F32)
    over = cells - breadth + EDGE
    for h in range(halves):
        part = row[:, h * LANES : (h + 1) * LANES]
        nat[h, SUBS : SUBS + breadth, :] = part
        nat[h, SUBS - EDGE : SUBS, :] = part[breadth - EDGE :]
        nat[h, SUBS + breadth : SUBS + breadth + over, :] = part[:over]
    for h in range(halves):
        for t in range(steps + 2 * EDGE):
            spread[h, slot, t] = nat[h, pl.ds(SUBS - EDGE + t, SUBS, stride=steps), :]


def gather_row(nat, h, breadth):
    return nat[h, SUBS : SUBS + breadth, :]


def fill_taps(kern_ref, taps, halves, flip):
    for i in range(7):
        for j in range(7):
            src = kern_ref[6 - i, 6 - j : 7 - j, :] if flip else kern_ref[i, j : j + 1, :]
            for h in range(halves):
                taps[h, i * 7 + j] = jnp.broadcast_to(src[:, h * LANES : (h + 1) * LANES], (SUBS, LANES))


def conv_run(cells_at, taps, h, row_taps, length, total):
    total = list(total)
    for i, slot in row_taps:
        weights = [taps[h, i * 7 + j] for j in range(7)]
        for u in range(length + 6):
            cell = cells_at(slot, u)
            for j in range(7):
                t = u - j
                if 0 <= t < length:
                    term = cell * weights[j]
                    total[t] = term if total[t] is None else total[t] + term
    return total


def own_taps(p, height):
    return [(i, p + i - EDGE) for i in range(7) if 0 <= p + i - EDGE < height]


def halo_taps(p, height):
    found = []
    for i in range(7):
        row = p + i
        if row < EDGE:
            found.append((i, row))
        elif row >= EDGE + height:
            found.append((i, row - height))
    return found


def runs_of(steps):
    length = steps // 2 if steps % 2 == 0 else steps
    return steps // length, length


def own_conv_rows(spread, taps, kern_ref, part_ref, height, steps, halves, flip):
    fill_taps(kern_ref, taps, halves, flip)
    n_runs, length = runs_of(steps)
    for p in range(height):

        def run_body(index, carry, p=p):
            h = index // n_runs
            start = (index % n_runs) * length
            total = conv_run(
                lambda slot, u: spread[h, slot, start + u], taps, h, own_taps(p, height), length, [None] * length
            )
            for t in range(length):
                part_ref[h, p * steps + start + t] = total[t]
            return carry

        lax.fori_loop(0, halves * n_runs, run_body, 0)


def own_conv_kernel(own_ref, kern_ref, part_ref, nat, spread, taps):
    height, breadth, channels = own_ref.shape
    halves = channels // LANES
    steps, cells = dims_of(breadth)
    def spread_own(p, carry):
        spread_row(own_ref[p], nat, spread, p, halves, breadth)
        return carry

    lax.fori_loop(0, height, spread_own, 0)
    own_conv_rows(spread, taps, kern_ref, part_ref, height, steps, halves, False)


def main_kernel(
    place_ref, own_ref, top_ref, bottom_ref, part_ref, cot_ref, mask_ref, kern_ref, cbias_ref, gain_ref, nbias_ref, w_in_ref,
    b_in_ref, w_out_ref, b_out_ref, scale_ref,
    out_ref, gconv_ref, keep_ref, send_ref, hsum_ref, chan_ref,
    nat, out_s, spread, taps, conv, units, cots, state_s, mixed_s, gnorm_s, ocean_s, inv_s, normed_s, act_s, gmix_s, ghid_s,
):
    height, breadth, channels = own_ref.shape
    hidden_units = w_in_ref.shape[1]
    halves = channels // LANES
    steps, cells = dims_of(breadth)

    fill_taps(kern_ref, taps, halves, False)
    for r in range(EDGE):
        spread_row(top_ref[r], nat, spread, r, halves, breadth)
        spread_row(bottom_ref[r], nat, spread, EDGE + r, halves, breadth)
    n_runs, length = runs_of(steps)
    for p in range(height):

        def conv_body(index, carry, p=p):
            h = index // n_runs
            start = (index % n_runs) * length
            base = p * steps + start
            total = conv_run(
                lambda slot, u: spread[h, slot, start + u],
                taps,
                h,
                halo_taps(p, height),
                length,
                [part_ref[h, base + t] for t in range(length)],
            )
            for t in range(length):
                conv[h, pl.ds(pl.multiple_of((base + t) * SUBS, SUBS), SUBS), :] = total[t]
            return carry

        lax.fori_loop(0, halves * n_runs, conv_body, 0)

    hsum_ref[...] = jnp.zeros_like(hsum_ref)
    chan_ref[...] = jnp.zeros_like(chan_ref)
    width = 256
    inv_c = 1.0 / channels
    sides = range(halves)
    lanes = [slice(h * LANES, (h + 1) * LANES) for h in sides]

    def column_sum(values):
        return jnp.sum(values.reshape(values.shape[0] // SUBS, SUBS, values.shape[1]), axis=0)

    def mean_of(parts):
        return jnp.sum(functools.reduce(jnp.add, parts), axis=1, keepdims=True) * inv_c

    pack = 2 if height % 2 == 0 else 1

    def row_body(pp, carry):
        base2 = pl.multiple_of(pp * (pack * cells), 16)
        rows = pl.ds(base2, pack * cells)
        for q in range(pack):
            p = pp * pack + q
            base = pl.multiple_of(base2 + q * cells, 16)
            cot = cot_ref[p].astype(F32)
            for h in sides:
                nat[h, SUBS : SUBS + breadth, :] = cot[:, lanes[h]]
                out_s[h, SUBS : SUBS + breadth, :] = own_ref[p, :, lanes[h]].astype(F32)
            land = mask_ref[p]
            for t in range(0, steps, 2):
                here = pl.ds(base + t * SUBS, 2 * SUBS)
                local = slice(q * cells + t * SUBS, q * cells + (t + 2) * SUBS)
                values = [conv[h, here, :] + cbias_ref[:, lanes[h]] for h in sides]
                center = mean_of(values)
                deviation = [v - center for v in values]
                inv_std = lax.rsqrt(mean_of([d * d for d in deviation]) + EPSILON)
                inv_s[local, :] = jnp.broadcast_to(inv_std, (2 * SUBS, LANES))
                ocean = jnp.concatenate([jnp.broadcast_to(land[:, t + k : t + k + 1], (SUBS, LANES)) for k in range(2)], axis=0)
                ocean_s[local, :] = ocean
                for h in sides:
                    unit = deviation[h] * inv_std
                    units[local, lanes[h]] = unit
                    normed_s[here, lanes[h]] = (unit * gain_ref[:, lanes[h]] + nbias_ref[:, lanes[h]]).astype(BF16)
                    cell = jnp.concatenate(
                        [nat[h, pl.ds(SUBS + t + k, SUBS, stride=steps), :] for k in range(2)], axis=0
                    )
                    upstream = jnp.where(ocean > 0, cell, 0.0)
                    cots[local, lanes[h]] = upstream
                    state_s[local, lanes[h]] = jnp.concatenate(
                        [out_s[h, pl.ds(SUBS + t + k, SUBS, stride=steps), :] for k in range(2)], axis=0
                    )
                    gmix_s[here, lanes[h]] = (scale_ref[:, lanes[h]] * upstream).astype(BF16)
        normed = normed_s[rows, :]
        gmix = gmix_s[rows, :]
        for c in range(0, hidden_units, width):
            cols = slice(c, c + width)
            hidden = jnp.dot(normed, w_in_ref[:, cols], preferred_element_type=F32) + b_in_ref[:, cols]
            grad_act = lax.dot_general(
                gmix, w_out_ref[cols, :], (((1,), (1,)), ((), ())), preferred_element_type=F32
            )
            square = hidden * hidden
            inner = hidden * (ROOT_TERM * CUBIC * square + ROOT_TERM)
            half_tanh = 0.5 * jnp.tanh(inner)
            gate = 0.5 + half_tanh
            active = hidden * gate
            slope = gate + active * (0.5 - half_tanh) * (6.0 * CUBIC * ROOT_TERM * square + 2.0 * ROOT_TERM)
            act = active.astype(BF16)
            act_s[rows, cols] = act
            mixed = jnp.dot(act, w_out_ref[cols, :], preferred_element_type=F32)
            ghid = (grad_act * slope).astype(BF16)
            ghid_s[rows, cols] = ghid
            hsum_ref[:, cols] += column_sum(ghid.astype(F32))
            grad_normed = lax.dot_general(
                ghid, w_in_ref[:, cols], (((1,), (1,)), ((), ())), preferred_element_type=F32
            )
            if c:
                mixed_s[...] += mixed
                gnorm_s[...] += grad_normed
            else:
                mixed_s[...] = mixed
                gnorm_s[...] = grad_normed
        for q in range(pack):
            p = pp * pack + q
            base = pl.multiple_of(base2 + q * cells, 16)
            sums = [[None] * halves for _ in range(5)]

            def add_to(n, h, values):
                folded = values[:SUBS] + values[SUBS:]
                sums[n][h] = folded if sums[n][h] is None else sums[n][h] + folded

            for t in range(0, steps, 2):
                here = pl.ds(base + t * SUBS, 2 * SUBS)
                local = slice(q * cells + t * SUBS, q * cells + (t + 2) * SUBS)
                ocean = ocean_s[local, :]
                scaled, products, units_here = [], [], []
                for h in sides:
                    mixed = mixed_s[local, lanes[h]] + b_out_ref[:, lanes[h]]
                    add_to(4, h, cots[local, lanes[h]] * mixed)
                    residual = jnp.where(ocean > 0, scale_ref[:, lanes[h]] * mixed, 0.0)
                    result = state_s[local, lanes[h]] + residual
                    for k in range(2):
                        out_s[h, pl.ds(SUBS + t + k, SUBS, stride=steps), :] = result[k * SUBS : (k + 1) * SUBS]
                    grad_normed = gnorm_s[local, lanes[h]]
                    unit = units[local, lanes[h]]
                    add_to(1, h, grad_normed * unit)
                    add_to(2, h, grad_normed)
                    add_to(3, h, gmix_s[here, lanes[h]].astype(F32))
                    scaled.append(grad_normed * gain_ref[:, lanes[h]])
                    units_here.append(unit)
                    products.append(scaled[h] * unit)
                mean_scaled = mean_of(scaled)
                mean_product = mean_of(products)
                inv_std = inv_s[local, :]
                for h in sides:
                    grad_conv = (inv_std * (scaled[h] - mean_scaled - units_here[h] * mean_product)).astype(BF16).astype(F32)
                    add_to(0, h, grad_conv)
                    for k in range(2):
                        nat[h, pl.ds(SUBS + t + k, SUBS, stride=steps), :] = grad_conv[k * SUBS : (k + 1) * SUBS]
            for n in range(5):
                for h in sides:
                    chan_ref[n, :, lanes[h]] += sums[n][h]
            for h in sides:
                out_ref[p, :, lanes[h]] = gather_row(out_s, h, breadth).astype(BF16)
                gconv_ref[p, :, lanes[h]] = gather_row(nat, h, breadth).astype(BF16)
        return carry

    lax.fori_loop(0, height // pack, row_body, 0)

    first = (((0,), (0,)), ((), ()))

    def store_block(half, c, block):
        @pl.when(place_ref[0] == half)
        def _():
            keep_ref[c : c + width, :] = block

        @pl.when(place_ref[0] != half)
        def _():
            send_ref[c : c + width, :] = block.astype(BF16)

    w_in_grad = lax.dot_general(normed_s[...], ghid_s[...], first, preferred_element_type=F32)
    for c in range(0, hidden_units, width):
        store_block(0, c, w_in_grad[:, c : c + width])
    w_out_grad = lax.dot_general(act_s[...], gmix_s[...], first, preferred_element_type=F32)
    for c in range(0, hidden_units, width):
        store_block(1, c, w_out_grad[c : c + width])


def grads_kernel(
    own_ref, top_ref, bottom_ref, gconv_ref, kern_ref, hsum_ref, chan_ref, small_ref, part_ref,
    nat, spread, grads, taps, sums, total,
):
    height, breadth, channels = own_ref.shape
    halves = channels // LANES
    steps, cells = dims_of(breadth)
    for r in range(EDGE):
        spread_row(top_ref[r], nat, spread, r, halves, breadth)
        spread_row(bottom_ref[r], nat, spread, EDGE + height + r, halves, breadth)

    def spread_own(p, carry):
        spread_row(own_ref[p], nat, spread, EDGE + p, halves, breadth)
        spread_row(gconv_ref[p], nat, grads, p, halves, breadth)
        return carry

    lax.fori_loop(0, height, spread_own, 0)
    own_conv_rows(grads, taps, kern_ref, part_ref, height, steps, halves, True)
    sublane = lax.broadcasted_iota(jnp.int32, (SUBS, LANES), 0)

    def grad_at(h, p, t):
        grad = grads[h, p, EDGE + t]
        for s in range(SUBS):
            if s * steps + t >= breadth:
                grad = jnp.where(sublane == s, 0.0, grad)
        return grad

    def tap_body(i, carry):
        total = [[None] * 7 for _ in range(halves)]
        for p in range(height):
            window = [[spread[h, p + i, t] for t in range(6)] for h in range(halves)]
            for t in range(steps):
                for h in range(halves):
                    window[h].append(spread[h, p + i, t + 6])
                    grad = grad_at(h, p, t)
                    for j in range(7):
                        term = window[h][t + j] * grad
                        total[h][j] = term if total[h][j] is None else total[h][j] + term
        for h in range(halves):
            for j in range(7):
                sums[h, i * 7 + j] = jnp.sum(total[h][j], axis=0, keepdims=True)
        return carry

    lax.fori_loop(0, 7, tap_body, 0)
    total[...] = jnp.zeros_like(total)
    for h in range(halves):
        total[0:49, h * LANES : (h + 1) * LANES] = sums[h].reshape(49, LANES)
    rows = hsum_ref.shape[1] // channels
    at = 49
    for c in range(rows):
        total[at + c : at + c + 1, :] = jnp.sum(hsum_ref[:, c * channels : (c + 1) * channels], axis=0, keepdims=True)
    at += rows
    for c in range(5):
        total[at + c : at + c + 1, :] = jnp.sum(chan_ref[c], axis=0, keepdims=True)
    small_ref[...] = total[...]


def input_grad_kernel(top_ref, bottom_ref, part_ref, kern_ref, cot_ref, grad_ref, nat, spread, taps):
    height, breadth, channels = cot_ref.shape
    halves = channels // LANES
    steps, cells = dims_of(breadth)
    fill_taps(kern_ref, taps, halves, True)
    for r in range(EDGE):
        spread_row(top_ref[r], nat, spread, r, halves, breadth)
        spread_row(bottom_ref[r], nat, spread, EDGE + r, halves, breadth)
    n_runs, length = runs_of(steps)
    for p in range(height):

        def run_body(index, carry, p=p):
            h = index // n_runs
            start = (index % n_runs) * length
            base = p * steps + start
            total = conv_run(
                lambda slot, u: spread[h, slot, start + u],
                taps,
                h,
                halo_taps(p, height),
                length,
                [part_ref[h, base + t] for t in range(length)],
            )
            for t in range(length):
                nat[h, pl.ds(SUBS + start + t, SUBS, stride=steps), :] = total[t]
            return carry

        lax.fori_loop(0, halves * n_runs, run_body, 0)
        for h in range(halves):
            lanes = slice(h * LANES, (h + 1) * LANES)
            grad_ref[p, :, lanes] = (cot_ref[p, :, lanes].astype(F32) + gather_row(nat, h, breadth)).astype(BF16)


def call(kernel, out_shape, scratch, flops, nbytes, name, limit=VMEM_LIMIT):
    def run(*operands):
        whole = pl.BlockSpec(memory_space=pltpu.VMEM)
        scalars = pl.BlockSpec(memory_space=pltpu.SMEM)
        return pl.pallas_call(
            kernel,
            out_shape=out_shape,
            in_specs=[scalars if x.dtype == jnp.int32 else whole for x in operands],
            out_specs=jax.tree.map(lambda _: whole, out_shape),
            scratch_shapes=scratch,
            compiler_params=pltpu.CompilerParams(vmem_limit_bytes=limit),
            cost_estimate=pl.CostEstimate(flops=flops, bytes_accessed=nbytes, transcendentals=0),
            name=name,
        )(*operands)

    return run


def place_kernel(digits, rows, factor, place_ref, here_ref, across_ref, other_ref, other_across_ref, *rest):
    w_in_ref, w_out_ref, kernel_ref, hidden_ref, chan_ref, total = rest
    channels = here_ref.shape[1]
    order = [[]]
    for stride, size in digits[1:]:
        order = [tail + [k] for k in range(size) for tail in order]
    share = (here_ref.shape[0] - SMALL) // len(order)
    draw = place_ref[0]
    small = jnp.zeros((SMALL, channels), F32)
    for flip, refs in ((0, (here_ref, across_ref)), (1, (other_ref, other_across_ref))):
        for last, ref in enumerate(refs):
            values = ref[...].astype(F32)
            small = small + values[-SMALL:]
            for n, ks in enumerate(order):
                extent = rows
                start = 0
                for d, (stride, size) in enumerate(digits):
                    extent = extent // size
                    k = ks[d - 1] if d else last
                    start = start + (place_ref[1 + d] ^ k) * extent
                start = pl.multiple_of(start, SUBS)
                total[draw ^ flip, pl.ds(start, share), :] = values[n * share : (n + 1) * share]
    big = w_out_ref.shape[0]
    for c in range(big // channels):
        cols = slice(c * channels, (c + 1) * channels)
        w_in_ref[:, cols] = total[0, cols, :] * factor
    w_out_ref[...] = total[1, 0:big, :] * factor
    small = small * factor
    for i in range(7):
        kernel_ref[i] = small[i * 7 : i * 7 + 7]
    blocks = big // channels
    halves = channels // LANES
    for c in range(blocks):
        for h in range(halves):
            hidden_ref[c * halves + h : c * halves + h + 1, :] = small[49 + c : 50 + c, h * LANES : (h + 1) * LANES]
    chan_ref[...] = small[49 + blocks : 54 + blocks]


def digits_of(count):
    digits = []
    stride = 2
    while stride < count:
        size = min(4, count // stride)
        digits.append((stride, size))
        stride *= size
    return [(1, 2)] + digits[::-1]


def exchange(values, count, stride, size, k):
    pairs = []
    for i in range(count):
        digit = i // stride % size
        pairs.append((i, i + ((digit ^ k) - digit) * stride))
    return lax.ppermute(values, "tile", pairs)


def other_core(values, draws):
    return lax.ppermute(values, "draw", [(i, i ^ 1) for i in range(draws)])


def halo(cells, tiles):
    after = [(i, i + 1) for i in range(tiles - 1)]
    before = [(i + 1, i) for i in range(tiles - 1)]
    top = lax.ppermute(cells[-EDGE:], "tile", after)
    bottom = lax.ppermute(cells[:EDGE], "tile", before)
    return top, bottom


def per_device(
    tiles,
    draws,
    inputs,
    land_mask,
    kernel,
    conv_bias,
    norm_gain,
    norm_bias,
    w_in,
    b_in,
    w_out,
    b_out,
    layer_scale,
    cotangent,
):
    _, height, breadth, channels = inputs.shape
    hidden_units = w_in.shape[1]
    halves = channels // LANES
    steps, cells = dims_of(breadth)
    own = inputs[0]
    cot = cotangent[0]
    top, bottom = halo(own, tiles)
    mask = jnp.pad(land_mask.astype(F32), ((0, 0), (0, cells - breadth)))
    mask = mask.reshape(height, SUBS, steps)

    def row(vector):
        return vector.reshape(1, -1)

    nat = pltpu.VMEM((halves, cells + 2 * SUBS, LANES), F32)

    def spread(slots):
        return pltpu.VMEM((halves, slots, steps + 2 * EDGE, SUBS, LANES), F32)

    taps = pltpu.VMEM((halves, 49, SUBS, LANES), F32)
    big_row = pltpu.VMEM((2 * cells, channels), F32)
    narrow = pltpu.VMEM((2 * cells, LANES), F32)
    count = height * cells
    big = hidden_units
    digits = digits_of(tiles)
    unit = tiles * SUBS
    rows = -(-big // unit) * unit
    tile = lax.axis_index("tile")
    place = jnp.stack([lax.axis_index("draw")] + [tile // stride % size for stride, size in digits]).astype(jnp.int32)
    part_shape = jax.ShapeDtypeStruct((halves, height * steps, SUBS, LANES), F32)
    mega = 1024 * 1024

    part = call(own_conv_kernel, part_shape, [nat, spread(height), taps], 1, 1, "own_conv")(own, kernel)
    out, gconv, keep, send, hsum, chan = call(
        main_kernel,
        (
            jax.ShapeDtypeStruct((height, breadth, channels), BF16),
            jax.ShapeDtypeStruct((height, breadth, channels), BF16),
            jax.ShapeDtypeStruct((big, channels), F32),
            jax.ShapeDtypeStruct((big, channels), BF16),
            jax.ShapeDtypeStruct((SUBS, hidden_units), F32),
            jax.ShapeDtypeStruct((5, SUBS, channels), F32),
        ),
        [
            nat,
            nat,
            spread(2 * EDGE),
            taps,
            pltpu.VMEM((halves, count, LANES), F32),
            big_row,
            big_row,
            big_row,
            big_row,
            big_row,
            narrow,
            narrow,
            pltpu.VMEM((count, channels), BF16),
            pltpu.VMEM((count, hidden_units), BF16),
            pltpu.VMEM((count, channels), BF16),
            pltpu.VMEM((count, hidden_units), BF16),
        ],
        12 * count * channels * hidden_units,
        8 * mega,
        "block_main",
    )(
        place, own, top, bottom, part, cot, mask, kernel, row(conv_bias), row(norm_gain), row(norm_bias), w_in, row(b_in),
        w_out, row(b_out), row(layer_scale),
    )
    got = other_core(send, draws)

    if rows > big:
        keep = jnp.pad(keep, ((0, rows - big), (0, 0)))
        got = jnp.pad(got, ((0, rows - big), (0, 0)))
    for step, (stride, size) in enumerate(digits):
        share = keep.shape[0] // size
        mine = place[1 + step]
        pieces = []
        for k in range(size):
            piece = lax.dynamic_slice_in_dim(keep, (mine ^ k) * share, share, 0)
            if not step:
                piece = piece + lax.dynamic_slice_in_dim(got, (mine ^ k) * share, share, 0).astype(F32)
            pieces.append(piece)
        sends = [piece.astype(BF16) for piece in pieces[1:]]
        if not step:
            sends, gconv, hsum = lax.optimization_barrier((sends, gconv, hsum))
            grad_top, grad_bottom = halo(gconv, tiles)
            small, grad_part = call(
                grads_kernel,
                (jax.ShapeDtypeStruct((SMALL, channels), F32), part_shape),
                [
                    nat,
                    spread(height + 2 * EDGE),
                    spread(height),
                    taps,
                    pltpu.VMEM((halves, 49, 1, LANES), F32),
                    pltpu.VMEM((SMALL, channels), F32),
                ],
                1,
                1,
                "kernel_grad",
            )(own, top, bottom, gconv, kernel, hsum, chan)
        received = [exchange(sends[k - 1], tiles, stride, size, k) for k in range(1, size)]
        if not step:
            received, small, grad_part = lax.optimization_barrier((received, small, grad_part))
        elif step == 1:
            received, grad_top, grad_bottom = lax.optimization_barrier((received, grad_top, grad_bottom))
        keep = pieces[0]
        for piece in received:
            keep = keep + piece.astype(F32)
    gathered = keep.astype(BF16)
    for stride, size in digits[1:]:
        payload = jnp.concatenate([gathered, small.astype(BF16)], axis=0)
        if (stride, size) == digits[1]:
            payload, grad_part = lax.optimization_barrier((payload, grad_part))
            input_grad = call(
                input_grad_kernel,
                jax.ShapeDtypeStruct((height, breadth, channels), BF16),
                [nat, spread(2 * EDGE), taps],
                1,
                1,
                "input_grad",
            )(grad_top, grad_bottom, grad_part, kernel, cot)
        received = [payload] + [exchange(payload, tiles, stride, size, k) for k in range(1, size)]
        if (stride, size) == digits[1]:
            received, input_grad = lax.optimization_barrier((received, input_grad))
        gathered = jnp.concatenate([piece[:-SMALL] for piece in received], axis=0)
        small = functools.reduce(jnp.add, [piece[-SMALL:].astype(F32) for piece in received])
    gathered = jnp.concatenate([gathered, small.astype(BF16)], axis=0)
    stride, size = digits[0]
    across = exchange(gathered, tiles, stride, size, 1)
    other = other_core(gathered, draws)
    lon_first = Layout((0, 2, 1, 3))
    out = with_layout_constraint(out[None], lon_first)
    input_grad = with_layout_constraint(input_grad[None], lon_first)
    across, out, input_grad = lax.optimization_barrier((across, out, input_grad))
    other_across = other_core(across, draws)
    factor = float(1.0 / np.sqrt(np.float32(draws * height * tiles * breadth)))
    w_in_sum, w_out_sum, kernel_sum, hidden_sum, chan_sum = call(
        functools.partial(place_kernel, digits, rows, factor),
        (
            jax.ShapeDtypeStruct((channels, hidden_units), F32),
            jax.ShapeDtypeStruct((hidden_units, channels), F32),
            jax.ShapeDtypeStruct((7, 7, channels), F32),
            jax.ShapeDtypeStruct((hidden_units // LANES, LANES), F32),
            jax.ShapeDtypeStruct((5, channels), F32),
        ),
        [pltpu.VMEM((2, rows, channels), F32)],
        mega,
        4 * mega,
        "place",
        16 * mega,
    )(place, gathered, across, other, other_across)
    return (
        out,
        input_grad,
        kernel_sum,
        w_in_sum,
        w_out_sum,
        hidden_sum.reshape(-1),
        chan_sum,
    )


def solution(mesh):
    placed = (
        P(("group", "draw"), "tile", None, None),
        P("tile", None),
        P(),
        P(),
        P(),
        P(),
        P(),
        P(),
        P(),
        P(),
        P(),
        P(("group", "draw"), "tile", None, None),
    )
    return jax.shard_map(
        functools.partial(per_device, mesh.shape["tile"], mesh.shape["draw"]),
        mesh=mesh,
        in_specs=placed,
        out_specs=(
            P(("group", "draw"), "tile", None, None),
            P(("group", "draw"), "tile", None, None),
            P("group", None, None),
            P("group", None),
            P("group", None),
            P("group"),
            P("group", None),
        ),
        check_vma=False,
    )
```

```python
import functools

import jax
import jax.numpy as jnp
import numpy as np
from jax import lax
from jax.experimental import pallas as pl
from jax.experimental.layout import Layout, with_layout_constraint
from jax.experimental.pallas import tpu as pltpu
from jax.sharding import PartitionSpec as P

ROOT_TERM = 0.7978845608028654
CUBIC = 0.044715
EPSILON = 1e-06
F32 = jnp.float32
BF16 = jnp.bfloat16
LANES = 128
SUBS = 8
EDGE = 3
SMALL = 64
VMEM_LIMIT = 56 * 1024 * 1024


def dims_of(breadth):
    steps = -(-breadth // SUBS)
    return steps, steps * SUBS


def spread_row(row, nat, spread, slot, halves, breadth):
    steps, cells = dims_of(breadth)
    row = row.astype(F32)
    over = cells - breadth + EDGE
    for h in range(halves):
        part = row[:, h * LANES : (h + 1) * LANES]
        nat[h, SUBS : SUBS + breadth, :] = part
        nat[h, SUBS - EDGE : SUBS, :] = part[breadth - EDGE :]
        nat[h, SUBS + breadth : SUBS + breadth + over, :] = part[:over]
    for h in range(halves):
        for t in range(steps + 2 * EDGE):
            spread[h, slot, t] = nat[h, pl.ds(SUBS - EDGE + t, SUBS, stride=steps), :]


def gather_row(nat, h, breadth):
    return nat[h, SUBS : SUBS + breadth, :]


def fill_taps(kern_ref, taps, halves, flip):
    for i in range(7):
        for j in range(7):
            src = kern_ref[6 - i, 6 - j : 7 - j, :] if flip else kern_ref[i, j : j + 1, :]
            for h in range(halves):
                taps[h, i * 7 + j] = jnp.broadcast_to(src[:, h * LANES : (h + 1) * LANES], (SUBS, LANES))


def conv_run(cells_at, taps, h, row_taps, length, total):
    total = list(total)
    for i, slot in row_taps:
        weights = [taps[h, i * 7 + j] for j in range(7)]
        for u in range(length + 6):
            cell = cells_at(slot, u)
            for j in range(7):
                t = u - j
                if 0 <= t < length:
                    term = cell * weights[j]
                    total[t] = term if total[t] is None else total[t] + term
    return total


def own_taps(p, height):
    return [(i, p + i - EDGE) for i in range(7) if 0 <= p + i - EDGE < height]


def halo_taps(p, height):
    found = []
    for i in range(7):
        row = p + i
        if row < EDGE:
            found.append((i, row))
        elif row >= EDGE + height:
            found.append((i, row - height))
    return found


def runs_of(steps):
    length = steps // 2 if steps % 2 == 0 else steps
    return steps // length, length


def own_conv_rows(spread, taps, kern_ref, part_ref, height, steps, halves, flip):
    fill_taps(kern_ref, taps, halves, flip)
    n_runs, length = runs_of(steps)
    for p in range(height):

        def run_body(index, carry, p=p):
            h = index // n_runs
            start = (index % n_runs) * length
            total = conv_run(
                lambda slot, u: spread[h, slot, start + u], taps, h, own_taps(p, height), length, [None] * length
            )
            for t in range(length):
                part_ref[h, p * steps + start + t] = total[t]
            return carry

        lax.fori_loop(0, halves * n_runs, run_body, 0)


def own_conv_kernel(own_ref, kern_ref, part_ref, nat, spread, taps):
    height, breadth, channels = own_ref.shape
    halves = channels // LANES
    steps, cells = dims_of(breadth)
    def spread_own(p, carry):
        spread_row(own_ref[p], nat, spread, p, halves, breadth)
        return carry

    lax.fori_loop(0, height, spread_own, 0)
    own_conv_rows(spread, taps, kern_ref, part_ref, height, steps, halves, False)


def main_kernel(
    place_ref, own_ref, top_ref, bottom_ref, part_ref, cot_ref, mask_ref, kern_ref, cbias_ref, gain_ref, nbias_ref, w_in_ref,
    b_in_ref, w_out_ref, b_out_ref, scale_ref,
    out_ref, gconv_ref, keep_ref, send_ref, hsum_ref, chan_ref,
    nat, out_s, spread, taps, conv, units, cots, state_s, mixed_s, gnorm_s, ocean_s, inv_s, normed_s, act_s, gmix_s, ghid_s,
):
    height, breadth, channels = own_ref.shape
    hidden_units = w_in_ref.shape[1]
    halves = channels // LANES
    steps, cells = dims_of(breadth)

    fill_taps(kern_ref, taps, halves, False)
    for r in range(EDGE):
        spread_row(top_ref[r], nat, spread, r, halves, breadth)
        spread_row(bottom_ref[r], nat, spread, EDGE + r, halves, breadth)
    n_runs, length = runs_of(steps)
    for p in range(height):

        def conv_body(index, carry, p=p):
            h = index // n_runs
            start = (index % n_runs) * length
            base = p * steps + start
            total = conv_run(
                lambda slot, u: spread[h, slot, start + u],
                taps,
                h,
                halo_taps(p, height),
                length,
                [part_ref[h, base + t] for t in range(length)],
            )
            for t in range(length):
                conv[h, pl.ds(pl.multiple_of((base + t) * SUBS, SUBS), SUBS), :] = total[t]
            return carry

        lax.fori_loop(0, halves * n_runs, conv_body, 0)

    hsum_ref[...] = jnp.zeros_like(hsum_ref)
    chan_ref[...] = jnp.zeros_like(chan_ref)
    width = 256
    inv_c = 1.0 / channels
    sides = range(halves)
    lanes = [slice(h * LANES, (h + 1) * LANES) for h in sides]

    def column_sum(values):
        return jnp.sum(values.reshape(values.shape[0] // SUBS, SUBS, values.shape[1]), axis=0)

    def mean_of(parts):
        return jnp.sum(functools.reduce(jnp.add, parts), axis=1, keepdims=True) * inv_c

    pack = 2 if height % 2 == 0 else 1

    def row_body(pp, carry):
        base2 = pl.multiple_of(pp * (pack * cells), 16)
        rows = pl.ds(base2, pack * cells)
        for q in range(pack):
            p = pp * pack + q
            base = pl.multiple_of(base2 + q * cells, 16)
            cot = cot_ref[p].astype(F32)
            for h in sides:
                nat[h, SUBS : SUBS + breadth, :] = cot[:, lanes[h]]
                out_s[h, SUBS : SUBS + breadth, :] = own_ref[p, :, lanes[h]].astype(F32)
            land = mask_ref[p]
            for t in range(0, steps, 2):
                here = pl.ds(base + t * SUBS, 2 * SUBS)
                local = slice(q * cells + t * SUBS, q * cells + (t + 2) * SUBS)
                values = [conv[h, here, :] + cbias_ref[:, lanes[h]] for h in sides]
                center = mean_of(values)
                deviation = [v - center for v in values]
                inv_std = lax.rsqrt(mean_of([d * d for d in deviation]) + EPSILON)
                inv_s[local, :] = jnp.broadcast_to(inv_std, (2 * SUBS, LANES))
                ocean = jnp.concatenate([jnp.broadcast_to(land[:, t + k : t + k + 1], (SUBS, LANES)) for k in range(2)], axis=0)
                ocean_s[local, :] = ocean
                for h in sides:
                    unit = deviation[h] * inv_std
                    units[local, lanes[h]] = unit
                    normed_s[here, lanes[h]] = (unit * gain_ref[:, lanes[h]] + nbias_ref[:, lanes[h]]).astype(BF16)
                    cell = jnp.concatenate(
                        [nat[h, pl.ds(SUBS + t + k, SUBS, stride=steps), :] for k in range(2)], axis=0
                    )
                    upstream = jnp.where(ocean > 0, cell, 0.0)
                    cots[local, lanes[h]] = upstream
                    state_s[local, lanes[h]] = jnp.concatenate(
                        [out_s[h, pl.ds(SUBS + t + k, SUBS, stride=steps), :] for k in range(2)], axis=0
                    )
                    gmix_s[here, lanes[h]] = (scale_ref[:, lanes[h]] * upstream).astype(BF16)
        normed = normed_s[rows, :]
        gmix = gmix_s[rows, :]
        for c in range(0, hidden_units, width):
            cols = slice(c, c + width)
            hidden = jnp.dot(normed, w_in_ref[:, cols], preferred_element_type=F32) + b_in_ref[:, cols]
            grad_act = lax.dot_general(
                gmix, w_out_ref[cols, :], (((1,), (1,)), ((), ())), preferred_element_type=F32
            )
            square = hidden * hidden
            inner = hidden * (ROOT_TERM * CUBIC * square + ROOT_TERM)
            half_tanh = 0.5 * jnp.tanh(inner)
            gate = 0.5 + half_tanh
            active = hidden * gate
            slope = gate + active * (0.5 - half_tanh) * (6.0 * CUBIC * ROOT_TERM * square + 2.0 * ROOT_TERM)
            act = active.astype(BF16)
            act_s[rows, cols] = act
            mixed = jnp.dot(act, w_out_ref[cols, :], preferred_element_type=F32)
            ghid = (grad_act * slope).astype(BF16)
            ghid_s[rows, cols] = ghid
            hsum_ref[:, cols] += column_sum(ghid.astype(F32))
            grad_normed = lax.dot_general(
                ghid, w_in_ref[:, cols], (((1,), (1,)), ((), ())), preferred_element_type=F32
            )
            if c:
                mixed_s[...] += mixed
                gnorm_s[...] += grad_normed
            else:
                mixed_s[...] = mixed
                gnorm_s[...] = grad_normed
        for q in range(pack):
            p = pp * pack + q
            base = pl.multiple_of(base2 + q * cells, 16)
            sums = [[None] * halves for _ in range(5)]

            def add_to(n, h, values):
                folded = values[:SUBS] + values[SUBS:]
                sums[n][h] = folded if sums[n][h] is None else sums[n][h] + folded

            for t in range(0, steps, 2):
                here = pl.ds(base + t * SUBS, 2 * SUBS)
                local = slice(q * cells + t * SUBS, q * cells + (t + 2) * SUBS)
                ocean = ocean_s[local, :]
                scaled, products, units_here = [], [], []
                for h in sides:
                    mixed = mixed_s[local, lanes[h]] + b_out_ref[:, lanes[h]]
                    add_to(4, h, cots[local, lanes[h]] * mixed)
                    residual = jnp.where(ocean > 0, scale_ref[:, lanes[h]] * mixed, 0.0)
                    result = state_s[local, lanes[h]] + residual
                    for k in range(2):
                        out_s[h, pl.ds(SUBS + t + k, SUBS, stride=steps), :] = result[k * SUBS : (k + 1) * SUBS]
                    grad_normed = gnorm_s[local, lanes[h]]
                    unit = units[local, lanes[h]]
                    add_to(1, h, grad_normed * unit)
                    add_to(2, h, grad_normed)
                    add_to(3, h, gmix_s[here, lanes[h]].astype(F32))
                    scaled.append(grad_normed * gain_ref[:, lanes[h]])
                    units_here.append(unit)
                    products.append(scaled[h] * unit)
                mean_scaled = mean_of(scaled)
                mean_product = mean_of(products)
                inv_std = inv_s[local, :]
                for h in sides:
                    grad_conv = (inv_std * (scaled[h] - mean_scaled - units_here[h] * mean_product)).astype(BF16).astype(F32)
                    add_to(0, h, grad_conv)
                    for k in range(2):
                        nat[h, pl.ds(SUBS + t + k, SUBS, stride=steps), :] = grad_conv[k * SUBS : (k + 1) * SUBS]
            for n in range(5):
                for h in sides:
                    chan_ref[n, :, lanes[h]] += sums[n][h]
            for h in sides:
                out_ref[p, :, lanes[h]] = gather_row(out_s, h, breadth).astype(BF16)
                gconv_ref[p, :, lanes[h]] = gather_row(nat, h, breadth).astype(BF16)
        return carry

    lax.fori_loop(0, height // pack, row_body, 0)

    first = (((0,), (0,)), ((), ()))

    def store_block(half, c, block):
        @pl.when(place_ref[0] == half)
        def _():
            keep_ref[c : c + width, :] = block

        @pl.when(place_ref[0] != half)
        def _():
            send_ref[c : c + width, :] = block.astype(BF16)

    w_in_grad = lax.dot_general(normed_s[...], ghid_s[...], first, preferred_element_type=F32)
    for c in range(0, hidden_units, width):
        store_block(0, c, w_in_grad[:, c : c + width])
    w_out_grad = lax.dot_general(act_s[...], gmix_s[...], first, preferred_element_type=F32)
    for c in range(0, hidden_units, width):
        store_block(1, c, w_out_grad[c : c + width])


def grads_kernel(
    own_ref, top_ref, bottom_ref, gconv_ref, kern_ref, hsum_ref, chan_ref, small_ref, part_ref,
    nat, spread, grads, taps, sums, total,
):
    height, breadth, channels = own_ref.shape
    halves = channels // LANES
    steps, cells = dims_of(breadth)
    for r in range(EDGE):
        spread_row(top_ref[r], nat, spread, r, halves, breadth)
        spread_row(bottom_ref[r], nat, spread, EDGE + height + r, halves, breadth)

    def spread_own(p, carry):
        spread_row(own_ref[p], nat, spread, EDGE + p, halves, breadth)
        spread_row(gconv_ref[p], nat, grads, p, halves, breadth)
        return carry

    lax.fori_loop(0, height, spread_own, 0)
    own_conv_rows(grads, taps, kern_ref, part_ref, height, steps, halves, True)
    sublane = lax.broadcasted_iota(jnp.int32, (SUBS, LANES), 0)

    def grad_at(h, p, t):
        grad = grads[h, p, EDGE + t]
        for s in range(SUBS):
            if s * steps + t >= breadth:
                grad = jnp.where(sublane == s, 0.0, grad)
        return grad

    def tap_body(i, carry):
        total = [[None] * 7 for _ in range(halves)]
        for p in range(height):
            window = [[spread[h, p + i, t] for t in range(6)] for h in range(halves)]
            for t in range(steps):
                for h in range(halves):
                    window[h].append(spread[h, p + i, t + 6])
                    grad = grad_at(h, p, t)
                    for j in range(7):
                        term = window[h][t + j] * grad
                        total[h][j] = term if total[h][j] is None else total[h][j] + term
        for h in range(halves):
            for j in range(7):
                sums[h, i * 7 + j] = jnp.sum(total[h][j], axis=0, keepdims=True)
        return carry

    lax.fori_loop(0, 7, tap_body, 0)
    total[...] = jnp.zeros_like(total)
    for h in range(halves):
        total[0:49, h * LANES : (h + 1) * LANES] = sums[h].reshape(49, LANES)
    rows = hsum_ref.shape[1] // channels
    at = 49
    for c in range(rows):
        total[at + c : at + c + 1, :] = jnp.sum(hsum_ref[:, c * channels : (c + 1) * channels], axis=0, keepdims=True)
    at += rows
    for c in range(5):
        total[at + c : at + c + 1, :] = jnp.sum(chan_ref[c], axis=0, keepdims=True)
    small_ref[...] = total[...]


def input_grad_kernel(top_ref, bottom_ref, part_ref, kern_ref, cot_ref, grad_ref, nat, spread, taps):
    height, breadth, channels = cot_ref.shape
    halves = channels // LANES
    steps, cells = dims_of(breadth)
    fill_taps(kern_ref, taps, halves, True)
    for r in range(EDGE):
        spread_row(top_ref[r], nat, spread, r, halves, breadth)
        spread_row(bottom_ref[r], nat, spread, EDGE + r, halves, breadth)
    n_runs, length = runs_of(steps)
    for p in range(height):

        def run_body(index, carry, p=p):
            h = index // n_runs
            start = (index % n_runs) * length
            base = p * steps + start
            total = conv_run(
                lambda slot, u: spread[h, slot, start + u],
                taps,
                h,
                halo_taps(p, height),
                length,
                [part_ref[h, base + t] for t in range(length)],
            )
            for t in range(length):
                nat[h, pl.ds(SUBS + start + t, SUBS, stride=steps), :] = total[t]
            return carry

        lax.fori_loop(0, halves * n_runs, run_body, 0)
        for h in range(halves):
            lanes = slice(h * LANES, (h + 1) * LANES)
            grad_ref[p, :, lanes] = (cot_ref[p, :, lanes].astype(F32) + gather_row(nat, h, breadth)).astype(BF16)


def call(kernel, out_shape, scratch, flops, nbytes, name, limit=VMEM_LIMIT):
    def run(*operands):
        whole = pl.BlockSpec(memory_space=pltpu.VMEM)
        scalars = pl.BlockSpec(memory_space=pltpu.SMEM)
        return pl.pallas_call(
            kernel,
            out_shape=out_shape,
            in_specs=[scalars if x.dtype == jnp.int32 else whole for x in operands],
            out_specs=jax.tree.map(lambda _: whole, out_shape),
            scratch_shapes=scratch,
            compiler_params=pltpu.CompilerParams(vmem_limit_bytes=limit),
            cost_estimate=pl.CostEstimate(flops=flops, bytes_accessed=nbytes, transcendentals=0),
            name=name,
        )(*operands)

    return run


def place_kernel(digits, rows, factor, place_ref, here_ref, across_ref, other_ref, other_across_ref, *rest):
    w_in_ref, w_out_ref, kernel_ref, hidden_ref, chan_ref, total = rest
    channels = here_ref.shape[1]
    order = [[]]
    for stride, size in digits[1:]:
        order = [tail + [k] for k in range(size) for tail in order]
    share = (here_ref.shape[0] - SMALL) // len(order)
    draw = place_ref[0]
    small = jnp.zeros((SMALL, channels), F32)
    for flip, refs in ((0, (here_ref, across_ref)), (1, (other_ref, other_across_ref))):
        for last, ref in enumerate(refs):
            values = ref[...].astype(F32)
            small = small + values[-SMALL:]
            for n, ks in enumerate(order):
                extent = rows
                start = 0
                for d in scatter_order(digits):
                    extent = extent // digits[d][1]
                    k = ks[d - 1] if d else last
                    start = start + (place_ref[1 + d] ^ k) * extent
                start = pl.multiple_of(start, SUBS)
                total[draw ^ flip, pl.ds(start, share), :] = values[n * share : (n + 1) * share]
    big = w_out_ref.shape[0]
    for c in range(big // channels):
        cols = slice(c * channels, (c + 1) * channels)
        w_in_ref[:, cols] = total[0, cols, :] * factor
    w_out_ref[...] = total[1, 0:big, :] * factor
    small = small * factor
    for i in range(7):
        kernel_ref[i] = small[i * 7 : i * 7 + 7]
    blocks = big // channels
    halves = channels // LANES
    for c in range(blocks):
        for h in range(halves):
            hidden_ref[c * halves + h : c * halves + h + 1, :] = small[49 + c : 50 + c, h * LANES : (h + 1) * LANES]
    chan_ref[...] = small[49 + blocks : 54 + blocks]


def digits_of(count):
    digits = []
    stride = 2
    while stride < count:
        size = min(4, count // stride)
        digits.append((stride, size))
        stride *= size
    return [(1, 2)] + digits[::-1]


def scatter_order(digits):
    return [*range(1, len(digits)), 0]


def exchange(values, count, stride, size, k):
    pairs = []
    for i in range(count):
        digit = i // stride % size
        pairs.append((i, i + ((digit ^ k) - digit) * stride))
    return lax.ppermute(values, "tile", pairs)


def other_core(values, draws):
    return lax.ppermute(values, "draw", [(i, i ^ 1) for i in range(draws)])


def halo(cells, tiles):
    after = [(i, i + 1) for i in range(tiles - 1)]
    before = [(i + 1, i) for i in range(tiles - 1)]
    top = lax.ppermute(cells[-EDGE:], "tile", after)
    bottom = lax.ppermute(cells[:EDGE], "tile", before)
    return top, bottom


def per_device(
    tiles,
    draws,
    inputs,
    land_mask,
    kernel,
    conv_bias,
    norm_gain,
    norm_bias,
    w_in,
    b_in,
    w_out,
    b_out,
    layer_scale,
    cotangent,
):
    _, height, breadth, channels = inputs.shape
    hidden_units = w_in.shape[1]
    halves = channels // LANES
    steps, cells = dims_of(breadth)
    own = inputs[0]
    cot = cotangent[0]
    top, bottom = halo(own, tiles)
    mask = jnp.pad(land_mask.astype(F32), ((0, 0), (0, cells - breadth)))
    mask = mask.reshape(height, SUBS, steps)

    def row(vector):
        return vector.reshape(1, -1)

    nat = pltpu.VMEM((halves, cells + 2 * SUBS, LANES), F32)

    def spread(slots):
        return pltpu.VMEM((halves, slots, steps + 2 * EDGE, SUBS, LANES), F32)

    taps = pltpu.VMEM((halves, 49, SUBS, LANES), F32)
    big_row = pltpu.VMEM((2 * cells, channels), F32)
    narrow = pltpu.VMEM((2 * cells, LANES), F32)
    count = height * cells
    big = hidden_units
    digits = digits_of(tiles)
    unit = tiles * SUBS
    rows = -(-big // unit) * unit
    tile = lax.axis_index("tile")
    place = jnp.stack([lax.axis_index("draw")] + [tile // stride % size for stride, size in digits]).astype(jnp.int32)
    part_shape = jax.ShapeDtypeStruct((halves, height * steps, SUBS, LANES), F32)
    mega = 1024 * 1024

    part = call(own_conv_kernel, part_shape, [nat, spread(height), taps], 1, 1, "own_conv")(own, kernel)
    out, gconv, keep, send, hsum, chan = call(
        main_kernel,
        (
            jax.ShapeDtypeStruct((height, breadth, channels), BF16),
            jax.ShapeDtypeStruct((height, breadth, channels), BF16),
            jax.ShapeDtypeStruct((big, channels), F32),
            jax.ShapeDtypeStruct((big, channels), BF16),
            jax.ShapeDtypeStruct((SUBS, hidden_units), F32),
            jax.ShapeDtypeStruct((5, SUBS, channels), F32),
        ),
        [
            nat,
            nat,
            spread(2 * EDGE),
            taps,
            pltpu.VMEM((halves, count, LANES), F32),
            big_row,
            big_row,
            big_row,
            big_row,
            big_row,
            narrow,
            narrow,
            pltpu.VMEM((count, channels), BF16),
            pltpu.VMEM((count, hidden_units), BF16),
            pltpu.VMEM((count, channels), BF16),
            pltpu.VMEM((count, hidden_units), BF16),
        ],
        12 * count * channels * hidden_units,
        8 * mega,
        "block_main",
    )(
        place, own, top, bottom, part, cot, mask, kernel, row(conv_bias), row(norm_gain), row(norm_bias), w_in, row(b_in),
        w_out, row(b_out), row(layer_scale),
    )
    got = other_core(send, draws)

    if rows > big:
        keep = jnp.pad(keep, ((0, rows - big), (0, 0)))
        got = jnp.pad(got, ((0, rows - big), (0, 0)))
    for step, digit in enumerate(scatter_order(digits)):
        stride, size = digits[digit]
        share = keep.shape[0] // size
        mine = place[1 + digit]
        pieces = []
        for k in range(size):
            piece = lax.dynamic_slice_in_dim(keep, (mine ^ k) * share, share, 0)
            if not step:
                piece = piece + lax.dynamic_slice_in_dim(got, (mine ^ k) * share, share, 0).astype(F32)
            pieces.append(piece)
        sends = [piece.astype(BF16) for piece in pieces[1:]]
        if not step:
            sends, gconv, hsum = lax.optimization_barrier((sends, gconv, hsum))
            grad_top, grad_bottom = halo(gconv, tiles)
            small, grad_part = call(
                grads_kernel,
                (jax.ShapeDtypeStruct((SMALL, channels), F32), part_shape),
                [
                    nat,
                    spread(height + 2 * EDGE),
                    spread(height),
                    taps,
                    pltpu.VMEM((halves, 49, 1, LANES), F32),
                    pltpu.VMEM((SMALL, channels), F32),
                ],
                1,
                1,
                "kernel_grad",
            )(own, top, bottom, gconv, kernel, hsum, chan)
        received = [exchange(sends[k - 1], tiles, stride, size, k) for k in range(1, size)]
        if not step:
            received, small, grad_part = lax.optimization_barrier((received, small, grad_part))
        elif step == len(digits) - 1:
            received, grad_top, grad_bottom = lax.optimization_barrier((received, grad_top, grad_bottom))
        keep = pieces[0]
        for piece in received:
            keep = keep + piece.astype(F32)
    gathered = keep.astype(BF16)
    for stride, size in digits[1:]:
        payload = jnp.concatenate([gathered, small.astype(BF16)], axis=0)
        if (stride, size) == digits[1]:
            payload, grad_part = lax.optimization_barrier((payload, grad_part))
            input_grad = call(
                input_grad_kernel,
                jax.ShapeDtypeStruct((height, breadth, channels), BF16),
                [nat, spread(2 * EDGE), taps],
                1,
                1,
                "input_grad",
            )(grad_top, grad_bottom, grad_part, kernel, cot)
        received = [payload] + [exchange(payload, tiles, stride, size, k) for k in range(1, size)]
        if (stride, size) == digits[1]:
            received, input_grad = lax.optimization_barrier((received, input_grad))
        gathered = jnp.concatenate([piece[:-SMALL] for piece in received], axis=0)
        small = functools.reduce(jnp.add, [piece[-SMALL:].astype(F32) for piece in received])
    gathered = jnp.concatenate([gathered, small.astype(BF16)], axis=0)
    stride, size = digits[0]
    across = exchange(gathered, tiles, stride, size, 1)
    other = other_core(gathered, draws)
    lon_first = Layout((0, 2, 1, 3))
    out = with_layout_constraint(out[None], lon_first)
    input_grad = with_layout_constraint(input_grad[None], lon_first)
    across, out, input_grad = lax.optimization_barrier((across, out, input_grad))
    other_across = other_core(across, draws)
    factor = float(1.0 / np.sqrt(np.float32(draws * height * tiles * breadth)))
    w_in_sum, w_out_sum, kernel_sum, hidden_sum, chan_sum = call(
        functools.partial(place_kernel, digits, rows, factor),
        (
            jax.ShapeDtypeStruct((channels, hidden_units), F32),
            jax.ShapeDtypeStruct((hidden_units, channels), F32),
            jax.ShapeDtypeStruct((7, 7, channels), F32),
            jax.ShapeDtypeStruct((hidden_units // LANES, LANES), F32),
            jax.ShapeDtypeStruct((5, channels), F32),
        ),
        [pltpu.VMEM((2, rows, channels), F32)],
        mega,
        4 * mega,
        "place",
        16 * mega,
    )(place, gathered, across, other, other_across)
    return (
        out,
        input_grad,
        kernel_sum,
        w_in_sum,
        w_out_sum,
        hidden_sum.reshape(-1),
        chan_sum,
    )


def solution(mesh):
    placed = (
        P(("group", "draw"), "tile", None, None),
        P("tile", None),
        P(),
        P(),
        P(),
        P(),
        P(),
        P(),
        P(),
        P(),
        P(),
        P(("group", "draw"), "tile", None, None),
    )
    return jax.shard_map(
        functools.partial(per_device, mesh.shape["tile"], mesh.shape["draw"]),
        mesh=mesh,
        in_specs=placed,
        out_specs=(
            P(("group", "draw"), "tile", None, None),
            P(("group", "draw"), "tile", None, None),
            P("group", None, None),
            P("group", None),
            P("group", None),
            P("group"),
            P("group", None),
        ),
        check_vma=False,
    )
```

```python
import functools

import jax
import jax.numpy as jnp
import numpy as np
from jax import lax
from jax.experimental import pallas as pl
from jax.experimental.layout import Layout, with_layout_constraint
from jax.experimental.pallas import tpu as pltpu
from jax.sharding import PartitionSpec as P

ROOT_TERM = 0.7978845608028654
CUBIC = 0.044715
EPSILON = 1e-06
F32 = jnp.float32
BF16 = jnp.bfloat16
LANES = 128
SUBS = 8
EDGE = 3
SMALL = 64
VMEM_LIMIT = 56 * 1024 * 1024


def dims_of(breadth):
    steps = -(-breadth // SUBS)
    return steps, steps * SUBS


def spread_row(row, nat, spread, slot, halves, breadth):
    steps, cells = dims_of(breadth)
    row = row.astype(F32)
    over = cells - breadth + EDGE
    for h in range(halves):
        part = row[:, h * LANES : (h + 1) * LANES]
        nat[h, SUBS : SUBS + breadth, :] = part
        nat[h, SUBS - EDGE : SUBS, :] = part[breadth - EDGE :]
        nat[h, SUBS + breadth : SUBS + breadth + over, :] = part[:over]
    for h in range(halves):
        for t in range(steps + 2 * EDGE):
            spread[h, slot, t] = nat[h, pl.ds(SUBS - EDGE + t, SUBS, stride=steps), :]


def gather_row(nat, h, breadth):
    return nat[h, SUBS : SUBS + breadth, :]


def fill_taps(kern_ref, taps, halves, flip):
    for i in range(7):
        for j in range(7):
            src = kern_ref[6 - i, 6 - j : 7 - j, :] if flip else kern_ref[i, j : j + 1, :]
            for h in range(halves):
                taps[h, i * 7 + j] = jnp.broadcast_to(src[:, h * LANES : (h + 1) * LANES], (SUBS, LANES))


def conv_run(cells_at, taps, h, row_taps, length, total):
    total = list(total)
    for i, slot in row_taps:
        weights = [taps[h, i * 7 + j] for j in range(7)]
        for u in range(length + 6):
            cell = cells_at(slot, u)
            for j in range(7):
                t = u - j
                if 0 <= t < length:
                    term = cell * weights[j]
                    total[t] = term if total[t] is None else total[t] + term
    return total


def own_taps(p, height):
    return [(i, p + i - EDGE) for i in range(7) if 0 <= p + i - EDGE < height]


def halo_taps(p, height):
    found = []
    for i in range(7):
        row = p + i
        if row < EDGE:
            found.append((i, row))
        elif row >= EDGE + height:
            found.append((i, row - height))
    return found


def runs_of(steps):
    length = steps // 2 if steps % 2 == 0 else steps
    return steps // length, length


def own_conv_rows(spread, taps, kern_ref, part_ref, height, steps, halves, flip):
    fill_taps(kern_ref, taps, halves, flip)
    n_runs, length = runs_of(steps)
    for p in range(height):

        def run_body(index, carry, p=p):
            h = index // n_runs
            start = (index % n_runs) * length
            total = conv_run(
                lambda slot, u: spread[h, slot, start + u], taps, h, own_taps(p, height), length, [None] * length
            )
            for t in range(length):
                part_ref[h, p * steps + start + t] = total[t]
            return carry

        lax.fori_loop(0, halves * n_runs, run_body, 0)


def own_conv_kernel(own_ref, kern_ref, part_ref, nat, spread, taps):
    height, breadth, channels = own_ref.shape
    halves = channels // LANES
    steps, cells = dims_of(breadth)
    def spread_own(p, carry):
        spread_row(own_ref[p], nat, spread, p, halves, breadth)
        return carry

    lax.fori_loop(0, height, spread_own, 0)
    own_conv_rows(spread, taps, kern_ref, part_ref, height, steps, halves, False)


def main_kernel(
    place_ref, own_ref, top_ref, bottom_ref, part_ref, cot_ref, mask_ref, kern_ref, cbias_ref, gain_ref, nbias_ref, w_in_ref,
    b_in_ref, w_out_ref, b_out_ref, scale_ref,
    out_ref, gconv_ref, head_ref, tail_ref, keep_ref, send_ref, hsum_ref, chan_ref,
    nat, out_s, spread, taps, conv, units, cots, state_s, mixed_s, gnorm_s, ocean_s, inv_s, normed_s, act_s, gmix_s, ghid_s,
):
    height, breadth, channels = own_ref.shape
    hidden_units = w_in_ref.shape[1]
    halves = channels // LANES
    steps, cells = dims_of(breadth)

    fill_taps(kern_ref, taps, halves, False)
    for r in range(EDGE):
        spread_row(top_ref[r], nat, spread, r, halves, breadth)
        spread_row(bottom_ref[r], nat, spread, EDGE + r, halves, breadth)
    n_runs, length = runs_of(steps)
    for p in range(height):

        def conv_body(index, carry, p=p):
            h = index // n_runs
            start = (index % n_runs) * length
            base = p * steps + start
            total = conv_run(
                lambda slot, u: spread[h, slot, start + u],
                taps,
                h,
                halo_taps(p, height),
                length,
                [part_ref[h, base + t] for t in range(length)],
            )
            for t in range(length):
                conv[h, pl.ds(pl.multiple_of((base + t) * SUBS, SUBS), SUBS), :] = total[t]
            return carry

        lax.fori_loop(0, halves * n_runs, conv_body, 0)

    hsum_ref[...] = jnp.zeros_like(hsum_ref)
    chan_ref[...] = jnp.zeros_like(chan_ref)
    width = 256
    inv_c = 1.0 / channels
    sides = range(halves)
    lanes = [slice(h * LANES, (h + 1) * LANES) for h in sides]

    def column_sum(values):
        return jnp.sum(values.reshape(values.shape[0] // SUBS, SUBS, values.shape[1]), axis=0)

    def mean_of(parts):
        return jnp.sum(functools.reduce(jnp.add, parts), axis=1, keepdims=True) * inv_c

    pack = 2 if height % 2 == 0 else 1

    def row_body(pp, carry):
        base2 = pl.multiple_of(pp * (pack * cells), 16)
        rows = pl.ds(base2, pack * cells)
        for q in range(pack):
            p = pp * pack + q
            base = pl.multiple_of(base2 + q * cells, 16)
            cot = cot_ref[p].astype(F32)
            for h in sides:
                nat[h, SUBS : SUBS + breadth, :] = cot[:, lanes[h]]
                out_s[h, SUBS : SUBS + breadth, :] = own_ref[p, :, lanes[h]].astype(F32)
            land = mask_ref[p]
            for t in range(0, steps, 2):
                here = pl.ds(base + t * SUBS, 2 * SUBS)
                local = slice(q * cells + t * SUBS, q * cells + (t + 2) * SUBS)
                values = [conv[h, here, :] + cbias_ref[:, lanes[h]] for h in sides]
                center = mean_of(values)
                deviation = [v - center for v in values]
                inv_std = lax.rsqrt(mean_of([d * d for d in deviation]) + EPSILON)
                inv_s[local, :] = jnp.broadcast_to(inv_std, (2 * SUBS, LANES))
                ocean = jnp.concatenate([jnp.broadcast_to(land[:, t + k : t + k + 1], (SUBS, LANES)) for k in range(2)], axis=0)
                ocean_s[local, :] = ocean
                for h in sides:
                    unit = deviation[h] * inv_std
                    units[local, lanes[h]] = unit
                    normed_s[here, lanes[h]] = (unit * gain_ref[:, lanes[h]] + nbias_ref[:, lanes[h]]).astype(BF16)
                    cell = jnp.concatenate(
                        [nat[h, pl.ds(SUBS + t + k, SUBS, stride=steps), :] for k in range(2)], axis=0
                    )
                    upstream = jnp.where(ocean > 0, cell, 0.0)
                    cots[local, lanes[h]] = upstream
                    state_s[local, lanes[h]] = jnp.concatenate(
                        [out_s[h, pl.ds(SUBS + t + k, SUBS, stride=steps), :] for k in range(2)], axis=0
                    )
                    gmix_s[here, lanes[h]] = (scale_ref[:, lanes[h]] * upstream).astype(BF16)
        normed = normed_s[rows, :]
        gmix = gmix_s[rows, :]
        for c in range(0, hidden_units, width):
            cols = slice(c, c + width)
            hidden = jnp.dot(normed, w_in_ref[:, cols], preferred_element_type=F32) + b_in_ref[:, cols]
            grad_act = lax.dot_general(
                gmix, w_out_ref[cols, :], (((1,), (1,)), ((), ())), preferred_element_type=F32
            )
            square = hidden * hidden
            inner = hidden * (ROOT_TERM * CUBIC * square + ROOT_TERM)
            half_tanh = 0.5 * jnp.tanh(inner)
            gate = 0.5 + half_tanh
            active = hidden * gate
            slope = gate + active * (0.5 - half_tanh) * (6.0 * CUBIC * ROOT_TERM * square + 2.0 * ROOT_TERM)
            act = active.astype(BF16)
            act_s[rows, cols] = act
            mixed = jnp.dot(act, w_out_ref[cols, :], preferred_element_type=F32)
            ghid = (grad_act * slope).astype(BF16)
            ghid_s[rows, cols] = ghid
            hsum_ref[:, cols] += column_sum(ghid.astype(F32))
            grad_normed = lax.dot_general(
                ghid, w_in_ref[:, cols], (((1,), (1,)), ((), ())), preferred_element_type=F32
            )
            if c:
                mixed_s[...] += mixed
                gnorm_s[...] += grad_normed
            else:
                mixed_s[...] = mixed
                gnorm_s[...] = grad_normed
        for q in range(pack):
            p = pp * pack + q
            base = pl.multiple_of(base2 + q * cells, 16)
            sums = [[None] * halves for _ in range(5)]

            def add_to(n, h, values):
                folded = values[:SUBS] + values[SUBS:]
                sums[n][h] = folded if sums[n][h] is None else sums[n][h] + folded

            for t in range(0, steps, 2):
                here = pl.ds(base + t * SUBS, 2 * SUBS)
                local = slice(q * cells + t * SUBS, q * cells + (t + 2) * SUBS)
                ocean = ocean_s[local, :]
                scaled, products, units_here = [], [], []
                for h in sides:
                    mixed = mixed_s[local, lanes[h]] + b_out_ref[:, lanes[h]]
                    add_to(4, h, cots[local, lanes[h]] * mixed)
                    residual = jnp.where(ocean > 0, scale_ref[:, lanes[h]] * mixed, 0.0)
                    result = state_s[local, lanes[h]] + residual
                    for k in range(2):
                        out_s[h, pl.ds(SUBS + t + k, SUBS, stride=steps), :] = result[k * SUBS : (k + 1) * SUBS]
                    grad_normed = gnorm_s[local, lanes[h]]
                    unit = units[local, lanes[h]]
                    add_to(1, h, grad_normed * unit)
                    add_to(2, h, grad_normed)
                    add_to(3, h, gmix_s[here, lanes[h]].astype(F32))
                    scaled.append(grad_normed * gain_ref[:, lanes[h]])
                    units_here.append(unit)
                    products.append(scaled[h] * unit)
                mean_scaled = mean_of(scaled)
                mean_product = mean_of(products)
                inv_std = inv_s[local, :]
                for h in sides:
                    grad_conv = (inv_std * (scaled[h] - mean_scaled - units_here[h] * mean_product)).astype(BF16).astype(F32)
                    add_to(0, h, grad_conv)
                    for k in range(2):
                        nat[h, pl.ds(SUBS + t + k, SUBS, stride=steps), :] = grad_conv[k * SUBS : (k + 1) * SUBS]
            for n in range(5):
                for h in sides:
                    chan_ref[n, :, lanes[h]] += sums[n][h]
            for h in sides:
                out_ref[p, :, lanes[h]] = gather_row(out_s, h, breadth).astype(BF16)
                gradient = gather_row(nat, h, breadth).astype(BF16)
                gconv_ref[p, :, lanes[h]] = gradient

                @pl.when(p < EDGE)
                def _(h=h, p=p, gradient=gradient):
                    head_ref[p, :, lanes[h]] = gradient

                @pl.when(p >= height - EDGE)
                def _(h=h, p=p, gradient=gradient):
                    tail_ref[p - (height - EDGE), :, lanes[h]] = gradient

        return carry

    lax.fori_loop(0, height // pack, row_body, 0)

    first = (((0,), (0,)), ((), ()))

    def store_block(half, c, block):
        @pl.when(place_ref[0] == half)
        def _():
            keep_ref[c : c + width, :] = block

        @pl.when(place_ref[0] != half)
        def _():
            send_ref[c : c + width, :] = block.astype(BF16)

    w_in_grad = lax.dot_general(normed_s[...], ghid_s[...], first, preferred_element_type=F32)
    for c in range(0, hidden_units, width):
        store_block(0, c, w_in_grad[:, c : c + width])
    w_out_grad = lax.dot_general(act_s[...], gmix_s[...], first, preferred_element_type=F32)
    for c in range(0, hidden_units, width):
        store_block(1, c, w_out_grad[c : c + width])


def grads_kernel(
    own_ref, top_ref, bottom_ref, gconv_ref, kern_ref, hsum_ref, chan_ref, small_ref, part_ref,
    nat, spread, grads, taps, sums, total,
):
    height, breadth, channels = own_ref.shape
    halves = channels // LANES
    steps, cells = dims_of(breadth)
    for r in range(EDGE):
        spread_row(top_ref[r], nat, spread, r, halves, breadth)
        spread_row(bottom_ref[r], nat, spread, EDGE + height + r, halves, breadth)

    def spread_own(p, carry):
        spread_row(own_ref[p], nat, spread, EDGE + p, halves, breadth)
        spread_row(gconv_ref[p], nat, grads, p, halves, breadth)
        return carry

    lax.fori_loop(0, height, spread_own, 0)
    own_conv_rows(grads, taps, kern_ref, part_ref, height, steps, halves, True)
    sublane = lax.broadcasted_iota(jnp.int32, (SUBS, LANES), 0)

    def grad_at(h, p, t):
        grad = grads[h, p, EDGE + t]
        for s in range(SUBS):
            if s * steps + t >= breadth:
                grad = jnp.where(sublane == s, 0.0, grad)
        return grad

    def tap_body(i, carry):
        total = [[None] * 7 for _ in range(halves)]
        for p in range(height):
            window = [[spread[h, p + i, t] for t in range(6)] for h in range(halves)]
            for t in range(steps):
                for h in range(halves):
                    window[h].append(spread[h, p + i, t + 6])
                    grad = grad_at(h, p, t)
                    for j in range(7):
                        term = window[h][t + j] * grad
                        total[h][j] = term if total[h][j] is None else total[h][j] + term
        for h in range(halves):
            for j in range(7):
                sums[h, i * 7 + j] = jnp.sum(total[h][j], axis=0, keepdims=True)
        return carry

    lax.fori_loop(0, 7, tap_body, 0)
    total[...] = jnp.zeros_like(total)
    for h in range(halves):
        total[0:49, h * LANES : (h + 1) * LANES] = sums[h].reshape(49, LANES)
    rows = hsum_ref.shape[1] // channels
    at = 49
    for c in range(rows):
        total[at + c : at + c + 1, :] = jnp.sum(hsum_ref[:, c * channels : (c + 1) * channels], axis=0, keepdims=True)
    at += rows
    for c in range(5):
        total[at + c : at + c + 1, :] = jnp.sum(chan_ref[c], axis=0, keepdims=True)
    small_ref[...] = total[...]


def input_grad_kernel(top_ref, bottom_ref, part_ref, kern_ref, cot_ref, grad_ref, nat, spread, taps):
    height, breadth, channels = cot_ref.shape
    halves = channels // LANES
    steps, cells = dims_of(breadth)
    fill_taps(kern_ref, taps, halves, True)
    for r in range(EDGE):
        spread_row(top_ref[r], nat, spread, r, halves, breadth)
        spread_row(bottom_ref[r], nat, spread, EDGE + r, halves, breadth)
    n_runs, length = runs_of(steps)
    for p in range(height):

        def run_body(index, carry, p=p):
            h = index // n_runs
            start = (index % n_runs) * length
            base = p * steps + start
            total = conv_run(
                lambda slot, u: spread[h, slot, start + u],
                taps,
                h,
                halo_taps(p, height),
                length,
                [part_ref[h, base + t] for t in range(length)],
            )
            for t in range(length):
                nat[h, pl.ds(SUBS + start + t, SUBS, stride=steps), :] = total[t]
            return carry

        lax.fori_loop(0, halves * n_runs, run_body, 0)
        for h in range(halves):
            lanes = slice(h * LANES, (h + 1) * LANES)
            grad_ref[p, :, lanes] = (cot_ref[p, :, lanes].astype(F32) + gather_row(nat, h, breadth)).astype(BF16)


def call(kernel, out_shape, scratch, flops, nbytes, name, limit=VMEM_LIMIT):
    def run(*operands):
        whole = pl.BlockSpec(memory_space=pltpu.VMEM)
        scalars = pl.BlockSpec(memory_space=pltpu.SMEM)
        return pl.pallas_call(
            kernel,
            out_shape=out_shape,
            in_specs=[scalars if x.dtype == jnp.int32 else whole for x in operands],
            out_specs=jax.tree.map(lambda _: whole, out_shape),
            scratch_shapes=scratch,
            compiler_params=pltpu.CompilerParams(vmem_limit_bytes=limit),
            cost_estimate=pl.CostEstimate(flops=flops, bytes_accessed=nbytes, transcendentals=0),
            name=name,
        )(*operands)

    return run


def place_kernel(digits, rows, factor, place_ref, here_ref, across_ref, other_ref, other_across_ref, *rest):
    w_in_ref, w_out_ref, kernel_ref, hidden_ref, chan_ref, total = rest
    channels = here_ref.shape[1]
    order = [[]]
    for stride, size in digits[1:]:
        order = [tail + [k] for k in range(size) for tail in order]
    share = (here_ref.shape[0] - SMALL) // len(order)
    draw = place_ref[0]
    small = jnp.zeros((SMALL, channels), F32)
    for flip, refs in ((0, (here_ref, across_ref)), (1, (other_ref, other_across_ref))):
        for last, ref in enumerate(refs):
            values = ref[...].astype(F32)
            small = small + values[-SMALL:]
            for n, ks in enumerate(order):
                extent = rows
                start = 0
                for d in scatter_order(digits):
                    extent = extent // digits[d][1]
                    k = ks[d - 1] if d else last
                    start = start + (place_ref[1 + d] ^ k) * extent
                start = pl.multiple_of(start, SUBS)
                total[draw ^ flip, pl.ds(start, share), :] = values[n * share : (n + 1) * share]
    big = w_out_ref.shape[0]
    for c in range(big // channels):
        cols = slice(c * channels, (c + 1) * channels)
        w_in_ref[:, cols] = total[0, cols, :] * factor
    w_out_ref[...] = total[1, 0:big, :] * factor
    small = small * factor
    for i in range(7):
        kernel_ref[i] = small[i * 7 : i * 7 + 7]
    blocks = big // channels
    halves = channels // LANES
    for c in range(blocks):
        for h in range(halves):
            hidden_ref[c * halves + h : c * halves + h + 1, :] = small[49 + c : 50 + c, h * LANES : (h + 1) * LANES]
    chan_ref[...] = small[49 + blocks : 54 + blocks]


def digits_of(count):
    digits = []
    stride = 2
    while stride < count:
        size = min(4, count // stride)
        digits.append((stride, size))
        stride *= size
    return [(1, 2)] + digits[::-1]


def scatter_order(digits):
    return [*range(1, len(digits)), 0]


def exchange(values, count, stride, size, k):
    pairs = []
    for i in range(count):
        digit = i // stride % size
        pairs.append((i, i + ((digit ^ k) - digit) * stride))
    return lax.ppermute(values, "tile", pairs)


def other_core(values, draws):
    return lax.ppermute(values, "draw", [(i, i ^ 1) for i in range(draws)])


def halo(head, tail, tiles):
    after = [(i, i + 1) for i in range(tiles - 1)]
    before = [(i + 1, i) for i in range(tiles - 1)]
    return lax.ppermute(tail, "tile", after), lax.ppermute(head, "tile", before)


def per_device(
    tiles,
    draws,
    inputs,
    land_mask,
    kernel,
    conv_bias,
    norm_gain,
    norm_bias,
    w_in,
    b_in,
    w_out,
    b_out,
    layer_scale,
    cotangent,
):
    _, height, breadth, channels = inputs.shape
    hidden_units = w_in.shape[1]
    halves = channels // LANES
    steps, cells = dims_of(breadth)
    own = inputs[0]
    cot = cotangent[0]
    top, bottom = halo(own[:EDGE], own[-EDGE:], tiles)
    mask = jnp.pad(land_mask.astype(F32), ((0, 0), (0, cells - breadth)))
    mask = mask.reshape(height, SUBS, steps)

    def row(vector):
        return vector.reshape(1, -1)

    nat = pltpu.VMEM((halves, cells + 2 * SUBS, LANES), F32)

    def spread(slots):
        return pltpu.VMEM((halves, slots, steps + 2 * EDGE, SUBS, LANES), F32)

    taps = pltpu.VMEM((halves, 49, SUBS, LANES), F32)
    big_row = pltpu.VMEM((2 * cells, channels), F32)
    narrow = pltpu.VMEM((2 * cells, LANES), F32)
    count = height * cells
    big = hidden_units
    digits = digits_of(tiles)
    unit = tiles * SUBS
    rows = -(-big // unit) * unit
    tile = lax.axis_index("tile")
    place = jnp.stack([lax.axis_index("draw")] + [tile // stride % size for stride, size in digits]).astype(jnp.int32)
    part_shape = jax.ShapeDtypeStruct((halves, height * steps, SUBS, LANES), F32)
    mega = 1024 * 1024

    part = call(own_conv_kernel, part_shape, [nat, spread(height), taps], 1, 1, "own_conv")(own, kernel)
    edge_shape = jax.ShapeDtypeStruct((EDGE, breadth, channels), BF16)
    out, gconv, head, tail, keep, send, hsum, chan = call(
        main_kernel,
        (
            jax.ShapeDtypeStruct((height, breadth, channels), BF16),
            jax.ShapeDtypeStruct((height, breadth, channels), BF16),
            edge_shape,
            edge_shape,
            jax.ShapeDtypeStruct((big, channels), F32),
            jax.ShapeDtypeStruct((big, channels), BF16),
            jax.ShapeDtypeStruct((SUBS, hidden_units), F32),
            jax.ShapeDtypeStruct((5, SUBS, channels), F32),
        ),
        [
            nat,
            nat,
            spread(2 * EDGE),
            taps,
            pltpu.VMEM((halves, count, LANES), F32),
            big_row,
            big_row,
            big_row,
            big_row,
            big_row,
            narrow,
            narrow,
            pltpu.VMEM((count, channels), BF16),
            pltpu.VMEM((count, hidden_units), BF16),
            pltpu.VMEM((count, channels), BF16),
            pltpu.VMEM((count, hidden_units), BF16),
        ],
        12 * count * channels * hidden_units,
        8 * mega,
        "block_main",
    )(
        place, own, top, bottom, part, cot, mask, kernel, row(conv_bias), row(norm_gain), row(norm_bias), w_in, row(b_in),
        w_out, row(b_out), row(layer_scale),
    )
    got = other_core(send, draws)
    grad_top, grad_bottom = halo(head, tail, tiles)

    if rows > big:
        keep = jnp.pad(keep, ((0, rows - big), (0, 0)))
        got = jnp.pad(got, ((0, rows - big), (0, 0)))
    for step, digit in enumerate(scatter_order(digits)):
        stride, size = digits[digit]
        share = keep.shape[0] // size
        mine = place[1 + digit]
        pieces = []
        for k in range(size):
            piece = lax.dynamic_slice_in_dim(keep, (mine ^ k) * share, share, 0)
            if not step:
                piece = piece + lax.dynamic_slice_in_dim(got, (mine ^ k) * share, share, 0).astype(F32)
            pieces.append(piece)
        sends = [piece.astype(BF16) for piece in pieces[1:]]
        if not step:
            sends, hsum = lax.optimization_barrier((sends, hsum))
            small, grad_part = call(
                grads_kernel,
                (jax.ShapeDtypeStruct((SMALL, channels), F32), part_shape),
                [
                    nat,
                    spread(height + 2 * EDGE),
                    spread(height),
                    taps,
                    pltpu.VMEM((halves, 49, 1, LANES), F32),
                    pltpu.VMEM((SMALL, channels), F32),
                ],
                1,
                1,
                "kernel_grad",
            )(own, top, bottom, gconv, kernel, hsum, chan)
        received = [exchange(sends[k - 1], tiles, stride, size, k) for k in range(1, size)]
        if not step:
            received, small, grad_part, grad_top, grad_bottom = lax.optimization_barrier(
                (received, small, grad_part, grad_top, grad_bottom)
            )
        keep = pieces[0]
        for piece in received:
            keep = keep + piece.astype(F32)
    gathered = keep.astype(BF16)
    for stride, size in digits[1:]:
        payload = jnp.concatenate([gathered, small.astype(BF16)], axis=0)
        if (stride, size) == digits[1]:
            payload, grad_part = lax.optimization_barrier((payload, grad_part))
            input_grad = call(
                input_grad_kernel,
                jax.ShapeDtypeStruct((height, breadth, channels), BF16),
                [nat, spread(2 * EDGE), taps],
                1,
                1,
                "input_grad",
            )(grad_top, grad_bottom, grad_part, kernel, cot)
        received = [payload] + [exchange(payload, tiles, stride, size, k) for k in range(1, size)]
        if (stride, size) == digits[1]:
            received, input_grad = lax.optimization_barrier((received, input_grad))
        gathered = jnp.concatenate([piece[:-SMALL] for piece in received], axis=0)
        small = functools.reduce(jnp.add, [piece[-SMALL:].astype(F32) for piece in received])
    gathered = jnp.concatenate([gathered, small.astype(BF16)], axis=0)
    stride, size = digits[0]
    across = exchange(gathered, tiles, stride, size, 1)
    other = other_core(gathered, draws)
    lon_first = Layout((0, 2, 1, 3))
    out = with_layout_constraint(out[None], lon_first)
    input_grad = with_layout_constraint(input_grad[None], lon_first)
    across, out, input_grad = lax.optimization_barrier((across, out, input_grad))
    other_across = other_core(across, draws)
    factor = float(1.0 / np.sqrt(np.float32(draws * height * tiles * breadth)))
    w_in_sum, w_out_sum, kernel_sum, hidden_sum, chan_sum = call(
        functools.partial(place_kernel, digits, rows, factor),
        (
            jax.ShapeDtypeStruct((channels, hidden_units), F32),
            jax.ShapeDtypeStruct((hidden_units, channels), F32),
            jax.ShapeDtypeStruct((7, 7, channels), F32),
            jax.ShapeDtypeStruct((hidden_units // LANES, LANES), F32),
            jax.ShapeDtypeStruct((5, channels), F32),
        ),
        [pltpu.VMEM((2, rows, channels), F32)],
        mega,
        4 * mega,
        "place",
        16 * mega,
    )(place, gathered, across, other, other_across)
    return (
        out,
        input_grad,
        kernel_sum,
        w_in_sum,
        w_out_sum,
        hidden_sum.reshape(-1),
        chan_sum,
    )


def solution(mesh):
    placed = (
        P(("group", "draw"), "tile", None, None),
        P("tile", None),
        P(),
        P(),
        P(),
        P(),
        P(),
        P(),
        P(),
        P(),
        P(),
        P(("group", "draw"), "tile", None, None),
    )
    return jax.shard_map(
        functools.partial(per_device, mesh.shape["tile"], mesh.shape["draw"]),
        mesh=mesh,
        in_specs=placed,
        out_specs=(
            P(("group", "draw"), "tile", None, None),
            P(("group", "draw"), "tile", None, None),
            P("group", None, None),
            P("group", None),
            P("group", None),
            P("group"),
            P("group", None),
        ),
        check_vma=False,
    )
```

```python
import functools

import jax
import jax.numpy as jnp
import numpy as np
from jax import lax
from jax.experimental import pallas as pl
from jax.experimental.layout import Layout, with_layout_constraint
from jax.experimental.pallas import tpu as pltpu
from jax.sharding import PartitionSpec as P

ROOT_TERM = 0.7978845608028654
CUBIC = 0.044715
EPSILON = 1e-06
F32 = jnp.float32
BF16 = jnp.bfloat16
LANES = 128
SUBS = 8
EDGE = 3
SMALL = 64
VMEM_LIMIT = 56 * 1024 * 1024


def dims_of(breadth):
    steps = -(-breadth // SUBS)
    return steps, steps * SUBS


def spread_row(row, nat, spread, slot, halves, breadth):
    steps, cells = dims_of(breadth)
    row = row.astype(F32)
    over = cells - breadth + EDGE
    for h in range(halves):
        part = row[:, h * LANES : (h + 1) * LANES]
        nat[h, SUBS : SUBS + breadth, :] = part
        nat[h, SUBS - EDGE : SUBS, :] = part[breadth - EDGE :]
        nat[h, SUBS + breadth : SUBS + breadth + over, :] = part[:over]
    for h in range(halves):
        for t in range(steps + 2 * EDGE):
            spread[h, slot, t] = nat[h, pl.ds(SUBS - EDGE + t, SUBS, stride=steps), :]


def gather_row(nat, h, breadth):
    return nat[h, SUBS : SUBS + breadth, :]


def fill_taps(kern_ref, taps, halves, flip):
    for i in range(7):
        for j in range(7):
            src = kern_ref[6 - i, 6 - j : 7 - j, :] if flip else kern_ref[i, j : j + 1, :]
            for h in range(halves):
                taps[h, i * 7 + j] = jnp.broadcast_to(src[:, h * LANES : (h + 1) * LANES], (SUBS, LANES))


def conv_run(cells_at, taps, h, row_taps, length, total):
    total = list(total)
    for i, slot in row_taps:
        weights = [taps[h, i * 7 + j] for j in range(7)]
        for u in range(length + 6):
            cell = cells_at(slot, u)
            for j in range(7):
                t = u - j
                if 0 <= t < length:
                    term = cell * weights[j]
                    total[t] = term if total[t] is None else total[t] + term
    return total


def own_taps(p, height):
    return [(i, p + i - EDGE) for i in range(7) if 0 <= p + i - EDGE < height]


def halo_taps(p, height):
    found = []
    for i in range(7):
        row = p + i
        if row < EDGE:
            found.append((i, row))
        elif row >= EDGE + height:
            found.append((i, row - height))
    return found


def runs_of(steps):
    length = steps // 2 if steps % 2 == 0 else steps
    return steps // length, length


def own_conv_rows(spread, taps, kern_ref, part_ref, height, steps, halves, flip):
    fill_taps(kern_ref, taps, halves, flip)
    n_runs, length = runs_of(steps)
    for p in range(height):

        def run_body(index, carry, p=p):
            h = index // n_runs
            start = (index % n_runs) * length
            total = conv_run(
                lambda slot, u: spread[h, slot, start + u], taps, h, own_taps(p, height), length, [None] * length
            )
            for t in range(length):
                part_ref[h, p * steps + start + t] = total[t]
            return carry

        lax.fori_loop(0, halves * n_runs, run_body, 0)


def own_conv_kernel(own_ref, kern_ref, part_ref, nat, spread, taps):
    height, breadth, channels = own_ref.shape
    halves = channels // LANES
    steps, cells = dims_of(breadth)
    def spread_own(p, carry):
        spread_row(own_ref[p], nat, spread, p, halves, breadth)
        return carry

    lax.fori_loop(0, height, spread_own, 0)
    own_conv_rows(spread, taps, kern_ref, part_ref, height, steps, halves, False)


def main_kernel(
    place_ref, own_ref, top_ref, bottom_ref, part_ref, cot_ref, mask_ref, kern_ref, cbias_ref, gain_ref, nbias_ref, w_in_ref,
    b_in_ref, w_out_ref, b_out_ref, scale_ref,
    out_ref, gconv_ref, head_ref, tail_ref, keep_ref, send_ref, hsum_ref, chan_ref,
    nat, out_s, spread, taps, conv, units, cots, state_s, mixed_s, gnorm_s, ocean_s, inv_s, normed_s, act_s, gmix_s, ghid_s,
):
    height, breadth, channels = own_ref.shape
    hidden_units = w_in_ref.shape[1]
    halves = channels // LANES
    steps, cells = dims_of(breadth)

    fill_taps(kern_ref, taps, halves, False)
    for r in range(EDGE):
        spread_row(top_ref[r], nat, spread, r, halves, breadth)
        spread_row(bottom_ref[r], nat, spread, EDGE + r, halves, breadth)
    n_runs, length = runs_of(steps)
    for p in range(height):

        def conv_body(index, carry, p=p):
            h = index // n_runs
            start = (index % n_runs) * length
            base = p * steps + start
            total = conv_run(
                lambda slot, u: spread[h, slot, start + u],
                taps,
                h,
                halo_taps(p, height),
                length,
                [part_ref[h, base + t] for t in range(length)],
            )
            for t in range(length):
                conv[h, pl.ds(pl.multiple_of((base + t) * SUBS, SUBS), SUBS), :] = total[t]
            return carry

        lax.fori_loop(0, halves * n_runs, conv_body, 0)

    hsum_ref[...] = jnp.zeros_like(hsum_ref)
    chan_ref[...] = jnp.zeros_like(chan_ref)
    width = 256
    inv_c = 1.0 / channels
    sides = range(halves)
    lanes = [slice(h * LANES, (h + 1) * LANES) for h in sides]

    def column_sum(values):
        return jnp.sum(values.reshape(values.shape[0] // SUBS, SUBS, values.shape[1]), axis=0)

    def mean_of(parts):
        return jnp.sum(functools.reduce(jnp.add, parts), axis=1, keepdims=True) * inv_c

    pack = 2 if height % 2 == 0 else 1

    def row_body(pp, carry):
        base2 = pl.multiple_of(pp * (pack * cells), 16)
        rows = pl.ds(base2, pack * cells)
        for q in range(pack):
            p = pp * pack + q
            base = pl.multiple_of(base2 + q * cells, 16)
            cot = cot_ref[p].astype(F32)
            for h in sides:
                nat[h, SUBS : SUBS + breadth, :] = cot[:, lanes[h]]
                out_s[h, SUBS : SUBS + breadth, :] = own_ref[p, :, lanes[h]].astype(F32)
            land = mask_ref[p]
            for t in range(0, steps, 2):
                here = pl.ds(base + t * SUBS, 2 * SUBS)
                local = slice(q * cells + t * SUBS, q * cells + (t + 2) * SUBS)
                values = [conv[h, here, :] + cbias_ref[:, lanes[h]] for h in sides]
                center = mean_of(values)
                deviation = [v - center for v in values]
                inv_std = lax.rsqrt(mean_of([d * d for d in deviation]) + EPSILON)
                inv_s[local, :] = jnp.broadcast_to(inv_std, (2 * SUBS, LANES))
                ocean = jnp.concatenate([jnp.broadcast_to(land[:, t + k : t + k + 1], (SUBS, LANES)) for k in range(2)], axis=0)
                ocean_s[local, :] = ocean
                for h in sides:
                    unit = deviation[h] * inv_std
                    units[local, lanes[h]] = unit
                    normed_s[here, lanes[h]] = (unit * gain_ref[:, lanes[h]] + nbias_ref[:, lanes[h]]).astype(BF16)
                    cell = jnp.concatenate(
                        [nat[h, pl.ds(SUBS + t + k, SUBS, stride=steps), :] for k in range(2)], axis=0
                    )
                    upstream = jnp.where(ocean > 0, cell, 0.0)
                    cots[local, lanes[h]] = upstream
                    state_s[local, lanes[h]] = jnp.concatenate(
                        [out_s[h, pl.ds(SUBS + t + k, SUBS, stride=steps), :] for k in range(2)], axis=0
                    )
                    gmix_s[here, lanes[h]] = (scale_ref[:, lanes[h]] * upstream).astype(BF16)
        normed = normed_s[rows, :]
        gmix = gmix_s[rows, :]
        for c in range(0, hidden_units, width):
            cols = slice(c, c + width)
            hidden = jnp.dot(normed, w_in_ref[:, cols], preferred_element_type=F32) + b_in_ref[:, cols]
            grad_act = lax.dot_general(
                gmix, w_out_ref[cols, :], (((1,), (1,)), ((), ())), preferred_element_type=F32
            )
            square = hidden * hidden
            inner = hidden * (ROOT_TERM * CUBIC * square + ROOT_TERM)
            half_tanh = 0.5 * jnp.tanh(inner)
            gate = 0.5 + half_tanh
            active = hidden * gate
            slope = gate + active * (0.5 - half_tanh) * (6.0 * CUBIC * ROOT_TERM * square + 2.0 * ROOT_TERM)
            act = active.astype(BF16)
            act_s[rows, cols] = act
            mixed = jnp.dot(act, w_out_ref[cols, :], preferred_element_type=F32)
            ghid = (grad_act * slope).astype(BF16)
            ghid_s[rows, cols] = ghid
            hsum_ref[:, cols] += column_sum(ghid.astype(F32))
            grad_normed = lax.dot_general(
                ghid, w_in_ref[:, cols], (((1,), (1,)), ((), ())), preferred_element_type=F32
            )
            if c:
                mixed_s[...] += mixed
                gnorm_s[...] += grad_normed
            else:
                mixed_s[...] = mixed
                gnorm_s[...] = grad_normed
        for q in range(pack):
            p = pp * pack + q
            base = pl.multiple_of(base2 + q * cells, 16)
            sums = [[None] * halves for _ in range(5)]

            def add_to(n, h, values):
                folded = values[:SUBS] + values[SUBS:]
                sums[n][h] = folded if sums[n][h] is None else sums[n][h] + folded

            for t in range(0, steps, 2):
                here = pl.ds(base + t * SUBS, 2 * SUBS)
                local = slice(q * cells + t * SUBS, q * cells + (t + 2) * SUBS)
                ocean = ocean_s[local, :]
                scaled, products, units_here = [], [], []
                for h in sides:
                    mixed = mixed_s[local, lanes[h]] + b_out_ref[:, lanes[h]]
                    add_to(4, h, cots[local, lanes[h]] * mixed)
                    residual = jnp.where(ocean > 0, scale_ref[:, lanes[h]] * mixed, 0.0)
                    result = state_s[local, lanes[h]] + residual
                    for k in range(2):
                        out_s[h, pl.ds(SUBS + t + k, SUBS, stride=steps), :] = result[k * SUBS : (k + 1) * SUBS]
                    grad_normed = gnorm_s[local, lanes[h]]
                    unit = units[local, lanes[h]]
                    add_to(1, h, grad_normed * unit)
                    add_to(2, h, grad_normed)
                    add_to(3, h, gmix_s[here, lanes[h]].astype(F32))
                    scaled.append(grad_normed * gain_ref[:, lanes[h]])
                    units_here.append(unit)
                    products.append(scaled[h] * unit)
                mean_scaled = mean_of(scaled)
                mean_product = mean_of(products)
                inv_std = inv_s[local, :]
                for h in sides:
                    grad_conv = (inv_std * (scaled[h] - mean_scaled - units_here[h] * mean_product)).astype(BF16).astype(F32)
                    add_to(0, h, grad_conv)
                    for k in range(2):
                        nat[h, pl.ds(SUBS + t + k, SUBS, stride=steps), :] = grad_conv[k * SUBS : (k + 1) * SUBS]
            for n in range(5):
                for h in sides:
                    chan_ref[n, :, lanes[h]] += sums[n][h]
            for h in sides:
                out_ref[p, :, lanes[h]] = gather_row(out_s, h, breadth).astype(BF16)
                gradient = gather_row(nat, h, breadth).astype(BF16)
                gconv_ref[p, :, lanes[h]] = gradient

                @pl.when(p < EDGE)
                def _(h=h, p=p, gradient=gradient):
                    head_ref[p, :, lanes[h]] = gradient

                @pl.when(p >= height - EDGE)
                def _(h=h, p=p, gradient=gradient):
                    tail_ref[p - (height - EDGE), :, lanes[h]] = gradient

        return carry

    lax.fori_loop(0, height // pack, row_body, 0)

    first = (((0,), (0,)), ((), ()))

    def store_block(half, c, block):
        @pl.when(place_ref[0] == half)
        def _():
            keep_ref[c : c + width, :] = block

        @pl.when(place_ref[0] != half)
        def _():
            send_ref[c : c + width, :] = block.astype(BF16)

    w_in_grad = lax.dot_general(normed_s[...], ghid_s[...], first, preferred_element_type=F32)
    for c in range(0, hidden_units, width):
        store_block(0, c, w_in_grad[:, c : c + width])
    w_out_grad = lax.dot_general(act_s[...], gmix_s[...], first, preferred_element_type=F32)
    for c in range(0, hidden_units, width):
        store_block(1, c, w_out_grad[c : c + width])


def grads_kernel(
    own_ref, top_ref, bottom_ref, gconv_ref, kern_ref, hsum_ref, chan_ref, small_ref, part_ref,
    nat, spread, grads, taps, sums, total,
):
    height, breadth, channels = own_ref.shape
    halves = channels // LANES
    steps, cells = dims_of(breadth)
    for r in range(EDGE):
        spread_row(top_ref[r], nat, spread, r, halves, breadth)
        spread_row(bottom_ref[r], nat, spread, EDGE + height + r, halves, breadth)

    def spread_own(p, carry):
        spread_row(own_ref[p], nat, spread, EDGE + p, halves, breadth)
        spread_row(gconv_ref[p], nat, grads, p, halves, breadth)
        return carry

    lax.fori_loop(0, height, spread_own, 0)
    own_conv_rows(grads, taps, kern_ref, part_ref, height, steps, halves, True)
    sublane = lax.broadcasted_iota(jnp.int32, (SUBS, LANES), 0)

    def grad_at(h, p, t):
        grad = grads[h, p, EDGE + t]
        for s in range(SUBS):
            if s * steps + t >= breadth:
                grad = jnp.where(sublane == s, 0.0, grad)
        return grad

    def tap_body(i, carry):
        total = [[None] * 7 for _ in range(halves)]
        for p in range(height):
            window = [[spread[h, p + i, t] for t in range(6)] for h in range(halves)]
            for t in range(steps):
                for h in range(halves):
                    window[h].append(spread[h, p + i, t + 6])
                    grad = grad_at(h, p, t)
                    for j in range(7):
                        term = window[h][t + j] * grad
                        total[h][j] = term if total[h][j] is None else total[h][j] + term
        for h in range(halves):
            for j in range(7):
                sums[h, i * 7 + j] = jnp.sum(total[h][j], axis=0, keepdims=True)
        return carry

    lax.fori_loop(0, 7, tap_body, 0)
    total[...] = jnp.zeros_like(total)
    for h in range(halves):
        total[0:49, h * LANES : (h + 1) * LANES] = sums[h].reshape(49, LANES)
    rows = hsum_ref.shape[1] // channels
    at = 49
    for c in range(rows):
        total[at + c : at + c + 1, :] = jnp.sum(hsum_ref[:, c * channels : (c + 1) * channels], axis=0, keepdims=True)
    at += rows
    for c in range(5):
        total[at + c : at + c + 1, :] = jnp.sum(chan_ref[c], axis=0, keepdims=True)
    small_ref[...] = total[...]


def input_grad_kernel(top_ref, bottom_ref, part_ref, kern_ref, cot_ref, grad_ref, nat, spread, taps):
    height, breadth, channels = cot_ref.shape
    halves = channels // LANES
    steps, cells = dims_of(breadth)
    fill_taps(kern_ref, taps, halves, True)
    for r in range(EDGE):
        spread_row(top_ref[r], nat, spread, r, halves, breadth)
        spread_row(bottom_ref[r], nat, spread, EDGE + r, halves, breadth)
    n_runs, length = runs_of(steps)
    for p in range(height):

        def run_body(index, carry, p=p):
            h = index // n_runs
            start = (index % n_runs) * length
            base = p * steps + start
            total = conv_run(
                lambda slot, u: spread[h, slot, start + u],
                taps,
                h,
                halo_taps(p, height),
                length,
                [part_ref[h, base + t] for t in range(length)],
            )
            for t in range(length):
                nat[h, pl.ds(SUBS + start + t, SUBS, stride=steps), :] = total[t]
            return carry

        lax.fori_loop(0, halves * n_runs, run_body, 0)
        for h in range(halves):
            lanes = slice(h * LANES, (h + 1) * LANES)
            grad_ref[p, :, lanes] = (cot_ref[p, :, lanes].astype(F32) + gather_row(nat, h, breadth)).astype(BF16)


def call(kernel, out_shape, scratch, flops, nbytes, name, limit=VMEM_LIMIT):
    def run(*operands):
        whole = pl.BlockSpec(memory_space=pltpu.VMEM)
        scalars = pl.BlockSpec(memory_space=pltpu.SMEM)
        return pl.pallas_call(
            kernel,
            out_shape=out_shape,
            in_specs=[scalars if x.dtype == jnp.int32 else whole for x in operands],
            out_specs=jax.tree.map(lambda _: whole, out_shape),
            scratch_shapes=scratch,
            compiler_params=pltpu.CompilerParams(vmem_limit_bytes=limit),
            cost_estimate=pl.CostEstimate(flops=flops, bytes_accessed=nbytes, transcendentals=0),
            name=name,
        )(*operands)

    return run


def place_kernel(digits, rows, factor, place_ref, here_ref, across_ref, other_ref, other_across_ref, *rest):
    w_in_ref, w_out_ref, kernel_ref, hidden_ref, chan_ref, total = rest
    channels = here_ref.shape[1]
    order = [[]]
    for stride, size in digits[1:]:
        order = [tail + [k] for k in range(size) for tail in order]
    share = (here_ref.shape[0] - SMALL) // len(order)
    draw = place_ref[0]
    small = jnp.zeros((SMALL, channels), F32)
    for flip, refs in ((0, (here_ref, across_ref)), (1, (other_ref, other_across_ref))):
        for last, ref in enumerate(refs):
            values = ref[...].astype(F32)
            small = small + values[-SMALL:]
            for n, ks in enumerate(order):
                extent = rows
                start = 0
                for d, (stride, size) in enumerate(digits):
                    extent = extent // size
                    k = ks[d - 1] if d else last
                    start = start + (place_ref[1 + d] ^ k) * extent
                start = pl.multiple_of(start, SUBS)
                total[draw ^ flip, pl.ds(start, share), :] = values[n * share : (n + 1) * share]
    big = w_out_ref.shape[0]
    for c in range(big // channels):
        cols = slice(c * channels, (c + 1) * channels)
        w_in_ref[:, cols] = total[0, cols, :] * factor
    w_out_ref[...] = total[1, 0:big, :] * factor
    small = small * factor
    for i in range(7):
        kernel_ref[i] = small[i * 7 : i * 7 + 7]
    blocks = big // channels
    halves = channels // LANES
    for c in range(blocks):
        for h in range(halves):
            hidden_ref[c * halves + h : c * halves + h + 1, :] = small[49 + c : 50 + c, h * LANES : (h + 1) * LANES]
    chan_ref[...] = small[49 + blocks : 54 + blocks]


def digits_of(count):
    digits = []
    stride = 2
    while stride < count:
        size = min(4, count // stride)
        digits.append((stride, size))
        stride *= size
    return [(1, 2)] + digits[::-1]


def exchange(values, count, stride, size, k):
    pairs = []
    for i in range(count):
        digit = i // stride % size
        pairs.append((i, i + ((digit ^ k) - digit) * stride))
    return lax.ppermute(values, "tile", pairs)


def other_core(values, draws):
    return lax.ppermute(values, "draw", [(i, i ^ 1) for i in range(draws)])


def halo(head, tail, tiles):
    after = [(i, i + 1) for i in range(tiles - 1)]
    before = [(i + 1, i) for i in range(tiles - 1)]
    return lax.ppermute(tail, "tile", after), lax.ppermute(head, "tile", before)


def per_device(
    tiles,
    draws,
    inputs,
    land_mask,
    kernel,
    conv_bias,
    norm_gain,
    norm_bias,
    w_in,
    b_in,
    w_out,
    b_out,
    layer_scale,
    cotangent,
):
    _, height, breadth, channels = inputs.shape
    hidden_units = w_in.shape[1]
    halves = channels // LANES
    steps, cells = dims_of(breadth)
    own = inputs[0]
    cot = cotangent[0]
    top, bottom = halo(own[:EDGE], own[-EDGE:], tiles)
    mask = jnp.pad(land_mask.astype(F32), ((0, 0), (0, cells - breadth)))
    mask = mask.reshape(height, SUBS, steps)

    def row(vector):
        return vector.reshape(1, -1)

    nat = pltpu.VMEM((halves, cells + 2 * SUBS, LANES), F32)

    def spread(slots):
        return pltpu.VMEM((halves, slots, steps + 2 * EDGE, SUBS, LANES), F32)

    taps = pltpu.VMEM((halves, 49, SUBS, LANES), F32)
    big_row = pltpu.VMEM((2 * cells, channels), F32)
    narrow = pltpu.VMEM((2 * cells, LANES), F32)
    count = height * cells
    big = hidden_units
    digits = digits_of(tiles)
    unit = tiles * SUBS
    rows = -(-big // unit) * unit
    tile = lax.axis_index("tile")
    place = jnp.stack([lax.axis_index("draw")] + [tile // stride % size for stride, size in digits]).astype(jnp.int32)
    part_shape = jax.ShapeDtypeStruct((halves, height * steps, SUBS, LANES), F32)
    mega = 1024 * 1024

    part = call(own_conv_kernel, part_shape, [nat, spread(height), taps], 1, 1, "own_conv")(own, kernel)
    edge_shape = jax.ShapeDtypeStruct((EDGE, breadth, channels), BF16)
    out, gconv, head, tail, keep, send, hsum, chan = call(
        main_kernel,
        (
            jax.ShapeDtypeStruct((height, breadth, channels), BF16),
            jax.ShapeDtypeStruct((height, breadth, channels), BF16),
            edge_shape,
            edge_shape,
            jax.ShapeDtypeStruct((big, channels), F32),
            jax.ShapeDtypeStruct((big, channels), BF16),
            jax.ShapeDtypeStruct((SUBS, hidden_units), F32),
            jax.ShapeDtypeStruct((5, SUBS, channels), F32),
        ),
        [
            nat,
            nat,
            spread(2 * EDGE),
            taps,
            pltpu.VMEM((halves, count, LANES), F32),
            big_row,
            big_row,
            big_row,
            big_row,
            big_row,
            narrow,
            narrow,
            pltpu.VMEM((count, channels), BF16),
            pltpu.VMEM((count, hidden_units), BF16),
            pltpu.VMEM((count, channels), BF16),
            pltpu.VMEM((count, hidden_units), BF16),
        ],
        12 * count * channels * hidden_units,
        8 * mega,
        "block_main",
    )(
        place, own, top, bottom, part, cot, mask, kernel, row(conv_bias), row(norm_gain), row(norm_bias), w_in, row(b_in),
        w_out, row(b_out), row(layer_scale),
    )
    got = other_core(send, draws)
    grad_top, grad_bottom = halo(head, tail, tiles)

    if rows > big:
        keep = jnp.pad(keep, ((0, rows - big), (0, 0)))
        got = jnp.pad(got, ((0, rows - big), (0, 0)))
    for step, (stride, size) in enumerate(digits):
        share = keep.shape[0] // size
        mine = place[1 + step]
        pieces = []
        for k in range(size):
            piece = lax.dynamic_slice_in_dim(keep, (mine ^ k) * share, share, 0)
            if not step:
                piece = piece + lax.dynamic_slice_in_dim(got, (mine ^ k) * share, share, 0).astype(F32)
            pieces.append(piece)
        sends = [piece.astype(BF16) for piece in pieces[1:]]
        if not step:
            sends, hsum = lax.optimization_barrier((sends, hsum))
            small, grad_part = call(
                grads_kernel,
                (jax.ShapeDtypeStruct((SMALL, channels), F32), part_shape),
                [
                    nat,
                    spread(height + 2 * EDGE),
                    spread(height),
                    taps,
                    pltpu.VMEM((halves, 49, 1, LANES), F32),
                    pltpu.VMEM((SMALL, channels), F32),
                ],
                1,
                1,
                "kernel_grad",
            )(own, top, bottom, gconv, kernel, hsum, chan)
        received = [exchange(sends[k - 1], tiles, stride, size, k) for k in range(1, size)]
        if not step:
            received, small, grad_part, grad_top, grad_bottom = lax.optimization_barrier(
                (received, small, grad_part, grad_top, grad_bottom)
            )
        keep = pieces[0]
        for piece in received:
            keep = keep + piece.astype(F32)
    gathered = keep.astype(BF16)
    for stride, size in digits[1:]:
        payload = jnp.concatenate([gathered, small.astype(BF16)], axis=0)
        if (stride, size) == digits[1]:
            payload, grad_part = lax.optimization_barrier((payload, grad_part))
            input_grad = call(
                input_grad_kernel,
                jax.ShapeDtypeStruct((height, breadth, channels), BF16),
                [nat, spread(2 * EDGE), taps],
                1,
                1,
                "input_grad",
            )(grad_top, grad_bottom, grad_part, kernel, cot)
        received = [payload] + [exchange(payload, tiles, stride, size, k) for k in range(1, size)]
        if (stride, size) == digits[1]:
            received, input_grad = lax.optimization_barrier((received, input_grad))
        gathered = jnp.concatenate([piece[:-SMALL] for piece in received], axis=0)
        small = functools.reduce(jnp.add, [piece[-SMALL:].astype(F32) for piece in received])
    gathered = jnp.concatenate([gathered, small.astype(BF16)], axis=0)
    stride, size = digits[0]
    across = exchange(gathered, tiles, stride, size, 1)
    other = other_core(gathered, draws)
    lon_first = Layout((0, 2, 1, 3))
    out = with_layout_constraint(out[None], lon_first)
    input_grad = with_layout_constraint(input_grad[None], lon_first)
    across, out, input_grad = lax.optimization_barrier((across, out, input_grad))
    other_across = other_core(across, draws)
    factor = float(1.0 / np.sqrt(np.float32(draws * height * tiles * breadth)))
    w_in_sum, w_out_sum, kernel_sum, hidden_sum, chan_sum = call(
        functools.partial(place_kernel, digits, rows, factor),
        (
            jax.ShapeDtypeStruct((channels, hidden_units), F32),
            jax.ShapeDtypeStruct((hidden_units, channels), F32),
            jax.ShapeDtypeStruct((7, 7, channels), F32),
            jax.ShapeDtypeStruct((hidden_units // LANES, LANES), F32),
            jax.ShapeDtypeStruct((5, channels), F32),
        ),
        [pltpu.VMEM((2, rows, channels), F32)],
        mega,
        4 * mega,
        "place",
        16 * mega,
    )(place, gathered, across, other, other_across)
    return (
        out,
        input_grad,
        kernel_sum,
        w_in_sum,
        w_out_sum,
        hidden_sum.reshape(-1),
        chan_sum,
    )


def solution(mesh):
    placed = (
        P(("group", "draw"), "tile", None, None),
        P("tile", None),
        P(),
        P(),
        P(),
        P(),
        P(),
        P(),
        P(),
        P(),
        P(),
        P(("group", "draw"), "tile", None, None),
    )
    return jax.shard_map(
        functools.partial(per_device, mesh.shape["tile"], mesh.shape["draw"]),
        mesh=mesh,
        in_specs=placed,
        out_specs=(
            P(("group", "draw"), "tile", None, None),
            P(("group", "draw"), "tile", None, None),
            P("group", None, None),
            P("group", None),
            P("group", None),
            P("group"),
            P("group", None),
        ),
        check_vma=False,
    )
```

```python
import functools

import jax
import jax.numpy as jnp
import numpy as np
from jax import lax
from jax.experimental import pallas as pl
from jax.experimental.layout import Layout, with_layout_constraint
from jax.experimental.pallas import tpu as pltpu
from jax.sharding import PartitionSpec as P

ROOT_TERM = 0.7978845608028654
CUBIC = 0.044715
EPSILON = 1e-06
F32 = jnp.float32
BF16 = jnp.bfloat16
LANES = 128
SUBS = 8
EDGE = 3
SMALL = 64
VMEM_LIMIT = 56 * 1024 * 1024


def dims_of(breadth):
    steps = -(-breadth // SUBS)
    return steps, steps * SUBS


def spread_row(row, nat, spread, slot, halves, breadth):
    steps, cells = dims_of(breadth)
    row = row.astype(F32)
    over = cells - breadth + EDGE
    for h in range(halves):
        part = row[:, h * LANES : (h + 1) * LANES]
        nat[h, SUBS : SUBS + breadth, :] = part
        nat[h, SUBS - EDGE : SUBS, :] = part[breadth - EDGE :]
        nat[h, SUBS + breadth : SUBS + breadth + over, :] = part[:over]
    for h in range(halves):
        for t in range(steps + 2 * EDGE):
            spread[h, slot, t] = nat[h, pl.ds(SUBS - EDGE + t, SUBS, stride=steps), :]


def gather_row(nat, h, breadth):
    return nat[h, SUBS : SUBS + breadth, :]


def fill_taps(kern_ref, taps, halves, flip):
    for i in range(7):
        for j in range(7):
            src = kern_ref[6 - i, 6 - j : 7 - j, :] if flip else kern_ref[i, j : j + 1, :]
            for h in range(halves):
                taps[h, i * 7 + j] = jnp.broadcast_to(src[:, h * LANES : (h + 1) * LANES], (SUBS, LANES))


def conv_run(cells_at, taps, h, row_taps, length, total):
    total = list(total)
    for i, slot in row_taps:
        weights = [taps[h, i * 7 + j] for j in range(7)]
        for u in range(length + 6):
            cell = cells_at(slot, u)
            for j in range(7):
                t = u - j
                if 0 <= t < length:
                    term = cell * weights[j]
                    total[t] = term if total[t] is None else total[t] + term
    return total


def own_taps(p, height):
    return [(i, p + i - EDGE) for i in range(7) if 0 <= p + i - EDGE < height]


def halo_taps(p, height):
    found = []
    for i in range(7):
        row = p + i
        if row < EDGE:
            found.append((i, row))
        elif row >= EDGE + height:
            found.append((i, row - height))
    return found


def runs_of(steps):
    length = steps // 2 if steps % 2 == 0 else steps
    return steps // length, length


def own_conv_rows(spread, taps, kern_ref, part_ref, height, steps, halves, flip):
    fill_taps(kern_ref, taps, halves, flip)
    n_runs, length = runs_of(steps)
    for p in range(height):

        def run_body(index, carry, p=p):
            h = index // n_runs
            start = (index % n_runs) * length
            total = conv_run(
                lambda slot, u: spread[h, slot, start + u], taps, h, own_taps(p, height), length, [None] * length
            )
            for t in range(length):
                part_ref[h, p * steps + start + t] = total[t]
            return carry

        lax.fori_loop(0, halves * n_runs, run_body, 0)


def own_conv_kernel(own_ref, kern_ref, part_ref, nat, spread, taps):
    height, breadth, channels = own_ref.shape
    halves = channels // LANES
    steps, cells = dims_of(breadth)
    def spread_own(p, carry):
        spread_row(own_ref[p], nat, spread, p, halves, breadth)
        return carry

    lax.fori_loop(0, height, spread_own, 0)
    own_conv_rows(spread, taps, kern_ref, part_ref, height, steps, halves, False)


def main_kernel(
    place_ref, own_ref, top_ref, bottom_ref, part_ref, cot_ref, mask_ref, kern_ref, cbias_ref, gain_ref, nbias_ref, w_in_ref,
    b_in_ref, w_out_ref, b_out_ref, scale_ref,
    out_ref, gconv_ref, keep_ref, send_ref, hsum_ref, chan_ref,
    nat, out_s, spread, taps, conv, units, cots, state_s, mixed_s, gnorm_s, ocean_s, inv_s, normed_s, act_s, gmix_s, ghid_s,
):
    height, breadth, channels = own_ref.shape
    hidden_units = w_in_ref.shape[1]
    halves = channels // LANES
    steps, cells = dims_of(breadth)

    fill_taps(kern_ref, taps, halves, False)
    for r in range(EDGE):
        spread_row(top_ref[r], nat, spread, r, halves, breadth)
        spread_row(bottom_ref[r], nat, spread, EDGE + r, halves, breadth)
    n_runs, length = runs_of(steps)
    for p in range(height):

        def conv_body(index, carry, p=p):
            h = index // n_runs
            start = (index % n_runs) * length
            base = p * steps + start
            total = conv_run(
                lambda slot, u: spread[h, slot, start + u],
                taps,
                h,
                halo_taps(p, height),
                length,
                [part_ref[h, base + t] for t in range(length)],
            )
            for t in range(length):
                conv[h, pl.ds(pl.multiple_of((base + t) * SUBS, SUBS), SUBS), :] = total[t]
            return carry

        lax.fori_loop(0, halves * n_runs, conv_body, 0)

    hsum_ref[...] = jnp.zeros_like(hsum_ref)
    chan_ref[...] = jnp.zeros_like(chan_ref)
    width = 256
    inv_c = 1.0 / channels
    sides = range(halves)
    lanes = [slice(h * LANES, (h + 1) * LANES) for h in sides]

    def column_sum(values):
        return jnp.sum(values.reshape(values.shape[0] // SUBS, SUBS, values.shape[1]), axis=0)

    def mean_of(parts):
        return jnp.sum(functools.reduce(jnp.add, parts), axis=1, keepdims=True) * inv_c

    pack = 2 if height % 2 == 0 else 1

    def row_body(pp, carry):
        base2 = pl.multiple_of(pp * (pack * cells), 16)
        rows = pl.ds(base2, pack * cells)
        for q in range(pack):
            p = pp * pack + q
            base = pl.multiple_of(base2 + q * cells, 16)
            cot = cot_ref[p].astype(F32)
            for h in sides:
                nat[h, SUBS : SUBS + breadth, :] = cot[:, lanes[h]]
                out_s[h, SUBS : SUBS + breadth, :] = own_ref[p, :, lanes[h]].astype(F32)
            land = mask_ref[p]
            for t in range(0, steps, 2):
                here = pl.ds(base + t * SUBS, 2 * SUBS)
                local = slice(q * cells + t * SUBS, q * cells + (t + 2) * SUBS)
                values = [conv[h, here, :] + cbias_ref[:, lanes[h]] for h in sides]
                center = mean_of(values)
                deviation = [v - center for v in values]
                inv_std = lax.rsqrt(mean_of([d * d for d in deviation]) + EPSILON)
                inv_s[local, :] = jnp.broadcast_to(inv_std, (2 * SUBS, LANES))
                ocean = jnp.concatenate([jnp.broadcast_to(land[:, t + k : t + k + 1], (SUBS, LANES)) for k in range(2)], axis=0)
                ocean_s[local, :] = ocean
                for h in sides:
                    unit = deviation[h] * inv_std
                    units[local, lanes[h]] = unit
                    normed_s[here, lanes[h]] = (unit * gain_ref[:, lanes[h]] + nbias_ref[:, lanes[h]]).astype(BF16)
                    cell = jnp.concatenate(
                        [nat[h, pl.ds(SUBS + t + k, SUBS, stride=steps), :] for k in range(2)], axis=0
                    )
                    upstream = jnp.where(ocean > 0, cell, 0.0)
                    cots[local, lanes[h]] = upstream
                    state_s[local, lanes[h]] = jnp.concatenate(
                        [out_s[h, pl.ds(SUBS + t + k, SUBS, stride=steps), :] for k in range(2)], axis=0
                    )
                    gmix_s[here, lanes[h]] = (scale_ref[:, lanes[h]] * upstream).astype(BF16)
        normed = normed_s[rows, :]
        gmix = gmix_s[rows, :]
        for c in range(0, hidden_units, width):
            cols = slice(c, c + width)
            hidden = jnp.dot(normed, w_in_ref[:, cols], preferred_element_type=F32) + b_in_ref[:, cols]
            grad_act = lax.dot_general(
                gmix, w_out_ref[cols, :], (((1,), (1,)), ((), ())), preferred_element_type=F32
            )
            square = hidden * hidden
            inner = hidden * (ROOT_TERM * CUBIC * square + ROOT_TERM)
            half_tanh = 0.5 * jnp.tanh(inner)
            gate = 0.5 + half_tanh
            active = hidden * gate
            slope = gate + active * (0.5 - half_tanh) * (6.0 * CUBIC * ROOT_TERM * square + 2.0 * ROOT_TERM)
            act = active.astype(BF16)
            act_s[rows, cols] = act
            mixed = jnp.dot(act, w_out_ref[cols, :], preferred_element_type=F32)
            ghid = (grad_act * slope).astype(BF16)
            ghid_s[rows, cols] = ghid
            hsum_ref[:, cols] += column_sum(ghid.astype(F32))
            grad_normed = lax.dot_general(
                ghid, w_in_ref[:, cols], (((1,), (1,)), ((), ())), preferred_element_type=F32
            )
            if c:
                mixed_s[...] += mixed
                gnorm_s[...] += grad_normed
            else:
                mixed_s[...] = mixed
                gnorm_s[...] = grad_normed
        for q in range(pack):
            p = pp * pack + q
            base = pl.multiple_of(base2 + q * cells, 16)
            sums = [[None] * halves for _ in range(5)]

            def add_to(n, h, values):
                folded = values[:SUBS] + values[SUBS:]
                sums[n][h] = folded if sums[n][h] is None else sums[n][h] + folded

            for t in range(0, steps, 2):
                here = pl.ds(base + t * SUBS, 2 * SUBS)
                local = slice(q * cells + t * SUBS, q * cells + (t + 2) * SUBS)
                ocean = ocean_s[local, :]
                scaled, products, units_here = [], [], []
                for h in sides:
                    mixed = mixed_s[local, lanes[h]] + b_out_ref[:, lanes[h]]
                    add_to(4, h, cots[local, lanes[h]] * mixed)
                    residual = jnp.where(ocean > 0, scale_ref[:, lanes[h]] * mixed, 0.0)
                    result = state_s[local, lanes[h]] + residual
                    for k in range(2):
                        out_s[h, pl.ds(SUBS + t + k, SUBS, stride=steps), :] = result[k * SUBS : (k + 1) * SUBS]
                    grad_normed = gnorm_s[local, lanes[h]]
                    unit = units[local, lanes[h]]
                    add_to(1, h, grad_normed * unit)
                    add_to(2, h, grad_normed)
                    add_to(3, h, gmix_s[here, lanes[h]].astype(F32))
                    scaled.append(grad_normed * gain_ref[:, lanes[h]])
                    units_here.append(unit)
                    products.append(scaled[h] * unit)
                mean_scaled = mean_of(scaled)
                mean_product = mean_of(products)
                inv_std = inv_s[local, :]
                for h in sides:
                    grad_conv = (inv_std * (scaled[h] - mean_scaled - units_here[h] * mean_product)).astype(BF16).astype(F32)
                    add_to(0, h, grad_conv)
                    for k in range(2):
                        nat[h, pl.ds(SUBS + t + k, SUBS, stride=steps), :] = grad_conv[k * SUBS : (k + 1) * SUBS]
            for n in range(5):
                for h in sides:
                    chan_ref[n, :, lanes[h]] += sums[n][h]
            for h in sides:
                out_ref[p, :, lanes[h]] = gather_row(out_s, h, breadth).astype(BF16)
                gconv_ref[p, :, lanes[h]] = gather_row(nat, h, breadth).astype(BF16)
        return carry

    lax.fori_loop(0, height // pack, row_body, 0)

    first = (((0,), (0,)), ((), ()))

    def store_block(half, c, block):
        @pl.when(place_ref[0] == half)
        def _():
            keep_ref[c : c + width, :] = block

        @pl.when(place_ref[0] != half)
        def _():
            send_ref[c : c + width, :] = block.astype(BF16)

    w_in_grad = lax.dot_general(normed_s[...], ghid_s[...], first, preferred_element_type=F32)
    for c in range(0, hidden_units, width):
        store_block(0, c, w_in_grad[:, c : c + width])
    w_out_grad = lax.dot_general(act_s[...], gmix_s[...], first, preferred_element_type=F32)
    for c in range(0, hidden_units, width):
        store_block(1, c, w_out_grad[c : c + width])


def grads_kernel(
    own_ref, top_ref, bottom_ref, gconv_ref, kern_ref, hsum_ref, chan_ref, small_ref, part_ref,
    nat, spread, grads, taps, sums, total,
):
    height, breadth, channels = own_ref.shape
    halves = channels // LANES
    steps, cells = dims_of(breadth)
    for r in range(EDGE):
        spread_row(top_ref[r], nat, spread, r, halves, breadth)
        spread_row(bottom_ref[r], nat, spread, EDGE + height + r, halves, breadth)

    def spread_own(p, carry):
        spread_row(own_ref[p], nat, spread, EDGE + p, halves, breadth)
        spread_row(gconv_ref[p], nat, grads, p, halves, breadth)
        return carry

    lax.fori_loop(0, height, spread_own, 0)
    own_conv_rows(grads, taps, kern_ref, part_ref, height, steps, halves, True)
    sublane = lax.broadcasted_iota(jnp.int32, (SUBS, LANES), 0)

    def grad_at(h, p, t):
        grad = grads[h, p, EDGE + t]
        for s in range(SUBS):
            if s * steps + t >= breadth:
                grad = jnp.where(sublane == s, 0.0, grad)
        return grad

    def tap_body(i, carry):
        total = [[None] * 7 for _ in range(halves)]
        for p in range(height):
            window = [[spread[h, p + i, t] for t in range(6)] for h in range(halves)]
            for t in range(steps):
                for h in range(halves):
                    window[h].append(spread[h, p + i, t + 6])
                    grad = grad_at(h, p, t)
                    for j in range(7):
                        term = window[h][t + j] * grad
                        total[h][j] = term if total[h][j] is None else total[h][j] + term
        for h in range(halves):
            for j in range(7):
                sums[h, i * 7 + j] = jnp.sum(total[h][j], axis=0, keepdims=True)
        return carry

    lax.fori_loop(0, 7, tap_body, 0)
    total[...] = jnp.zeros_like(total)
    for h in range(halves):
        total[0:49, h * LANES : (h + 1) * LANES] = sums[h].reshape(49, LANES)
    rows = hsum_ref.shape[1] // channels
    at = 49
    for c in range(rows):
        total[at + c : at + c + 1, :] = jnp.sum(hsum_ref[:, c * channels : (c + 1) * channels], axis=0, keepdims=True)
    at += rows
    for c in range(5):
        total[at + c : at + c + 1, :] = jnp.sum(chan_ref[c], axis=0, keepdims=True)
    small_ref[...] = total[...]


def input_grad_kernel(top_ref, bottom_ref, part_ref, kern_ref, cot_ref, grad_ref, nat, spread, taps):
    height, breadth, channels = cot_ref.shape
    halves = channels // LANES
    steps, cells = dims_of(breadth)
    fill_taps(kern_ref, taps, halves, True)
    for r in range(EDGE):
        spread_row(top_ref[r], nat, spread, r, halves, breadth)
        spread_row(bottom_ref[r], nat, spread, EDGE + r, halves, breadth)
    n_runs, length = runs_of(steps)
    for p in range(height):

        def run_body(index, carry, p=p):
            h = index // n_runs
            start = (index % n_runs) * length
            base = p * steps + start
            total = conv_run(
                lambda slot, u: spread[h, slot, start + u],
                taps,
                h,
                halo_taps(p, height),
                length,
                [part_ref[h, base + t] for t in range(length)],
            )
            for t in range(length):
                nat[h, pl.ds(SUBS + start + t, SUBS, stride=steps), :] = total[t]
            return carry

        lax.fori_loop(0, halves * n_runs, run_body, 0)
        for h in range(halves):
            lanes = slice(h * LANES, (h + 1) * LANES)
            grad_ref[p, :, lanes] = (cot_ref[p, :, lanes].astype(F32) + gather_row(nat, h, breadth)).astype(BF16)


def call(kernel, out_shape, scratch, flops, nbytes, name, limit=VMEM_LIMIT):
    def run(*operands):
        whole = pl.BlockSpec(memory_space=pltpu.VMEM)
        scalars = pl.BlockSpec(memory_space=pltpu.SMEM)
        return pl.pallas_call(
            kernel,
            out_shape=out_shape,
            in_specs=[scalars if x.dtype == jnp.int32 else whole for x in operands],
            out_specs=jax.tree.map(lambda _: whole, out_shape),
            scratch_shapes=scratch,
            compiler_params=pltpu.CompilerParams(vmem_limit_bytes=limit),
            cost_estimate=pl.CostEstimate(flops=flops, bytes_accessed=nbytes, transcendentals=0),
            name=name,
        )(*operands)

    return run


def place_kernel(digits, rows, factor, place_ref, here_ref, across_ref, other_ref, other_across_ref, *rest):
    w_in_ref, w_out_ref, kernel_ref, hidden_ref, chan_ref, total, small_s = rest
    channels = here_ref.shape[1]
    order = [[]]
    for stride, size in digits[1:]:
        order = [tail + [k] for k in range(size) for tail in order]
    share = (here_ref.shape[0] - SMALL) // len(order)
    draw = place_ref[0]
    small = jnp.zeros((SMALL, channels), F32)
    for flip, refs in ((0, (here_ref, across_ref)), (1, (other_ref, other_across_ref))):
        for last, ref in enumerate(refs):
            values = ref[...].astype(F32)
            small = small + values[-SMALL:]
            for n, ks in enumerate(order):
                extent = rows
                start = 0
                for d, (stride, size) in enumerate(digits):
                    extent = extent // size
                    k = ks[d - 1] if d else last
                    start = start + (place_ref[1 + d] ^ k) * extent
                start = pl.multiple_of(start, SUBS)
                total[draw ^ flip, pl.ds(start, share), :] = values[n * share : (n + 1) * share]
    big = w_out_ref.shape[0]
    for c in range(big // channels):
        cols = slice(c * channels, (c + 1) * channels)
        w_in_ref[:, cols] = total[0, cols, :] * factor
    w_out_ref[...] = total[1, 0:big, :] * factor
    parts = digits[1][1] if len(digits) > 1 else 1
    part_rows = SMALL // parts
    for k in range(parts):
        at = (place_ref[2] ^ k) * part_rows if parts > 1 else 0
        small_s[pl.ds(pl.multiple_of(at, SUBS), part_rows), :] = small[k * part_rows : (k + 1) * part_rows]
    small = small_s[...] * factor
    for i in range(7):
        kernel_ref[i] = small[i * 7 : i * 7 + 7]
    blocks = big // channels
    halves = channels // LANES
    for c in range(blocks):
        for h in range(halves):
            hidden_ref[c * halves + h : c * halves + h + 1, :] = small[49 + c : 50 + c, h * LANES : (h + 1) * LANES]
    chan_ref[...] = small[49 + blocks : 54 + blocks]


def digits_of(count):
    digits = []
    stride = 2
    while stride < count:
        size = min(4, count // stride)
        digits.append((stride, size))
        stride *= size
    return [(1, 2)] + digits[::-1]


def exchange(values, count, stride, size, k):
    pairs = []
    for i in range(count):
        digit = i // stride % size
        pairs.append((i, i + ((digit ^ k) - digit) * stride))
    return lax.ppermute(values, "tile", pairs)


def other_core(values, draws):
    return lax.ppermute(values, "draw", [(i, i ^ 1) for i in range(draws)])


def halo(cells, tiles):
    after = [(i, i + 1) for i in range(tiles - 1)]
    before = [(i + 1, i) for i in range(tiles - 1)]
    top = lax.ppermute(cells[-EDGE:], "tile", after)
    bottom = lax.ppermute(cells[:EDGE], "tile", before)
    return top, bottom


def per_device(
    tiles,
    draws,
    inputs,
    land_mask,
    kernel,
    conv_bias,
    norm_gain,
    norm_bias,
    w_in,
    b_in,
    w_out,
    b_out,
    layer_scale,
    cotangent,
):
    _, height, breadth, channels = inputs.shape
    hidden_units = w_in.shape[1]
    halves = channels // LANES
    steps, cells = dims_of(breadth)
    own = inputs[0]
    cot = cotangent[0]
    top, bottom = halo(own, tiles)
    mask = jnp.pad(land_mask.astype(F32), ((0, 0), (0, cells - breadth)))
    mask = mask.reshape(height, SUBS, steps)

    def row(vector):
        return vector.reshape(1, -1)

    nat = pltpu.VMEM((halves, cells + 2 * SUBS, LANES), F32)

    def spread(slots):
        return pltpu.VMEM((halves, slots, steps + 2 * EDGE, SUBS, LANES), F32)

    taps = pltpu.VMEM((halves, 49, SUBS, LANES), F32)
    big_row = pltpu.VMEM((2 * cells, channels), F32)
    narrow = pltpu.VMEM((2 * cells, LANES), F32)
    count = height * cells
    big = hidden_units
    digits = digits_of(tiles)
    unit = tiles * SUBS
    rows = -(-big // unit) * unit
    tile = lax.axis_index("tile")
    place = jnp.stack([lax.axis_index("draw")] + [tile // stride % size for stride, size in digits]).astype(jnp.int32)
    part_shape = jax.ShapeDtypeStruct((halves, height * steps, SUBS, LANES), F32)
    mega = 1024 * 1024

    part = call(own_conv_kernel, part_shape, [nat, spread(height), taps], 1, 1, "own_conv")(own, kernel)
    out, gconv, keep, send, hsum, chan = call(
        main_kernel,
        (
            jax.ShapeDtypeStruct((height, breadth, channels), BF16),
            jax.ShapeDtypeStruct((height, breadth, channels), BF16),
            jax.ShapeDtypeStruct((big, channels), F32),
            jax.ShapeDtypeStruct((big, channels), BF16),
            jax.ShapeDtypeStruct((SUBS, hidden_units), F32),
            jax.ShapeDtypeStruct((5, SUBS, channels), F32),
        ),
        [
            nat,
            nat,
            spread(2 * EDGE),
            taps,
            pltpu.VMEM((halves, count, LANES), F32),
            big_row,
            big_row,
            big_row,
            big_row,
            big_row,
            narrow,
            narrow,
            pltpu.VMEM((count, channels), BF16),
            pltpu.VMEM((count, hidden_units), BF16),
            pltpu.VMEM((count, channels), BF16),
            pltpu.VMEM((count, hidden_units), BF16),
        ],
        12 * count * channels * hidden_units,
        8 * mega,
        "block_main",
    )(
        place, own, top, bottom, part, cot, mask, kernel, row(conv_bias), row(norm_gain), row(norm_bias), w_in, row(b_in),
        w_out, row(b_out), row(layer_scale),
    )
    got = other_core(send, draws)

    if rows > big:
        keep = jnp.pad(keep, ((0, rows - big), (0, 0)))
        got = jnp.pad(got, ((0, rows - big), (0, 0)))
    for step, (stride, size) in enumerate(digits):
        share = keep.shape[0] // size
        mine = place[1 + step]
        pieces = []
        for k in range(size):
            piece = lax.dynamic_slice_in_dim(keep, (mine ^ k) * share, share, 0)
            if not step:
                piece = piece + lax.dynamic_slice_in_dim(got, (mine ^ k) * share, share, 0).astype(F32)
            pieces.append(piece)
        if step == 1:
            part_rows = SMALL // size
            pieces = [
                jnp.concatenate([pieces[k], lax.dynamic_slice_in_dim(small, (mine ^ k) * part_rows, part_rows, 0)], axis=0)
                for k in range(size)
            ]
        sends = [piece.astype(BF16) for piece in pieces[1:]]
        if not step:
            sends, gconv, hsum = lax.optimization_barrier((sends, gconv, hsum))
            grad_top, grad_bottom = halo(gconv, tiles)
            small, grad_part = call(
                grads_kernel,
                (jax.ShapeDtypeStruct((SMALL, channels), F32), part_shape),
                [
                    nat,
                    spread(height + 2 * EDGE),
                    spread(height),
                    taps,
                    pltpu.VMEM((halves, 49, 1, LANES), F32),
                    pltpu.VMEM((SMALL, channels), F32),
                ],
                1,
                1,
                "kernel_grad",
            )(own, top, bottom, gconv, kernel, hsum, chan)
        received = [exchange(sends[k - 1], tiles, stride, size, k) for k in range(1, size)]
        if not step:
            received, small, grad_part = lax.optimization_barrier((received, small, grad_part))
        elif step == 1:
            received, grad_top, grad_bottom = lax.optimization_barrier((received, grad_top, grad_bottom))
        keep = pieces[0]
        for piece in received:
            keep = keep + piece.astype(F32)
        if step == 1:
            keep, small = keep[:share], keep[share:]
    gathered = keep.astype(BF16)
    for stride, size in digits[1:]:
        payload = jnp.concatenate([gathered, small.astype(BF16)], axis=0)
        if (stride, size) == digits[1]:
            payload, grad_part = lax.optimization_barrier((payload, grad_part))
            input_grad = call(
                input_grad_kernel,
                jax.ShapeDtypeStruct((height, breadth, channels), BF16),
                [nat, spread(2 * EDGE), taps],
                1,
                1,
                "input_grad",
            )(grad_top, grad_bottom, grad_part, kernel, cot)
        received = [payload] + [exchange(payload, tiles, stride, size, k) for k in range(1, size)]
        if (stride, size) == digits[1]:
            received, input_grad = lax.optimization_barrier((received, input_grad))
        extra = small.shape[0]
        gathered = jnp.concatenate([piece[:-extra] for piece in received], axis=0)
        if (stride, size) == digits[1]:
            small = jnp.concatenate([piece[-extra:] for piece in received], axis=0)
        else:
            small = functools.reduce(jnp.add, [piece[-extra:].astype(F32) for piece in received])
    gathered = jnp.concatenate([gathered, small.astype(BF16)], axis=0)
    stride, size = digits[0]
    across = exchange(gathered, tiles, stride, size, 1)
    other = other_core(gathered, draws)
    lon_first = Layout((0, 2, 1, 3))
    out = with_layout_constraint(out[None], lon_first)
    input_grad = with_layout_constraint(input_grad[None], lon_first)
    across, out, input_grad = lax.optimization_barrier((across, out, input_grad))
    other_across = other_core(across, draws)
    factor = float(1.0 / np.sqrt(np.float32(draws * height * tiles * breadth)))
    w_in_sum, w_out_sum, kernel_sum, hidden_sum, chan_sum = call(
        functools.partial(place_kernel, digits, rows, factor),
        (
            jax.ShapeDtypeStruct((channels, hidden_units), F32),
            jax.ShapeDtypeStruct((hidden_units, channels), F32),
            jax.ShapeDtypeStruct((7, 7, channels), F32),
            jax.ShapeDtypeStruct((hidden_units // LANES, LANES), F32),
            jax.ShapeDtypeStruct((5, channels), F32),
        ),
        [pltpu.VMEM((2, rows, channels), F32), pltpu.VMEM((SMALL, channels), F32)],
        mega,
        4 * mega,
        "place",
        16 * mega,
    )(place, gathered, across, other, other_across)
    return (
        out,
        input_grad,
        kernel_sum,
        w_in_sum,
        w_out_sum,
        hidden_sum.reshape(-1),
        chan_sum,
    )


def solution(mesh):
    placed = (
        P(("group", "draw"), "tile", None, None),
        P("tile", None),
        P(),
        P(),
        P(),
        P(),
        P(),
        P(),
        P(),
        P(),
        P(),
        P(("group", "draw"), "tile", None, None),
    )
    return jax.shard_map(
        functools.partial(per_device, mesh.shape["tile"], mesh.shape["draw"]),
        mesh=mesh,
        in_specs=placed,
        out_specs=(
            P(("group", "draw"), "tile", None, None),
            P(("group", "draw"), "tile", None, None),
            P("group", None, None),
            P("group", None),
            P("group", None),
            P("group"),
            P("group", None),
        ),
        check_vma=False,
    )
```

```python
import functools

import jax
import jax.numpy as jnp
import numpy as np
from jax import lax
from jax.experimental import pallas as pl
from jax.experimental.layout import Layout, with_layout_constraint
from jax.experimental.pallas import tpu as pltpu
from jax.sharding import PartitionSpec as P

ROOT_TERM = 0.7978845608028654
CUBIC = 0.044715
EPSILON = 1e-06
F32 = jnp.float32
BF16 = jnp.bfloat16
LANES = 128
SUBS = 8
EDGE = 3
SMALL = 64
VMEM_LIMIT = 56 * 1024 * 1024


def dims_of(breadth):
    steps = -(-breadth // SUBS)
    return steps, steps * SUBS


def spread_row(row, nat, spread, slot, halves, breadth):
    steps, cells = dims_of(breadth)
    row = row.astype(F32)
    over = cells - breadth + EDGE
    for h in range(halves):
        part = row[:, h * LANES : (h + 1) * LANES]
        nat[h, SUBS : SUBS + breadth, :] = part
        nat[h, SUBS - EDGE : SUBS, :] = part[breadth - EDGE :]
        nat[h, SUBS + breadth : SUBS + breadth + over, :] = part[:over]
    for h in range(halves):
        for t in range(steps + 2 * EDGE):
            spread[h, slot, t] = nat[h, pl.ds(SUBS - EDGE + t, SUBS, stride=steps), :]


def gather_row(nat, h, breadth):
    return nat[h, SUBS : SUBS + breadth, :]


def fill_taps(kern_ref, taps, halves, flip):
    for i in range(7):
        for j in range(7):
            src = kern_ref[6 - i, 6 - j : 7 - j, :] if flip else kern_ref[i, j : j + 1, :]
            for h in range(halves):
                taps[h, i * 7 + j] = jnp.broadcast_to(src[:, h * LANES : (h + 1) * LANES], (SUBS, LANES))


def conv_run(cells_at, taps, h, row_taps, length, total):
    total = list(total)
    for i, slot in row_taps:
        weights = [taps[h, i * 7 + j] for j in range(7)]
        for u in range(length + 6):
            cell = cells_at(slot, u)
            for j in range(7):
                t = u - j
                if 0 <= t < length:
                    term = cell * weights[j]
                    total[t] = term if total[t] is None else total[t] + term
    return total


def own_taps(p, height):
    return [(i, p + i - EDGE) for i in range(7) if 0 <= p + i - EDGE < height]


def halo_taps(p, height):
    found = []
    for i in range(7):
        row = p + i
        if row < EDGE:
            found.append((i, row))
        elif row >= EDGE + height:
            found.append((i, row - height))
    return found


def runs_of(steps):
    length = steps // 2 if steps % 2 == 0 else steps
    return steps // length, length


def own_conv_rows(spread, taps, kern_ref, part_ref, height, steps, halves, flip):
    fill_taps(kern_ref, taps, halves, flip)
    n_runs, length = runs_of(steps)
    for p in range(height):

        def run_body(index, carry, p=p):
            h = index // n_runs
            start = (index % n_runs) * length
            total = conv_run(
                lambda slot, u: spread[h, slot, start + u], taps, h, own_taps(p, height), length, [None] * length
            )
            for t in range(length):
                part_ref[h, p * steps + start + t] = total[t]
            return carry

        lax.fori_loop(0, halves * n_runs, run_body, 0)


def own_conv_kernel(own_ref, kern_ref, part_ref, nat, spread, taps):
    height, breadth, channels = own_ref.shape
    halves = channels // LANES
    steps, cells = dims_of(breadth)
    def spread_own(p, carry):
        spread_row(own_ref[p], nat, spread, p, halves, breadth)
        return carry

    lax.fori_loop(0, height, spread_own, 0)
    own_conv_rows(spread, taps, kern_ref, part_ref, height, steps, halves, False)


def main_kernel(
    place_ref, own_far, top_ref, bottom_ref, part_ref, cot_far, mask_ref, kern_ref, cbias_ref, gain_ref, nbias_ref, w_in_far,
    b_in_ref, w_out_far, b_out_ref, scale_ref,
    out_ref, gconv_ref, keep_ref, send_ref, hsum_ref, chan_ref,
    nat, out_s, spread, taps, conv, units, cots, state_s, mixed_s, gnorm_s, ocean_s, inv_s, normed_s, act_s, gmix_s, ghid_s,
    own_ref, cot_ref, w_in_ref, w_out_ref, arrived,
):
    height, breadth, channels = own_ref.shape
    hidden_units = w_in_ref.shape[1]
    halves = channels // LANES
    steps, cells = dims_of(breadth)

    late = ((own_far, own_ref), (cot_far, cot_ref), (w_in_far, w_in_ref), (w_out_far, w_out_ref))
    copies = [pltpu.make_async_copy(far, near, arrived.at[n]) for n, (far, near) in enumerate(late)]
    for copy in copies:
        copy.start()
    fill_taps(kern_ref, taps, halves, False)
    for r in range(EDGE):
        spread_row(top_ref[r], nat, spread, r, halves, breadth)
        spread_row(bottom_ref[r], nat, spread, EDGE + r, halves, breadth)
    n_runs, length = runs_of(steps)
    for p in range(height):

        def conv_body(index, carry, p=p):
            h = index // n_runs
            start = (index % n_runs) * length
            base = p * steps + start
            total = conv_run(
                lambda slot, u: spread[h, slot, start + u],
                taps,
                h,
                halo_taps(p, height),
                length,
                [part_ref[h, base + t] for t in range(length)],
            )
            for t in range(length):
                conv[h, pl.ds(pl.multiple_of((base + t) * SUBS, SUBS), SUBS), :] = total[t]
            return carry

        lax.fori_loop(0, halves * n_runs, conv_body, 0)

    for copy in copies:
        copy.wait()
    hsum_ref[...] = jnp.zeros_like(hsum_ref)
    chan_ref[...] = jnp.zeros_like(chan_ref)
    width = 256
    inv_c = 1.0 / channels
    sides = range(halves)
    lanes = [slice(h * LANES, (h + 1) * LANES) for h in sides]

    def column_sum(values):
        return jnp.sum(values.reshape(values.shape[0] // SUBS, SUBS, values.shape[1]), axis=0)

    def mean_of(parts):
        return jnp.sum(functools.reduce(jnp.add, parts), axis=1, keepdims=True) * inv_c

    pack = 2 if height % 2 == 0 else 1

    def row_body(pp, carry):
        base2 = pl.multiple_of(pp * (pack * cells), 16)
        rows = pl.ds(base2, pack * cells)
        for q in range(pack):
            p = pp * pack + q
            base = pl.multiple_of(base2 + q * cells, 16)
            cot = cot_ref[p].astype(F32)
            for h in sides:
                nat[h, SUBS : SUBS + breadth, :] = cot[:, lanes[h]]
                out_s[h, SUBS : SUBS + breadth, :] = own_ref[p, :, lanes[h]].astype(F32)
            land = mask_ref[p]
            for t in range(0, steps, 2):
                here = pl.ds(base + t * SUBS, 2 * SUBS)
                local = slice(q * cells + t * SUBS, q * cells + (t + 2) * SUBS)
                values = [conv[h, here, :] + cbias_ref[:, lanes[h]] for h in sides]
                center = mean_of(values)
                deviation = [v - center for v in values]
                inv_std = lax.rsqrt(mean_of([d * d for d in deviation]) + EPSILON)
                inv_s[local, :] = jnp.broadcast_to(inv_std, (2 * SUBS, LANES))
                ocean = jnp.concatenate([jnp.broadcast_to(land[:, t + k : t + k + 1], (SUBS, LANES)) for k in range(2)], axis=0)
                ocean_s[local, :] = ocean
                for h in sides:
                    unit = deviation[h] * inv_std
                    units[local, lanes[h]] = unit
                    normed_s[here, lanes[h]] = (unit * gain_ref[:, lanes[h]] + nbias_ref[:, lanes[h]]).astype(BF16)
                    cell = jnp.concatenate(
                        [nat[h, pl.ds(SUBS + t + k, SUBS, stride=steps), :] for k in range(2)], axis=0
                    )
                    upstream = jnp.where(ocean > 0, cell, 0.0)
                    cots[local, lanes[h]] = upstream
                    state_s[local, lanes[h]] = jnp.concatenate(
                        [out_s[h, pl.ds(SUBS + t + k, SUBS, stride=steps), :] for k in range(2)], axis=0
                    )
                    gmix_s[here, lanes[h]] = (scale_ref[:, lanes[h]] * upstream).astype(BF16)
        normed = normed_s[rows, :]
        gmix = gmix_s[rows, :]
        for c in range(0, hidden_units, width):
            cols = slice(c, c + width)
            hidden = jnp.dot(normed, w_in_ref[:, cols], preferred_element_type=F32) + b_in_ref[:, cols]
            grad_act = lax.dot_general(
                gmix, w_out_ref[cols, :], (((1,), (1,)), ((), ())), preferred_element_type=F32
            )
            square = hidden * hidden
            inner = hidden * (ROOT_TERM * CUBIC * square + ROOT_TERM)
            half_tanh = 0.5 * jnp.tanh(inner)
            gate = 0.5 + half_tanh
            active = hidden * gate
            slope = gate + active * (0.5 - half_tanh) * (6.0 * CUBIC * ROOT_TERM * square + 2.0 * ROOT_TERM)
            act = active.astype(BF16)
            act_s[rows, cols] = act
            mixed = jnp.dot(act, w_out_ref[cols, :], preferred_element_type=F32)
            ghid = (grad_act * slope).astype(BF16)
            ghid_s[rows, cols] = ghid
            hsum_ref[:, cols] += column_sum(ghid.astype(F32))
            grad_normed = lax.dot_general(
                ghid, w_in_ref[:, cols], (((1,), (1,)), ((), ())), preferred_element_type=F32
            )
            if c:
                mixed_s[...] += mixed
                gnorm_s[...] += grad_normed
            else:
                mixed_s[...] = mixed
                gnorm_s[...] = grad_normed
        for q in range(pack):
            p = pp * pack + q
            base = pl.multiple_of(base2 + q * cells, 16)
            sums = [[None] * halves for _ in range(5)]

            def add_to(n, h, values):
                folded = values[:SUBS] + values[SUBS:]
                sums[n][h] = folded if sums[n][h] is None else sums[n][h] + folded

            for t in range(0, steps, 2):
                here = pl.ds(base + t * SUBS, 2 * SUBS)
                local = slice(q * cells + t * SUBS, q * cells + (t + 2) * SUBS)
                ocean = ocean_s[local, :]
                scaled, products, units_here = [], [], []
                for h in sides:
                    mixed = mixed_s[local, lanes[h]] + b_out_ref[:, lanes[h]]
                    add_to(4, h, cots[local, lanes[h]] * mixed)
                    residual = jnp.where(ocean > 0, scale_ref[:, lanes[h]] * mixed, 0.0)
                    result = state_s[local, lanes[h]] + residual
                    for k in range(2):
                        out_s[h, pl.ds(SUBS + t + k, SUBS, stride=steps), :] = result[k * SUBS : (k + 1) * SUBS]
                    grad_normed = gnorm_s[local, lanes[h]]
                    unit = units[local, lanes[h]]
                    add_to(1, h, grad_normed * unit)
                    add_to(2, h, grad_normed)
                    add_to(3, h, gmix_s[here, lanes[h]].astype(F32))
                    scaled.append(grad_normed * gain_ref[:, lanes[h]])
                    units_here.append(unit)
                    products.append(scaled[h] * unit)
                mean_scaled = mean_of(scaled)
                mean_product = mean_of(products)
                inv_std = inv_s[local, :]
                for h in sides:
                    grad_conv = (inv_std * (scaled[h] - mean_scaled - units_here[h] * mean_product)).astype(BF16).astype(F32)
                    add_to(0, h, grad_conv)
                    for k in range(2):
                        nat[h, pl.ds(SUBS + t + k, SUBS, stride=steps), :] = grad_conv[k * SUBS : (k + 1) * SUBS]
            for n in range(5):
                for h in sides:
                    chan_ref[n, :, lanes[h]] += sums[n][h]
            for h in sides:
                out_ref[p, :, lanes[h]] = gather_row(out_s, h, breadth).astype(BF16)
                gconv_ref[p, :, lanes[h]] = gather_row(nat, h, breadth).astype(BF16)
        return carry

    lax.fori_loop(0, height // pack, row_body, 0)

    first = (((0,), (0,)), ((), ()))

    def store_block(half, c, block):
        @pl.when(place_ref[0] == half)
        def _():
            keep_ref[c : c + width, :] = block

        @pl.when(place_ref[0] != half)
        def _():
            send_ref[c : c + width, :] = block.astype(BF16)

    w_in_grad = lax.dot_general(normed_s[...], ghid_s[...], first, preferred_element_type=F32)
    for c in range(0, hidden_units, width):
        store_block(0, c, w_in_grad[:, c : c + width])
    w_out_grad = lax.dot_general(act_s[...], gmix_s[...], first, preferred_element_type=F32)
    for c in range(0, hidden_units, width):
        store_block(1, c, w_out_grad[c : c + width])


def grads_kernel(
    own_ref, top_ref, bottom_ref, gconv_ref, kern_ref, hsum_ref, chan_ref, small_ref, part_ref,
    nat, spread, grads, taps, sums, total,
):
    height, breadth, channels = own_ref.shape
    halves = channels // LANES
    steps, cells = dims_of(breadth)
    for r in range(EDGE):
        spread_row(top_ref[r], nat, spread, r, halves, breadth)
        spread_row(bottom_ref[r], nat, spread, EDGE + height + r, halves, breadth)

    def spread_own(p, carry):
        spread_row(own_ref[p], nat, spread, EDGE + p, halves, breadth)
        spread_row(gconv_ref[p], nat, grads, p, halves, breadth)
        return carry

    lax.fori_loop(0, height, spread_own, 0)
    own_conv_rows(grads, taps, kern_ref, part_ref, height, steps, halves, True)
    sublane = lax.broadcasted_iota(jnp.int32, (SUBS, LANES), 0)

    def grad_at(h, p, t):
        grad = grads[h, p, EDGE + t]
        for s in range(SUBS):
            if s * steps + t >= breadth:
                grad = jnp.where(sublane == s, 0.0, grad)
        return grad

    def tap_body(i, carry):
        total = [[None] * 7 for _ in range(halves)]
        for p in range(height):
            window = [[spread[h, p + i, t] for t in range(6)] for h in range(halves)]
            for t in range(steps):
                for h in range(halves):
                    window[h].append(spread[h, p + i, t + 6])
                    grad = grad_at(h, p, t)
                    for j in range(7):
                        term = window[h][t + j] * grad
                        total[h][j] = term if total[h][j] is None else total[h][j] + term
        for h in range(halves):
            for j in range(7):
                sums[h, i * 7 + j] = jnp.sum(total[h][j], axis=0, keepdims=True)
        return carry

    lax.fori_loop(0, 7, tap_body, 0)
    total[...] = jnp.zeros_like(total)
    for h in range(halves):
        total[0:49, h * LANES : (h + 1) * LANES] = sums[h].reshape(49, LANES)
    rows = hsum_ref.shape[1] // channels
    at = 49
    for c in range(rows):
        total[at + c : at + c + 1, :] = jnp.sum(hsum_ref[:, c * channels : (c + 1) * channels], axis=0, keepdims=True)
    at += rows
    for c in range(5):
        total[at + c : at + c + 1, :] = jnp.sum(chan_ref[c], axis=0, keepdims=True)
    small_ref[...] = total[...]


def input_grad_kernel(top_ref, bottom_ref, part_ref, kern_ref, cot_ref, grad_ref, nat, spread, taps):
    height, breadth, channels = cot_ref.shape
    halves = channels // LANES
    steps, cells = dims_of(breadth)
    fill_taps(kern_ref, taps, halves, True)
    for r in range(EDGE):
        spread_row(top_ref[r], nat, spread, r, halves, breadth)
        spread_row(bottom_ref[r], nat, spread, EDGE + r, halves, breadth)
    n_runs, length = runs_of(steps)
    for p in range(height):

        def run_body(index, carry, p=p):
            h = index // n_runs
            start = (index % n_runs) * length
            base = p * steps + start
            total = conv_run(
                lambda slot, u: spread[h, slot, start + u],
                taps,
                h,
                halo_taps(p, height),
                length,
                [part_ref[h, base + t] for t in range(length)],
            )
            for t in range(length):
                nat[h, pl.ds(SUBS + start + t, SUBS, stride=steps), :] = total[t]
            return carry

        lax.fori_loop(0, halves * n_runs, run_body, 0)
        for h in range(halves):
            lanes = slice(h * LANES, (h + 1) * LANES)
            grad_ref[p, :, lanes] = (cot_ref[p, :, lanes].astype(F32) + gather_row(nat, h, breadth)).astype(BF16)


def call(kernel, out_shape, scratch, flops, nbytes, name, limit=VMEM_LIMIT, late=()):
    def run(*operands):
        whole = pl.BlockSpec(memory_space=pltpu.VMEM)
        scalars = pl.BlockSpec(memory_space=pltpu.SMEM)
        return pl.pallas_call(
            kernel,
            out_shape=out_shape,
            in_specs=[
                pl.BlockSpec(memory_space=pl.ANY) if n in late else scalars if x.dtype == jnp.int32 else whole
                for n, x in enumerate(operands)
            ],
            out_specs=jax.tree.map(lambda _: whole, out_shape),
            scratch_shapes=scratch,
            compiler_params=pltpu.CompilerParams(vmem_limit_bytes=limit),
            cost_estimate=pl.CostEstimate(flops=flops, bytes_accessed=nbytes, transcendentals=0),
            name=name,
        )(*operands)

    return run


def place_kernel(digits, rows, factor, place_ref, here_ref, across_ref, other_ref, other_across_ref, *rest):
    w_in_ref, w_out_ref, kernel_ref, hidden_ref, chan_ref, total = rest
    channels = here_ref.shape[1]
    order = [[]]
    for stride, size in digits[1:]:
        order = [tail + [k] for k in range(size) for tail in order]
    share = (here_ref.shape[0] - SMALL) // len(order)
    draw = place_ref[0]
    small = jnp.zeros((SMALL, channels), F32)
    for flip, refs in ((0, (here_ref, across_ref)), (1, (other_ref, other_across_ref))):
        for last, ref in enumerate(refs):
            values = ref[...].astype(F32)
            small = small + values[-SMALL:]
            for n, ks in enumerate(order):
                extent = rows
                start = 0
                for d, (stride, size) in enumerate(digits):
                    extent = extent // size
                    k = ks[d - 1] if d else last
                    start = start + (place_ref[1 + d] ^ k) * extent
                start = pl.multiple_of(start, SUBS)
                total[draw ^ flip, pl.ds(start, share), :] = values[n * share : (n + 1) * share]
    big = w_out_ref.shape[0]
    for c in range(big // channels):
        cols = slice(c * channels, (c + 1) * channels)
        w_in_ref[:, cols] = total[0, cols, :] * factor
    w_out_ref[...] = total[1, 0:big, :] * factor
    small = small * factor
    for i in range(7):
        kernel_ref[i] = small[i * 7 : i * 7 + 7]
    blocks = big // channels
    halves = channels // LANES
    for c in range(blocks):
        for h in range(halves):
            hidden_ref[c * halves + h : c * halves + h + 1, :] = small[49 + c : 50 + c, h * LANES : (h + 1) * LANES]
    chan_ref[...] = small[49 + blocks : 54 + blocks]


def digits_of(count):
    digits = []
    stride = 2
    while stride < count:
        size = min(4, count // stride)
        digits.append((stride, size))
        stride *= size
    return [(1, 2)] + digits[::-1]


def exchange(values, count, stride, size, k):
    pairs = []
    for i in range(count):
        digit = i // stride % size
        pairs.append((i, i + ((digit ^ k) - digit) * stride))
    return lax.ppermute(values, "tile", pairs)


def other_core(values, draws):
    return lax.ppermute(values, "draw", [(i, i ^ 1) for i in range(draws)])


def halo(cells, tiles):
    after = [(i, i + 1) for i in range(tiles - 1)]
    before = [(i + 1, i) for i in range(tiles - 1)]
    top = lax.ppermute(cells[-EDGE:], "tile", after)
    bottom = lax.ppermute(cells[:EDGE], "tile", before)
    return top, bottom


def per_device(
    tiles,
    draws,
    inputs,
    land_mask,
    kernel,
    conv_bias,
    norm_gain,
    norm_bias,
    w_in,
    b_in,
    w_out,
    b_out,
    layer_scale,
    cotangent,
):
    _, height, breadth, channels = inputs.shape
    hidden_units = w_in.shape[1]
    halves = channels // LANES
    steps, cells = dims_of(breadth)
    own = inputs[0]
    cot = cotangent[0]
    top, bottom = halo(own, tiles)
    mask = jnp.pad(land_mask.astype(F32), ((0, 0), (0, cells - breadth)))
    mask = mask.reshape(height, SUBS, steps)

    def row(vector):
        return vector.reshape(1, -1)

    nat = pltpu.VMEM((halves, cells + 2 * SUBS, LANES), F32)

    def spread(slots):
        return pltpu.VMEM((halves, slots, steps + 2 * EDGE, SUBS, LANES), F32)

    taps = pltpu.VMEM((halves, 49, SUBS, LANES), F32)
    big_row = pltpu.VMEM((2 * cells, channels), F32)
    narrow = pltpu.VMEM((2 * cells, LANES), F32)
    count = height * cells
    big = hidden_units
    digits = digits_of(tiles)
    unit = tiles * SUBS
    rows = -(-big // unit) * unit
    tile = lax.axis_index("tile")
    place = jnp.stack([lax.axis_index("draw")] + [tile // stride % size for stride, size in digits]).astype(jnp.int32)
    part_shape = jax.ShapeDtypeStruct((halves, height * steps, SUBS, LANES), F32)
    mega = 1024 * 1024

    part = call(own_conv_kernel, part_shape, [nat, spread(height), taps], 1, 1, "own_conv")(own, kernel)
    out, gconv, keep, send, hsum, chan = call(
        main_kernel,
        (
            jax.ShapeDtypeStruct((height, breadth, channels), BF16),
            jax.ShapeDtypeStruct((height, breadth, channels), BF16),
            jax.ShapeDtypeStruct((big, channels), F32),
            jax.ShapeDtypeStruct((big, channels), BF16),
            jax.ShapeDtypeStruct((SUBS, hidden_units), F32),
            jax.ShapeDtypeStruct((5, SUBS, channels), F32),
        ),
        [
            nat,
            nat,
            spread(2 * EDGE),
            taps,
            pltpu.VMEM((halves, count, LANES), F32),
            big_row,
            big_row,
            big_row,
            big_row,
            big_row,
            narrow,
            narrow,
            pltpu.VMEM((count, channels), BF16),
            pltpu.VMEM((count, hidden_units), BF16),
            pltpu.VMEM((count, channels), BF16),
            pltpu.VMEM((count, hidden_units), BF16),
            pltpu.VMEM((height, breadth, channels), BF16),
            pltpu.VMEM((height, breadth, channels), BF16),
            pltpu.VMEM((channels, hidden_units), BF16),
            pltpu.VMEM((hidden_units, channels), BF16),
            pltpu.SemaphoreType.DMA((4,)),
        ],
        12 * count * channels * hidden_units,
        8 * mega,
        "block_main",
        late=(1, 5, 11, 13),
    )(
        place, own, top, bottom, part, cot, mask, kernel, row(conv_bias), row(norm_gain), row(norm_bias), w_in, row(b_in),
        w_out, row(b_out), row(layer_scale),
    )
    got = other_core(send, draws)

    if rows > big:
        keep = jnp.pad(keep, ((0, rows - big), (0, 0)))
        got = jnp.pad(got, ((0, rows - big), (0, 0)))
    for step, (stride, size) in enumerate(digits):
        share = keep.shape[0] // size
        mine = place[1 + step]
        pieces = []
        for k in range(size):
            piece = lax.dynamic_slice_in_dim(keep, (mine ^ k) * share, share, 0)
            if not step:
                piece = piece + lax.dynamic_slice_in_dim(got, (mine ^ k) * share, share, 0).astype(F32)
            pieces.append(piece)
        sends = [piece.astype(BF16) for piece in pieces[1:]]
        if not step:
            sends, gconv, hsum = lax.optimization_barrier((sends, gconv, hsum))
            grad_top, grad_bottom = halo(gconv, tiles)
            small, grad_part = call(
                grads_kernel,
                (jax.ShapeDtypeStruct((SMALL, channels), F32), part_shape),
                [
                    nat,
                    spread(height + 2 * EDGE),
                    spread(height),
                    taps,
                    pltpu.VMEM((halves, 49, 1, LANES), F32),
                    pltpu.VMEM((SMALL, channels), F32),
                ],
                1,
                1,
                "kernel_grad",
            )(own, top, bottom, gconv, kernel, hsum, chan)
        received = [exchange(sends[k - 1], tiles, stride, size, k) for k in range(1, size)]
        if not step:
            received, small, grad_part = lax.optimization_barrier((received, small, grad_part))
        elif step == 1:
            received, grad_top, grad_bottom = lax.optimization_barrier((received, grad_top, grad_bottom))
        keep = pieces[0]
        for piece in received:
            keep = keep + piece.astype(F32)
    gathered = keep.astype(BF16)
    for stride, size in digits[1:]:
        payload = jnp.concatenate([gathered, small.astype(BF16)], axis=0)
        if (stride, size) == digits[1]:
            payload, grad_part = lax.optimization_barrier((payload, grad_part))
            input_grad = call(
                input_grad_kernel,
                jax.ShapeDtypeStruct((height, breadth, channels), BF16),
                [nat, spread(2 * EDGE), taps],
                1,
                1,
                "input_grad",
            )(grad_top, grad_bottom, grad_part, kernel, cot)
        received = [payload] + [exchange(payload, tiles, stride, size, k) for k in range(1, size)]
        if (stride, size) == digits[1]:
            received, input_grad = lax.optimization_barrier((received, input_grad))
        gathered = jnp.concatenate([piece[:-SMALL] for piece in received], axis=0)
        small = functools.reduce(jnp.add, [piece[-SMALL:].astype(F32) for piece in received])
    gathered = jnp.concatenate([gathered, small.astype(BF16)], axis=0)
    stride, size = digits[0]
    across = exchange(gathered, tiles, stride, size, 1)
    other = other_core(gathered, draws)
    lon_first = Layout((0, 2, 1, 3))
    out = with_layout_constraint(out[None], lon_first)
    input_grad = with_layout_constraint(input_grad[None], lon_first)
    across, out, input_grad = lax.optimization_barrier((across, out, input_grad))
    other_across = other_core(across, draws)
    factor = float(1.0 / np.sqrt(np.float32(draws * height * tiles * breadth)))
    w_in_sum, w_out_sum, kernel_sum, hidden_sum, chan_sum = call(
        functools.partial(place_kernel, digits, rows, factor),
        (
            jax.ShapeDtypeStruct((channels, hidden_units), F32),
            jax.ShapeDtypeStruct((hidden_units, channels), F32),
            jax.ShapeDtypeStruct((7, 7, channels), F32),
            jax.ShapeDtypeStruct((hidden_units // LANES, LANES), F32),
            jax.ShapeDtypeStruct((5, channels), F32),
        ),
        [pltpu.VMEM((2, rows, channels), F32)],
        mega,
        4 * mega,
        "place",
        16 * mega,
    )(place, gathered, across, other, other_across)
    return (
        out,
        input_grad,
        kernel_sum,
        w_in_sum,
        w_out_sum,
        hidden_sum.reshape(-1),
        chan_sum,
    )


def solution(mesh):
    placed = (
        P(("group", "draw"), "tile", None, None),
        P("tile", None),
        P(),
        P(),
        P(),
        P(),
        P(),
        P(),
        P(),
        P(),
        P(),
        P(("group", "draw"), "tile", None, None),
    )
    return jax.shard_map(
        functools.partial(per_device, mesh.shape["tile"], mesh.shape["draw"]),
        mesh=mesh,
        in_specs=placed,
        out_specs=(
            P(("group", "draw"), "tile", None, None),
            P(("group", "draw"), "tile", None, None),
            P("group", None, None),
            P("group", None),
            P("group", None),
            P("group"),
            P("group", None),
        ),
        check_vma=False,
    )
```

```python
import functools

import jax
import jax.numpy as jnp
import numpy as np
from jax import lax
from jax.experimental import pallas as pl
from jax.experimental.layout import Layout, with_layout_constraint
from jax.experimental.pallas import tpu as pltpu
from jax.sharding import PartitionSpec as P

ROOT_TERM = 0.7978845608028654
CUBIC = 0.044715
EPSILON = 1e-06
F32 = jnp.float32
BF16 = jnp.bfloat16
LANES = 128
SUBS = 8
EDGE = 3
SMALL = 64
VMEM_LIMIT = 56 * 1024 * 1024


def dims_of(breadth):
    steps = -(-breadth // SUBS)
    return steps, steps * SUBS


def spread_row(row, nat, spread, slot, halves, breadth):
    steps, cells = dims_of(breadth)
    row = row.astype(F32)
    over = cells - breadth + EDGE
    for h in range(halves):
        part = row[:, h * LANES : (h + 1) * LANES]
        nat[h, SUBS : SUBS + breadth, :] = part
        nat[h, SUBS - EDGE : SUBS, :] = part[breadth - EDGE :]
        nat[h, SUBS + breadth : SUBS + breadth + over, :] = part[:over]
    for h in range(halves):
        for t in range(steps + 2 * EDGE):
            spread[h, slot, t] = nat[h, pl.ds(SUBS - EDGE + t, SUBS, stride=steps), :]


def gather_row(nat, h, breadth):
    return nat[h, SUBS : SUBS + breadth, :]


def fill_taps(kern_ref, taps, halves, flip):
    for i in range(7):
        for j in range(7):
            src = kern_ref[6 - i, 6 - j : 7 - j, :] if flip else kern_ref[i, j : j + 1, :]
            for h in range(halves):
                taps[h, i * 7 + j] = jnp.broadcast_to(src[:, h * LANES : (h + 1) * LANES], (SUBS, LANES))


def conv_run(cells_at, taps, h, row_taps, length, total):
    total = list(total)
    for i, slot in row_taps:
        weights = [taps[h, i * 7 + j] for j in range(7)]
        for u in range(length + 6):
            cell = cells_at(slot, u)
            for j in range(7):
                t = u - j
                if 0 <= t < length:
                    term = cell * weights[j]
                    total[t] = term if total[t] is None else total[t] + term
    return total


def own_taps(p, height):
    return [(i, p + i - EDGE) for i in range(7) if 0 <= p + i - EDGE < height]


def halo_taps(p, height):
    found = []
    for i in range(7):
        row = p + i
        if row < EDGE:
            found.append((i, row))
        elif row >= EDGE + height:
            found.append((i, row - height))
    return found


def runs_of(steps):
    length = steps // 2 if steps % 2 == 0 else steps
    return steps // length, length


def own_conv_rows(spread, taps, kern_ref, part_ref, height, steps, halves, flip):
    fill_taps(kern_ref, taps, halves, flip)
    n_runs, length = runs_of(steps)
    for p in range(height):

        def run_body(index, carry, p=p):
            h = index // n_runs
            start = (index % n_runs) * length
            total = conv_run(
                lambda slot, u: spread[h, slot, start + u], taps, h, own_taps(p, height), length, [None] * length
            )
            for t in range(length):
                part_ref[h, p * steps + start + t] = total[t]
            return carry

        lax.fori_loop(0, halves * n_runs, run_body, 0)


def own_conv_kernel(own_ref, kern_ref, part_ref, nat, spread, taps):
    height, breadth, channels = own_ref.shape
    halves = channels // LANES
    steps, cells = dims_of(breadth)
    def spread_own(p, carry):
        spread_row(own_ref[p], nat, spread, p, halves, breadth)
        return carry

    lax.fori_loop(0, height, spread_own, 0)
    own_conv_rows(spread, taps, kern_ref, part_ref, height, steps, halves, False)


def main_kernel(
    place_ref, own_far, top_ref, bottom_ref, part_ref, cot_far, mask_ref, kern_ref, cbias_ref, gain_ref, nbias_ref, w_in_far,
    b_in_ref, w_out_far, b_out_ref, scale_ref,
    out_ref, gconv_ref, keep_ref, send_ref, hsum_ref, chan_ref,
    nat, out_s, spread, taps, conv, units, cots, state_s, mixed_s, gnorm_s, ocean_s, inv_s, normed_s, act_s, gmix_s, ghid_s,
    own_ref, cot_ref, w_in_ref, w_out_ref, arrived,
):
    height, breadth, channels = own_ref.shape
    hidden_units = w_in_ref.shape[1]
    halves = channels // LANES
    steps, cells = dims_of(breadth)

    late = ((own_far, own_ref), (cot_far, cot_ref), (w_in_far, w_in_ref), (w_out_far, w_out_ref))
    copies = [pltpu.make_async_copy(far, near, arrived.at[n]) for n, (far, near) in enumerate(late)]
    for copy in copies:
        copy.start()
    fill_taps(kern_ref, taps, halves, False)
    for r in range(EDGE):
        spread_row(top_ref[r], nat, spread, r, halves, breadth)
        spread_row(bottom_ref[r], nat, spread, EDGE + r, halves, breadth)
    n_runs, length = runs_of(steps)
    for p in range(height):

        def conv_body(index, carry, p=p):
            h = index // n_runs
            start = (index % n_runs) * length
            base = p * steps + start
            total = conv_run(
                lambda slot, u: spread[h, slot, start + u],
                taps,
                h,
                halo_taps(p, height),
                length,
                [part_ref[h, base + t] for t in range(length)],
            )
            for t in range(length):
                conv[h, pl.ds(pl.multiple_of((base + t) * SUBS, SUBS), SUBS), :] = total[t]
            return carry

        lax.fori_loop(0, halves * n_runs, conv_body, 0)

    for copy in copies:
        copy.wait()
    hsum_ref[...] = jnp.zeros_like(hsum_ref)
    chan_ref[...] = jnp.zeros_like(chan_ref)
    width = 256
    inv_c = 1.0 / channels
    sides = range(halves)
    lanes = [slice(h * LANES, (h + 1) * LANES) for h in sides]

    def column_sum(values):
        return jnp.sum(values.reshape(values.shape[0] // SUBS, SUBS, values.shape[1]), axis=0)

    def mean_of(parts):
        return jnp.sum(functools.reduce(jnp.add, parts), axis=1, keepdims=True) * inv_c

    pack = 2 if height % 2 == 0 else 1

    def row_body(pp, carry):
        base2 = pl.multiple_of(pp * (pack * cells), 16)
        rows = pl.ds(base2, pack * cells)
        for q in range(pack):
            p = pp * pack + q
            base = pl.multiple_of(base2 + q * cells, 16)
            cot = cot_ref[p].astype(F32)
            for h in sides:
                nat[h, SUBS : SUBS + breadth, :] = cot[:, lanes[h]]
                out_s[h, SUBS : SUBS + breadth, :] = own_ref[p, :, lanes[h]].astype(F32)
            land = mask_ref[p]
            for t in range(0, steps, 2):
                here = pl.ds(base + t * SUBS, 2 * SUBS)
                local = slice(q * cells + t * SUBS, q * cells + (t + 2) * SUBS)
                values = [conv[h, here, :] + cbias_ref[:, lanes[h]] for h in sides]
                center = mean_of(values)
                deviation = [v - center for v in values]
                inv_std = lax.rsqrt(mean_of([d * d for d in deviation]) + EPSILON)
                inv_s[local, :] = jnp.broadcast_to(inv_std, (2 * SUBS, LANES))
                ocean = jnp.concatenate([jnp.broadcast_to(land[:, t + k : t + k + 1], (SUBS, LANES)) for k in range(2)], axis=0)
                ocean_s[local, :] = ocean
                for h in sides:
                    unit = deviation[h] * inv_std
                    units[local, lanes[h]] = unit
                    normed_s[here, lanes[h]] = (unit * gain_ref[:, lanes[h]] + nbias_ref[:, lanes[h]]).astype(BF16)
                    cell = jnp.concatenate(
                        [nat[h, pl.ds(SUBS + t + k, SUBS, stride=steps), :] for k in range(2)], axis=0
                    )
                    upstream = jnp.where(ocean > 0, cell, 0.0)
                    cots[local, lanes[h]] = upstream
                    state_s[local, lanes[h]] = jnp.concatenate(
                        [out_s[h, pl.ds(SUBS + t + k, SUBS, stride=steps), :] for k in range(2)], axis=0
                    )
                    gmix_s[here, lanes[h]] = (scale_ref[:, lanes[h]] * upstream).astype(BF16)
        normed = normed_s[rows, :]
        gmix = gmix_s[rows, :]
        for c in range(0, hidden_units, width):
            cols = slice(c, c + width)
            hidden = jnp.dot(normed, w_in_ref[:, cols], preferred_element_type=F32) + b_in_ref[:, cols]
            grad_act = lax.dot_general(
                gmix, w_out_ref[cols, :], (((1,), (1,)), ((), ())), preferred_element_type=F32
            )
            square = hidden * hidden
            inner = hidden * (ROOT_TERM * CUBIC * square + ROOT_TERM)
            half_tanh = 0.5 * jnp.tanh(inner)
            gate = 0.5 + half_tanh
            active = hidden * gate
            slope = gate + active * (0.5 - half_tanh) * (6.0 * CUBIC * ROOT_TERM * square + 2.0 * ROOT_TERM)
            act = active.astype(BF16)
            act_s[rows, cols] = act
            mixed = jnp.dot(act, w_out_ref[cols, :], preferred_element_type=F32)
            ghid = (grad_act * slope).astype(BF16)
            ghid_s[rows, cols] = ghid
            hsum_ref[:, cols] += column_sum(ghid.astype(F32))
            grad_normed = lax.dot_general(
                ghid, w_in_ref[:, cols], (((1,), (1,)), ((), ())), preferred_element_type=F32
            )
            if c:
                mixed_s[...] += mixed
                gnorm_s[...] += grad_normed
            else:
                mixed_s[...] = mixed
                gnorm_s[...] = grad_normed
        for q in range(pack):
            p = pp * pack + q
            base = pl.multiple_of(base2 + q * cells, 16)
            sums = [[None] * halves for _ in range(5)]

            def add_to(n, h, values):
                folded = values[:SUBS] + values[SUBS:]
                sums[n][h] = folded if sums[n][h] is None else sums[n][h] + folded

            for t in range(0, steps, 2):
                here = pl.ds(base + t * SUBS, 2 * SUBS)
                local = slice(q * cells + t * SUBS, q * cells + (t + 2) * SUBS)
                ocean = ocean_s[local, :]
                scaled, products, units_here = [], [], []
                for h in sides:
                    mixed = mixed_s[local, lanes[h]] + b_out_ref[:, lanes[h]]
                    add_to(4, h, cots[local, lanes[h]] * mixed)
                    residual = jnp.where(ocean > 0, scale_ref[:, lanes[h]] * mixed, 0.0)
                    result = state_s[local, lanes[h]] + residual
                    for k in range(2):
                        out_s[h, pl.ds(SUBS + t + k, SUBS, stride=steps), :] = result[k * SUBS : (k + 1) * SUBS]
                    grad_normed = gnorm_s[local, lanes[h]]
                    unit = units[local, lanes[h]]
                    add_to(1, h, grad_normed * unit)
                    add_to(2, h, grad_normed)
                    add_to(3, h, gmix_s[here, lanes[h]].astype(F32))
                    scaled.append(grad_normed * gain_ref[:, lanes[h]])
                    units_here.append(unit)
                    products.append(scaled[h] * unit)
                mean_scaled = mean_of(scaled)
                mean_product = mean_of(products)
                inv_std = inv_s[local, :]
                for h in sides:
                    grad_conv = (inv_std * (scaled[h] - mean_scaled - units_here[h] * mean_product)).astype(BF16).astype(F32)
                    add_to(0, h, grad_conv)
                    for k in range(2):
                        nat[h, pl.ds(SUBS + t + k, SUBS, stride=steps), :] = grad_conv[k * SUBS : (k + 1) * SUBS]
            for n in range(5):
                for h in sides:
                    chan_ref[n, :, lanes[h]] += sums[n][h]
            for h in sides:
                out_ref[p, :, lanes[h]] = gather_row(out_s, h, breadth).astype(BF16)
                gconv_ref[p, :, lanes[h]] = gather_row(nat, h, breadth).astype(BF16)
        return carry

    lax.fori_loop(0, height // pack, row_body, 0)

    first = (((0,), (0,)), ((), ()))

    def store_block(half, c, block):
        @pl.when(place_ref[0] == half)
        def _():
            keep_ref[c : c + width, :] = block

        @pl.when(place_ref[0] != half)
        def _():
            send_ref[c : c + width, :] = block.astype(BF16)

    w_in_grad = lax.dot_general(normed_s[...], ghid_s[...], first, preferred_element_type=F32)
    for c in range(0, hidden_units, width):
        store_block(0, c, w_in_grad[:, c : c + width])
    w_out_grad = lax.dot_general(act_s[...], gmix_s[...], first, preferred_element_type=F32)
    for c in range(0, hidden_units, width):
        store_block(1, c, w_out_grad[c : c + width])


def grads_kernel(
    own_ref, top_ref, bottom_ref, gconv_ref, kern_ref, hsum_ref, chan_ref, small_ref, part_ref,
    nat, spread, grads, taps, sums, total,
):
    height, breadth, channels = own_ref.shape
    halves = channels // LANES
    steps, cells = dims_of(breadth)
    for r in range(EDGE):
        spread_row(top_ref[r], nat, spread, r, halves, breadth)
        spread_row(bottom_ref[r], nat, spread, EDGE + height + r, halves, breadth)

    def spread_own(p, carry):
        spread_row(own_ref[p], nat, spread, EDGE + p, halves, breadth)
        spread_row(gconv_ref[p], nat, grads, p, halves, breadth)
        return carry

    lax.fori_loop(0, height, spread_own, 0)
    own_conv_rows(grads, taps, kern_ref, part_ref, height, steps, halves, True)
    sublane = lax.broadcasted_iota(jnp.int32, (SUBS, LANES), 0)

    def grad_at(h, p, t):
        grad = grads[h, p, EDGE + t]
        for s in range(SUBS):
            if s * steps + t >= breadth:
                grad = jnp.where(sublane == s, 0.0, grad)
        return grad

    def tap_body(i, carry):
        total = [[None] * 7 for _ in range(halves)]
        for p in range(height):
            window = [[spread[h, p + i, t] for t in range(6)] for h in range(halves)]
            for t in range(steps):
                for h in range(halves):
                    window[h].append(spread[h, p + i, t + 6])
                    grad = grad_at(h, p, t)
                    for j in range(7):
                        term = window[h][t + j] * grad
                        total[h][j] = term if total[h][j] is None else total[h][j] + term
        for h in range(halves):
            for j in range(7):
                sums[h, i * 7 + j] = jnp.sum(total[h][j], axis=0, keepdims=True)
        return carry

    lax.fori_loop(0, 7, tap_body, 0)
    total[...] = jnp.zeros_like(total)
    for h in range(halves):
        total[0:49, h * LANES : (h + 1) * LANES] = sums[h].reshape(49, LANES)
    rows = hsum_ref.shape[1] // channels
    at = 49
    for c in range(rows):
        total[at + c : at + c + 1, :] = jnp.sum(hsum_ref[:, c * channels : (c + 1) * channels], axis=0, keepdims=True)
    at += rows
    for c in range(5):
        total[at + c : at + c + 1, :] = jnp.sum(chan_ref[c], axis=0, keepdims=True)
    small_ref[...] = total[...]


def input_grad_kernel(top_ref, bottom_ref, part_ref, kern_ref, cot_ref, grad_ref, nat, spread, taps):
    height, breadth, channels = cot_ref.shape
    halves = channels // LANES
    steps, cells = dims_of(breadth)
    fill_taps(kern_ref, taps, halves, True)
    for r in range(EDGE):
        spread_row(top_ref[r], nat, spread, r, halves, breadth)
        spread_row(bottom_ref[r], nat, spread, EDGE + r, halves, breadth)
    n_runs, length = runs_of(steps)
    for p in range(height):

        def run_body(index, carry, p=p):
            h = index // n_runs
            start = (index % n_runs) * length
            base = p * steps + start
            total = conv_run(
                lambda slot, u: spread[h, slot, start + u],
                taps,
                h,
                halo_taps(p, height),
                length,
                [part_ref[h, base + t] for t in range(length)],
            )
            for t in range(length):
                nat[h, pl.ds(SUBS + start + t, SUBS, stride=steps), :] = total[t]
            return carry

        lax.fori_loop(0, halves * n_runs, run_body, 0)
        for h in range(halves):
            lanes = slice(h * LANES, (h + 1) * LANES)
            grad_ref[p, :, lanes] = (cot_ref[p, :, lanes].astype(F32) + gather_row(nat, h, breadth)).astype(BF16)


def call(kernel, out_shape, scratch, flops, nbytes, name, limit=VMEM_LIMIT, late=()):
    def run(*operands):
        whole = pl.BlockSpec(memory_space=pltpu.VMEM)
        scalars = pl.BlockSpec(memory_space=pltpu.SMEM)
        return pl.pallas_call(
            kernel,
            out_shape=out_shape,
            in_specs=[
                pl.BlockSpec(memory_space=pl.ANY) if n in late else scalars if x.dtype == jnp.int32 else whole
                for n, x in enumerate(operands)
            ],
            out_specs=jax.tree.map(lambda _: whole, out_shape),
            scratch_shapes=scratch,
            compiler_params=pltpu.CompilerParams(vmem_limit_bytes=limit),
            cost_estimate=pl.CostEstimate(flops=flops, bytes_accessed=nbytes, transcendentals=0),
            name=name,
        )(*operands)

    return run


def place_kernel(digits, rows, factor, place_ref, here_ref, across_ref, other_ref, other_across_ref, *rest):
    w_in_ref, w_out_ref, kernel_ref, hidden_ref, chan_ref, total = rest
    channels = here_ref.shape[1]
    order = [[]]
    for stride, size in digits[1:]:
        order = [tail + [k] for k in range(size) for tail in order]
    share = (here_ref.shape[0] - SMALL) // len(order)
    draw = place_ref[0]
    small = jnp.zeros((SMALL, channels), F32)
    for flip, refs in ((0, (here_ref, across_ref)), (1, (other_ref, other_across_ref))):
        for last, ref in enumerate(refs):
            values = ref[...].astype(F32)
            small = small + values[-SMALL:]
            for n, ks in enumerate(order):
                extent = rows
                start = 0
                for d, (stride, size) in enumerate(digits):
                    extent = extent // size
                    k = ks[d - 1] if d else last
                    start = start + (place_ref[1 + d] ^ k) * extent
                start = pl.multiple_of(start, SUBS)
                total[draw ^ flip, pl.ds(start, share), :] = values[n * share : (n + 1) * share]
    big = w_out_ref.shape[0]
    for c in range(big // channels):
        cols = slice(c * channels, (c + 1) * channels)
        w_in_ref[:, cols] = total[0, cols, :] * factor
    w_out_ref[...] = total[1, 0:big, :] * factor
    small = small * factor
    for i in range(7):
        kernel_ref[i] = small[i * 7 : i * 7 + 7]
    blocks = big // channels
    halves = channels // LANES
    for c in range(blocks):
        for h in range(halves):
            hidden_ref[c * halves + h : c * halves + h + 1, :] = small[49 + c : 50 + c, h * LANES : (h + 1) * LANES]
    chan_ref[...] = small[49 + blocks : 54 + blocks]


def digits_of(count):
    digits = []
    stride = 2
    while stride < count:
        size = min(4, count // stride)
        digits.append((stride, size))
        stride *= size
    return [(1, 2)] + digits[::-1]


def exchange(values, count, stride, size, k):
    pairs = []
    for i in range(count):
        digit = i // stride % size
        pairs.append((i, i + ((digit ^ k) - digit) * stride))
    return lax.ppermute(values, "tile", pairs)


def other_core(values, draws):
    return lax.ppermute(values, "draw", [(i, i ^ 1) for i in range(draws)])


def halo(cells, tiles):
    after = [(i, i + 1) for i in range(tiles - 1)]
    before = [(i + 1, i) for i in range(tiles - 1)]
    top = lax.ppermute(cells[-EDGE:], "tile", after)
    bottom = lax.ppermute(cells[:EDGE], "tile", before)
    return top, bottom


def per_device(
    tiles,
    draws,
    inputs,
    land_mask,
    kernel,
    conv_bias,
    norm_gain,
    norm_bias,
    w_in,
    b_in,
    w_out,
    b_out,
    layer_scale,
    cotangent,
):
    _, height, breadth, channels = inputs.shape
    hidden_units = w_in.shape[1]
    halves = channels // LANES
    steps, cells = dims_of(breadth)
    own = inputs[0]
    cot = cotangent[0]
    top, bottom = halo(own, tiles)
    mask = jnp.pad(land_mask.astype(F32), ((0, 0), (0, cells - breadth)))
    mask = mask.reshape(height, SUBS, steps)

    def row(vector):
        return vector.reshape(1, -1)

    nat = pltpu.VMEM((halves, cells + 6 * SUBS, LANES), F32)

    def spread(slots):
        return pltpu.VMEM((halves, slots, steps + 2 * EDGE, SUBS, LANES), F32)

    taps = pltpu.VMEM((halves, 49, SUBS, LANES), F32)
    big_row = pltpu.VMEM((2 * cells, channels), F32)
    narrow = pltpu.VMEM((2 * cells, LANES), F32)
    count = height * cells
    big = hidden_units
    digits = digits_of(tiles)
    unit = tiles * SUBS
    rows = -(-big // unit) * unit
    tile = lax.axis_index("tile")
    place = jnp.stack([lax.axis_index("draw")] + [tile // stride % size for stride, size in digits]).astype(jnp.int32)
    part_shape = jax.ShapeDtypeStruct((halves, height * steps, SUBS, LANES), F32)
    mega = 1024 * 1024

    part = call(own_conv_kernel, part_shape, [nat, spread(height), taps], 1, 1, "own_conv")(own, kernel)
    out, gconv, keep, send, hsum, chan = call(
        main_kernel,
        (
            jax.ShapeDtypeStruct((height, breadth, channels), BF16),
            jax.ShapeDtypeStruct((height, breadth, channels), BF16),
            jax.ShapeDtypeStruct((big, channels), F32),
            jax.ShapeDtypeStruct((big, channels), BF16),
            jax.ShapeDtypeStruct((SUBS, hidden_units), F32),
            jax.ShapeDtypeStruct((5, SUBS, channels), F32),
        ),
        [
            nat,
            nat,
            spread(2 * EDGE),
            taps,
            pltpu.VMEM((halves, count, LANES), F32),
            big_row,
            big_row,
            big_row,
            big_row,
            big_row,
            narrow,
            narrow,
            pltpu.VMEM((count, channels), BF16),
            pltpu.VMEM((count, hidden_units), BF16),
            pltpu.VMEM((count, channels), BF16),
            pltpu.VMEM((count, hidden_units), BF16),
            pltpu.VMEM((height, breadth, channels), BF16),
            pltpu.VMEM((height, breadth, channels), BF16),
            pltpu.VMEM((channels, hidden_units), BF16),
            pltpu.VMEM((hidden_units, channels), BF16),
            pltpu.SemaphoreType.DMA((4,)),
        ],
        12 * count * channels * hidden_units,
        8 * mega,
        "block_main",
        late=(1, 5, 11, 13),
    )(
        place, own, top, bottom, part, cot, mask, kernel, row(conv_bias), row(norm_gain), row(norm_bias), w_in, row(b_in),
        w_out, row(b_out), row(layer_scale),
    )
    got = other_core(send, draws)

    if rows > big:
        keep = jnp.pad(keep, ((0, rows - big), (0, 0)))
        got = jnp.pad(got, ((0, rows - big), (0, 0)))
    for step, (stride, size) in enumerate(digits):
        share = keep.shape[0] // size
        mine = place[1 + step]
        pieces = []
        for k in range(size):
            piece = lax.dynamic_slice_in_dim(keep, (mine ^ k) * share, share, 0)
            if not step:
                piece = piece + lax.dynamic_slice_in_dim(got, (mine ^ k) * share, share, 0).astype(F32)
            pieces.append(piece)
        sends = [piece.astype(BF16) for piece in pieces[1:]]
        if not step:
            sends, gconv, hsum = lax.optimization_barrier((sends, gconv, hsum))
            grad_top, grad_bottom = halo(gconv, tiles)
            small, grad_part = call(
                grads_kernel,
                (jax.ShapeDtypeStruct((SMALL, channels), F32), part_shape),
                [
                    nat,
                    spread(height + 2 * EDGE),
                    spread(height),
                    taps,
                    pltpu.VMEM((halves, 49, 1, LANES), F32),
                    pltpu.VMEM((SMALL, channels), F32),
                ],
                1,
                1,
                "kernel_grad",
            )(own, top, bottom, gconv, kernel, hsum, chan)
        received = [exchange(sends[k - 1], tiles, stride, size, k) for k in range(1, size)]
        if not step:
            received, small, grad_part = lax.optimization_barrier((received, small, grad_part))
        elif step == 1:
            received, grad_top, grad_bottom = lax.optimization_barrier((received, grad_top, grad_bottom))
        keep = pieces[0]
        for piece in received:
            keep = keep + piece.astype(F32)
    gathered = keep.astype(BF16)
    for stride, size in digits[1:]:
        payload = jnp.concatenate([gathered, small.astype(BF16)], axis=0)
        if (stride, size) == digits[1]:
            payload, grad_part = lax.optimization_barrier((payload, grad_part))
            input_grad = call(
                input_grad_kernel,
                jax.ShapeDtypeStruct((height, breadth, channels), BF16),
                [nat, spread(2 * EDGE), taps],
                1,
                1,
                "input_grad",
            )(grad_top, grad_bottom, grad_part, kernel, cot)
        received = [payload] + [exchange(payload, tiles, stride, size, k) for k in range(1, size)]
        if (stride, size) == digits[1]:
            received, input_grad = lax.optimization_barrier((received, input_grad))
        gathered = jnp.concatenate([piece[:-SMALL] for piece in received], axis=0)
        small = functools.reduce(jnp.add, [piece[-SMALL:].astype(F32) for piece in received])
    gathered = jnp.concatenate([gathered, small.astype(BF16)], axis=0)
    stride, size = digits[0]
    across = exchange(gathered, tiles, stride, size, 1)
    other = other_core(gathered, draws)
    lon_first = Layout((0, 2, 1, 3))
    out = with_layout_constraint(out[None], lon_first)
    input_grad = with_layout_constraint(input_grad[None], lon_first)
    across, out, input_grad = lax.optimization_barrier((across, out, input_grad))
    other_across = other_core(across, draws)
    factor = float(1.0 / np.sqrt(np.float32(draws * height * tiles * breadth)))
    w_in_sum, w_out_sum, kernel_sum, hidden_sum, chan_sum = call(
        functools.partial(place_kernel, digits, rows, factor),
        (
            jax.ShapeDtypeStruct((channels, hidden_units), F32),
            jax.ShapeDtypeStruct((hidden_units, channels), F32),
            jax.ShapeDtypeStruct((7, 7, channels), F32),
            jax.ShapeDtypeStruct((hidden_units // LANES, LANES), F32),
            jax.ShapeDtypeStruct((5, channels), F32),
        ),
        [pltpu.VMEM((2, rows, channels), F32)],
        mega,
        4 * mega,
        "place",
        16 * mega,
    )(place, gathered, across, other, other_across)
    return (
        out,
        input_grad,
        kernel_sum,
        w_in_sum,
        w_out_sum,
        hidden_sum.reshape(-1),
        chan_sum,
    )


def solution(mesh):
    placed = (
        P(("group", "draw"), "tile", None, None),
        P("tile", None),
        P(),
        P(),
        P(),
        P(),
        P(),
        P(),
        P(),
        P(),
        P(),
        P(("group", "draw"), "tile", None, None),
    )
    return jax.shard_map(
        functools.partial(per_device, mesh.shape["tile"], mesh.shape["draw"]),
        mesh=mesh,
        in_specs=placed,
        out_specs=(
            P(("group", "draw"), "tile", None, None),
            P(("group", "draw"), "tile", None, None),
            P("group", None, None),
            P("group", None),
            P("group", None),
            P("group"),
            P("group", None),
        ),
        check_vma=False,
    )
```
